32 devices in a mesh: dp: 16 (over z, x, core), expert: 2 (over y).
Axes of the slice: x: 2, y: 2, z: 4, core: 2. Of those that a mesh axis runs over, the one named last changes fastest.
Arguments:
- tokens: bfloat16 [2, 3584, 1536], P('expert', 'dp'), may hold values from -6 to 6
- attn_gain: bfloat16 [1536], P('dp'), may hold values from 0.099609375 to 1.8984375
- query_weight: bfloat16 [1536, 1536], P('dp'), may hold values from -0.15625 to 0.15625
- key_weight: bfloat16 [1536, 256], P('dp'), may hold values from -0.15625 to 0.15625
- value_weight: bfloat16 [1536, 256], P('dp'), may hold values from -0.15625 to 0.15625
- out_weight: bfloat16 [1536, 1536], P('dp'), may hold values from -0.875 to 0.875
- moe_gain: bfloat16 [1536], P('dp'), may hold values from 0.099609375 to 1.8984375
- router_weight: bfloat16 [1536, 32], P('dp'), may hold values from -0.063964844 to 0.063964844
- gate_weight: bfloat16 [32, 1536, 768], P('expert', 'dp'), may hold values from -0.15625 to 0.15625
- up_weight: bfloat16 [32, 1536, 768], P('expert', 'dp'), may hold values from -0.15625 to 0.15625
- down_weight: bfloat16 [32, 768, 1536], P('expert', 'dp'), may hold values from -0.4375 to 0.4375
- parents: int32 [2, 16], P('expert'), may hold values from 0 to 14, as said below
- routes: int32 [2, 3584, 4], P('expert', 'dp'), may hold values from 0 to 31, all different within a row
- claim_order: int32 [2, 16, 896], P('expert', 'dp'), may hold values from 0 to 895, each once within a row
- cotangent: bfloat16 [2, 3584, 1536], P('expert', 'dp'), may hold values from -6 to 6
Outputs:
- block_out: bfloat16 [2, 3584, 1536], P('expert', 'dp')
- grad_tokens: float32 [2, 3584, 1536], P('expert', 'dp')
- grad_attn_gain: float32 [1536], P('dp')
- grad_query: float32 [1536, 1536], P('dp')
- grad_key: float32 [1536, 256], P('dp')
- grad_value: float32 [1536, 256], P('dp')
- grad_out: float32 [1536, 1536], P('dp')
- grad_moe_gain: float32 [1536], P('dp')
- grad_router: float32 [1536, 32], P('dp')
- grad_gate: float32 [32, 1536, 768], P('expert', 'dp')
- grad_up: float32 [32, 1536, 768], P('expert', 'dp')
- grad_down: float32 [32, 768, 1536], P('expert', 'dp')
The draws below stay inside these ranges and needn't reach their ends.
Inputs may be any that keep to these rules, and one draw needn't show every extreme that they name: parents[g, 0] = 0 and parents[g, s] < s for s >= 1. `routes`: each token names 4 different experts. `claim_order`: within each segment a permutation of its pairs, numbered token * 4 + choice within the segment.
All inputs are finite; a program needn't handle non-finite values.
Results may differ from the reference program's by a relative error of at most 0.024.
Values may be sent and summed in bfloat16 or wider, within the bound.
A program may use at most 384 MiB of HBM per device.

```python
import jax
import jax.numpy as jnp
from jax import lax

D = 1536
HEADS = 12
KV_HEADS = 2
HEAD = 128
EXPERTS = 32
FF = 768
TOP = 4
TOK_DEV = 224
GROUPS = 2
GROUP_TOK = 3584
CAP = 28
PAIRS = 896
N_DP = 16


def draw_parents(key, part):
    key = jax.random.fold_in(key, 17)
    labels = jnp.arange(N_DP, dtype=jnp.int32)
    trunk_end = N_DP // 4
    random_bits = jax.random.randint(key, (GROUPS, N_DP), 0, 1 << 20, dtype=jnp.int32)
    widths = jnp.maximum(labels - trunk_end, 1)
    picked = trunk_end + random_bits % widths[None, :]
    chained = jnp.maximum(labels - 1, 0)
    settled = (labels <= trunk_end) | (labels == N_DP - 1)
    return jnp.where(settled[None, :], chained[None, :], picked).astype(jnp.int32)


def levels(stream_key, dims, shards, smallest, largest):
    def one(axis_at, shards_of):
        heights = jax.random.uniform(jax.random.fold_in(jax.random.fold_in(stream_key, 6), axis_at), (shards_of,), jnp.float32, smallest / len(shards), largest / len(shards))
        return jnp.repeat(jnp.exp(heights), dims[axis_at] // shards_of).reshape((-1,) + (1,) * (len(dims) - axis_at - 1))

    factor_of = one(*shards[0])
    for cut in shards[1:]:
        factor_of = factor_of * one(*cut)
    return factor_of


def different_ones(key, rows, number_of, top, lift):
    ranking = jax.random.permutation(jax.random.fold_in(key, 1), number_of)
    pull = ranking
    for power in range(3):
        pull = pull * pull // number_of
    pull = pull * lift // number_of
    chance = jax.random.randint(jax.random.fold_in(key, 2), (rows, number_of), 0, 4096) + pull
    sure = jax.random.permutation(jax.random.fold_in(key, 3), rows)[jnp.arange(number_of) % rows]
    chance = jnp.where(jnp.arange(rows)[:, None] == sure[None, :], 1 << 14, chance)
    merit = chance * number_of + jnp.arange(number_of)
    return lax.top_k(merit.astype(jnp.int32), top)[1].astype(jnp.int32)


def gaussian(own_key, dims, deviation, most, cuts=(), kind=jnp.bfloat16):
    values = deviation * jax.random.normal(own_key, dims, jnp.float32)
    if cuts:
        values = values * levels(own_key, dims, cuts, -0.22, 0.18)
    return jnp.clip(values, -most, most).astype(kind)


def setup_inputs(seed: int = 0) -> dict:
    arg_keys = jax.random.split(jax.random.key(seed), 16)
    return {
        "tokens": gaussian(arg_keys[0], (GROUPS, GROUP_TOK, D), 1.0, 6.0, ((0, 2), (1, 16))),
        "attn_gain": jnp.clip(1.0 + 0.18 * jax.random.normal(arg_keys[1], (D,), jnp.float32), 0.099609375, 1.8984375).astype(jnp.bfloat16),
        "query_weight": gaussian(arg_keys[2], (D, D), D ** -0.5, 0.15625, ((0, 16),)),
        "key_weight": gaussian(arg_keys[3], (D, KV_HEADS * HEAD), D ** -0.5, 0.15625, ((0, 16),)),
        "value_weight": gaussian(arg_keys[4], (D, KV_HEADS * HEAD), D ** -0.5, 0.15625, ((0, 16),)),
        "out_weight": gaussian(arg_keys[5], (D, D), (D // 32) ** -0.5, 0.875, ((0, 16),)),
        "moe_gain": jnp.clip(1.0 + 0.18 * jax.random.normal(arg_keys[6], (D,), jnp.float32), 0.099609375, 1.8984375).astype(jnp.bfloat16),
        "router_weight": gaussian(arg_keys[7], (D, EXPERTS), 0.0128, 0.063964844, ((0, 16),)),
        "gate_weight": gaussian(arg_keys[8], (EXPERTS, D, FF), D ** -0.5, 0.15625, ((0, 2), (1, 16))),
        "up_weight": gaussian(arg_keys[9], (EXPERTS, D, FF), D ** -0.5, 0.15625, ((0, 2), (1, 16))),
        "down_weight": gaussian(arg_keys[10], (EXPERTS, FF, D), (FF // 4) ** -0.5, 0.4375, ((0, 2), (1, 16))),
        "parents": draw_parents(jax.random.fold_in(arg_keys[15], 71), 0),
        "routes": different_ones(arg_keys[12], GROUPS * GROUP_TOK, EXPERTS, TOP, 1024).reshape((GROUPS, GROUP_TOK, TOP)),
        "claim_order": jax.vmap(lambda own: jax.random.permutation(own, PAIRS))(jax.random.split(arg_keys[13], GROUPS * N_DP)).reshape((GROUPS, N_DP, PAIRS)).astype(jnp.int32),
        "cotangent": gaussian(arg_keys[14], (GROUPS, GROUP_TOK, D), 1.0, 6.0, ((0, 2), (1, 16))),
    }


epsilon = 1e-06
theta = 10000.0
block_rows = 256
highest = lax.Precision.HIGHEST

@jax.custom_vjp
def low(v):
    return lax.optimization_barrier(v.astype(jnp.bfloat16)).astype(jnp.float32)

@jax.custom_vjp
def low_back(v):
    return v

def low_keep(v):
    return (low(v), None)

def low_pass(kept, grad):
    return (grad,)

def back_keep(v):
    return (v, None)

def back_low(kept, grad):
    return (low(grad),)
low.defvjp(low_keep, low_pass)
low_back.defvjp(back_keep, back_low)

def ancestry(parents):
    row_count = parents.shape[0]
    labels = jnp.arange(row_count, dtype=jnp.int32)
    linked = (parents[:, None] == labels[None, :]).astype(jnp.float32)
    reach_all = jnp.minimum(jnp.eye(row_count, dtype=jnp.float32) + linked, 1.0)
    for doubling in range(max(1, (row_count - 1).bit_length())):
        reach_all = jnp.minimum(jnp.dot(reach_all, reach_all, precision=highest), 1.0)
    return reach_all

def rope_tables(positions, head_size):
    halfway = head_size // 2
    frequency = theta ** (-jnp.arange(halfway, dtype=jnp.float32) * 2.0 / head_size)
    angles = positions[:, None] * frequency[None, :]
    return (jnp.cos(angles)[:, None, :], jnp.sin(angles)[:, None, :])

def rotate(values, cosine, sine_part):
    halfway = values.shape[-1] // 2
    first_half = values[..., :halfway]
    second = values[..., halfway:]
    return jnp.concatenate([first_half * cosine - second * sine_part, second * cosine + first_half * sine_part], axis=-1)

def attention_paths(query_rot, key_rot, value_rows, reach_all):
    row_count = query_rot.shape[0]
    repeat_heads = HEADS // KV_HEADS
    blocks = row_count // block_rows
    queries = query_rot.reshape(blocks, block_rows, KV_HEADS, repeat_heads, HEAD)
    starts = jnp.arange(blocks, dtype=jnp.int32) * block_rows
    key_index = jnp.arange(row_count, dtype=jnp.int32)
    key_segment = key_index // TOK_DEV

    def one_block(inputs_block):
        query_block, block_start = inputs_block
        query_index = block_start + jnp.arange(block_rows, dtype=jnp.int32)
        query_segment = query_index // TOK_DEV
        ancestor = reach_all[query_segment][:, key_segment] > 0.5
        allowed = ancestor & ((query_segment[:, None] != key_segment[None, :]) | (key_index[None, :] <= query_index[:, None]))
        scores = low_back(jnp.einsum('qgrh,kgh->grqk', query_block, key_rot, precision=highest) * HEAD ** (-0.5))
        scores = jnp.where(allowed[None, None], scores, -1000000000.0)
        prob_block = jax.nn.softmax(scores, axis=-1)
        return jnp.einsum('grqk,kgh->qgrh', low(prob_block), value_rows, precision=highest)
    attended = lax.map(jax.checkpoint(one_block), (queries, starts))
    return attended.reshape(row_count, HEADS * HEAD)

def slot_plan(expert_ids, claim_order):
    pair_count = expert_ids.shape[0]
    member = (expert_ids[:, None] == jnp.arange(EXPERTS, dtype=jnp.int32)[None, :]).astype(jnp.float32)
    earlier = (claim_order[None, :] < claim_order[:, None]).astype(jnp.float32)
    before = jnp.dot(earlier, member, precision=highest)
    slot_index = lax.optimization_barrier(jnp.sum(before * member, axis=1)).astype(jnp.int32)
    target = jnp.where(slot_index < CAP, expert_ids * CAP + slot_index, EXPERTS * CAP)
    slot_pairs = jnp.full((EXPERTS * CAP + 1,), pair_count, jnp.int32).at[target].set(jnp.arange(pair_count, dtype=jnp.int32))
    return (slot_pairs[:EXPERTS * CAP], target)

def gather_rows(block, index):
    return block[index]

def group_forward(inputs, params, parents, routes, claim_order):
    attn_gain, query_weight, key_weight, value_weight, out_weight, moe_gain, router_weight, gate_weight, up_weight, down_weight = params
    row_count = inputs.shape[0]
    reach_all = ancestry(parents)
    path_depth = lax.optimization_barrier(jnp.sum(reach_all, axis=1)) - 1.0
    index = jnp.arange(row_count, dtype=jnp.int32)
    segment_of = index // TOK_DEV
    positions = path_depth[segment_of] * TOK_DEV + (index - segment_of * TOK_DEV).astype(jnp.float32)
    scale_one = lax.rsqrt(lax.optimization_barrier(jnp.mean(inputs * inputs, axis=-1, keepdims=True)) + epsilon)
    hidden_one = low(inputs * scale_one * attn_gain)
    query_raw = low_back(jnp.dot(hidden_one, query_weight, precision=highest))
    key_raw = low_back(jnp.dot(hidden_one, key_weight, precision=highest))
    value_low = low(low_back(jnp.dot(hidden_one, value_weight, precision=highest)))
    cosine, sine_part = rope_tables(positions, HEAD)
    query_rot = low(rotate(query_raw.reshape(row_count, HEADS, HEAD), cosine, sine_part))
    key_rot = low(rotate(key_raw.reshape(row_count, KV_HEADS, HEAD), cosine, sine_part))
    attended = attention_paths(query_rot, key_rot, value_low.reshape(row_count, KV_HEADS, HEAD), reach_all)
    attended = low(low_back(attended))
    branch = low_back(jnp.dot(attended, out_weight, precision=highest))
    middle = inputs + branch
    scale_two = lax.rsqrt(lax.optimization_barrier(jnp.mean(middle * middle, axis=-1, keepdims=True)) + epsilon)
    hidden_two = low(middle * scale_two * moe_gain)
    logits = low_back(jnp.dot(hidden_two, router_weight, precision=highest))
    chosen = jnp.take_along_axis(logits, routes, axis=1)
    gate_probs = jax.nn.softmax(chosen, axis=-1)
    slot_pairs, targets = jax.vmap(slot_plan)(routes.reshape(N_DP, PAIRS), claim_order)
    device_rows = hidden_two.reshape(N_DP, TOK_DEV, D)
    padded = jnp.concatenate([device_rows, jnp.zeros((N_DP, 1, D), jnp.float32)], axis=1)
    rows = jax.vmap(gather_rows)(padded, slot_pairs // TOP)
    rows = low_back(rows.reshape(N_DP, EXPERTS, CAP, D).transpose(1, 0, 2, 3).reshape(EXPERTS, N_DP * CAP, D))
    gate_act = low_back(jnp.einsum('erd,edf->erf', rows, gate_weight, precision=highest))
    up_act = low_back(jnp.einsum('erd,edf->erf', rows, up_weight, precision=highest))
    inner = low(jax.nn.silu(gate_act) * up_act)
    expert_out = low(low_back(jnp.einsum('erf,efd->erd', inner, down_weight, precision=highest)))
    returned = expert_out.reshape(EXPERTS, N_DP, CAP, D).transpose(1, 0, 2, 3).reshape(N_DP, EXPERTS * CAP, D)
    returned = jnp.concatenate([returned, jnp.zeros((N_DP, 1, D), jnp.float32)], axis=1)
    pair_out = jax.vmap(gather_rows)(returned, targets).reshape(row_count, TOP, D)
    mixture = lax.optimization_barrier(jnp.sum(gate_probs[:, :, None] * pair_out, axis=1))
    return middle + mixture

def reference(tokens, attn_gain, query_weight, key_weight, value_weight, out_weight, moe_gain, router_weight, gate_weight, up_weight, down_weight, parents, routes, claim_order, cotangent):
    weights = tuple((weight.astype(jnp.float32) for weight in (attn_gain, query_weight, key_weight, value_weight, out_weight, moe_gain, router_weight, gate_weight, up_weight, down_weight)))

    def one_group(totals, group):
        group_tokens, group_parents, group_routes, group_order, group_cotangent = group

        def forward(inputs, params):
            return group_forward(inputs, params, group_parents, group_routes, group_order)
        result, pullback = jax.vjp(forward, group_tokens, weights)
        grad_inputs, grad_weights = pullback(group_cotangent)
        totals = jax.tree.map(jnp.add, totals, grad_weights)
        return (totals, (result.astype(jnp.bfloat16), grad_inputs))
    zeros = jax.tree.map(jnp.zeros_like, weights)
    totals, (block_out, grad_tokens) = lax.scan(one_group, zeros, (tokens.astype(jnp.float32), parents, routes, claim_order, cotangent.astype(jnp.float32)))
    return (block_out, grad_tokens, totals[0], totals[1], totals[2], totals[3], totals[4], totals[5], totals[6], totals[7], totals[8], totals[9])
```

```python
import functools

import jax
import jax.numpy as jnp
from jax import lax
from jax.experimental import pallas as pl
from jax.experimental.pallas import tpu as pltpu
from jax.sharding import PartitionSpec as P

HEADS = 12
KV_HEADS = 2
HEAD = 128
EXPERTS = 32
TOP = 4
CAP = 28


epsilon = 1e-06
theta = 10000.0
highest = lax.Precision.HIGHEST


def ancestry(parents):
    row_count = parents.shape[0]
    labels = jnp.arange(row_count, dtype=jnp.int32)
    linked = (parents[:, None] == labels[None, :]).astype(jnp.float32)
    reach_all = jnp.minimum(jnp.eye(row_count, dtype=jnp.float32) + linked, 1.0)
    for doubling in range(max(1, (row_count - 1).bit_length())):
        reach_all = jnp.minimum(jnp.dot(reach_all, reach_all, precision=highest), 1.0)
    return reach_all


def rope_tables(positions, head_size):
    halfway = head_size // 2
    frequency = theta ** (-jnp.arange(halfway, dtype=jnp.float32) * 2.0 / head_size)
    angles = positions[:, None] * frequency[None, :]
    return (jnp.cos(angles)[:, None, :], jnp.sin(angles)[:, None, :])


def rotate(values, cosine, sine_part):
    halfway = values.shape[-1] // 2
    first_half = values[..., :halfway]
    second = values[..., halfway:]
    return jnp.concatenate(
        [first_half * cosine - second * sine_part, second * cosine + first_half * sine_part],
        axis=-1,
    )


def norm_backward(grad_hidden, normed, row_scale, gain):
    grad_normed = grad_hidden * gain
    grad_gain = jnp.sum(grad_hidden * normed, axis=0)
    grad_rows = row_scale * (
        grad_normed - normed * jnp.mean(grad_normed * normed, axis=-1, keepdims=True)
    )
    return (grad_rows, grad_gain)


def local_gathered(
    tokens,
    attn_gain,
    query_weight,
    key_weight,
    value_weight,
    out_weight,
    moe_gain,
    router_weight,
    gate_weight,
    up_weight,
    down_weight,
    parents,
    routes,
    claim_order,
    cotangent,
):
    (
        gain_one,
        query_full,
        key_full,
        value_full,
        out_full,
        gain_two,
        router_full,
        gate_full,
        up_full,
        down_full,
    ) = (
        lax.all_gather(attn_gain, "dp", axis=0, tiled=True),
        lax.all_gather(query_weight, "dp", axis=0, tiled=True),
        lax.all_gather(key_weight, "dp", axis=0, tiled=True),
        lax.all_gather(value_weight, "dp", axis=0, tiled=True),
        lax.all_gather(out_weight, "dp", axis=0, tiled=True),
        lax.all_gather(moe_gain, "dp", axis=0, tiled=True),
        lax.all_gather(router_weight, "dp", axis=0, tiled=True),
        lax.all_gather(gate_weight, "dp", axis=1, tiled=True),
        lax.all_gather(up_weight, "dp", axis=1, tiled=True),
        lax.all_gather(down_weight, "dp", axis=1, tiled=True),
    )
    tok_count = tokens.shape[1]
    model_width = tokens.shape[2]
    segment = lax.axis_index("dp")
    segment_count = lax.axis_size("dp")
    expert_peers = lax.axis_size("expert")
    local_experts = gate_weight.shape[0]
    repeat_heads = HEADS // KV_HEADS
    score_scale = HEAD ** (-0.5)
    query_rows = repeat_heads * tok_count
    reach_all = ancestry(parents[0])
    reach_row = reach_all[segment]
    path_depth = jnp.sum(reach_row) - 1.0
    positions = path_depth * tok_count + jnp.arange(tok_count, dtype=jnp.float32)
    cosine, sine_part = rope_tables(positions, HEAD)
    inputs = tokens[0].astype(jnp.float32)
    scale_one = lax.rsqrt(jnp.mean(inputs * inputs, axis=-1, keepdims=True) + epsilon)
    normed_one = inputs * scale_one
    gain_first = gain_one.astype(jnp.float32)
    hidden_one = (normed_one * gain_first).astype(jnp.bfloat16)
    query_raw = jnp.dot(hidden_one, query_full, preferred_element_type=jnp.float32).reshape(
        tok_count, HEADS, HEAD
    )
    key_raw = jnp.dot(hidden_one, key_full, preferred_element_type=jnp.float32).reshape(
        tok_count, KV_HEADS, HEAD
    )
    value_low = jnp.dot(hidden_one, value_full, preferred_element_type=jnp.float32).astype(
        jnp.bfloat16
    )
    query_rot = rotate(query_raw, cosine, sine_part).astype(jnp.bfloat16)
    key_rot = (
        rotate(key_raw, cosine, sine_part).astype(jnp.bfloat16).reshape(tok_count, KV_HEADS * HEAD)
    )
    key_all, value_all = (
        lax.all_gather(key_rot, "dp", axis=0, tiled=True),
        lax.all_gather(value_low, "dp", axis=0, tiled=True),
    )
    total_keys = key_all.shape[0]
    key_blocks = key_all.reshape(segment_count, tok_count, KV_HEADS, HEAD)
    value_blocks = value_all.reshape(segment_count, tok_count, KV_HEADS, HEAD)
    segment_labels = jnp.arange(segment_count, dtype=jnp.int32)
    query_groups = (
        query_rot.reshape(tok_count, KV_HEADS, repeat_heads, HEAD)
        .transpose(1, 2, 0, 3)
        .reshape(KV_HEADS, query_rows, HEAD)
    )
    query_offsets = jnp.arange(tok_count, dtype=jnp.int32)
    causal_tile = jnp.tile(query_offsets[None, :] <= query_offsets[:, None], (repeat_heads, 1))

    def scores_of(key_block, label):
        raw_scores = (
            jnp.einsum("grh,kgh->grk", query_groups, key_block, preferred_element_type=jnp.float32)
            * score_scale
        )
        allowed = causal_tile | (label != segment)
        return jnp.where(allowed[None], raw_scores, -1000000000.0)

    def on_path(label):
        return reach_row[label] > 0.5

    def pass_stats(state_pair, inputs_block):
        key_block, value_block, label = inputs_block

        def visit(state):
            row_max, row_sum = state
            scores = scores_of(key_block, label)
            new_max = jnp.maximum(row_max, jnp.max(scores, axis=-1))
            new_sum = row_sum * jnp.exp(row_max - new_max) + jnp.sum(
                jnp.exp(scores - new_max[..., None]), axis=-1
            )
            return (new_max, new_sum)

        return (lax.cond(on_path(label), visit, lambda state: state, state_pair), None)

    start_max = jnp.full((KV_HEADS, query_rows), -1e30, jnp.float32)
    start_sum = jnp.zeros((KV_HEADS, query_rows), jnp.float32)
    (row_max, row_sum), unused = lax.scan(
        pass_stats, (start_max, start_sum), (key_blocks, value_blocks, segment_labels)
    )

    def probs_of(key_block, label):
        return jnp.exp(scores_of(key_block, label) - row_max[..., None]) / row_sum[..., None]

    def pass_values(state_pair, inputs_block):
        key_block, value_block, label = inputs_block

        def visit(state):
            accumulated, exact_out = state
            prob_block = probs_of(key_block, label)
            accumulated = accumulated + jnp.einsum(
                "grk,kgh->grh",
                prob_block.astype(jnp.bfloat16),
                value_block,
                preferred_element_type=jnp.float32,
            )
            exact_out = exact_out + jnp.einsum(
                "grk,kgh->grh",
                prob_block,
                value_block.astype(jnp.float32),
                preferred_element_type=jnp.float32,
                precision=highest,
            )
            return (accumulated, exact_out)

        return (lax.cond(on_path(label), visit, lambda state: state, state_pair), None)

    zero_out = jnp.zeros((KV_HEADS, query_rows, HEAD), jnp.float32)
    (accumulated, exact_out), unused = lax.scan(
        pass_values, (zero_out, zero_out), (key_blocks, value_blocks, segment_labels)
    )
    attended = (
        accumulated.reshape(KV_HEADS, repeat_heads, tok_count, HEAD)
        .transpose(2, 0, 1, 3)
        .reshape(tok_count, HEADS * HEAD)
        .astype(jnp.bfloat16)
    )
    branch = jnp.dot(attended, out_full, preferred_element_type=jnp.float32)
    middle = inputs + branch
    scale_two = lax.rsqrt(jnp.mean(middle * middle, axis=-1, keepdims=True) + epsilon)
    normed_two = middle * scale_two
    gain_second = gain_two.astype(jnp.float32)
    hidden_two = (normed_two * gain_second).astype(jnp.bfloat16)
    logits = jnp.dot(hidden_two, router_full, preferred_element_type=jnp.float32)
    picked_one = (
        routes[0][:, :, None] == jnp.arange(EXPERTS, dtype=jnp.int32)[None, None, :]
    ).astype(jnp.float32)
    chosen = jnp.sum(picked_one * logits[:, None, :], axis=-1)
    gate_probs = jax.nn.softmax(chosen, axis=-1)
    expert_ids = routes[0].reshape(-1)
    order_row = claim_order[0, 0]
    pair_count = expert_ids.shape[0]
    member = (expert_ids[:, None] == jnp.arange(EXPERTS, dtype=jnp.int32)[None, :]).astype(
        jnp.bfloat16
    )
    earlier = (order_row[None, :] < order_row[:, None]).astype(jnp.bfloat16)
    before = jnp.dot(earlier, member, preferred_element_type=jnp.float32)
    slot_index = jnp.sum(before * member.astype(jnp.float32), axis=1).astype(jnp.int32)
    owner_rank = expert_ids // local_experts
    local_rank = expert_ids % local_experts
    target = jnp.where(
        slot_index < CAP, (local_rank * expert_peers + owner_rank) * CAP + slot_index, EXPERTS * CAP
    )
    slot_pairs = (
        jnp.full((EXPERTS * CAP + 1,), pair_count, jnp.int32)
        .at[target]
        .set(jnp.arange(pair_count, dtype=jnp.int32))[: EXPERTS * CAP]
    )
    padded_two = jnp.concatenate([hidden_two, jnp.zeros((1, model_width), jnp.bfloat16)], axis=0)
    send_rows = padded_two[slot_pairs // TOP].reshape(local_experts, expert_peers, CAP, model_width)
    arrived = lax.all_to_all(send_rows, "expert", split_axis=1, concat_axis=1, tiled=True)
    expert_rows = arrived.reshape(local_experts, expert_peers * CAP, model_width)
    gate_act = jnp.einsum(
        "erd,edf->erf", expert_rows, gate_full, preferred_element_type=jnp.float32
    )
    up_act = jnp.einsum("erd,edf->erf", expert_rows, up_full, preferred_element_type=jnp.float32)
    inner = (jax.nn.silu(gate_act) * up_act).astype(jnp.bfloat16)
    expert_out = jnp.einsum(
        "erf,efd->erd", inner, down_full, preferred_element_type=jnp.float32
    ).astype(jnp.bfloat16)
    returned = lax.all_to_all(
        expert_out.reshape(local_experts, expert_peers, CAP, model_width),
        "expert",
        split_axis=1,
        concat_axis=1,
        tiled=True,
    )
    returned = jnp.concatenate(
        [returned.reshape(EXPERTS * CAP, model_width), jnp.zeros((1, model_width), jnp.bfloat16)],
        axis=0,
    )
    pair_out = returned[target].reshape(tok_count, TOP, model_width).astype(jnp.float32)
    mixture = jnp.sum(gate_probs[:, :, None] * pair_out, axis=1)
    block_out = (middle + mixture).astype(jnp.bfloat16)
    grad_result = cotangent[0].astype(jnp.float32)
    grad_gates = jnp.sum(pair_out * grad_result[:, None, :], axis=-1)
    grad_pairs = (
        (gate_probs[:, :, None] * grad_result[:, None, :])
        .astype(jnp.bfloat16)
        .reshape(pair_count, model_width)
    )
    grad_padded = jnp.concatenate([grad_pairs, jnp.zeros((1, model_width), jnp.bfloat16)], axis=0)
    grad_send = grad_padded[slot_pairs].reshape(local_experts, expert_peers, CAP, model_width)
    grad_arrived, rows_back = (
        lax.all_to_all(grad_send, "expert", split_axis=1, concat_axis=1, tiled=True),
        lax.all_to_all(send_rows, "expert", split_axis=1, concat_axis=1, tiled=True),
    )
    rows_again = rows_back.reshape(local_experts, expert_peers * CAP, model_width)
    gate_again = jnp.einsum(
        "erd,edf->erf", rows_again, gate_full, preferred_element_type=jnp.float32
    )
    up_again = jnp.einsum("erd,edf->erf", rows_again, up_full, preferred_element_type=jnp.float32)
    inner_again = (jax.nn.silu(gate_again) * up_again).astype(jnp.bfloat16)
    grad_expert_out = grad_arrived.reshape(local_experts, expert_peers * CAP, model_width)
    grad_inner = jnp.einsum(
        "erd,efd->erf", grad_expert_out, down_full, preferred_element_type=jnp.float32
    )
    grad_down_local = jnp.einsum(
        "erf,erd->efd", inner_again, grad_expert_out, preferred_element_type=jnp.float32
    )
    sigmoid_gate = jax.nn.sigmoid(gate_again)
    swish = gate_again * sigmoid_gate
    grad_gate_act = (
        grad_inner * up_again * (sigmoid_gate * (1.0 + gate_again * (1.0 - sigmoid_gate)))
    ).astype(jnp.bfloat16)
    grad_up_act = (grad_inner * swish).astype(jnp.bfloat16)
    grad_gate_local = jnp.einsum(
        "erd,erf->edf", rows_again, grad_gate_act, preferred_element_type=jnp.float32
    )
    grad_up_local = jnp.einsum(
        "erd,erf->edf", rows_again, grad_up_act, preferred_element_type=jnp.float32
    )
    grad_rows = (
        jnp.einsum("erf,edf->erd", grad_gate_act, gate_full, preferred_element_type=jnp.float32)
        + jnp.einsum("erf,edf->erd", grad_up_act, up_full, preferred_element_type=jnp.float32)
    ).astype(jnp.bfloat16)
    grad_back = lax.all_to_all(
        grad_rows.reshape(local_experts, expert_peers, CAP, model_width),
        "expert",
        split_axis=1,
        concat_axis=1,
        tiled=True,
    )
    grad_back = jnp.concatenate(
        [grad_back.reshape(EXPERTS * CAP, model_width), jnp.zeros((1, model_width), jnp.bfloat16)],
        axis=0,
    )
    grad_hidden_two = jnp.sum(
        grad_back[target].reshape(tok_count, TOP, model_width).astype(jnp.float32), axis=1
    )
    grad_chosen = gate_probs * (
        grad_gates - jnp.sum(gate_probs * grad_gates, axis=-1, keepdims=True)
    )
    grad_logits = jnp.sum(picked_one * grad_chosen[:, :, None], axis=1).astype(jnp.bfloat16)
    grad_hidden_two = grad_hidden_two + jnp.dot(
        grad_logits, router_full.T, preferred_element_type=jnp.float32
    )
    grad_router_local = jnp.dot(hidden_two.T, grad_logits, preferred_element_type=jnp.float32)
    grad_middle_norm, grad_gain_two = norm_backward(
        grad_hidden_two, normed_two, scale_two, gain_second
    )
    grad_middle = grad_result + grad_middle_norm
    grad_branch = grad_middle.astype(jnp.bfloat16)
    grad_out_local = jnp.dot(attended.T, grad_branch, preferred_element_type=jnp.float32)
    grad_attended = jnp.dot(grad_branch, out_full.T, preferred_element_type=jnp.float32).astype(
        jnp.bfloat16
    )
    grad_groups = (
        grad_attended.reshape(tok_count, KV_HEADS, repeat_heads, HEAD)
        .transpose(1, 2, 0, 3)
        .reshape(KV_HEADS, query_rows, HEAD)
    )
    row_delta = jnp.sum(grad_groups.astype(jnp.float32) * exact_out, axis=-1)
    zero_key = jnp.zeros((tok_count, KV_HEADS, HEAD), jnp.float32)

    def pass_grads(grad_query, inputs_block):
        key_block, value_block, label = inputs_block

        def visit(carried):
            prob_block = probs_of(key_block, label)
            grad_probs = jnp.einsum(
                "grh,kgh->grk", grad_groups, value_block, preferred_element_type=jnp.float32
            )
            grad_scores = (prob_block * (grad_probs - row_delta[..., None])).astype(jnp.bfloat16)
            carried = carried + jnp.einsum(
                "grk,kgh->grh", grad_scores, key_block, preferred_element_type=jnp.float32
            )
            grad_key_block = (
                jnp.einsum(
                    "grk,grh->kgh", grad_scores, query_groups, preferred_element_type=jnp.float32
                )
                * score_scale
            )
            grad_value_block = jnp.einsum(
                "grk,grh->kgh",
                prob_block.astype(jnp.bfloat16),
                grad_groups,
                preferred_element_type=jnp.float32,
            )
            return (carried, (grad_key_block, grad_value_block))

        def skip(carried):
            return (carried, (zero_key, zero_key))

        return lax.cond(on_path(label), visit, skip, grad_query)

    grad_query_groups, (grad_key_blocks, grad_value_blocks) = lax.scan(
        pass_grads,
        jnp.zeros((KV_HEADS, query_rows, HEAD), jnp.float32),
        (key_blocks, value_blocks, segment_labels),
    )
    grad_key_all = grad_key_blocks.reshape(total_keys, KV_HEADS * HEAD)
    grad_value_all = grad_value_blocks.reshape(total_keys, KV_HEADS * HEAD)
    grad_key_mine, grad_value_mine = (
        lax.psum_scatter(
            grad_key_all.astype(jnp.bfloat16), "dp", scatter_dimension=0, tiled=True
        ).astype(jnp.float32),
        lax.psum_scatter(
            grad_value_all.astype(jnp.bfloat16), "dp", scatter_dimension=0, tiled=True
        ).astype(jnp.float32),
    )
    grad_query_rot = (
        (grad_query_groups * score_scale)
        .reshape(KV_HEADS, repeat_heads, tok_count, HEAD)
        .transpose(2, 0, 1, 3)
        .reshape(tok_count, HEADS, HEAD)
    )
    grad_query_raw = (
        rotate(grad_query_rot, cosine, -sine_part)
        .reshape(tok_count, HEADS * HEAD)
        .astype(jnp.bfloat16)
    )
    grad_key_raw = (
        rotate(grad_key_mine.reshape(tok_count, KV_HEADS, HEAD), cosine, -sine_part)
        .reshape(tok_count, KV_HEADS * HEAD)
        .astype(jnp.bfloat16)
    )
    grad_value_raw = grad_value_mine.astype(jnp.bfloat16)
    grad_query_local = jnp.dot(hidden_one.T, grad_query_raw, preferred_element_type=jnp.float32)
    grad_key_local = jnp.dot(hidden_one.T, grad_key_raw, preferred_element_type=jnp.float32)
    grad_value_local = jnp.dot(hidden_one.T, grad_value_raw, preferred_element_type=jnp.float32)
    grad_hidden_one = (
        jnp.dot(grad_query_raw, query_full.T, preferred_element_type=jnp.float32)
        + jnp.dot(grad_key_raw, key_full.T, preferred_element_type=jnp.float32)
        + jnp.dot(grad_value_raw, value_full.T, preferred_element_type=jnp.float32)
    )
    grad_inputs_norm, grad_gain_one = norm_backward(
        grad_hidden_one, normed_one, scale_one, gain_first
    )
    grad_inputs = grad_middle + grad_inputs_norm
    grad_gate_mine, grad_up_mine, grad_down_mine = (
        lax.psum_scatter(
            grad_gate_local.astype(jnp.bfloat16), "dp", scatter_dimension=1, tiled=True
        ).astype(jnp.float32),
        lax.psum_scatter(
            grad_up_local.astype(jnp.bfloat16), "dp", scatter_dimension=1, tiled=True
        ).astype(jnp.float32),
        lax.psum_scatter(
            grad_down_local.astype(jnp.bfloat16), "dp", scatter_dimension=1, tiled=True
        ).astype(jnp.float32),
    )
    shard_rows = (
        lax.psum_scatter(
            grad_gain_one.astype(jnp.bfloat16), "dp", scatter_dimension=0, tiled=True
        ).astype(jnp.float32),
        lax.psum_scatter(
            grad_query_local.astype(jnp.bfloat16), "dp", scatter_dimension=0, tiled=True
        ).astype(jnp.float32),
        lax.psum_scatter(
            grad_key_local.astype(jnp.bfloat16), "dp", scatter_dimension=0, tiled=True
        ).astype(jnp.float32),
        lax.psum_scatter(
            grad_value_local.astype(jnp.bfloat16), "dp", scatter_dimension=0, tiled=True
        ).astype(jnp.float32),
        lax.psum_scatter(
            grad_out_local.astype(jnp.bfloat16), "dp", scatter_dimension=0, tiled=True
        ).astype(jnp.float32),
        lax.psum_scatter(
            grad_gain_two.astype(jnp.bfloat16), "dp", scatter_dimension=0, tiled=True
        ).astype(jnp.float32),
        lax.psum_scatter(
            grad_router_local.astype(jnp.bfloat16), "dp", scatter_dimension=0, tiled=True
        ).astype(jnp.float32),
    )
    shared = (
        lax.psum(shard_rows[0].astype(jnp.bfloat16), "expert").astype(jnp.float32),
        lax.psum(shard_rows[1].astype(jnp.bfloat16), "expert").astype(jnp.float32),
        lax.psum(shard_rows[2].astype(jnp.bfloat16), "expert").astype(jnp.float32),
        lax.psum(shard_rows[3].astype(jnp.bfloat16), "expert").astype(jnp.float32),
        lax.psum(shard_rows[4].astype(jnp.bfloat16), "expert").astype(jnp.float32),
        lax.psum(shard_rows[5].astype(jnp.bfloat16), "expert").astype(jnp.float32),
        lax.psum(shard_rows[6].astype(jnp.bfloat16), "expert").astype(jnp.float32),
    )
    return (
        block_out[None],
        grad_inputs[None],
        shared[0],
        shared[1],
        shared[2],
        shared[3],
        shared[4],
        shared[5],
        shared[6],
        grad_gate_mine,
        grad_up_mine,
        grad_down_mine,
    )


SLOTS = 32
log2e = 1.4426950408889634


def dot_f32(a, b, dims):
    return lax.dot_general(a, b, (dims, ((), ())), preferred_element_type=jnp.float32)


def attend_kernel(path_ref, query_ref, keys_ref, out_ref, exact_ref, stat_ref, acc, top, total):
    tok_count = query_ref.shape[0]
    repeat_heads = HEADS // KV_HEADS
    factor = log2e * HEAD ** (-0.5)
    segment_count = keys_ref.shape[0]
    segment = path_ref[segment_count]
    row = lax.broadcasted_iota(jnp.int32, (tok_count, tok_count), 0)
    column = lax.broadcasted_iota(jnp.int32, (tok_count, tok_count), 1)
    causal = column <= row

    def visit(label, own):
        for head in range(HEADS):
            group = head // repeat_heads
            query = query_ref[:, head * HEAD : (head + 1) * HEAD]
            key = keys_ref[label, :, group * HEAD : (group + 1) * HEAD]
            value = keys_ref[label, :, (KV_HEADS + group) * HEAD : (KV_HEADS + group + 1) * HEAD]
            scores = dot_f32(query, key, ((1,), (1,)))
            if own:
                scores = jnp.where(causal, scores, -1e30)
                peak = jnp.max(scores, axis=-1, keepdims=True)
            else:
                peak = jnp.maximum(top[head], jnp.max(scores, axis=-1, keepdims=True))
            prob = jnp.exp2((scores - peak) * factor)
            prob_high = prob.astype(jnp.bfloat16)
            prob_low = (prob - prob_high.astype(jnp.float32)).astype(jnp.bfloat16)
            part = dot_f32(prob_high, value, ((1,), (0,))) + dot_f32(prob_low, value, ((1,), (0,)))
            part_total = jnp.sum(prob, axis=-1, keepdims=True)
            if own:
                acc[head] = part
                total[head] = part_total
            else:
                fade = jnp.exp2((top[head] - peak) * factor)
                acc[head] = acc[head] * fade + part
                total[head] = total[head] * fade + part_total
            top[head] = peak

    visit(segment, True)

    @pl.loop(0, segment_count)
    def _(label):
        @pl.when((path_ref[label] > 0) & (label != segment))
        def _():
            visit(label, False)

    lane = lax.broadcasted_iota(jnp.int32, (tok_count, HEAD), 1)
    stats = jnp.zeros((tok_count, HEAD), jnp.float32)
    for head in range(HEADS):
        exact = acc[head] / total[head]
        exact_ref[:, head * HEAD : (head + 1) * HEAD] = exact
        out_ref[:, head * HEAD : (head + 1) * HEAD] = exact.astype(jnp.bfloat16)
        stats = jnp.where(lane == head, top[head] * factor + jnp.log2(total[head]), stats)
    stat_ref[...] = stats


def attend(path, query, keys):
    tok_count = query.shape[0]
    vmem = pl.BlockSpec(memory_space=pltpu.VMEM)
    return pl.pallas_call(
        attend_kernel,
        out_shape=(
            jax.ShapeDtypeStruct(query.shape, jnp.bfloat16),
            jax.ShapeDtypeStruct(query.shape, jnp.float32),
            jax.ShapeDtypeStruct((tok_count, HEAD), jnp.float32),
        ),
        in_specs=[pl.BlockSpec(memory_space=pltpu.SMEM), vmem, vmem],
        out_specs=(vmem, vmem, vmem),
        scratch_shapes=[
            pltpu.VMEM((HEADS, tok_count, HEAD), jnp.float32),
            pltpu.VMEM((HEADS, tok_count, 1), jnp.float32),
            pltpu.VMEM((HEADS, tok_count, 1), jnp.float32),
        ],
        compiler_params=pltpu.CompilerParams(vmem_limit_bytes=40 * 1024 * 1024),
    )(path, query, keys)


def attend_grad_kernel(
    path_ref, query_ref, keys_ref, grad_ref, exact_ref, stat_ref, grad_query_ref, grad_keys_ref, acc, delta
):
    tok_count = query_ref.shape[0]
    repeat_heads = HEADS // KV_HEADS
    scale = HEAD ** (-0.5)
    factor = log2e * scale
    segment_count = keys_ref.shape[0]
    segment = path_ref[segment_count]
    row = lax.broadcasted_iota(jnp.int32, (tok_count, tok_count), 0)
    column = lax.broadcasted_iota(jnp.int32, (tok_count, tok_count), 1)
    causal = column <= row
    for head in range(HEADS):
        cut = slice(head * HEAD, (head + 1) * HEAD)
        delta[head] = jnp.sum(
            grad_ref[:, cut].astype(jnp.float32) * exact_ref[:, cut], axis=-1, keepdims=True
        )

    def visit(label, own):
        for group in range(KV_HEADS):
            key_cut = slice(group * HEAD, (group + 1) * HEAD)
            value_cut = slice((KV_HEADS + group) * HEAD, (KV_HEADS + group + 1) * HEAD)
            key = keys_ref[label, :, key_cut]
            value = keys_ref[label, :, value_cut]
            grad_key = jnp.zeros((tok_count, HEAD), jnp.float32)
            grad_value = jnp.zeros((tok_count, HEAD), jnp.float32)
            for head in range(group * repeat_heads, (group + 1) * repeat_heads):
                cut = slice(head * HEAD, (head + 1) * HEAD)
                query = query_ref[:, cut]
                grad = grad_ref[:, cut]
                scores = dot_f32(query, key, ((1,), (1,)))
                prob = jnp.exp2(scores * factor - stat_ref[:, head : head + 1])
                if own:
                    prob = jnp.where(causal, prob, 0.0)
                grad_prob = dot_f32(grad, value, ((1,), (1,)))
                grad_score = (prob * (grad_prob - delta[head])).astype(jnp.bfloat16)
                grad_value += dot_f32(prob.astype(jnp.bfloat16), grad, ((0,), (0,)))
                grad_key += dot_f32(grad_score, query, ((0,), (0,)))
                grad_query = dot_f32(grad_score, key, ((1,), (0,)))
                if own:
                    acc[head] = grad_query
                else:
                    acc[head] += grad_query
            grad_keys_ref[label, :, key_cut] = (grad_key * scale).astype(jnp.bfloat16)
            grad_keys_ref[label, :, value_cut] = grad_value.astype(jnp.bfloat16)

    visit(segment, True)

    @pl.loop(0, segment_count)
    def _(label):
        @pl.when((path_ref[label] > 0) & (label != segment))
        def _():
            visit(label, False)

        @pl.when(path_ref[label] == 0)
        def _():
            grad_keys_ref[label] = jnp.zeros(grad_keys_ref.shape[1:], jnp.bfloat16)

    for head in range(HEADS):
        grad_query_ref[:, head * HEAD : (head + 1) * HEAD] = acc[head] * scale


def attend_grad(path, query, keys, grad, exact, stats):
    tok_count = query.shape[0]
    vmem = pl.BlockSpec(memory_space=pltpu.VMEM)
    return pl.pallas_call(
        attend_grad_kernel,
        out_shape=(
            jax.ShapeDtypeStruct(query.shape, jnp.float32),
            jax.ShapeDtypeStruct(keys.shape, jnp.bfloat16),
        ),
        in_specs=[pl.BlockSpec(memory_space=pltpu.SMEM)] + [vmem] * 5,
        out_specs=(vmem, vmem),
        scratch_shapes=[
            pltpu.VMEM((HEADS, tok_count, HEAD), jnp.float32),
            pltpu.VMEM((HEADS, tok_count, 1), jnp.float32),
        ],
        compiler_params=pltpu.CompilerParams(vmem_limit_bytes=40 * 1024 * 1024),
    )(path, query, keys, grad, exact, stats)


def local_owned(
    tokens,
    attn_gain,
    query_weight,
    key_weight,
    value_weight,
    out_weight,
    moe_gain,
    router_weight,
    gate_weight,
    up_weight,
    down_weight,
    parents,
    routes,
    claim_order,
    cotangent,
):
    tok_count = tokens.shape[1]
    model_width = tokens.shape[2]
    ff_width = gate_weight.shape[2]
    segment = lax.axis_index("dp")
    segment_count = lax.axis_size("dp")
    everyone = ("expert", "dp")
    device_count = segment_count * lax.axis_size("expert")
    query_width = HEADS * HEAD
    key_width = KV_HEADS * HEAD

    expert_ids = routes[0].reshape(-1)
    order_row = claim_order[0, 0]
    member = (expert_ids[:, None] == jnp.arange(EXPERTS, dtype=jnp.int32)[None, :]).astype(
        jnp.bfloat16
    )
    earlier = (order_row[None, :] < order_row[:, None]).astype(jnp.bfloat16)
    before = jnp.dot(earlier, member, preferred_element_type=jnp.float32)
    slot_index = jnp.sum(before * member.astype(jnp.float32), axis=1).astype(jnp.int32)
    target = jnp.where(slot_index < CAP, expert_ids * SLOTS + slot_index, -1).reshape(
        tok_count, TOP
    )
    row_labels = jnp.arange(EXPERTS * SLOTS, dtype=jnp.int32)
    hits = (target[:, :, None] == row_labels[None, None, :]).astype(jnp.float32)
    placed_rows = jnp.sum(hits, axis=1).astype(jnp.bfloat16)

    def exchange(rows):
        return lax.all_to_all(
            rows.reshape(device_count, SLOTS, rows.shape[-1]),
            everyone,
            split_axis=0,
            concat_axis=0,
            tiled=True,
        ).reshape(EXPERTS * SLOTS, rows.shape[-1])

    grad_rows_in = exchange(
        dot_f32(placed_rows, cotangent[0], ((0,), (0,))).astype(jnp.bfloat16)
    )

    def own(weight):
        return lax.all_to_all(weight, "dp", split_axis=0, concat_axis=1, tiled=True)[0]

    gate_own, up_own, down_own = own(gate_weight), own(up_weight), own(down_weight)

    small = jnp.concatenate(
        [
            router_weight,
            attn_gain[:, None],
            moe_gain[:, None],
            jnp.zeros((router_weight.shape[0], HEAD - EXPERTS - 2), jnp.bfloat16),
        ],
        axis=1,
    )
    small_full = lax.all_gather(small, "dp", axis=0, tiled=True)
    router_full = small_full[:, :EXPERTS]
    gain_first = small_full[:, EXPERTS].astype(jnp.float32)
    gain_second = small_full[:, EXPERTS + 1].astype(jnp.float32)
    project = lax.all_gather(
        jnp.concatenate([query_weight, key_weight, value_weight], axis=1),
        "dp",
        axis=0,
        tiled=True,
    )
    out_full = lax.all_gather(out_weight, "dp", axis=0, tiled=True)

    reach_row = ancestry(parents[0])[segment]
    path_depth = jnp.sum(reach_row) - 1.0
    positions = path_depth * tok_count + jnp.arange(tok_count, dtype=jnp.float32)
    cosine, sine_part = rope_tables(positions, HEAD)
    path = jnp.concatenate([(reach_row > 0.5).astype(jnp.int32), segment[None].astype(jnp.int32)])
    inputs = tokens[0].astype(jnp.float32)
    scale_one = lax.rsqrt(jnp.mean(inputs * inputs, axis=-1, keepdims=True) + epsilon)
    normed_one = inputs * scale_one
    hidden_one = (normed_one * gain_first).astype(jnp.bfloat16)
    projected = jnp.dot(hidden_one, project, preferred_element_type=jnp.float32)
    query_rot = (
        rotate(projected[:, :query_width].reshape(tok_count, HEADS, HEAD), cosine, sine_part)
        .astype(jnp.bfloat16)
        .reshape(tok_count, query_width)
    )
    key_rot = (
        rotate(
            projected[:, query_width : query_width + key_width].reshape(tok_count, KV_HEADS, HEAD),
            cosine,
            sine_part,
        )
        .astype(jnp.bfloat16)
        .reshape(tok_count, key_width)
    )
    value_low = projected[:, query_width + key_width :].astype(jnp.bfloat16)
    keys = lax.all_gather(
        jnp.concatenate([key_rot, value_low], axis=1), "dp", axis=0, tiled=False
    )
    attended, exact_out, stats = attend(path, query_rot, keys)
    middle = inputs + jnp.dot(attended, out_full, preferred_element_type=jnp.float32)
    scale_two = lax.rsqrt(jnp.mean(middle * middle, axis=-1, keepdims=True) + epsilon)
    normed_two = middle * scale_two
    hidden_two = (normed_two * gain_second).astype(jnp.bfloat16)
    rows_in = exchange(dot_f32(placed_rows, hidden_two, ((0,), (0,))).astype(jnp.bfloat16))
    logits = jnp.dot(hidden_two, router_full, preferred_element_type=jnp.float32)
    picked_one = (
        routes[0][:, :, None] == jnp.arange(EXPERTS, dtype=jnp.int32)[None, None, :]
    ).astype(jnp.float32)
    chosen = jnp.sum(picked_one * logits[:, None, :], axis=-1)
    gate_probs = jax.nn.softmax(chosen, axis=-1)
    gate_rows = jnp.sum(hits * gate_probs[:, :, None], axis=(0, 1))
    gates_in = lax.all_to_all(
        gate_rows.reshape(device_count, SLOTS), everyone, split_axis=0, concat_axis=0, tiled=True
    ).reshape(-1)

    gate_act = jnp.dot(rows_in, gate_own, preferred_element_type=jnp.float32)
    up_act = jnp.dot(rows_in, up_own, preferred_element_type=jnp.float32)
    sigmoid_gate = jax.nn.sigmoid(gate_act)
    swish = gate_act * sigmoid_gate
    inner = (swish * up_act).astype(jnp.bfloat16)
    expert_out = jnp.dot(inner, down_own, preferred_element_type=jnp.float32).astype(jnp.bfloat16)
    grad_in = grad_rows_in.astype(jnp.float32)
    grad_gate_rows = jnp.sum(expert_out.astype(jnp.float32) * grad_in, axis=-1)
    grad_expert_out = (gates_in[:, None] * grad_in).astype(jnp.bfloat16)
    grad_inner = dot_f32(grad_expert_out, down_own, ((1,), (1,)))
    grad_gate_act = (
        grad_inner * up_act * (sigmoid_gate * (1.0 + gate_act * (1.0 - sigmoid_gate)))
    ).astype(jnp.bfloat16)
    grad_up_act = (grad_inner * swish).astype(jnp.bfloat16)
    grad_rows = (
        dot_f32(grad_gate_act, gate_own, ((1,), (1,)))
        + dot_f32(grad_up_act, up_own, ((1,), (1,)))
    ).astype(jnp.bfloat16)
    grad_rows_back = exchange(grad_rows)
    grad_gates_back = lax.all_to_all(
        grad_gate_rows.reshape(device_count, SLOTS),
        everyone,
        split_axis=0,
        concat_axis=0,
        tiled=True,
    ).reshape(-1)
    rows_back = exchange(expert_out)

    def give(grad):
        parts = grad.astype(jnp.bfloat16).reshape(segment_count, -1, grad.shape[-1])
        return lax.all_to_all(parts, "dp", split_axis=0, concat_axis=0, tiled=True).astype(
            jnp.float32
        )

    grad_down_mine = give(dot_f32(inner, grad_expert_out, ((0,), (0,))))
    grad_gate_mine = give(dot_f32(rows_in, grad_gate_act, ((0,), (0,))))
    grad_up_mine = give(dot_f32(rows_in, grad_up_act, ((0,), (0,))))

    gate_placed = jnp.sum(hits * gate_probs[:, :, None], axis=1)
    gate_high = gate_placed.astype(jnp.bfloat16)
    gate_low = (gate_placed - gate_high.astype(jnp.float32)).astype(jnp.bfloat16)
    mixture = jnp.dot(gate_high, rows_back, preferred_element_type=jnp.float32) + jnp.dot(
        gate_low, rows_back, preferred_element_type=jnp.float32
    )
    block_out = (middle + mixture).astype(jnp.bfloat16)
    grad_result = cotangent[0].astype(jnp.float32)
    grad_gates = jnp.sum(hits * grad_gates_back[None, None, :], axis=-1)
    grad_hidden_two = jnp.dot(placed_rows, grad_rows_back, preferred_element_type=jnp.float32)
    grad_chosen = gate_probs * (
        grad_gates - jnp.sum(gate_probs * grad_gates, axis=-1, keepdims=True)
    )
    grad_logits = jnp.sum(picked_one * grad_chosen[:, :, None], axis=1).astype(jnp.bfloat16)
    grad_hidden_two = grad_hidden_two + dot_f32(grad_logits, router_full, ((1,), (1,)))
    grad_router_local = dot_f32(hidden_two, grad_logits, ((0,), (0,)))
    grad_middle_norm, grad_gain_two = norm_backward(
        grad_hidden_two, normed_two, scale_two, gain_second
    )
    grad_middle = grad_result + grad_middle_norm
    grad_branch = grad_middle.astype(jnp.bfloat16)
    grad_out_local = dot_f32(attended, grad_branch, ((0,), (0,)))
    grad_attended = dot_f32(grad_branch, out_full, ((1,), (1,))).astype(jnp.bfloat16)
    grad_query_rot, grad_keys = attend_grad(
        path, query_rot, keys, grad_attended, exact_out, stats
    )
    grad_keys_mine = lax.psum_scatter(
        grad_keys.reshape(segment_count * tok_count, 2 * key_width),
        "dp",
        scatter_dimension=0,
        tiled=True,
    ).astype(jnp.float32)
    grad_query_raw = (
        rotate(grad_query_rot.reshape(tok_count, HEADS, HEAD), cosine, -sine_part)
        .reshape(tok_count, query_width)
        .astype(jnp.bfloat16)
    )
    grad_key_raw = (
        rotate(grad_keys_mine[:, :key_width].reshape(tok_count, KV_HEADS, HEAD), cosine, -sine_part)
        .reshape(tok_count, key_width)
        .astype(jnp.bfloat16)
    )
    grad_projected = jnp.concatenate(
        [grad_query_raw, grad_key_raw, grad_keys_mine[:, key_width:].astype(jnp.bfloat16)], axis=1
    )
    grad_project_local = dot_f32(hidden_one, grad_projected, ((0,), (0,)))
    grad_hidden_one = dot_f32(grad_projected, project, ((1,), (1,)))
    grad_inputs_norm, grad_gain_one = norm_backward(
        grad_hidden_one, normed_one, scale_one, gain_first
    )
    grad_inputs = grad_middle + grad_inputs_norm

    def scatter(grad):
        part = lax.psum_scatter(
            grad.astype(jnp.bfloat16), "dp", scatter_dimension=0, tiled=True
        )
        return lax.psum(part, "expert").astype(jnp.float32)

    grad_small = jnp.concatenate(
        [
            grad_router_local,
            grad_gain_one[:, None],
            grad_gain_two[:, None],
            jnp.zeros((model_width, HEAD - EXPERTS - 2), jnp.float32),
        ],
        axis=1,
    )
    grad_out_mine = scatter(grad_out_local)
    grad_project_mine = scatter(jnp.concatenate([grad_project_local, grad_small], axis=1))
    small_at = query_width + 2 * key_width
    return (
        block_out[None],
        grad_inputs[None],
        grad_project_mine[:, small_at + EXPERTS],
        grad_project_mine[:, :query_width],
        grad_project_mine[:, query_width : query_width + key_width],
        grad_project_mine[:, query_width + key_width : small_at],
        grad_out_mine,
        grad_project_mine[:, small_at + EXPERTS + 1],
        grad_project_mine[:, small_at : small_at + EXPERTS],
        grad_gate_mine,
        grad_up_mine,
        grad_down_mine,
    )


def solution(mesh):
    placed = (
        P("expert", "dp", None),
        P("dp"),
        P("dp", None),
        P("dp", None),
        P("dp", None),
        P("dp", None),
        P("dp"),
        P("dp", None),
        P("expert", "dp", None),
        P("expert", "dp", None),
        P("expert", "dp", None),
        P("expert", None),
        P("expert", "dp", None),
        P("expert", "dp", None),
        P("expert", "dp", None),
    )
    owned = EXPERTS // mesh.shape["expert"] == mesh.shape["dp"]
    return jax.shard_map(
        local_owned if owned else local_gathered,
        mesh=mesh,
        in_specs=placed,
        out_specs=(
            P("expert", "dp", None),
            P("expert", "dp", None),
            P("dp"),
            P("dp", None),
            P("dp", None),
            P("dp", None),
            P("dp", None),
            P("dp"),
            P("dp", None),
            P("expert", "dp", None),
            P("expert", "dp", None),
            P("expert", "dp", None),
        ),
        check_vma=False,
    )
```

```python
import functools

import jax
import jax.numpy as jnp
from jax import lax
from jax.experimental import pallas as pl
from jax.experimental.pallas import tpu as pltpu
from jax.sharding import PartitionSpec as P

HEADS = 12
KV_HEADS = 2
HEAD = 128
EXPERTS = 32
TOP = 4
CAP = 28


epsilon = 1e-06
theta = 10000.0
highest = lax.Precision.HIGHEST


def ancestry(parents):
    row_count = parents.shape[0]
    labels = jnp.arange(row_count, dtype=jnp.int32)
    linked = (parents[:, None] == labels[None, :]).astype(jnp.float32)
    reach_all = jnp.minimum(jnp.eye(row_count, dtype=jnp.float32) + linked, 1.0)
    for doubling in range(max(1, (row_count - 1).bit_length())):
        reach_all = jnp.minimum(jnp.dot(reach_all, reach_all, precision=highest), 1.0)
    return reach_all


def rope_tables(positions, head_size):
    halfway = head_size // 2
    frequency = theta ** (-jnp.arange(halfway, dtype=jnp.float32) * 2.0 / head_size)
    angles = positions[:, None] * frequency[None, :]
    return (jnp.cos(angles)[:, None, :], jnp.sin(angles)[:, None, :])


def rotate(values, cosine, sine_part):
    halfway = values.shape[-1] // 2
    first_half = values[..., :halfway]
    second = values[..., halfway:]
    return jnp.concatenate(
        [first_half * cosine - second * sine_part, second * cosine + first_half * sine_part],
        axis=-1,
    )


def norm_backward(grad_hidden, normed, row_scale, gain):
    grad_normed = grad_hidden * gain
    grad_gain = jnp.sum(grad_hidden * normed, axis=0)
    grad_rows = row_scale * (
        grad_normed - normed * jnp.mean(grad_normed * normed, axis=-1, keepdims=True)
    )
    return (grad_rows, grad_gain)


def local_gathered(
    tokens,
    attn_gain,
    query_weight,
    key_weight,
    value_weight,
    out_weight,
    moe_gain,
    router_weight,
    gate_weight,
    up_weight,
    down_weight,
    parents,
    routes,
    claim_order,
    cotangent,
):
    (
        gain_one,
        query_full,
        key_full,
        value_full,
        out_full,
        gain_two,
        router_full,
        gate_full,
        up_full,
        down_full,
    ) = (
        lax.all_gather(attn_gain, "dp", axis=0, tiled=True),
        lax.all_gather(query_weight, "dp", axis=0, tiled=True),
        lax.all_gather(key_weight, "dp", axis=0, tiled=True),
        lax.all_gather(value_weight, "dp", axis=0, tiled=True),
        lax.all_gather(out_weight, "dp", axis=0, tiled=True),
        lax.all_gather(moe_gain, "dp", axis=0, tiled=True),
        lax.all_gather(router_weight, "dp", axis=0, tiled=True),
        lax.all_gather(gate_weight, "dp", axis=1, tiled=True),
        lax.all_gather(up_weight, "dp", axis=1, tiled=True),
        lax.all_gather(down_weight, "dp", axis=1, tiled=True),
    )
    tok_count = tokens.shape[1]
    model_width = tokens.shape[2]
    segment = lax.axis_index("dp")
    segment_count = lax.axis_size("dp")
    expert_peers = lax.axis_size("expert")
    local_experts = gate_weight.shape[0]
    repeat_heads = HEADS // KV_HEADS
    score_scale = HEAD ** (-0.5)
    query_rows = repeat_heads * tok_count
    reach_all = ancestry(parents[0])
    reach_row = reach_all[segment]
    path_depth = jnp.sum(reach_row) - 1.0
    positions = path_depth * tok_count + jnp.arange(tok_count, dtype=jnp.float32)
    cosine, sine_part = rope_tables(positions, HEAD)
    inputs = tokens[0].astype(jnp.float32)
    scale_one = lax.rsqrt(jnp.mean(inputs * inputs, axis=-1, keepdims=True) + epsilon)
    normed_one = inputs * scale_one
    gain_first = gain_one.astype(jnp.float32)
    hidden_one = (normed_one * gain_first).astype(jnp.bfloat16)
    query_raw = jnp.dot(hidden_one, query_full, preferred_element_type=jnp.float32).reshape(
        tok_count, HEADS, HEAD
    )
    key_raw = jnp.dot(hidden_one, key_full, preferred_element_type=jnp.float32).reshape(
        tok_count, KV_HEADS, HEAD
    )
    value_low = jnp.dot(hidden_one, value_full, preferred_element_type=jnp.float32).astype(
        jnp.bfloat16
    )
    query_rot = rotate(query_raw, cosine, sine_part).astype(jnp.bfloat16)
    key_rot = (
        rotate(key_raw, cosine, sine_part).astype(jnp.bfloat16).reshape(tok_count, KV_HEADS * HEAD)
    )
    key_all, value_all = (
        lax.all_gather(key_rot, "dp", axis=0, tiled=True),
        lax.all_gather(value_low, "dp", axis=0, tiled=True),
    )
    total_keys = key_all.shape[0]
    key_blocks = key_all.reshape(segment_count, tok_count, KV_HEADS, HEAD)
    value_blocks = value_all.reshape(segment_count, tok_count, KV_HEADS, HEAD)
    segment_labels = jnp.arange(segment_count, dtype=jnp.int32)
    query_groups = (
        query_rot.reshape(tok_count, KV_HEADS, repeat_heads, HEAD)
        .transpose(1, 2, 0, 3)
        .reshape(KV_HEADS, query_rows, HEAD)
    )
    query_offsets = jnp.arange(tok_count, dtype=jnp.int32)
    causal_tile = jnp.tile(query_offsets[None, :] <= query_offsets[:, None], (repeat_heads, 1))

    def scores_of(key_block, label):
        raw_scores = (
            jnp.einsum("grh,kgh->grk", query_groups, key_block, preferred_element_type=jnp.float32)
            * score_scale
        )
        allowed = causal_tile | (label != segment)
        return jnp.where(allowed[None], raw_scores, -1000000000.0)

    def on_path(label):
        return reach_row[label] > 0.5

    def pass_stats(state_pair, inputs_block):
        key_block, value_block, label = inputs_block

        def visit(state):
            row_max, row_sum = state
            scores = scores_of(key_block, label)
            new_max = jnp.maximum(row_max, jnp.max(scores, axis=-1))
            new_sum = row_sum * jnp.exp(row_max - new_max) + jnp.sum(
                jnp.exp(scores - new_max[..., None]), axis=-1
            )
            return (new_max, new_sum)

        return (lax.cond(on_path(label), visit, lambda state: state, state_pair), None)

    start_max = jnp.full((KV_HEADS, query_rows), -1e30, jnp.float32)
    start_sum = jnp.zeros((KV_HEADS, query_rows), jnp.float32)
    (row_max, row_sum), unused = lax.scan(
        pass_stats, (start_max, start_sum), (key_blocks, value_blocks, segment_labels)
    )

    def probs_of(key_block, label):
        return jnp.exp(scores_of(key_block, label) - row_max[..., None]) / row_sum[..., None]

    def pass_values(state_pair, inputs_block):
        key_block, value_block, label = inputs_block

        def visit(state):
            accumulated, exact_out = state
            prob_block = probs_of(key_block, label)
            accumulated = accumulated + jnp.einsum(
                "grk,kgh->grh",
                prob_block.astype(jnp.bfloat16),
                value_block,
                preferred_element_type=jnp.float32,
            )
            exact_out = exact_out + jnp.einsum(
                "grk,kgh->grh",
                prob_block,
                value_block.astype(jnp.float32),
                preferred_element_type=jnp.float32,
                precision=highest,
            )
            return (accumulated, exact_out)

        return (lax.cond(on_path(label), visit, lambda state: state, state_pair), None)

    zero_out = jnp.zeros((KV_HEADS, query_rows, HEAD), jnp.float32)
    (accumulated, exact_out), unused = lax.scan(
        pass_values, (zero_out, zero_out), (key_blocks, value_blocks, segment_labels)
    )
    attended = (
        accumulated.reshape(KV_HEADS, repeat_heads, tok_count, HEAD)
        .transpose(2, 0, 1, 3)
        .reshape(tok_count, HEADS * HEAD)
        .astype(jnp.bfloat16)
    )
    branch = jnp.dot(attended, out_full, preferred_element_type=jnp.float32)
    middle = inputs + branch
    scale_two = lax.rsqrt(jnp.mean(middle * middle, axis=-1, keepdims=True) + epsilon)
    normed_two = middle * scale_two
    gain_second = gain_two.astype(jnp.float32)
    hidden_two = (normed_two * gain_second).astype(jnp.bfloat16)
    logits = jnp.dot(hidden_two, router_full, preferred_element_type=jnp.float32)
    picked_one = (
        routes[0][:, :, None] == jnp.arange(EXPERTS, dtype=jnp.int32)[None, None, :]
    ).astype(jnp.float32)
    chosen = jnp.sum(picked_one * logits[:, None, :], axis=-1)
    gate_probs = jax.nn.softmax(chosen, axis=-1)
    expert_ids = routes[0].reshape(-1)
    order_row = claim_order[0, 0]
    pair_count = expert_ids.shape[0]
    member = (expert_ids[:, None] == jnp.arange(EXPERTS, dtype=jnp.int32)[None, :]).astype(
        jnp.bfloat16
    )
    earlier = (order_row[None, :] < order_row[:, None]).astype(jnp.bfloat16)
    before = jnp.dot(earlier, member, preferred_element_type=jnp.float32)
    slot_index = jnp.sum(before * member.astype(jnp.float32), axis=1).astype(jnp.int32)
    owner_rank = expert_ids // local_experts
    local_rank = expert_ids % local_experts
    target = jnp.where(
        slot_index < CAP, (local_rank * expert_peers + owner_rank) * CAP + slot_index, EXPERTS * CAP
    )
    slot_pairs = (
        jnp.full((EXPERTS * CAP + 1,), pair_count, jnp.int32)
        .at[target]
        .set(jnp.arange(pair_count, dtype=jnp.int32))[: EXPERTS * CAP]
    )
    padded_two = jnp.concatenate([hidden_two, jnp.zeros((1, model_width), jnp.bfloat16)], axis=0)
    send_rows = padded_two[slot_pairs // TOP].reshape(local_experts, expert_peers, CAP, model_width)
    arrived = lax.all_to_all(send_rows, "expert", split_axis=1, concat_axis=1, tiled=True)
    expert_rows = arrived.reshape(local_experts, expert_peers * CAP, model_width)
    gate_act = jnp.einsum(
        "erd,edf->erf", expert_rows, gate_full, preferred_element_type=jnp.float32
    )
    up_act = jnp.einsum("erd,edf->erf", expert_rows, up_full, preferred_element_type=jnp.float32)
    inner = (jax.nn.silu(gate_act) * up_act).astype(jnp.bfloat16)
    expert_out = jnp.einsum(
        "erf,efd->erd", inner, down_full, preferred_element_type=jnp.float32
    ).astype(jnp.bfloat16)
    returned = lax.all_to_all(
        expert_out.reshape(local_experts, expert_peers, CAP, model_width),
        "expert",
        split_axis=1,
        concat_axis=1,
        tiled=True,
    )
    returned = jnp.concatenate(
        [returned.reshape(EXPERTS * CAP, model_width), jnp.zeros((1, model_width), jnp.bfloat16)],
        axis=0,
    )
    pair_out = returned[target].reshape(tok_count, TOP, model_width).astype(jnp.float32)
    mixture = jnp.sum(gate_probs[:, :, None] * pair_out, axis=1)
    block_out = (middle + mixture).astype(jnp.bfloat16)
    grad_result = cotangent[0].astype(jnp.float32)
    grad_gates = jnp.sum(pair_out * grad_result[:, None, :], axis=-1)
    grad_pairs = (
        (gate_probs[:, :, None] * grad_result[:, None, :])
        .astype(jnp.bfloat16)
        .reshape(pair_count, model_width)
    )
    grad_padded = jnp.concatenate([grad_pairs, jnp.zeros((1, model_width), jnp.bfloat16)], axis=0)
    grad_send = grad_padded[slot_pairs].reshape(local_experts, expert_peers, CAP, model_width)
    grad_arrived, rows_back = (
        lax.all_to_all(grad_send, "expert", split_axis=1, concat_axis=1, tiled=True),
        lax.all_to_all(send_rows, "expert", split_axis=1, concat_axis=1, tiled=True),
    )
    rows_again = rows_back.reshape(local_experts, expert_peers * CAP, model_width)
    gate_again = jnp.einsum(
        "erd,edf->erf", rows_again, gate_full, preferred_element_type=jnp.float32
    )
    up_again = jnp.einsum("erd,edf->erf", rows_again, up_full, preferred_element_type=jnp.float32)
    inner_again = (jax.nn.silu(gate_again) * up_again).astype(jnp.bfloat16)
    grad_expert_out = grad_arrived.reshape(local_experts, expert_peers * CAP, model_width)
    grad_inner = jnp.einsum(
        "erd,efd->erf", grad_expert_out, down_full, preferred_element_type=jnp.float32
    )
    grad_down_local = jnp.einsum(
        "erf,erd->efd", inner_again, grad_expert_out, preferred_element_type=jnp.float32
    )
    sigmoid_gate = jax.nn.sigmoid(gate_again)
    swish = gate_again * sigmoid_gate
    grad_gate_act = (
        grad_inner * up_again * (sigmoid_gate * (1.0 + gate_again * (1.0 - sigmoid_gate)))
    ).astype(jnp.bfloat16)
    grad_up_act = (grad_inner * swish).astype(jnp.bfloat16)
    grad_gate_local = jnp.einsum(
        "erd,erf->edf", rows_again, grad_gate_act, preferred_element_type=jnp.float32
    )
    grad_up_local = jnp.einsum(
        "erd,erf->edf", rows_again, grad_up_act, preferred_element_type=jnp.float32
    )
    grad_rows = (
        jnp.einsum("erf,edf->erd", grad_gate_act, gate_full, preferred_element_type=jnp.float32)
        + jnp.einsum("erf,edf->erd", grad_up_act, up_full, preferred_element_type=jnp.float32)
    ).astype(jnp.bfloat16)
    grad_back = lax.all_to_all(
        grad_rows.reshape(local_experts, expert_peers, CAP, model_width),
        "expert",
        split_axis=1,
        concat_axis=1,
        tiled=True,
    )
    grad_back = jnp.concatenate(
        [grad_back.reshape(EXPERTS * CAP, model_width), jnp.zeros((1, model_width), jnp.bfloat16)],
        axis=0,
    )
    grad_hidden_two = jnp.sum(
        grad_back[target].reshape(tok_count, TOP, model_width).astype(jnp.float32), axis=1
    )
    grad_chosen = gate_probs * (
        grad_gates - jnp.sum(gate_probs * grad_gates, axis=-1, keepdims=True)
    )
    grad_logits = jnp.sum(picked_one * grad_chosen[:, :, None], axis=1).astype(jnp.bfloat16)
    grad_hidden_two = grad_hidden_two + jnp.dot(
        grad_logits, router_full.T, preferred_element_type=jnp.float32
    )
    grad_router_local = jnp.dot(hidden_two.T, grad_logits, preferred_element_type=jnp.float32)
    grad_middle_norm, grad_gain_two = norm_backward(
        grad_hidden_two, normed_two, scale_two, gain_second
    )
    grad_middle = grad_result + grad_middle_norm
    grad_branch = grad_middle.astype(jnp.bfloat16)
    grad_out_local = jnp.dot(attended.T, grad_branch, preferred_element_type=jnp.float32)
    grad_attended = jnp.dot(grad_branch, out_full.T, preferred_element_type=jnp.float32).astype(
        jnp.bfloat16
    )
    grad_groups = (
        grad_attended.reshape(tok_count, KV_HEADS, repeat_heads, HEAD)
        .transpose(1, 2, 0, 3)
        .reshape(KV_HEADS, query_rows, HEAD)
    )
    row_delta = jnp.sum(grad_groups.astype(jnp.float32) * exact_out, axis=-1)
    zero_key = jnp.zeros((tok_count, KV_HEADS, HEAD), jnp.float32)

    def pass_grads(grad_query, inputs_block):
        key_block, value_block, label = inputs_block

        def visit(carried):
            prob_block = probs_of(key_block, label)
            grad_probs = jnp.einsum(
                "grh,kgh->grk", grad_groups, value_block, preferred_element_type=jnp.float32
            )
            grad_scores = (prob_block * (grad_probs - row_delta[..., None])).astype(jnp.bfloat16)
            carried = carried + jnp.einsum(
                "grk,kgh->grh", grad_scores, key_block, preferred_element_type=jnp.float32
            )
            grad_key_block = (
                jnp.einsum(
                    "grk,grh->kgh", grad_scores, query_groups, preferred_element_type=jnp.float32
                )
                * score_scale
            )
            grad_value_block = jnp.einsum(
                "grk,grh->kgh",
                prob_block.astype(jnp.bfloat16),
                grad_groups,
                preferred_element_type=jnp.float32,
            )
            return (carried, (grad_key_block, grad_value_block))

        def skip(carried):
            return (carried, (zero_key, zero_key))

        return lax.cond(on_path(label), visit, skip, grad_query)

    grad_query_groups, (grad_key_blocks, grad_value_blocks) = lax.scan(
        pass_grads,
        jnp.zeros((KV_HEADS, query_rows, HEAD), jnp.float32),
        (key_blocks, value_blocks, segment_labels),
    )
    grad_key_all = grad_key_blocks.reshape(total_keys, KV_HEADS * HEAD)
    grad_value_all = grad_value_blocks.reshape(total_keys, KV_HEADS * HEAD)
    grad_key_mine, grad_value_mine = (
        lax.psum_scatter(
            grad_key_all.astype(jnp.bfloat16), "dp", scatter_dimension=0, tiled=True
        ).astype(jnp.float32),
        lax.psum_scatter(
            grad_value_all.astype(jnp.bfloat16), "dp", scatter_dimension=0, tiled=True
        ).astype(jnp.float32),
    )
    grad_query_rot = (
        (grad_query_groups * score_scale)
        .reshape(KV_HEADS, repeat_heads, tok_count, HEAD)
        .transpose(2, 0, 1, 3)
        .reshape(tok_count, HEADS, HEAD)
    )
    grad_query_raw = (
        rotate(grad_query_rot, cosine, -sine_part)
        .reshape(tok_count, HEADS * HEAD)
        .astype(jnp.bfloat16)
    )
    grad_key_raw = (
        rotate(grad_key_mine.reshape(tok_count, KV_HEADS, HEAD), cosine, -sine_part)
        .reshape(tok_count, KV_HEADS * HEAD)
        .astype(jnp.bfloat16)
    )
    grad_value_raw = grad_value_mine.astype(jnp.bfloat16)
    grad_query_local = jnp.dot(hidden_one.T, grad_query_raw, preferred_element_type=jnp.float32)
    grad_key_local = jnp.dot(hidden_one.T, grad_key_raw, preferred_element_type=jnp.float32)
    grad_value_local = jnp.dot(hidden_one.T, grad_value_raw, preferred_element_type=jnp.float32)
    grad_hidden_one = (
        jnp.dot(grad_query_raw, query_full.T, preferred_element_type=jnp.float32)
        + jnp.dot(grad_key_raw, key_full.T, preferred_element_type=jnp.float32)
        + jnp.dot(grad_value_raw, value_full.T, preferred_element_type=jnp.float32)
    )
    grad_inputs_norm, grad_gain_one = norm_backward(
        grad_hidden_one, normed_one, scale_one, gain_first
    )
    grad_inputs = grad_middle + grad_inputs_norm
    grad_gate_mine, grad_up_mine, grad_down_mine = (
        lax.psum_scatter(
            grad_gate_local.astype(jnp.bfloat16), "dp", scatter_dimension=1, tiled=True
        ).astype(jnp.float32),
        lax.psum_scatter(
            grad_up_local.astype(jnp.bfloat16), "dp", scatter_dimension=1, tiled=True
        ).astype(jnp.float32),
        lax.psum_scatter(
            grad_down_local.astype(jnp.bfloat16), "dp", scatter_dimension=1, tiled=True
        ).astype(jnp.float32),
    )
    shard_rows = (
        lax.psum_scatter(
            grad_gain_one.astype(jnp.bfloat16), "dp", scatter_dimension=0, tiled=True
        ).astype(jnp.float32),
        lax.psum_scatter(
            grad_query_local.astype(jnp.bfloat16), "dp", scatter_dimension=0, tiled=True
        ).astype(jnp.float32),
        lax.psum_scatter(
            grad_key_local.astype(jnp.bfloat16), "dp", scatter_dimension=0, tiled=True
        ).astype(jnp.float32),
        lax.psum_scatter(
            grad_value_local.astype(jnp.bfloat16), "dp", scatter_dimension=0, tiled=True
        ).astype(jnp.float32),
        lax.psum_scatter(
            grad_out_local.astype(jnp.bfloat16), "dp", scatter_dimension=0, tiled=True
        ).astype(jnp.float32),
        lax.psum_scatter(
            grad_gain_two.astype(jnp.bfloat16), "dp", scatter_dimension=0, tiled=True
        ).astype(jnp.float32),
        lax.psum_scatter(
            grad_router_local.astype(jnp.bfloat16), "dp", scatter_dimension=0, tiled=True
        ).astype(jnp.float32),
    )
    shared = (
        lax.psum(shard_rows[0].astype(jnp.bfloat16), "expert").astype(jnp.float32),
        lax.psum(shard_rows[1].astype(jnp.bfloat16), "expert").astype(jnp.float32),
        lax.psum(shard_rows[2].astype(jnp.bfloat16), "expert").astype(jnp.float32),
        lax.psum(shard_rows[3].astype(jnp.bfloat16), "expert").astype(jnp.float32),
        lax.psum(shard_rows[4].astype(jnp.bfloat16), "expert").astype(jnp.float32),
        lax.psum(shard_rows[5].astype(jnp.bfloat16), "expert").astype(jnp.float32),
        lax.psum(shard_rows[6].astype(jnp.bfloat16), "expert").astype(jnp.float32),
    )
    return (
        block_out[None],
        grad_inputs[None],
        shared[0],
        shared[1],
        shared[2],
        shared[3],
        shared[4],
        shared[5],
        shared[6],
        grad_gate_mine,
        grad_up_mine,
        grad_down_mine,
    )


SLOTS = 32
PAD_TOKENS = 32
LANES = 128
WAVE_FIRST = 3
TILE = 256
MESH = pl.DeviceIdType.MESH
log2e = 1.4426950408889634


def dot_f32(a, b, dims=((1,), (0,))):
    return lax.dot_general(a, b, (dims, ((), ())), preferred_element_type=jnp.float32)


def split3(value):
    high = value.astype(jnp.bfloat16)
    rest = value - high.astype(jnp.float32)
    middle = rest.astype(jnp.bfloat16)
    low = (rest - middle.astype(jnp.float32)).astype(jnp.bfloat16)
    return high, middle, low


def one_hot(shape, test):
    row = lax.broadcasted_iota(jnp.int32, shape, 0)
    column = lax.broadcasted_iota(jnp.int32, shape, 1)
    return jnp.where(test(row, column), 1.0, 0.0).astype(jnp.bfloat16)


class Place:
    def __init__(self):
        self.dp = lax.axis_index("dp")
        self.side = lax.axis_index("expert")
        self.z = self.dp // 4
        self.x = (self.dp // 2) % 2
        self.c = self.dp % 2

    def index(self, z, x, c):
        return z * 4 + x * 2 + c

    def others(self):
        return [self.z + 1 - 2 * (self.z % 2), (self.z + 2) % 4, 3 - self.z]


def remote(src, dst, send, recv, dp, side):
    return pltpu.make_async_remote_copy(
        src_ref=src,
        dst_ref=dst,
        send_sem=send,
        recv_sem=recv,
        device_id={"dp": dp, "expert": side},
        device_id_type=MESH,
    )


def enter(device_count, dp_count):
    rank = lax.axis_index("expert") * dp_count + lax.axis_index("dp")
    barrier = pltpu.get_barrier_semaphore()

    @pl.loop(1, device_count)
    def _(step):
        other = (rank + step) % device_count
        pl.semaphore_signal(
            barrier,
            inc=1,
            device_id={"dp": other % dp_count, "expert": other // dp_count},
            device_id_type=MESH,
        )

    pl.semaphore_wait(barrier, device_count - 1)


class Gather:
    def __init__(self, place, own, slot, send, recv, local):
        self.place, self.own, self.slot = place, own, slot
        self.send, self.recv, self.local = send, recv, local

    def copy(self, z, x, c, to_x, to_c, number, own=False, to_z=None):
        p = self.place
        shard = p.index(z, x, c)
        target = p.index(p.z if to_z is None else to_z, to_x, to_c)
        source = self.own if own else self.slot(shard)
        return remote(
            source, self.slot(shard), self.send.at[number], self.recv.at[shard], target, p.side
        )

    def first(self):
        p = self.place
        out = [
            self.copy(p.z, p.x, p.c, p.x, p.c, 2 + i, own=True, to_z=z)
            for i, z in enumerate(p.others())
        ]
        out.append(self.copy(p.z, p.x, p.c, 1 - p.x, p.c, 1, own=True))
        out.append(self.copy(p.z, p.x, p.c, p.x, 1 - p.c, 0, own=True))
        return out

    def second(self, i):
        p = self.place
        z = p.others()[i]
        return [
            self.copy(z, p.x, p.c, 1 - p.x, p.c, 5 + 2 * i),
            self.copy(z, p.x, p.c, p.x, 1 - p.c, 6 + 2 * i),
        ]

    def third(self, i):
        p = self.place
        z = ([p.z] + p.others())[i]
        return self.copy(z, 1 - p.x, p.c, p.x, 1 - p.c, 11 + i)

    def own_copy(self):
        p = self.place
        return pltpu.make_async_copy(self.own, self.slot(p.dp), self.local)

    def start(self):
        for copy in self.first():
            copy.start()
        self.own_copy().start()

    def forward_z(self):
        for i in range(3):
            copies = self.second(i)
            copies[0].wait_recv()
            for copy in copies:
                copy.start()

    def forward_x(self):
        for i in range(4):
            copy = self.third(i)
            copy.wait_recv()
            copy.start()

    def finish(self):
        p = self.place
        for z in range(4):
            for x in range(2):
                self.copy(z, x, 1 - p.c, p.x, 1 - p.c, 0).wait_recv()
        for copy in self.first():
            copy.wait_send()
        for i in range(3):
            for copy in self.second(i):
                copy.wait_send()
        for i in range(4):
            self.third(i).wait_send()
        self.own_copy().wait()


class RowSwap:
    def __init__(self, source, target, send, recv, local, dp_count, device_count):
        self.source, self.target = source, target
        self.send, self.recv, self.local = send, recv, local
        self.dp_count, self.device_count = dp_count, device_count
        self.rank = lax.axis_index("expert") * dp_count + lax.axis_index("dp")

    def block(self, ref, index):
        return ref.at[pl.ds(pl.multiple_of(index * SLOTS, SLOTS), SLOTS)]

    def copy(self, step, to, landing):
        return remote(
            self.block(self.source, to),
            self.block(self.target, landing),
            self.send.at[step],
            self.recv.at[step],
            to % self.dp_count,
            to // self.dp_count,
        )

    def own_copy(self):
        return pltpu.make_async_copy(
            self.block(self.source, self.rank), self.block(self.target, self.rank), self.local
        )

    def start(self):
        @pl.loop(1, self.device_count)
        def _(step):
            self.copy(step, (self.rank + step) % self.device_count, self.rank).start()

        self.own_copy().start()

    def finish(self):
        @pl.loop(1, self.device_count)
        def _(step):
            other = (self.rank + self.device_count - step) % self.device_count
            self.copy(step, other, other).wait()

        self.own_copy().wait()


class WeightSwap:
    def __init__(self, place, pairs, send, recv, local, dp_count):
        self.place, self.pairs = place, pairs
        self.send, self.recv, self.local = send, recv, local
        self.dp_count = dp_count

    def copies(self, step, to, landing):
        out = []
        for i, (source, target) in enumerate(self.pairs):
            rows = source.shape[1]
            out.append(
                remote(
                    source.at[to],
                    target.at[pl.ds(pl.multiple_of(landing * rows, rows), rows)],
                    self.send.at[step, i],
                    self.recv.at[step, i],
                    to,
                    self.place.side,
                )
            )
        return out

    def own_copies(self):
        dp = self.place.dp
        return [
            pltpu.make_async_copy(
                source.at[dp],
                target.at[pl.ds(pl.multiple_of(dp * source.shape[1], source.shape[1]), source.shape[1])],
                self.local.at[i],
            )
            for i, (source, target) in enumerate(self.pairs)
        ]

    def start(self, low, high):
        @pl.loop(low, high)
        def _(step):
            for copy in self.copies(step, (self.place.dp + step) % self.dp_count, self.place.dp):
                copy.start()

    def start_own(self):
        for copy in self.own_copies():
            copy.start()

    def finish(self):
        @pl.loop(1, self.dp_count)
        def _(step):
            other = (self.place.dp + self.dp_count - step) % self.dp_count
            for copy in self.copies(step, other, other):
                copy.wait()

        for copy in self.own_copies():
            copy.wait()


def columns(tile, width=TILE):
    return pl.ds(pl.multiple_of(tile * width, width), width)


def rows_of(index, count):
    return pl.ds(pl.multiple_of(index * count, count), count)


def front_kernel(
    bias_ref,
    tokens_ref,
    cotangent_ref,
    project_ref,
    out_ref,
    placed_ref,
    mask_ref,
    cosine_ref,
    sine_ref,
    gate_ref,
    up_ref,
    down_ref,
    project_full,
    out_full,
    keys_ref,
    query_ref,
    attended_ref,
    exact_ref,
    stat_ref,
    middle_ref,
    hidden_ref,
    probs_ref,
    rows_in,
    grads_in,
    gate_own,
    up_own,
    down_own,
    keys_own,
    hidden_one,
    row_send,
    grad_send,
    extended,
    acc,
    top,
    total,
    project_send,
    project_recv,
    out_send,
    out_recv,
    keys_send,
    keys_recv,
    row_send_sem,
    row_recv_sem,
    grad_send_sem,
    grad_recv_sem,
    weight_send,
    weight_recv,
    weight_local,
    local,
):
    dp_count = keys_ref.shape[0]
    device_count = row_send.shape[0] // SLOTS
    tok_count, model_width = tokens_ref.shape
    query_width = HEADS * HEAD
    key_width = KV_HEADS * HEAD
    repeat_heads = HEADS // KV_HEADS
    factor = log2e * HEAD ** (-0.5)
    place = Place()
    shard_rows = project_ref.shape[0]

    def shard_of(full):
        return lambda index: full.at[rows_of(index, shard_rows)]

    project = Gather(
        place, project_ref, shard_of(project_full), project_send, project_recv, local.at[0]
    )
    out = Gather(place, out_ref, shard_of(out_full), out_send, out_recv, local.at[1])
    keys = Gather(
        place, keys_own, lambda index: keys_ref.at[index], keys_send, keys_recv, local.at[2]
    )
    rows = RowSwap(row_send, rows_in, row_send_sem, row_recv_sem, local.at[3], dp_count, device_count)
    grads = RowSwap(
        grad_send, grads_in, grad_send_sem, grad_recv_sem, local.at[4], dp_count, device_count
    )
    weights = WeightSwap(
        place,
        ((gate_ref, gate_own), (up_ref, up_own), (down_ref, down_own)),
        weight_send,
        weight_recv,
        weight_local,
        dp_count,
    )

    enter(device_count, dp_count)
    project.start()
    weights.start(1, WAVE_FIRST)

    @pl.loop(0, model_width // TILE)
    def _(tile):
        grad_send[:, columns(tile)] = dot_f32(
            placed_ref[:, :tok_count], cotangent_ref[:, columns(tile)]
        ).astype(jnp.bfloat16)

    project.forward_z()
    project.forward_x()
    project.finish()

    lanes_of = one_hot((8, LANES), lambda row, column: column == row + EXPERTS)
    gains = dot_f32(lanes_of, project_full[:, query_width + 2 * key_width :], ((1,), (1,)))
    gain_first, gain_second = gains[0:1], gains[1:2]
    chunk = 32

    @pl.loop(0, tok_count // chunk)
    def _(index):
        value = tokens_ref[rows_of(index, chunk)].astype(jnp.float32)
        scale = lax.rsqrt(jnp.mean(value * value, axis=-1, keepdims=True) + epsilon)
        hidden_one[rows_of(index, chunk)] = (value * scale * gain_first).astype(jnp.bfloat16)

    def turned(tile):
        value = dot_f32(hidden_one[...], project_full[:, columns(tile)])
        halves = []
        for half in range(TILE // HEAD):
            part = value[:, half * HEAD : (half + 1) * HEAD]
            halves.append(
                part * cosine_ref[...] + pltpu.roll(part, HEAD // 2, 1) * sine_ref[...]
            )
        return jnp.concatenate(halves, axis=1).astype(jnp.bfloat16)

    keys_own[:, :key_width] = turned(query_width // TILE)
    keys_own[:, key_width:] = dot_f32(
        hidden_one[...], project_full[:, query_width + key_width : query_width + 2 * key_width]
    ).astype(jnp.bfloat16)
    keys.start()

    @pl.loop(0, query_width // TILE)
    def _(tile):
        query_ref[:, columns(tile)] = turned(tile)

    keys.forward_z()
    keys.forward_x()
    keys.finish()
    out.start()
    weights.start(WAVE_FIRST, dp_count)
    weights.start_own()
    out.forward_z()
    out.forward_x()
    grads.start()

    row = lax.broadcasted_iota(jnp.int32, (tok_count, tok_count), 0)
    column = lax.broadcasted_iota(jnp.int32, (tok_count, tok_count), 1)
    causal = column <= row

    def visit(label, own):
        for head in range(HEADS):
            group = head // repeat_heads
            query = query_ref[:, head * HEAD : (head + 1) * HEAD]
            key = keys_ref[label, :, group * HEAD : (group + 1) * HEAD]
            value = keys_ref[label, :, (KV_HEADS + group) * HEAD : (KV_HEADS + group + 1) * HEAD]
            scores = dot_f32(query, key, ((1,), (1,)))
            if own:
                scores = jnp.where(causal, scores, -1e30)
                peak = jnp.max(scores, axis=-1, keepdims=True)
                shift = peak
            else:
                bias = bias_ref[label]
                peak = jnp.maximum(top[head], jnp.max(scores, axis=-1, keepdims=True) + bias)
                shift = peak - bias
            prob = jnp.exp2((scores - shift) * factor)
            prob_high = prob.astype(jnp.bfloat16)
            prob_low = (prob - prob_high.astype(jnp.float32)).astype(jnp.bfloat16)
            part = dot_f32(prob_high, value) + dot_f32(prob_low, value)
            part_total = jnp.sum(prob, axis=-1, keepdims=True)
            if own:
                acc[head] = part
                total[head] = part_total
            else:
                fade = jnp.exp2((top[head] - peak) * factor)
                acc[head] = acc[head] * fade + part
                total[head] = total[head] * fade + part_total
            top[head] = peak

    visit(place.dp, True)

    @pl.loop(0, place.dp)
    def _(label):
        visit(label, False)

    lane = lax.broadcasted_iota(jnp.int32, (tok_count, LANES), 1)
    stats = jnp.zeros((tok_count, LANES), jnp.float32)
    for head in range(HEADS):
        exact = acc[head] / total[head]
        exact_ref[:, head * HEAD : (head + 1) * HEAD] = exact
        attended_ref[:, head * HEAD : (head + 1) * HEAD] = exact.astype(jnp.bfloat16)
        stats = jnp.where(lane == head, top[head] * factor + jnp.log2(total[head]), stats)
    stat_ref[...] = stats
    out.finish()

    @pl.loop(0, model_width // TILE)
    def _(tile):
        middle_ref[:, columns(tile)] = tokens_ref[:, columns(tile)].astype(jnp.float32) + dot_f32(
            attended_ref[...], out_full[:, columns(tile)]
        )

    @pl.loop(0, tok_count // chunk)
    def _(index):
        value = middle_ref[rows_of(index, chunk)]
        scale = lax.rsqrt(jnp.mean(value * value, axis=-1, keepdims=True) + epsilon)
        hidden_ref[rows_of(index, chunk)] = (value * scale * gain_second).astype(jnp.bfloat16)

    router = project_full[:, query_width + 2 * key_width :]
    logits = jnp.where(mask_ref[...] > 0, dot_f32(hidden_ref[...], router), -1e30)
    weight = jnp.exp(logits - jnp.max(logits, axis=-1, keepdims=True))
    probs = weight / jnp.sum(weight, axis=-1, keepdims=True)
    probs_ref[...] = probs
    spread = sum(dot_f32(placed_ref[:, :tok_count], part) for part in split3(probs))
    slot_row = lax.broadcasted_iota(jnp.int32, spread.shape, 0)
    slot_lane = lax.broadcasted_iota(jnp.int32, spread.shape, 1)
    gate = jnp.sum(jnp.where(slot_lane == slot_row // SLOTS, spread, 0.0), axis=-1, keepdims=True)
    high, mid, low = split3(gate)
    part = jnp.where(
        slot_lane < SLOTS,
        high.astype(jnp.float32),
        jnp.where(slot_lane < 2 * SLOTS, mid.astype(jnp.float32), low.astype(jnp.float32)),
    )
    part = jnp.where(
        (slot_lane % SLOTS == slot_row % SLOTS) & (slot_lane < 3 * SLOTS), part, 0.0
    ).astype(jnp.bfloat16)
    fold = one_hot((device_count, row_send.shape[0]), lambda r, col: col // SLOTS == r)
    extended[:tok_count] = hidden_ref[...]
    extended[tok_count:] = jnp.zeros((PAD_TOKENS, model_width), jnp.bfloat16)
    extended[tok_count:, :LANES] = dot_f32(fold, part).astype(jnp.bfloat16)

    @pl.loop(0, model_width // TILE)
    def _(tile):
        row_send[:, columns(tile)] = dot_f32(placed_ref[...], extended[:, columns(tile)]).astype(
            jnp.bfloat16
        )

    rows.start()
    weights.finish()
    grads.finish()
    rows.finish()


def front(bias, tokens, cotangent, project, out, placed, mask, cosine, sine, gate, up, down):
    dp_count = lax.axis_size("dp")
    device_count = dp_count * lax.axis_size("expert")
    tok_count, model_width = tokens.shape
    query_width = HEADS * HEAD
    key_width = KV_HEADS * HEAD
    vmem = pl.BlockSpec(memory_space=pltpu.VMEM)
    anywhere = pl.BlockSpec(memory_space=pl.ANY)
    slots = device_count * SLOTS
    low, full = jnp.bfloat16, jnp.float32
    shape = jax.ShapeDtypeStruct
    ff_width = gate.shape[2]
    outs = (
        (shape((model_width, project.shape[1]), low), vmem),
        (shape((model_width, model_width), low), vmem),
        (shape((dp_count, tok_count, 2 * key_width), low), vmem),
        (shape((tok_count, query_width), low), vmem),
        (shape((tok_count, query_width), low), vmem),
        (shape((tok_count, query_width), full), vmem),
        (shape((tok_count, LANES), full), vmem),
        (shape((tok_count, model_width), full), vmem),
        (shape((tok_count, model_width), low), vmem),
        (shape((tok_count, LANES), full), vmem),
        (shape((slots, model_width), low), anywhere),
        (shape((slots, model_width), low), anywhere),
        (shape((model_width, ff_width), low), anywhere),
        (shape((model_width, ff_width), low), anywhere),
        (shape((ff_width, model_width), low), anywhere),
    )
    dma = pltpu.SemaphoreType.DMA
    return pl.pallas_call(
        front_kernel,
        out_shape=tuple(o[0] for o in outs),
        in_specs=[pl.BlockSpec(memory_space=pltpu.SMEM)] + [vmem] * 8 + [anywhere] * 3,
        out_specs=tuple(o[1] for o in outs),
        scratch_shapes=[
            pltpu.VMEM((tok_count, 2 * key_width), low),
            pltpu.VMEM((tok_count, model_width), low),
            pltpu.VMEM((slots, model_width), low),
            pltpu.VMEM((slots, model_width), low),
            pltpu.VMEM((tok_count + PAD_TOKENS, model_width), low),
            pltpu.VMEM((HEADS, tok_count, HEAD), full),
            pltpu.VMEM((HEADS, tok_count, 1), full),
            pltpu.VMEM((HEADS, tok_count, 1), full),
        ]
        + [dma((15,)), dma((dp_count,))] * 3
        + [dma((device_count,))] * 4
        + [dma((dp_count, 3))] * 2
        + [dma((3,)), dma((5,))],
        compiler_params=pltpu.CompilerParams(
            collective_id=0, has_side_effects=True, vmem_limit_bytes=58 * 1024 * 1024
        ),
    )(bias, tokens, cotangent, project, out, placed, mask, cosine, sine, gate, up, down)


def attend_grad_kernel(
    path_ref, query_ref, keys_ref, grad_ref, exact_ref, stat_ref, grad_query_ref, grad_keys_ref, acc, delta
):
    tok_count = query_ref.shape[0]
    repeat_heads = HEADS // KV_HEADS
    scale = HEAD ** (-0.5)
    factor = log2e * scale
    segment_count = keys_ref.shape[0]
    segment = path_ref[segment_count]
    row = lax.broadcasted_iota(jnp.int32, (tok_count, tok_count), 0)
    column = lax.broadcasted_iota(jnp.int32, (tok_count, tok_count), 1)
    causal = column <= row
    for head in range(HEADS):
        cut = slice(head * HEAD, (head + 1) * HEAD)
        delta[head] = jnp.sum(
            grad_ref[:, cut].astype(jnp.float32) * exact_ref[:, cut], axis=-1, keepdims=True
        )

    def visit(label, own):
        for group in range(KV_HEADS):
            key_cut = slice(group * HEAD, (group + 1) * HEAD)
            value_cut = slice((KV_HEADS + group) * HEAD, (KV_HEADS + group + 1) * HEAD)
            key = keys_ref[label, :, key_cut]
            value = keys_ref[label, :, value_cut]
            grad_key = jnp.zeros((tok_count, HEAD), jnp.float32)
            grad_value = jnp.zeros((tok_count, HEAD), jnp.float32)
            for head in range(group * repeat_heads, (group + 1) * repeat_heads):
                cut = slice(head * HEAD, (head + 1) * HEAD)
                query = query_ref[:, cut]
                grad = grad_ref[:, cut]
                scores = dot_f32(query, key, ((1,), (1,)))
                prob = jnp.exp2(scores * factor - stat_ref[:, head : head + 1])
                if own:
                    prob = jnp.where(causal, prob, 0.0)
                grad_prob = dot_f32(grad, value, ((1,), (1,)))
                grad_score = (prob * (grad_prob - delta[head])).astype(jnp.bfloat16)
                grad_value += dot_f32(prob.astype(jnp.bfloat16), grad, ((0,), (0,)))
                grad_key += dot_f32(grad_score, query, ((0,), (0,)))
                grad_query = dot_f32(grad_score, key, ((1,), (0,)))
                if own:
                    acc[head] = grad_query
                else:
                    acc[head] += grad_query
            grad_keys_ref[label, :, key_cut] = (grad_key * scale).astype(jnp.bfloat16)
            grad_keys_ref[label, :, value_cut] = grad_value.astype(jnp.bfloat16)

    visit(segment, True)

    @pl.loop(0, segment_count)
    def _(label):
        @pl.when((path_ref[label] > 0) & (label != segment))
        def _():
            visit(label, False)

        @pl.when(path_ref[label] == 0)
        def _():
            grad_keys_ref[label] = jnp.zeros(grad_keys_ref.shape[1:], jnp.bfloat16)

    for head in range(HEADS):
        grad_query_ref[:, head * HEAD : (head + 1) * HEAD] = acc[head] * scale


def attend_grad(path, query, keys, grad, exact, stats):
    tok_count = query.shape[0]
    vmem = pl.BlockSpec(memory_space=pltpu.VMEM)
    return pl.pallas_call(
        attend_grad_kernel,
        out_shape=(
            jax.ShapeDtypeStruct(query.shape, jnp.float32),
            jax.ShapeDtypeStruct(keys.shape, jnp.bfloat16),
        ),
        in_specs=[pl.BlockSpec(memory_space=pltpu.SMEM)] + [vmem] * 5,
        out_specs=(vmem, vmem),
        scratch_shapes=[
            pltpu.VMEM((HEADS, tok_count, HEAD), jnp.float32),
            pltpu.VMEM((HEADS, tok_count, 1), jnp.float32),
        ],
        compiler_params=pltpu.CompilerParams(vmem_limit_bytes=40 * 1024 * 1024),
    )(path, query, keys, grad, exact, stats)


def local_owned(
    tokens,
    attn_gain,
    query_weight,
    key_weight,
    value_weight,
    out_weight,
    moe_gain,
    router_weight,
    gate_weight,
    up_weight,
    down_weight,
    parents,
    routes,
    claim_order,
    cotangent,
):
    tok_count = tokens.shape[1]
    model_width = tokens.shape[2]
    ff_width = gate_weight.shape[2]
    segment = lax.axis_index("dp")
    segment_count = lax.axis_size("dp")
    everyone = ("expert", "dp")
    device_count = segment_count * lax.axis_size("expert")
    query_width = HEADS * HEAD
    key_width = KV_HEADS * HEAD

    route_rows = routes[0]
    expert_ids = route_rows.reshape(-1)
    order_row = claim_order[0, 0]
    member = (expert_ids[:, None] == jnp.arange(EXPERTS, dtype=jnp.int32)[None, :]).astype(
        jnp.bfloat16
    )
    earlier = (order_row[None, :] < order_row[:, None]).astype(jnp.bfloat16)
    before = jnp.dot(earlier, member, preferred_element_type=jnp.float32)
    slot_index = jnp.sum(before * member.astype(jnp.float32), axis=1).astype(jnp.int32)
    target = jnp.where(slot_index < CAP, expert_ids * SLOTS + slot_index, -1).reshape(
        tok_count, TOP
    )
    row_labels = jnp.arange(EXPERTS * SLOTS, dtype=jnp.int32)
    placed_rows = sum(
        (target[:, c : c + 1] == row_labels[None, :]).astype(jnp.bfloat16) for c in range(TOP)
    )
    turned_target = target.T
    placed_by_slot = sum(
        (turned_target[c : c + 1] == row_labels[:, None]).astype(jnp.bfloat16) for c in range(TOP)
    )
    spare = row_labels[:, None] == (jnp.arange(EXPERTS) * SLOTS + CAP)[None, :]
    placed_by_slot = jnp.concatenate([placed_by_slot, spare.astype(jnp.bfloat16)], axis=1)
    experts_row = jnp.arange(LANES, dtype=jnp.int32)[None, :]
    mask = sum((route_rows[:, c : c + 1] == experts_row).astype(jnp.float32) for c in range(TOP))

    small = jnp.concatenate(
        [
            router_weight,
            attn_gain[:, None],
            moe_gain[:, None],
            jnp.zeros((router_weight.shape[0], LANES - EXPERTS - 2), jnp.bfloat16),
        ],
        axis=1,
    )
    project_shard = jnp.concatenate([query_weight, key_weight, value_weight, small], axis=1)
    reach_row = ancestry(parents[0])[segment]
    path_depth = jnp.sum(reach_row) - 1.0
    positions = path_depth * tok_count + jnp.arange(tok_count, dtype=jnp.float32)
    cosine, sine_part = rope_tables(positions, HEAD)
    cosine_wide = jnp.concatenate([cosine[:, 0], cosine[:, 0]], axis=1)
    sine_wide = jnp.concatenate([-sine_part[:, 0], sine_part[:, 0]], axis=1)
    on_path = reach_row > 0.5
    bias = jnp.where(on_path, 0.0, -1e30).astype(jnp.float32)
    path = jnp.concatenate([on_path.astype(jnp.int32), segment[None].astype(jnp.int32)])
    (
        project_full,
        out_full,
        keys,
        query_rot,
        attended,
        exact_out,
        stats,
        middle,
        hidden_two,
        probs,
        rows_in,
        grad_rows_in,
        gate_own,
        up_own,
        down_own,
    ) = front(
        bias,
        tokens[0],
        cotangent[0],
        project_shard,
        out_weight,
        placed_by_slot,
        mask,
        cosine_wide,
        sine_wide,
        gate_weight,
        up_weight,
        down_weight,
    )
    small_at = query_width + 2 * key_width
    project = project_full[:, :small_at]
    small_full = project_full[:, small_at:]
    router_full = small_full[:, :EXPERTS]
    gain_first = small_full[:, EXPERTS].astype(jnp.float32)
    gain_second = small_full[:, EXPERTS + 1].astype(jnp.float32)
    inputs = tokens[0].astype(jnp.float32)
    scale_one = lax.rsqrt(jnp.mean(inputs * inputs, axis=-1, keepdims=True) + epsilon)
    normed_one = inputs * scale_one
    hidden_one = (normed_one * gain_first).astype(jnp.bfloat16)
    scale_two = lax.rsqrt(jnp.mean(middle * middle, axis=-1, keepdims=True) + epsilon)
    normed_two = middle * scale_two
    gate_probs = probs[:, :EXPERTS]
    gate_parts = rows_in.reshape(device_count, SLOTS, model_width)[:, CAP, : 3 * SLOTS]
    gates_in = jnp.sum(
        gate_parts.reshape(device_count, 3, SLOTS).astype(jnp.float32), axis=1
    ).reshape(-1)
    spare_row = (jnp.arange(EXPERTS * SLOTS) % SLOTS >= CAP)[:, None]
    rows_in = jnp.where(spare_row, jnp.zeros_like(rows_in), rows_in)

    def exchange(rows):
        return lax.all_to_all(
            rows.reshape(device_count, SLOTS, rows.shape[-1]),
            everyone,
            split_axis=0,
            concat_axis=0,
            tiled=True,
        ).reshape(EXPERTS * SLOTS, rows.shape[-1])

    gate_act = jnp.dot(rows_in, gate_own, preferred_element_type=jnp.float32)
    up_act = jnp.dot(rows_in, up_own, preferred_element_type=jnp.float32)
    sigmoid_gate = jax.nn.sigmoid(gate_act)
    swish = gate_act * sigmoid_gate
    inner = (swish * up_act).astype(jnp.bfloat16)
    expert_out = jnp.dot(inner, down_own, preferred_element_type=jnp.float32).astype(jnp.bfloat16)
    grad_in = grad_rows_in.astype(jnp.float32)
    grad_gate_rows = jnp.sum(expert_out.astype(jnp.float32) * grad_in, axis=-1)
    grad_expert_out = (gates_in[:, None] * grad_in).astype(jnp.bfloat16)
    grad_inner = dot_f32(grad_expert_out, down_own, ((1,), (1,)))
    grad_gate_act = (
        grad_inner * up_act * (sigmoid_gate * (1.0 + gate_act * (1.0 - sigmoid_gate)))
    ).astype(jnp.bfloat16)
    grad_up_act = (grad_inner * swish).astype(jnp.bfloat16)
    grad_rows = (
        dot_f32(grad_gate_act, gate_own, ((1,), (1,)))
        + dot_f32(grad_up_act, up_own, ((1,), (1,)))
    ).astype(jnp.bfloat16)
    grad_rows_back = exchange(grad_rows)
    grad_gates_back = lax.all_to_all(
        grad_gate_rows.reshape(device_count, SLOTS),
        everyone,
        split_axis=0,
        concat_axis=0,
        tiled=True,
    ).reshape(-1)
    rows_back = exchange(expert_out)

    def give(grad):
        parts = grad.astype(jnp.bfloat16).reshape(segment_count, -1, grad.shape[-1])
        return lax.all_to_all(parts, "dp", split_axis=0, concat_axis=0, tiled=True).astype(
            jnp.float32
        )

    grad_down_mine = give(dot_f32(inner, grad_expert_out, ((0,), (0,))))
    grad_gate_mine = give(dot_f32(rows_in, grad_gate_act, ((0,), (0,))))
    grad_up_mine = give(dot_f32(rows_in, grad_up_act, ((0,), (0,))))

    gate_placed = jnp.repeat(gate_probs, SLOTS, axis=1) * placed_rows.astype(jnp.float32)
    gate_high = gate_placed.astype(jnp.bfloat16)
    gate_low = (gate_placed - gate_high.astype(jnp.float32)).astype(jnp.bfloat16)
    mixture = jnp.dot(gate_high, rows_back, preferred_element_type=jnp.float32) + jnp.dot(
        gate_low, rows_back, preferred_element_type=jnp.float32
    )
    block_out = (middle + mixture).astype(jnp.bfloat16)
    grad_result = cotangent[0].astype(jnp.float32)
    grad_gates = jnp.sum(
        (placed_rows.astype(jnp.float32) * grad_gates_back[None, :]).reshape(
            tok_count, EXPERTS, SLOTS
        ),
        axis=-1,
    )
    grad_hidden_two = jnp.dot(placed_rows, grad_rows_back, preferred_element_type=jnp.float32)
    grad_chosen = gate_probs * (
        grad_gates - jnp.sum(gate_probs * grad_gates, axis=-1, keepdims=True)
    )
    grad_logits = grad_chosen.astype(jnp.bfloat16)
    grad_hidden_two = grad_hidden_two + dot_f32(grad_logits, router_full, ((1,), (1,)))
    grad_router_local = dot_f32(hidden_two, grad_logits, ((0,), (0,)))
    grad_middle_norm, grad_gain_two = norm_backward(
        grad_hidden_two, normed_two, scale_two, gain_second
    )
    grad_middle = grad_result + grad_middle_norm
    grad_branch = grad_middle.astype(jnp.bfloat16)
    grad_out_local = dot_f32(attended, grad_branch, ((0,), (0,)))
    grad_attended = dot_f32(grad_branch, out_full, ((1,), (1,))).astype(jnp.bfloat16)
    grad_query_rot, grad_keys = attend_grad(
        path, query_rot, keys, grad_attended, exact_out, stats
    )
    grad_keys_mine = lax.psum_scatter(
        grad_keys.reshape(segment_count * tok_count, 2 * key_width),
        "dp",
        scatter_dimension=0,
        tiled=True,
    ).astype(jnp.float32)
    grad_query_raw = (
        rotate(grad_query_rot.reshape(tok_count, HEADS, HEAD), cosine, -sine_part)
        .reshape(tok_count, query_width)
        .astype(jnp.bfloat16)
    )
    grad_key_raw = (
        rotate(grad_keys_mine[:, :key_width].reshape(tok_count, KV_HEADS, HEAD), cosine, -sine_part)
        .reshape(tok_count, key_width)
        .astype(jnp.bfloat16)
    )
    grad_projected = jnp.concatenate(
        [grad_query_raw, grad_key_raw, grad_keys_mine[:, key_width:].astype(jnp.bfloat16)], axis=1
    )
    grad_project_local = dot_f32(hidden_one, grad_projected, ((0,), (0,)))
    grad_hidden_one = dot_f32(grad_projected, project, ((1,), (1,)))
    grad_inputs_norm, grad_gain_one = norm_backward(
        grad_hidden_one, normed_one, scale_one, gain_first
    )
    grad_inputs = grad_middle + grad_inputs_norm

    def scatter(grad):
        part = lax.psum_scatter(
            grad.astype(jnp.bfloat16), "dp", scatter_dimension=0, tiled=True
        )
        return lax.psum(part, "expert").astype(jnp.float32)

    grad_small = jnp.concatenate(
        [
            grad_router_local,
            grad_gain_one[:, None],
            grad_gain_two[:, None],
            jnp.zeros((model_width, HEAD - EXPERTS - 2), jnp.float32),
        ],
        axis=1,
    )
    grad_out_mine = scatter(grad_out_local)
    grad_project_mine = scatter(jnp.concatenate([grad_project_local, grad_small], axis=1))
    return (
        block_out[None],
        grad_inputs[None],
        grad_project_mine[:, small_at + EXPERTS],
        grad_project_mine[:, :query_width],
        grad_project_mine[:, query_width : query_width + key_width],
        grad_project_mine[:, query_width + key_width : small_at],
        grad_out_mine,
        grad_project_mine[:, small_at + EXPERTS + 1],
        grad_project_mine[:, small_at : small_at + EXPERTS],
        grad_gate_mine,
        grad_up_mine,
        grad_down_mine,
    )


def solution(mesh):
    placed = (
        P("expert", "dp", None),
        P("dp"),
        P("dp", None),
        P("dp", None),
        P("dp", None),
        P("dp", None),
        P("dp"),
        P("dp", None),
        P("expert", "dp", None),
        P("expert", "dp", None),
        P("expert", "dp", None),
        P("expert", None),
        P("expert", "dp", None),
        P("expert", "dp", None),
        P("expert", "dp", None),
    )
    owned = EXPERTS // mesh.shape["expert"] == mesh.shape["dp"]
    return jax.shard_map(
        local_owned if owned else local_gathered,
        mesh=mesh,
        in_specs=placed,
        out_specs=(
            P("expert", "dp", None),
            P("expert", "dp", None),
            P("dp"),
            P("dp", None),
            P("dp", None),
            P("dp", None),
            P("dp", None),
            P("dp"),
            P("dp", None),
            P("expert", "dp", None),
            P("expert", "dp", None),
            P("expert", "dp", None),
        ),
        check_vma=False,
    )
```

```python
import functools

import jax
import jax.numpy as jnp
from jax import lax
from jax.experimental import pallas as pl
from jax.experimental.pallas import tpu as pltpu
from jax.sharding import PartitionSpec as P

HEADS = 12
KV_HEADS = 2
HEAD = 128
EXPERTS = 32
TOP = 4
CAP = 28


epsilon = 1e-06
theta = 10000.0
highest = lax.Precision.HIGHEST


def ancestry(parents):
    row_count = parents.shape[0]
    labels = jnp.arange(row_count, dtype=jnp.int32)
    linked = (parents[:, None] == labels[None, :]).astype(jnp.float32)
    reach_all = jnp.minimum(jnp.eye(row_count, dtype=jnp.float32) + linked, 1.0)
    for doubling in range(max(1, (row_count - 1).bit_length())):
        reach_all = jnp.minimum(jnp.dot(reach_all, reach_all, precision=highest), 1.0)
    return reach_all


def rope_tables(positions, head_size):
    halfway = head_size // 2
    frequency = theta ** (-jnp.arange(halfway, dtype=jnp.float32) * 2.0 / head_size)
    angles = positions[:, None] * frequency[None, :]
    return (jnp.cos(angles)[:, None, :], jnp.sin(angles)[:, None, :])


def rotate(values, cosine, sine_part):
    halfway = values.shape[-1] // 2
    first_half = values[..., :halfway]
    second = values[..., halfway:]
    return jnp.concatenate(
        [first_half * cosine - second * sine_part, second * cosine + first_half * sine_part],
        axis=-1,
    )


def norm_backward(grad_hidden, normed, row_scale, gain):
    grad_normed = grad_hidden * gain
    grad_gain = jnp.sum(grad_hidden * normed, axis=0)
    grad_rows = row_scale * (
        grad_normed - normed * jnp.mean(grad_normed * normed, axis=-1, keepdims=True)
    )
    return (grad_rows, grad_gain)


def local_gathered(
    tokens,
    attn_gain,
    query_weight,
    key_weight,
    value_weight,
    out_weight,
    moe_gain,
    router_weight,
    gate_weight,
    up_weight,
    down_weight,
    parents,
    routes,
    claim_order,
    cotangent,
):
    (
        gain_one,
        query_full,
        key_full,
        value_full,
        out_full,
        gain_two,
        router_full,
        gate_full,
        up_full,
        down_full,
    ) = (
        lax.all_gather(attn_gain, "dp", axis=0, tiled=True),
        lax.all_gather(query_weight, "dp", axis=0, tiled=True),
        lax.all_gather(key_weight, "dp", axis=0, tiled=True),
        lax.all_gather(value_weight, "dp", axis=0, tiled=True),
        lax.all_gather(out_weight, "dp", axis=0, tiled=True),
        lax.all_gather(moe_gain, "dp", axis=0, tiled=True),
        lax.all_gather(router_weight, "dp", axis=0, tiled=True),
        lax.all_gather(gate_weight, "dp", axis=1, tiled=True),
        lax.all_gather(up_weight, "dp", axis=1, tiled=True),
        lax.all_gather(down_weight, "dp", axis=1, tiled=True),
    )
    tok_count = tokens.shape[1]
    model_width = tokens.shape[2]
    segment = lax.axis_index("dp")
    segment_count = lax.axis_size("dp")
    expert_peers = lax.axis_size("expert")
    local_experts = gate_weight.shape[0]
    repeat_heads = HEADS // KV_HEADS
    score_scale = HEAD ** (-0.5)
    query_rows = repeat_heads * tok_count
    reach_all = ancestry(parents[0])
    reach_row = reach_all[segment]
    path_depth = jnp.sum(reach_row) - 1.0
    positions = path_depth * tok_count + jnp.arange(tok_count, dtype=jnp.float32)
    cosine, sine_part = rope_tables(positions, HEAD)
    inputs = tokens[0].astype(jnp.float32)
    scale_one = lax.rsqrt(jnp.mean(inputs * inputs, axis=-1, keepdims=True) + epsilon)
    normed_one = inputs * scale_one
    gain_first = gain_one.astype(jnp.float32)
    hidden_one = (normed_one * gain_first).astype(jnp.bfloat16)
    query_raw = jnp.dot(hidden_one, query_full, preferred_element_type=jnp.float32).reshape(
        tok_count, HEADS, HEAD
    )
    key_raw = jnp.dot(hidden_one, key_full, preferred_element_type=jnp.float32).reshape(
        tok_count, KV_HEADS, HEAD
    )
    value_low = jnp.dot(hidden_one, value_full, preferred_element_type=jnp.float32).astype(
        jnp.bfloat16
    )
    query_rot = rotate(query_raw, cosine, sine_part).astype(jnp.bfloat16)
    key_rot = (
        rotate(key_raw, cosine, sine_part).astype(jnp.bfloat16).reshape(tok_count, KV_HEADS * HEAD)
    )
    key_all, value_all = (
        lax.all_gather(key_rot, "dp", axis=0, tiled=True),
        lax.all_gather(value_low, "dp", axis=0, tiled=True),
    )
    total_keys = key_all.shape[0]
    key_blocks = key_all.reshape(segment_count, tok_count, KV_HEADS, HEAD)
    value_blocks = value_all.reshape(segment_count, tok_count, KV_HEADS, HEAD)
    segment_labels = jnp.arange(segment_count, dtype=jnp.int32)
    query_groups = (
        query_rot.reshape(tok_count, KV_HEADS, repeat_heads, HEAD)
        .transpose(1, 2, 0, 3)
        .reshape(KV_HEADS, query_rows, HEAD)
    )
    query_offsets = jnp.arange(tok_count, dtype=jnp.int32)
    causal_tile = jnp.tile(query_offsets[None, :] <= query_offsets[:, None], (repeat_heads, 1))

    def scores_of(key_block, label):
        raw_scores = (
            jnp.einsum("grh,kgh->grk", query_groups, key_block, preferred_element_type=jnp.float32)
            * score_scale
        )
        allowed = causal_tile | (label != segment)
        return jnp.where(allowed[None], raw_scores, -1000000000.0)

    def on_path(label):
        return reach_row[label] > 0.5

    def pass_stats(state_pair, inputs_block):
        key_block, value_block, label = inputs_block

        def visit(state):
            row_max, row_sum = state
            scores = scores_of(key_block, label)
            new_max = jnp.maximum(row_max, jnp.max(scores, axis=-1))
            new_sum = row_sum * jnp.exp(row_max - new_max) + jnp.sum(
                jnp.exp(scores - new_max[..., None]), axis=-1
            )
            return (new_max, new_sum)

        return (lax.cond(on_path(label), visit, lambda state: state, state_pair), None)

    start_max = jnp.full((KV_HEADS, query_rows), -1e30, jnp.float32)
    start_sum = jnp.zeros((KV_HEADS, query_rows), jnp.float32)
    (row_max, row_sum), unused = lax.scan(
        pass_stats, (start_max, start_sum), (key_blocks, value_blocks, segment_labels)
    )

    def probs_of(key_block, label):
        return jnp.exp(scores_of(key_block, label) - row_max[..., None]) / row_sum[..., None]

    def pass_values(state_pair, inputs_block):
        key_block, value_block, label = inputs_block

        def visit(state):
            accumulated, exact_out = state
            prob_block = probs_of(key_block, label)
            accumulated = accumulated + jnp.einsum(
                "grk,kgh->grh",
                prob_block.astype(jnp.bfloat16),
                value_block,
                preferred_element_type=jnp.float32,
            )
            exact_out = exact_out + jnp.einsum(
                "grk,kgh->grh",
                prob_block,
                value_block.astype(jnp.float32),
                preferred_element_type=jnp.float32,
                precision=highest,
            )
            return (accumulated, exact_out)

        return (lax.cond(on_path(label), visit, lambda state: state, state_pair), None)

    zero_out = jnp.zeros((KV_HEADS, query_rows, HEAD), jnp.float32)
    (accumulated, exact_out), unused = lax.scan(
        pass_values, (zero_out, zero_out), (key_blocks, value_blocks, segment_labels)
    )
    attended = (
        accumulated.reshape(KV_HEADS, repeat_heads, tok_count, HEAD)
        .transpose(2, 0, 1, 3)
        .reshape(tok_count, HEADS * HEAD)
        .astype(jnp.bfloat16)
    )
    branch = jnp.dot(attended, out_full, preferred_element_type=jnp.float32)
    middle = inputs + branch
    scale_two = lax.rsqrt(jnp.mean(middle * middle, axis=-1, keepdims=True) + epsilon)
    normed_two = middle * scale_two
    gain_second = gain_two.astype(jnp.float32)
    hidden_two = (normed_two * gain_second).astype(jnp.bfloat16)
    logits = jnp.dot(hidden_two, router_full, preferred_element_type=jnp.float32)
    picked_one = (
        routes[0][:, :, None] == jnp.arange(EXPERTS, dtype=jnp.int32)[None, None, :]
    ).astype(jnp.float32)
    chosen = jnp.sum(picked_one * logits[:, None, :], axis=-1)
    gate_probs = jax.nn.softmax(chosen, axis=-1)
    expert_ids = routes[0].reshape(-1)
    order_row = claim_order[0, 0]
    pair_count = expert_ids.shape[0]
    member = (expert_ids[:, None] == jnp.arange(EXPERTS, dtype=jnp.int32)[None, :]).astype(
        jnp.bfloat16
    )
    earlier = (order_row[None, :] < order_row[:, None]).astype(jnp.bfloat16)
    before = jnp.dot(earlier, member, preferred_element_type=jnp.float32)
    slot_index = jnp.sum(before * member.astype(jnp.float32), axis=1).astype(jnp.int32)
    owner_rank = expert_ids // local_experts
    local_rank = expert_ids % local_experts
    target = jnp.where(
        slot_index < CAP, (local_rank * expert_peers + owner_rank) * CAP + slot_index, EXPERTS * CAP
    )
    slot_pairs = (
        jnp.full((EXPERTS * CAP + 1,), pair_count, jnp.int32)
        .at[target]
        .set(jnp.arange(pair_count, dtype=jnp.int32))[: EXPERTS * CAP]
    )
    padded_two = jnp.concatenate([hidden_two, jnp.zeros((1, model_width), jnp.bfloat16)], axis=0)
    send_rows = padded_two[slot_pairs // TOP].reshape(local_experts, expert_peers, CAP, model_width)
    arrived = lax.all_to_all(send_rows, "expert", split_axis=1, concat_axis=1, tiled=True)
    expert_rows = arrived.reshape(local_experts, expert_peers * CAP, model_width)
    gate_act = jnp.einsum(
        "erd,edf->erf", expert_rows, gate_full, preferred_element_type=jnp.float32
    )
    up_act = jnp.einsum("erd,edf->erf", expert_rows, up_full, preferred_element_type=jnp.float32)
    inner = (jax.nn.silu(gate_act) * up_act).astype(jnp.bfloat16)
    expert_out = jnp.einsum(
        "erf,efd->erd", inner, down_full, preferred_element_type=jnp.float32
    ).astype(jnp.bfloat16)
    returned = lax.all_to_all(
        expert_out.reshape(local_experts, expert_peers, CAP, model_width),
        "expert",
        split_axis=1,
        concat_axis=1,
        tiled=True,
    )
    returned = jnp.concatenate(
        [returned.reshape(EXPERTS * CAP, model_width), jnp.zeros((1, model_width), jnp.bfloat16)],
        axis=0,
    )
    pair_out = returned[target].reshape(tok_count, TOP, model_width).astype(jnp.float32)
    mixture = jnp.sum(gate_probs[:, :, None] * pair_out, axis=1)
    block_out = (middle + mixture).astype(jnp.bfloat16)
    grad_result = cotangent[0].astype(jnp.float32)
    grad_gates = jnp.sum(pair_out * grad_result[:, None, :], axis=-1)
    grad_pairs = (
        (gate_probs[:, :, None] * grad_result[:, None, :])
        .astype(jnp.bfloat16)
        .reshape(pair_count, model_width)
    )
    grad_padded = jnp.concatenate([grad_pairs, jnp.zeros((1, model_width), jnp.bfloat16)], axis=0)
    grad_send = grad_padded[slot_pairs].reshape(local_experts, expert_peers, CAP, model_width)
    grad_arrived, rows_back = (
        lax.all_to_all(grad_send, "expert", split_axis=1, concat_axis=1, tiled=True),
        lax.all_to_all(send_rows, "expert", split_axis=1, concat_axis=1, tiled=True),
    )
    rows_again = rows_back.reshape(local_experts, expert_peers * CAP, model_width)
    gate_again = jnp.einsum(
        "erd,edf->erf", rows_again, gate_full, preferred_element_type=jnp.float32
    )
    up_again = jnp.einsum("erd,edf->erf", rows_again, up_full, preferred_element_type=jnp.float32)
    inner_again = (jax.nn.silu(gate_again) * up_again).astype(jnp.bfloat16)
    grad_expert_out = grad_arrived.reshape(local_experts, expert_peers * CAP, model_width)
    grad_inner = jnp.einsum(
        "erd,efd->erf", grad_expert_out, down_full, preferred_element_type=jnp.float32
    )
    grad_down_local = jnp.einsum(
        "erf,erd->efd", inner_again, grad_expert_out, preferred_element_type=jnp.float32
    )
    sigmoid_gate = jax.nn.sigmoid(gate_again)
    swish = gate_again * sigmoid_gate
    grad_gate_act = (
        grad_inner * up_again * (sigmoid_gate * (1.0 + gate_again * (1.0 - sigmoid_gate)))
    ).astype(jnp.bfloat16)
    grad_up_act = (grad_inner * swish).astype(jnp.bfloat16)
    grad_gate_local = jnp.einsum(
        "erd,erf->edf", rows_again, grad_gate_act, preferred_element_type=jnp.float32
    )
    grad_up_local = jnp.einsum(
        "erd,erf->edf", rows_again, grad_up_act, preferred_element_type=jnp.float32
    )
    grad_rows = (
        jnp.einsum("erf,edf->erd", grad_gate_act, gate_full, preferred_element_type=jnp.float32)
        + jnp.einsum("erf,edf->erd", grad_up_act, up_full, preferred_element_type=jnp.float32)
    ).astype(jnp.bfloat16)
    grad_back = lax.all_to_all(
        grad_rows.reshape(local_experts, expert_peers, CAP, model_width),
        "expert",
        split_axis=1,
        concat_axis=1,
        tiled=True,
    )
    grad_back = jnp.concatenate(
        [grad_back.reshape(EXPERTS * CAP, model_width), jnp.zeros((1, model_width), jnp.bfloat16)],
        axis=0,
    )
    grad_hidden_two = jnp.sum(
        grad_back[target].reshape(tok_count, TOP, model_width).astype(jnp.float32), axis=1
    )
    grad_chosen = gate_probs * (
        grad_gates - jnp.sum(gate_probs * grad_gates, axis=-1, keepdims=True)
    )
    grad_logits = jnp.sum(picked_one * grad_chosen[:, :, None], axis=1).astype(jnp.bfloat16)
    grad_hidden_two = grad_hidden_two + jnp.dot(
        grad_logits, router_full.T, preferred_element_type=jnp.float32
    )
    grad_router_local = jnp.dot(hidden_two.T, grad_logits, preferred_element_type=jnp.float32)
    grad_middle_norm, grad_gain_two = norm_backward(
        grad_hidden_two, normed_two, scale_two, gain_second
    )
    grad_middle = grad_result + grad_middle_norm
    grad_branch = grad_middle.astype(jnp.bfloat16)
    grad_out_local = jnp.dot(attended.T, grad_branch, preferred_element_type=jnp.float32)
    grad_attended = jnp.dot(grad_branch, out_full.T, preferred_element_type=jnp.float32).astype(
        jnp.bfloat16
    )
    grad_groups = (
        grad_attended.reshape(tok_count, KV_HEADS, repeat_heads, HEAD)
        .transpose(1, 2, 0, 3)
        .reshape(KV_HEADS, query_rows, HEAD)
    )
    row_delta = jnp.sum(grad_groups.astype(jnp.float32) * exact_out, axis=-1)
    zero_key = jnp.zeros((tok_count, KV_HEADS, HEAD), jnp.float32)

    def pass_grads(grad_query, inputs_block):
        key_block, value_block, label = inputs_block

        def visit(carried):
            prob_block = probs_of(key_block, label)
            grad_probs = jnp.einsum(
                "grh,kgh->grk", grad_groups, value_block, preferred_element_type=jnp.float32
            )
            grad_scores = (prob_block * (grad_probs - row_delta[..., None])).astype(jnp.bfloat16)
            carried = carried + jnp.einsum(
                "grk,kgh->grh", grad_scores, key_block, preferred_element_type=jnp.float32
            )
            grad_key_block = (
                jnp.einsum(
                    "grk,grh->kgh", grad_scores, query_groups, preferred_element_type=jnp.float32
                )
                * score_scale
            )
            grad_value_block = jnp.einsum(
                "grk,grh->kgh",
                prob_block.astype(jnp.bfloat16),
                grad_groups,
                preferred_element_type=jnp.float32,
            )
            return (carried, (grad_key_block, grad_value_block))

        def skip(carried):
            return (carried, (zero_key, zero_key))

        return lax.cond(on_path(label), visit, skip, grad_query)

    grad_query_groups, (grad_key_blocks, grad_value_blocks) = lax.scan(
        pass_grads,
        jnp.zeros((KV_HEADS, query_rows, HEAD), jnp.float32),
        (key_blocks, value_blocks, segment_labels),
    )
    grad_key_all = grad_key_blocks.reshape(total_keys, KV_HEADS * HEAD)
    grad_value_all = grad_value_blocks.reshape(total_keys, KV_HEADS * HEAD)
    grad_key_mine, grad_value_mine = (
        lax.psum_scatter(
            grad_key_all.astype(jnp.bfloat16), "dp", scatter_dimension=0, tiled=True
        ).astype(jnp.float32),
        lax.psum_scatter(
            grad_value_all.astype(jnp.bfloat16), "dp", scatter_dimension=0, tiled=True
        ).astype(jnp.float32),
    )
    grad_query_rot = (
        (grad_query_groups * score_scale)
        .reshape(KV_HEADS, repeat_heads, tok_count, HEAD)
        .transpose(2, 0, 1, 3)
        .reshape(tok_count, HEADS, HEAD)
    )
    grad_query_raw = (
        rotate(grad_query_rot, cosine, -sine_part)
        .reshape(tok_count, HEADS * HEAD)
        .astype(jnp.bfloat16)
    )
    grad_key_raw = (
        rotate(grad_key_mine.reshape(tok_count, KV_HEADS, HEAD), cosine, -sine_part)
        .reshape(tok_count, KV_HEADS * HEAD)
        .astype(jnp.bfloat16)
    )
    grad_value_raw = grad_value_mine.astype(jnp.bfloat16)
    grad_query_local = jnp.dot(hidden_one.T, grad_query_raw, preferred_element_type=jnp.float32)
    grad_key_local = jnp.dot(hidden_one.T, grad_key_raw, preferred_element_type=jnp.float32)
    grad_value_local = jnp.dot(hidden_one.T, grad_value_raw, preferred_element_type=jnp.float32)
    grad_hidden_one = (
        jnp.dot(grad_query_raw, query_full.T, preferred_element_type=jnp.float32)
        + jnp.dot(grad_key_raw, key_full.T, preferred_element_type=jnp.float32)
        + jnp.dot(grad_value_raw, value_full.T, preferred_element_type=jnp.float32)
    )
    grad_inputs_norm, grad_gain_one = norm_backward(
        grad_hidden_one, normed_one, scale_one, gain_first
    )
    grad_inputs = grad_middle + grad_inputs_norm
    grad_gate_mine, grad_up_mine, grad_down_mine = (
        lax.psum_scatter(
            grad_gate_local.astype(jnp.bfloat16), "dp", scatter_dimension=1, tiled=True
        ).astype(jnp.float32),
        lax.psum_scatter(
            grad_up_local.astype(jnp.bfloat16), "dp", scatter_dimension=1, tiled=True
        ).astype(jnp.float32),
        lax.psum_scatter(
            grad_down_local.astype(jnp.bfloat16), "dp", scatter_dimension=1, tiled=True
        ).astype(jnp.float32),
    )
    shard_rows = (
        lax.psum_scatter(
            grad_gain_one.astype(jnp.bfloat16), "dp", scatter_dimension=0, tiled=True
        ).astype(jnp.float32),
        lax.psum_scatter(
            grad_query_local.astype(jnp.bfloat16), "dp", scatter_dimension=0, tiled=True
        ).astype(jnp.float32),
        lax.psum_scatter(
            grad_key_local.astype(jnp.bfloat16), "dp", scatter_dimension=0, tiled=True
        ).astype(jnp.float32),
        lax.psum_scatter(
            grad_value_local.astype(jnp.bfloat16), "dp", scatter_dimension=0, tiled=True
        ).astype(jnp.float32),
        lax.psum_scatter(
            grad_out_local.astype(jnp.bfloat16), "dp", scatter_dimension=0, tiled=True
        ).astype(jnp.float32),
        lax.psum_scatter(
            grad_gain_two.astype(jnp.bfloat16), "dp", scatter_dimension=0, tiled=True
        ).astype(jnp.float32),
        lax.psum_scatter(
            grad_router_local.astype(jnp.bfloat16), "dp", scatter_dimension=0, tiled=True
        ).astype(jnp.float32),
    )
    shared = (
        lax.psum(shard_rows[0].astype(jnp.bfloat16), "expert").astype(jnp.float32),
        lax.psum(shard_rows[1].astype(jnp.bfloat16), "expert").astype(jnp.float32),
        lax.psum(shard_rows[2].astype(jnp.bfloat16), "expert").astype(jnp.float32),
        lax.psum(shard_rows[3].astype(jnp.bfloat16), "expert").astype(jnp.float32),
        lax.psum(shard_rows[4].astype(jnp.bfloat16), "expert").astype(jnp.float32),
        lax.psum(shard_rows[5].astype(jnp.bfloat16), "expert").astype(jnp.float32),
        lax.psum(shard_rows[6].astype(jnp.bfloat16), "expert").astype(jnp.float32),
    )
    return (
        block_out[None],
        grad_inputs[None],
        shared[0],
        shared[1],
        shared[2],
        shared[3],
        shared[4],
        shared[5],
        shared[6],
        grad_gate_mine,
        grad_up_mine,
        grad_down_mine,
    )


SLOTS = 32
PAD_TOKENS = 32
LANES = 128
TILE = 256
MESH = pl.DeviceIdType.MESH
log2e = 1.4426950408889634


def dot_f32(a, b, dims=((1,), (0,))):
    return lax.dot_general(a, b, (dims, ((), ())), preferred_element_type=jnp.float32)


def split3(value):
    high = value.astype(jnp.bfloat16)
    rest = value - high.astype(jnp.float32)
    middle = rest.astype(jnp.bfloat16)
    low = (rest - middle.astype(jnp.float32)).astype(jnp.bfloat16)
    return high, middle, low


def one_hot(shape, test):
    row = lax.broadcasted_iota(jnp.int32, shape, 0)
    column = lax.broadcasted_iota(jnp.int32, shape, 1)
    return jnp.where(test(row, column), 1.0, 0.0).astype(jnp.bfloat16)


class Place:
    def __init__(self):
        self.dp = lax.axis_index("dp")
        self.side = lax.axis_index("expert")
        self.z = self.dp // 4
        self.x = (self.dp // 2) % 2
        self.c = self.dp % 2

    def index(self, z, x, c):
        return z * 4 + x * 2 + c

    def others(self):
        return [self.z + 1 - 2 * (self.z % 2), (self.z + 2) % 4, 3 - self.z]


def remote(src, dst, send, recv, dp, side):
    return pltpu.make_async_remote_copy(
        src_ref=src,
        dst_ref=dst,
        send_sem=send,
        recv_sem=recv,
        device_id={"dp": dp, "expert": side},
        device_id_type=MESH,
    )


def enter(device_count, dp_count):
    rank = lax.axis_index("expert") * dp_count + lax.axis_index("dp")
    barrier = pltpu.get_barrier_semaphore()

    @pl.loop(1, device_count)
    def _(step):
        other = (rank + step) % device_count
        pl.semaphore_signal(
            barrier,
            inc=1,
            device_id={"dp": other % dp_count, "expert": other // dp_count},
            device_id_type=MESH,
        )

    pl.semaphore_wait(barrier, device_count - 1)


class Column:
    def __init__(self, place, own, slot, send, recv, local):
        self.place, self.own, self.slot = place, own, slot
        self.send, self.recv, self.local = send, recv, local

    def hop(self, z, step, own=False):
        p = self.place
        source = self.own if own else self.slot(z)
        number = z if step > 0 else 4 + z
        target = p.index(p.z + step, p.x, p.c)
        return remote(source, self.slot(z), self.send.at[number], self.recv(z), target, p.side)

    def own_copy(self):
        return pltpu.make_async_copy(self.own, self.slot(self.place.z), self.local)

    def upward(self, act):
        pl.when(self.place.z < 3)(act)

    def downward(self, act):
        pl.when(self.place.z > 0)(act)

    def start(self):
        z = self.place.z
        self.upward(lambda: self.hop(z, 1, True).start())
        self.downward(lambda: self.hop(z, -1, True).start())
        self.own_copy().start()

    def forward(self, low=1, high=4, then=None):
        z = self.place.z

        @pl.loop(low, high)
        def _(away):
            @pl.when(z - away >= 0)
            def _():
                self.hop(z - away, 1).wait_recv()
                self.upward(lambda: self.hop(z - away, 1).start())
                if then is not None:
                    then(z - away)

            @pl.when(z + away <= 3)
            def _():
                self.hop(z + away, -1).wait_recv()
                self.downward(lambda: self.hop(z + away, -1).start())
                if then is not None:
                    then(z + away)

    def finish(self):
        z = self.place.z

        @pl.loop(0, 4)
        def _(origin):
            @pl.when((origin <= z) & (z < 3))
            def _():
                self.hop(origin, 1).wait_send()

            @pl.when((origin >= z) & (z > 0))
            def _():
                self.hop(origin, -1).wait_send()


class Gather:
    def __init__(self, place, own, slot, send, recv, local):
        self.place, self.own, self.slot = place, own, slot
        self.send, self.recv = send, recv
        self.column = Column(
            place,
            own,
            lambda z: slot(place.index(z, place.x, place.c)),
            send,
            lambda z: recv.at[place.index(z, place.x, place.c)],
            local,
        )

    def copy(self, z, x, c, to_x, to_c, number, own=False):
        p = self.place
        shard = p.index(z, x, c)
        source = self.own if own else self.slot(shard)
        target = p.index(p.z, to_x, to_c)
        return remote(
            source, self.slot(shard), self.send.at[number], self.recv.at[shard], target, p.side
        )

    def to_x(self, z, own=False):
        p = self.place
        return self.copy(z, p.x, p.c, 1 - p.x, p.c, 8 + z, own)

    def to_core(self, z, x, own=False):
        p = self.place
        return self.copy(z, x, p.c, p.x, 1 - p.c, 12 + z * 2 + x, own)

    def start(self):
        p = self.place
        self.column.start()
        self.to_x(p.z, True).start()
        self.to_core(p.z, p.x, True).start()

    def forward_z(self):
        def then(z):
            self.to_x(z).start()
            self.to_core(z, self.place.x).start()

        self.column.forward(then=then)

    def forward_x(self):
        p = self.place

        def pass_on(z):
            self.to_core(z, 1 - p.x).wait_recv()
            self.to_core(z, 1 - p.x).start()

        pass_on(p.z)

        @pl.loop(1, 4)
        def _(away):
            pl.when(p.z - away >= 0)(lambda: pass_on(p.z - away))
            pl.when(p.z + away <= 3)(lambda: pass_on(p.z + away))

    def finish(self):
        p = self.place

        @pl.loop(0, 4)
        def _(z):
            for x in range(2):
                self.copy(z, x, 1 - p.c, p.x, 1 - p.c, 12).wait_recv()
                self.to_core(z, x).wait_send()
            self.to_x(z).wait_send()

        self.column.finish()
        self.column.own_copy().wait()


class PlaneSwap:
    def __init__(self, place, source, target, send, recv, local, dp_count):
        self.place, self.source, self.target = place, source, target
        self.send, self.recv, self.local = send, recv, local
        self.dp_count = dp_count

    def of(self, member):
        return member // 4, (member // 2) % 2, member % 2

    def rank(self, z, side, x, c):
        return side * self.dp_count + self.place.index(z, x, c)

    def me(self):
        p = self.place
        return p.side * 4 + p.x * 2 + p.c

    def block(self, rank):
        return self.target.at[rows_of(rank, SLOTS)]

    def copy(self, z, step, to, origin):
        p = self.place
        side, x, c = self.of(to)
        return remote(
            self.source.at[z, rows_of(to, SLOTS)],
            self.block(self.rank(z, *self.of(origin))),
            self.send.at[z, step],
            self.recv.at[z, step],
            p.index(p.z, x, c),
            side,
        )

    def own_copy(self, z):
        return pltpu.make_async_copy(
            self.source.at[z, rows_of(self.me(), SLOTS)],
            self.block(self.rank(z, *self.of(self.me()))),
            self.local.at[z],
        )

    def start(self, z):
        for step in range(1, 8):
            self.copy(z, step, (self.me() + step) % 8, self.me()).start()
        self.own_copy(z).start()

    def finish(self):
        @pl.loop(0, 4)
        def _(z):
            for step in range(1, 8):
                other = (self.me() + 8 - step) % 8
                self.copy(z, step, other, other).wait()
            self.own_copy(z).wait()


class RowSwap:
    def __init__(self, source, target, send, recv, local, dp_count, device_count):
        self.source, self.target = source, target
        self.send, self.recv, self.local = send, recv, local
        self.dp_count, self.device_count = dp_count, device_count
        self.rank = lax.axis_index("expert") * dp_count + lax.axis_index("dp")

    def block(self, ref, index):
        return ref.at[pl.ds(pl.multiple_of(index * SLOTS, SLOTS), SLOTS)]

    def copy(self, step, to, landing):
        return remote(
            self.block(self.source, to),
            self.block(self.target, landing),
            self.send.at[step],
            self.recv.at[step],
            to % self.dp_count,
            to // self.dp_count,
        )

    def own_copy(self):
        return pltpu.make_async_copy(
            self.block(self.source, self.rank), self.block(self.target, self.rank), self.local
        )

    def start(self):
        @pl.loop(1, self.device_count)
        def _(step):
            self.copy(step, (self.rank + step) % self.device_count, self.rank).start()

        self.own_copy().start()

    def start_one(self, to):
        @pl.when(to != self.rank)
        def _():
            step = (to + self.device_count - self.rank) % self.device_count
            self.copy(step, to, self.rank).start()

    def finish(self):
        @pl.loop(1, self.device_count)
        def _(step):
            other = (self.rank + self.device_count - step) % self.device_count
            self.copy(step, other, other).wait()

        self.own_copy().wait()


class WeightSwap:
    def __init__(self, place, pairs, send, recv, local, dp_count):
        self.place, self.pairs = place, pairs
        self.send, self.recv, self.local = send, recv, local
        self.dp_count = dp_count

    def copies(self, step, to, landing):
        out = []
        for i, (source, target) in enumerate(self.pairs):
            rows = source.shape[1]
            out.append(
                remote(
                    source.at[to],
                    target.at[pl.ds(pl.multiple_of(landing * rows, rows), rows)],
                    self.send.at[step, i],
                    self.recv.at[step, i],
                    to,
                    self.place.side,
                )
            )
        return out

    def own_copies(self):
        dp = self.place.dp
        return [
            pltpu.make_async_copy(
                source.at[dp],
                target.at[pl.ds(pl.multiple_of(dp * source.shape[1], source.shape[1]), source.shape[1])],
                self.local.at[i],
            )
            for i, (source, target) in enumerate(self.pairs)
        ]

    def start(self, low, high):
        @pl.loop(low, high)
        def _(step):
            for copy in self.copies(step, (self.place.dp + step) % self.dp_count, self.place.dp):
                copy.start()

    def start_own(self):
        for copy in self.own_copies():
            copy.start()

    def finish(self):
        @pl.loop(1, self.dp_count)
        def _(step):
            other = (self.place.dp + self.dp_count - step) % self.dp_count
            for copy in self.copies(step, other, other):
                copy.wait()

        for copy in self.own_copies():
            copy.wait()


def columns(tile, width=TILE):
    return pl.ds(pl.multiple_of(tile * width, width), width)


def rows_of(index, count):
    return pl.ds(pl.multiple_of(index * count, count), count)


def front_kernel(
    bias_ref,
    tokens_ref,
    cotangent_ref,
    project_ref,
    out_ref,
    target_ref,
    route_ref,
    cosine_ref,
    sine_ref,
    gate_ref,
    up_ref,
    down_ref,
    project_full,
    out_full,
    keys_ref,
    query_ref,
    attended_ref,
    exact_ref,
    stat_ref,
    middle_ref,
    hidden_ref,
    probs_ref,
    rows_in,
    grads_in,
    gate_own,
    up_own,
    down_own,
    hidden_one,
    keys_own,
    row_send,
    grad_send,
    target_all,
    gate_own_row,
    gate_all,
    hidden_all,
    grad_all,
    placed,
    acc,
    top,
    total,
    project_send,
    project_recv,
    out_send,
    out_recv,
    keys_send,
    keys_recv,
    row_send_sem,
    row_recv_sem,
    row_local,
    grad_send_sem,
    grad_recv_sem,
    grad_local,
    column_send,
    column_recv,
    weight_send,
    weight_recv,
    weight_local,
    local,
):
    dp_count = keys_ref.shape[0]
    device_count = rows_in.shape[0] // SLOTS
    tok_count, model_width = tokens_ref.shape
    query_width = HEADS * HEAD
    key_width = KV_HEADS * HEAD
    repeat_heads = HEADS // KV_HEADS
    factor = log2e * HEAD ** (-0.5)
    place = Place()
    shard_rows = project_ref.shape[0]

    def shard_of(full):
        return lambda index: full.at[rows_of(index, shard_rows)]

    project = Gather(
        place, project_ref, shard_of(project_full), project_send, project_recv, local.at[0]
    )
    out = Gather(place, out_ref, shard_of(out_full), out_send, out_recv, local.at[1])
    keys = Gather(
        place, keys_own, lambda index: keys_ref.at[index], keys_send, keys_recv, local.at[2]
    )
    rows = PlaneSwap(place, row_send, rows_in, row_send_sem, row_recv_sem, row_local, dp_count)
    grads = PlaneSwap(place, grad_send, grads_in, grad_send_sem, grad_recv_sem, grad_local, dp_count)

    def column(number, own, land):
        return Column(
            place,
            own,
            land,
            column_send.at[number],
            lambda z: column_recv.at[number, z],
            local.at[3 + number],
        )

    targets = column(0, target_ref, lambda z: target_all.at[z])
    gates = column(1, gate_own_row, lambda z: gate_all.at[z])
    hidden = column(2, hidden_ref, lambda z: hidden_all.at[z, pl.ds(0, tok_count)])
    cotangents = column(3, cotangent_ref, lambda z: grad_all.at[z])
    weights = WeightSwap(
        place,
        ((gate_ref, gate_own), (up_ref, up_own), (down_ref, down_own)),
        weight_send,
        weight_recv,
        weight_local,
        dp_count,
    )

    enter(device_count, dp_count)
    targets.start()
    project.start()
    cotangents.start()
    plane_slots = 8 * SLOTS
    targets.forward()
    targets.own_copy().wait()
    slot_row = lax.broadcasted_iota(jnp.int32, (plane_slots, TILE), 0)
    slot_lane = lax.broadcasted_iota(jnp.int32, (plane_slots, TILE), 1)
    member = slot_row // SLOTS
    label = ((member // 4) * dp_count + place.z * 4 + member % 4) * SLOTS + slot_row % SLOTS
    label = label.astype(jnp.float32)
    spare = (slot_lane - tok_count == member) & (slot_row % SLOTS == CAP)

    def match(z, choice):
        return label == target_all[z, choice : choice + 1]

    for z in range(4):
        hit = spare
        for choice in range(TOP):
            hit = hit | match(z, choice)
        placed[z] = jnp.where(hit, 1.0, 0.0).astype(jnp.bfloat16)
    hidden_all[:, tok_count:] = jnp.zeros((4, PAD_TOKENS, model_width), jnp.bfloat16)

    project.forward_z()
    project.forward_x()
    project.finish()
    cotangents.forward(1, 2)

    lanes_of = one_hot((8, LANES), lambda row, column: column == row + EXPERTS)
    gains = dot_f32(lanes_of, project_full[:, query_width + 2 * key_width :], ((1,), (1,)))
    gain_first, gain_second = gains[0:1], gains[1:2]
    chunk = 32

    @pl.loop(0, tok_count // chunk)
    def _(index):
        value = tokens_ref[rows_of(index, chunk)].astype(jnp.float32)
        scale = lax.rsqrt(jnp.mean(value * value, axis=-1, keepdims=True) + epsilon)
        hidden_one[rows_of(index, chunk)] = (value * scale * gain_first).astype(jnp.bfloat16)

    def turned(tile):
        value = dot_f32(hidden_one[...], project_full[:, columns(tile)])
        halves = []
        for half in range(TILE // HEAD):
            part = value[:, half * HEAD : (half + 1) * HEAD]
            halves.append(
                part * cosine_ref[...] + pltpu.roll(part, HEAD // 2, 1) * sine_ref[...]
            )
        return jnp.concatenate(halves, axis=1).astype(jnp.bfloat16)

    keys_own[:, :key_width] = turned(query_width // TILE)
    keys_own[:, key_width:] = dot_f32(
        hidden_one[...], project_full[:, query_width + key_width : query_width + 2 * key_width]
    ).astype(jnp.bfloat16)
    keys.start()

    @pl.loop(0, query_width // TILE)
    def _(tile):
        query_ref[:, columns(tile)] = turned(tile)

    keys.forward_z()
    keys.forward_x()
    keys.finish()
    out.start()
    cotangents.forward(2, 4)
    weights.start(1, dp_count)
    weights.start_own()

    row = lax.broadcasted_iota(jnp.int32, (tok_count, tok_count), 0)
    column = lax.broadcasted_iota(jnp.int32, (tok_count, tok_count), 1)
    causal = column <= row

    def visit(label, own):
        for head in range(HEADS):
            group = head // repeat_heads
            query = query_ref[:, head * HEAD : (head + 1) * HEAD]
            key = keys_ref[label, :, group * HEAD : (group + 1) * HEAD]
            value = keys_ref[label, :, (KV_HEADS + group) * HEAD : (KV_HEADS + group + 1) * HEAD]
            scores = dot_f32(query, key, ((1,), (1,)))
            if own:
                scores = jnp.where(causal, scores, -1e30)
                peak = jnp.max(scores, axis=-1, keepdims=True)
                shift = peak
            else:
                bias = bias_ref[label]
                peak = jnp.maximum(top[head], jnp.max(scores, axis=-1, keepdims=True) + bias)
                shift = peak - bias
            prob = jnp.exp2((scores - shift) * factor)
            prob_high = prob.astype(jnp.bfloat16)
            prob_low = (prob - prob_high.astype(jnp.float32)).astype(jnp.bfloat16)
            part = dot_f32(prob_high, value) + dot_f32(prob_low, value)
            part_total = jnp.sum(prob, axis=-1, keepdims=True)
            if own:
                acc[head] = part
                total[head] = part_total
            else:
                fade = jnp.exp2((top[head] - peak) * factor)
                acc[head] = acc[head] * fade + part
                total[head] = total[head] * fade + part_total
            top[head] = peak

    visit(place.dp, True)

    @pl.loop(0, place.dp)
    def _(label):
        visit(label, False)

    out.forward_z()
    out.forward_x()
    cotangents.own_copy().wait()

    @pl.loop(0, 4)
    def _(z):
        @pl.loop(0, model_width // TILE)
        def _(tile):
            grad_send[z, :, columns(tile)] = dot_f32(
                placed[z, :, :tok_count], grad_all[z, :, columns(tile)]
            ).astype(jnp.bfloat16)

        grads.start(z)

    lane = lax.broadcasted_iota(jnp.int32, (tok_count, LANES), 1)
    stats = jnp.zeros((tok_count, LANES), jnp.float32)
    for head in range(HEADS):
        exact = acc[head] / total[head]
        exact_ref[:, head * HEAD : (head + 1) * HEAD] = exact
        attended_ref[:, head * HEAD : (head + 1) * HEAD] = exact.astype(jnp.bfloat16)
        stats = jnp.where(lane == head, top[head] * factor + jnp.log2(total[head]), stats)
    stat_ref[...] = stats
    out.finish()

    @pl.loop(0, model_width // TILE)
    def _(tile):
        middle_ref[:, columns(tile)] = tokens_ref[:, columns(tile)].astype(jnp.float32) + dot_f32(
            attended_ref[...], out_full[:, columns(tile)]
        )

    @pl.loop(0, tok_count // chunk)
    def _(index):
        value = middle_ref[rows_of(index, chunk)]
        scale = lax.rsqrt(jnp.mean(value * value, axis=-1, keepdims=True) + epsilon)
        hidden_ref[rows_of(index, chunk)] = (value * scale * gain_second).astype(jnp.bfloat16)

    hidden.start()
    router = project_full[:, query_width + 2 * key_width :]
    chosen = [route_ref[:, choice : choice + 1] == lane for choice in range(TOP)]
    mask = chosen[0]
    for choice in range(1, TOP):
        mask = mask | chosen[choice]
    logits = jnp.where(mask, dot_f32(hidden_ref[...], router), -1e30)
    weight = jnp.exp(logits - jnp.max(logits, axis=-1, keepdims=True))
    probs = weight / jnp.sum(weight, axis=-1, keepdims=True)
    probs_ref[...] = probs
    by_choice = jnp.zeros((tok_count, LANES), jnp.float32)
    for choice in range(TOP):
        gate = jnp.sum(jnp.where(chosen[choice], probs, 0.0), axis=-1, keepdims=True)
        by_choice = jnp.where(lane == choice, gate, by_choice)
    first_lanes = one_hot((8, LANES), lambda r, col: r == col)
    gate_own_row[...] = jnp.zeros(gate_own_row.shape, jnp.float32)
    gate_own_row[:, :tok_count] = sum(
        dot_f32(first_lanes, part, ((1,), (1,))) for part in split3(by_choice)
    )
    gates.start()
    fold = one_hot((8, plane_slots), lambda r, col: col // SLOTS == r)
    def dispatch(z):
        gate = jnp.zeros((plane_slots, 1), jnp.float32)
        for choice in range(TOP):
            gate += jnp.sum(
                jnp.where(match(z, choice), gate_all[z, choice : choice + 1], 0.0),
                axis=-1,
                keepdims=True,
            )
        numbers = dot_f32(fold, put_parts(gate)).astype(jnp.bfloat16)
        numbers = jnp.concatenate([numbers, jnp.zeros((8, LANES), jnp.bfloat16)], axis=0)
        hidden_all[z, tok_count : tok_count + 16, :LANES] = numbers

        @pl.loop(0, model_width // TILE)
        def _(tile):
            row_send[z, :, columns(tile)] = dot_f32(
                placed[z], hidden_all[z, :, columns(tile)]
            ).astype(jnp.bfloat16)

        rows.start(z)
    hidden.own_copy().wait()
    gates.own_copy().wait()
    dispatch(place.z)
    gates.forward()
    hidden.forward(then=dispatch)
    for gather in (targets, cotangents, hidden, gates):
        gather.finish()
    weights.finish()
    grads.finish()
    rows.finish()


def front(bias, tokens, cotangent, project, out, target, route, cosine, sine, gate, up, down):
    dp_count = lax.axis_size("dp")
    device_count = dp_count * lax.axis_size("expert")
    tok_count, model_width = tokens.shape
    query_width = HEADS * HEAD
    key_width = KV_HEADS * HEAD
    vmem = pl.BlockSpec(memory_space=pltpu.VMEM)
    anywhere = pl.BlockSpec(memory_space=pl.ANY)
    slots = device_count * SLOTS
    low, full = jnp.bfloat16, jnp.float32
    shape = jax.ShapeDtypeStruct
    ff_width = gate.shape[2]
    outs = (
        (shape((model_width, project.shape[1]), low), vmem),
        (shape((model_width, model_width), low), vmem),
        (shape((dp_count, tok_count, 2 * key_width), low), vmem),
        (shape((tok_count, query_width), low), vmem),
        (shape((tok_count, query_width), low), vmem),
        (shape((tok_count, query_width), full), vmem),
        (shape((tok_count, LANES), full), vmem),
        (shape((tok_count, model_width), full), vmem),
        (shape((tok_count, model_width), low), vmem),
        (shape((tok_count, LANES), full), vmem),
        (shape((slots, model_width), low), anywhere),
        (shape((slots, model_width), low), anywhere),
        (shape((model_width, ff_width), low), anywhere),
        (shape((model_width, ff_width), low), anywhere),
        (shape((ff_width, model_width), low), anywhere),
        (shape((tok_count, model_width), low), vmem),
    )
    dma = pltpu.SemaphoreType.DMA
    return pl.pallas_call(
        front_kernel,
        out_shape=tuple(o[0] for o in outs),
        in_specs=[pl.BlockSpec(memory_space=pltpu.SMEM)] + [vmem] * 8 + [anywhere] * 3,
        out_specs=tuple(o[1] for o in outs),
        scratch_shapes=[
            pltpu.VMEM((tok_count, 2 * key_width), low),
            pltpu.VMEM((4, 8 * SLOTS, model_width), low),
            pltpu.VMEM((4, 8 * SLOTS, model_width), low),
            pltpu.VMEM((4, 8, TILE), full),
            pltpu.VMEM((8, TILE), full),
            pltpu.VMEM((4, 8, TILE), full),
            pltpu.VMEM((4, tok_count + PAD_TOKENS, model_width), low),
            pltpu.VMEM((4, tok_count, model_width), low),
            pltpu.VMEM((4, 8 * SLOTS, TILE), low),
            pltpu.VMEM((HEADS, tok_count, HEAD), full),
            pltpu.VMEM((HEADS, tok_count, 1), full),
            pltpu.VMEM((HEADS, tok_count, 1), full),
        ]
        + [dma((20,)), dma((dp_count,))] * 3
        + [dma((4, 8)), dma((4, 8)), dma((4,))] * 2
        + [dma((4, 8)), dma((4, 4))]
        + [dma((dp_count, 3))] * 2
        + [dma((3,)), dma((7,))],
        compiler_params=pltpu.CompilerParams(
            collective_id=0, has_side_effects=True, vmem_limit_bytes=58 * 1024 * 1024
        ),
    )(bias, tokens, cotangent, project, out, target, route, cosine, sine, gate, up, down)


def pick_gates(block):
    rows = block.shape[0]
    blocks = rows // SLOTS
    spare = one_hot((blocks, rows), lambda r, col: col == r * SLOTS + CAP)
    member = one_hot((rows, blocks), lambda r, col: r // SLOTS == col)
    parts = dot_f32(member, dot_f32(spare, block).astype(jnp.bfloat16))
    row = lax.broadcasted_iota(jnp.int32, parts.shape, 0)
    lane = lax.broadcasted_iota(jnp.int32, parts.shape, 1)
    mine = (lane % SLOTS == row % SLOTS) & (lane < 3 * SLOTS)
    return jnp.sum(jnp.where(mine, parts, 0.0), axis=-1, keepdims=True)


def put_parts(column):
    shape = (column.shape[0], LANES)
    row = lax.broadcasted_iota(jnp.int32, shape, 0)
    lane = lax.broadcasted_iota(jnp.int32, shape, 1)
    high, mid, low = (part.astype(jnp.float32) for part in split3(column))
    part = jnp.where(lane < SLOTS, high, jnp.where(lane < 2 * SLOTS, mid, low))
    mine = (lane % SLOTS == row % SLOTS) & (lane < 3 * SLOTS)
    return jnp.where(mine, part, 0.0).astype(jnp.bfloat16)


def expert_kernel(
    rows_ref,
    grads_ref,
    gate_ref,
    up_ref,
    down_ref,
    rows_back,
    outs_back,
    gate_grad_ref,
    up_grad_ref,
    down_grad_ref,
    out_send,
    row_send,
    grad_out,
    inner_ref,
    gate_act_grad,
    up_act_grad,
    row_send_sem,
    row_recv_sem,
    out_send_sem,
    out_recv_sem,
    local,
):
    dp_count = lax.axis_size("dp")
    slots, model_width = rows_ref.shape
    ff_width = gate_ref.shape[1]
    device_count = slots // SLOTS
    enter(device_count, dp_count)
    rows = RowSwap(row_send, rows_back, row_send_sem, row_recv_sem, local.at[0], dp_count, device_count)
    outs = RowSwap(out_send, outs_back, out_send_sem, out_recv_sem, local.at[1], dp_count, device_count)
    tiles = slots // TILE
    per_tile = TILE // SLOTS

    @pl.loop(0, tiles)
    def _(step):
        tile = (step + rows.rank // per_tile) % tiles
        cut = rows_of(tile, TILE)
        row = rows_ref[cut]
        gate = pick_gates(row[:, :LANES])
        saved = []
        for n in range(ff_width // TILE):
            part = slice(n * TILE, (n + 1) * TILE)
            gate_act = dot_f32(row, gate_ref[:, part])
            up_act = dot_f32(row, up_ref[:, part])
            sigmoid = 1.0 / (1.0 + jnp.exp(-gate_act))
            swish = gate_act * sigmoid
            inner_ref[cut, part] = (swish * up_act).astype(jnp.bfloat16)
            saved.append((swish, up_act * (sigmoid * (1.0 + gate_act * (1.0 - sigmoid)))))
        inner = inner_ref[cut]
        gate_grad = jnp.zeros((TILE, 1), jnp.float32)
        for n in range(model_width // TILE):
            part = slice(n * TILE, (n + 1) * TILE)
            expert_out = dot_f32(inner, down_ref[:, part]).astype(jnp.bfloat16)
            out_send[cut, part] = expert_out
            grad = grads_ref[cut, part].astype(jnp.float32)
            gate_grad += jnp.sum(expert_out.astype(jnp.float32) * grad, axis=-1, keepdims=True)
            grad_out[cut, part] = (gate * grad).astype(jnp.bfloat16)
        grad = grad_out[cut]
        for n in range(ff_width // TILE):
            part = slice(n * TILE, (n + 1) * TILE)
            swish, slope = saved[n]
            grad_inner = dot_f32(grad, down_ref[part, :], ((1,), (1,)))
            gate_act_grad[cut, part] = (grad_inner * slope).astype(jnp.bfloat16)
            up_act_grad[cut, part] = (grad_inner * swish).astype(jnp.bfloat16)
        fold = one_hot((per_tile, TILE), lambda r, col: col // SLOTS == r)
        spread = one_hot((TILE, per_tile), lambda r, col: r == col * SLOTS + CAP)
        extra = dot_f32(spread, dot_f32(fold, put_parts(gate_grad)).astype(jnp.bfloat16))
        for n in range(model_width // TILE):
            part = slice(n * TILE, (n + 1) * TILE)
            back = dot_f32(gate_act_grad[cut], gate_ref[part, :], ((1,), (1,))) + dot_f32(
                up_act_grad[cut], up_ref[part, :], ((1,), (1,))
            )
            row_send[cut, part] = back.astype(jnp.bfloat16)
            if n == 0:
                row_send[cut, :LANES] = (back[:, :LANES] + extra).astype(jnp.bfloat16)

        @pl.loop(0, per_tile)
        def _(index):
            rows.start_one(tile * per_tile + index)

    rows.own_copy().start()
    outs.start()

    @pl.loop(0, model_width // TILE)
    def _(tile):
        row = rows_ref[:, columns(tile)]
        gate_grad_ref[rows_of(tile, TILE)] = dot_f32(row, gate_act_grad[...], ((0,), (0,))).astype(
            jnp.bfloat16
        )
        up_grad_ref[rows_of(tile, TILE)] = dot_f32(row, up_act_grad[...], ((0,), (0,))).astype(
            jnp.bfloat16
        )

    @pl.loop(0, ff_width // TILE)
    def _(tile):
        inner = inner_ref[:, columns(tile)]
        for n in range(model_width // ff_width):
            part = slice(n * ff_width, (n + 1) * ff_width)
            down_grad_ref[rows_of(tile, TILE), part] = dot_f32(
                inner, grad_out[:, part], ((0,), (0,))
            ).astype(jnp.bfloat16)

    rows.finish()
    outs.finish()


def experts(rows, grads, gate, up, down):
    slots, model_width = rows.shape
    ff_width = gate.shape[1]
    device_count = slots // SLOTS
    vmem = pl.BlockSpec(memory_space=pltpu.VMEM)
    anywhere = pl.BlockSpec(memory_space=pl.ANY)
    low = jnp.bfloat16
    shape = jax.ShapeDtypeStruct
    dma = pltpu.SemaphoreType.DMA
    return pl.pallas_call(
        expert_kernel,
        out_shape=(
            shape((slots, model_width), low),
            shape((slots, model_width), low),
            shape((model_width, ff_width), low),
            shape((model_width, ff_width), low),
            shape((ff_width, model_width), low),
        ),
        in_specs=[vmem] * 5,
        out_specs=(anywhere, anywhere, vmem, vmem, vmem),
        scratch_shapes=[
            pltpu.VMEM((slots, model_width), low),
            pltpu.VMEM((slots, model_width), low),
            pltpu.VMEM((slots, model_width), low),
            pltpu.VMEM((slots, ff_width), low),
            pltpu.VMEM((slots, ff_width), low),
            pltpu.VMEM((slots, ff_width), low),
        ]
        + [dma((device_count,))] * 4
        + [dma((2,))],
        compiler_params=pltpu.CompilerParams(
            collective_id=1, has_side_effects=True, vmem_limit_bytes=58 * 1024 * 1024
        ),
    )(rows, grads, gate, up, down)


def halves_turned(value, cosine, sine):
    parts = []
    for half in range(value.shape[1] // HEAD):
        part = value[:, half * HEAD : (half + 1) * HEAD]
        parts.append(part * cosine + pltpu.roll(part, HEAD // 2, 1) * sine)
    return jnp.concatenate(parts, axis=1)


def gain_rows(small):
    lanes_of = one_hot((8, LANES), lambda row, column: column == row + EXPERTS)
    return dot_f32(lanes_of, small, ((1,), (1,)))


class Scatter:
    def __init__(self, place, block, lands, send, recvs):
        self.place, self.block = place, block
        self.lands, self.send, self.recvs = lands, send, recvs

    def hop_core(self, z, x):
        p = self.place
        number = z * 2 + x
        return remote(
            self.block(p.index(z, x, 1 - p.c)),
            self.lands[0].at[number],
            self.send.at[number],
            self.recvs[0].at[number],
            p.index(p.z, p.x, 1 - p.c),
            p.side,
        )

    def hop_x(self, z):
        p = self.place
        return remote(
            self.block(p.index(z, 1 - p.x, p.c)),
            self.lands[1].at[z],
            self.send.at[8 + z],
            self.recvs[1].at[z],
            p.index(p.z, 1 - p.x, p.c),
            p.side,
        )

    def hop_z(self, i):
        p = self.place
        z = p.others()[i]
        return remote(
            self.block(p.index(z, p.x, p.c)),
            self.lands[2].at[i],
            self.send.at[12 + i],
            self.recvs[2].at[i],
            p.index(z, p.x, p.c),
            p.side,
        )

    def add(self, shard, land):
        block = self.block(shard)
        chunk = 32

        @pl.loop(0, block.shape[0] // chunk)
        def _(index):
            cut = rows_of(index, chunk)
            block[cut] = (block[cut].astype(jnp.float32) + land[cut].astype(jnp.float32)).astype(
                jnp.bfloat16
            )

    def start(self):
        for z in range(4):
            for x in range(2):
                self.hop_core(z, x).start()

    def order(self):
        return self.place.others() + [self.place.z]

    def pass_core(self):
        p = self.place
        for z in self.order():
            for x in (1 - p.x, p.x):
                self.hop_core(z, x).wait_recv()
                self.add(p.index(z, x, p.c), self.lands[0].at[z * 2 + x])
            self.hop_x(z).start()

    def pass_x(self):
        p = self.place
        for i, z in enumerate(self.order()):
            self.hop_x(z).wait_recv()
            self.add(p.index(z, p.x, p.c), self.lands[1].at[z])
            if i < 3:
                self.hop_z(i).start()

    def pass_z(self, put):
        p = self.place
        for i in range(3):
            self.hop_z(i).wait_recv()
        block = self.block(p.dp)
        chunk = 32

        @pl.loop(0, block.shape[0] // chunk)
        def _(index):
            cut = rows_of(index, chunk)
            value = block[cut].astype(jnp.float32)
            for i in range(3):
                value += self.lands[2][i, cut].astype(jnp.float32)
            put(cut, value)

    def finish(self):
        for z in range(4):
            for x in range(2):
                self.hop_core(z, x).wait_send()
            self.hop_x(z).wait_send()
        for i in range(3):
            self.hop_z(i).wait_send()


class WeightReturn(WeightSwap):
    def copies(self, step, to, landing):
        out = []
        for i, (source, target) in enumerate(self.pairs):
            rows = target.shape[1]
            out.append(
                remote(
                    source.at[rows_of(to, rows)],
                    target.at[landing],
                    self.send.at[step, i],
                    self.recv.at[step, i],
                    to,
                    self.place.side,
                )
            )
        return out

    def own_copies(self):
        dp = self.place.dp
        return [
            pltpu.make_async_copy(
                source.at[rows_of(dp, target.shape[1])], target.at[dp], self.local.at[i]
            )
            for i, (source, target) in enumerate(self.pairs)
        ]


def back_kernel(
    bias_ref,
    cotangent_ref,
    middle_ref,
    probs_ref,
    exact_ref,
    stat_ref,
    query_ref,
    keys_ref,
    small_ref,
    out_ref,
    placed_ref,
    rows_ref,
    outs_ref,
    cosine_ref,
    sine_ref,
    gate_ref,
    up_ref,
    result_ref,
    grad_middle_ref,
    grad_branch_ref,
    grad_logits_ref,
    grad_project_ref,
    gain_ref,
    gate_back,
    up_back,
    grad_hidden,
    grad_ref,
    acc,
    delta,
    grad_keys_ref,
    land_core,
    land_x,
    land_z,
    scatter_send,
    recv_core,
    recv_x,
    recv_z,
    weight_send,
    weight_recv,
    weight_local,
):
    dp_count = keys_ref.shape[0]
    slots = rows_ref.shape[0]
    device_count = slots // SLOTS
    tok_count, model_width = middle_ref.shape
    query_width = HEADS * HEAD
    key_width = KV_HEADS * HEAD
    repeat_heads = HEADS // KV_HEADS
    scale = HEAD ** (-0.5)
    factor = log2e * scale
    chunk = 32
    place = Place()
    enter(device_count, dp_count)
    weights = WeightReturn(
        place,
        ((gate_ref, gate_back), (up_ref, up_back)),
        weight_send,
        weight_recv,
        weight_local,
        dp_count,
    )
    weights.start(1, dp_count)
    weights.start_own()
    scatter = Scatter(
        place,
        lambda index: grad_keys_ref.at[index],
        (land_core, land_x, land_z),
        scatter_send,
        (recv_core, recv_x, recv_z),
    )

    probs = probs_ref[...]
    gate_grads = pick_gates(rows_ref[:, :LANES])
    slot_row = lax.broadcasted_iota(jnp.int32, (slots, LANES), 0)
    slot_lane = lax.broadcasted_iota(jnp.int32, (slots, LANES), 1)
    by_expert = jnp.where(slot_lane == slot_row // SLOTS, gate_grads, 0.0)
    grad_probs = sum(dot_f32(placed_ref[...], part) for part in split3(by_expert))
    grad_logits = (
        probs * (grad_probs - jnp.sum(probs * grad_probs, axis=-1, keepdims=True))
    ).astype(jnp.bfloat16)
    grad_logits_ref[...] = grad_logits

    @pl.loop(0, model_width // TILE)
    def _(tile):
        grad_hidden[:, columns(tile)] = dot_f32(
            placed_ref[...], rows_ref[:, columns(tile)]
        ) + dot_f32(grad_logits_ref[...], small_ref[rows_of(tile, TILE)], ((1,), (1,)))

    gain = gain_rows(small_ref[...])[1:2]
    gain_ref[...] = jnp.zeros(gain_ref.shape, jnp.float32)

    @pl.loop(0, tok_count // chunk)
    def _(index):
        cut = rows_of(index, chunk)
        value = middle_ref[cut]
        row_scale = lax.rsqrt(jnp.mean(value * value, axis=-1, keepdims=True) + epsilon)
        normed = value * row_scale
        grad = grad_hidden[cut]
        gain_ref[0:1] += jnp.sum(grad * normed, axis=0, keepdims=True)
        grad = grad * gain
        total = cotangent_ref[cut].astype(jnp.float32) + row_scale * (
            grad - normed * jnp.mean(grad * normed, axis=-1, keepdims=True)
        )
        grad_middle_ref[cut] = total
        grad_branch_ref[cut] = total.astype(jnp.bfloat16)

    @pl.loop(0, model_width // TILE)
    def _(tile):
        grad_ref[:, columns(tile)] = dot_f32(
            grad_branch_ref[...], out_ref[rows_of(tile, TILE)], ((1,), (1,))
        ).astype(jnp.bfloat16)

    for head in range(HEADS):
        cut = slice(head * HEAD, (head + 1) * HEAD)
        delta[head] = jnp.sum(
            grad_ref[:, cut].astype(jnp.float32) * exact_ref[:, cut], axis=-1, keepdims=True
        )
    row = lax.broadcasted_iota(jnp.int32, (tok_count, tok_count), 0)
    column = lax.broadcasted_iota(jnp.int32, (tok_count, tok_count), 1)
    causal = column <= row

    @pl.loop(place.dp + 1, dp_count)
    def _(label):
        grad_keys_ref[label] = jnp.zeros(grad_keys_ref.shape[1:], jnp.bfloat16)

    def visit(label, own):
        for group in range(KV_HEADS):
            key_cut = slice(group * HEAD, (group + 1) * HEAD)
            value_cut = slice((KV_HEADS + group) * HEAD, (KV_HEADS + group + 1) * HEAD)
            key = keys_ref[label, :, key_cut]
            value = keys_ref[label, :, value_cut]
            grad_key = jnp.zeros((tok_count, HEAD), jnp.float32)
            grad_value = jnp.zeros((tok_count, HEAD), jnp.float32)
            for head in range(group * repeat_heads, (group + 1) * repeat_heads):
                cut = slice(head * HEAD, (head + 1) * HEAD)
                query = query_ref[:, cut]
                grad = grad_ref[:, cut]
                shift = stat_ref[:, head : head + 1]
                if not own:
                    shift = shift - bias_ref[label]
                scores = dot_f32(query, key, ((1,), (1,)))
                prob = jnp.exp2(scores * factor - shift)
                if own:
                    prob = jnp.where(causal, prob, 0.0)
                grad_prob = dot_f32(grad, value, ((1,), (1,)))
                grad_score = (prob * (grad_prob - delta[head])).astype(jnp.bfloat16)
                grad_value += dot_f32(prob.astype(jnp.bfloat16), grad, ((0,), (0,)))
                grad_key += dot_f32(grad_score, query, ((0,), (0,)))
                grad_query = dot_f32(grad_score, key)
                if own:
                    acc[head] = grad_query
                else:
                    acc[head] += grad_query
            grad_keys_ref[label, :, key_cut] = (grad_key * scale).astype(jnp.bfloat16)
            grad_keys_ref[label, :, value_cut] = grad_value.astype(jnp.bfloat16)

    visit(place.dp, True)

    @pl.loop(0, place.dp)
    def _(label):
        visit(label, False)

    scatter.start()
    cosine, sine = cosine_ref[...], -sine_ref[...]
    for head in range(HEADS):
        grad_project_ref[:, head * HEAD : (head + 1) * HEAD] = halves_turned(
            acc[head] * scale, cosine, sine
        ).astype(jnp.bfloat16)
    scatter.pass_core()
    scatter.pass_x()

    expand = one_hot((LANES, slots), lambda r, col: col // SLOTS == r)
    high, mid, low = split3(probs_ref[...])
    gates = (dot_f32(high, expand) + dot_f32(mid, expand)) * placed_ref[...].astype(jnp.float32)
    gate_high = gates.astype(jnp.bfloat16)
    gate_low = (gates - gate_high.astype(jnp.float32)).astype(jnp.bfloat16)

    @pl.loop(0, model_width // TILE)
    def _(tile):
        outs = outs_ref[:, columns(tile)]
        result_ref[:, columns(tile)] = (
            middle_ref[:, columns(tile)] + dot_f32(gate_high, outs) + dot_f32(gate_low, outs)
        ).astype(jnp.bfloat16)

    def put(cut, value):
        grad_project_ref[cut, query_width : query_width + key_width] = halves_turned(
            value[:, :key_width], cosine_ref[cut], -sine_ref[cut]
        ).astype(jnp.bfloat16)
        grad_project_ref[cut, query_width + key_width :] = value[:, key_width:].astype(jnp.bfloat16)

    scatter.pass_z(put)
    scatter.finish()
    weights.finish()


def back(
    bias, cotangent, middle, probs, exact, stats, query, keys, small, out, placed, rows, outs,
    cosine, sine, gate_grad, up_grad, shard,
):
    dp_count, tok_count, both = keys.shape
    model_width = middle.shape[1]
    slots = rows.shape[0]
    ff_width = gate_grad.shape[1]
    vmem = pl.BlockSpec(memory_space=pltpu.VMEM)
    anywhere = pl.BlockSpec(memory_space=pl.ANY)
    low, full = jnp.bfloat16, jnp.float32
    shape = jax.ShapeDtypeStruct
    dma = pltpu.SemaphoreType.DMA
    return pl.pallas_call(
        back_kernel,
        out_shape=(
            shape((tok_count, model_width), low),
            shape((tok_count, model_width), full),
            shape((tok_count, model_width), low),
            shape((tok_count, LANES), low),
            shape((tok_count, query.shape[1] + both), low),
            shape((8, model_width), full),
            shape((dp_count, shard, ff_width), low),
            shape((dp_count, shard, ff_width), low),
        ),
        in_specs=[pl.BlockSpec(memory_space=pltpu.SMEM)] + [vmem] * 14 + [anywhere] * 2,
        out_specs=(vmem,) * 6 + (anywhere,) * 2,
        scratch_shapes=[
            pltpu.VMEM((tok_count, model_width), full),
            pltpu.VMEM((tok_count, model_width), low),
            pltpu.VMEM((HEADS, tok_count, HEAD), full),
            pltpu.VMEM((HEADS, tok_count, 1), full),
            pltpu.VMEM((dp_count, tok_count, both), low),
            pltpu.VMEM((8, tok_count, both), low),
            pltpu.VMEM((4, tok_count, both), low),
            pltpu.VMEM((3, tok_count, both), low),
            dma((15,)),
            dma((8,)),
            dma((4,)),
            dma((3,)),
            dma((dp_count, 2)),
            dma((dp_count, 2)),
            dma((2,)),
        ],
        compiler_params=pltpu.CompilerParams(
            collective_id=2, has_side_effects=True, vmem_limit_bytes=60 * 1024 * 1024
        ),
    )(
        bias, cotangent, middle, probs, exact, stats, query, keys, small, out, placed, rows, outs,
        cosine, sine, gate_grad, up_grad,
    )


def finish_kernel(
    tokens_ref,
    hidden_one,
    hidden_two,
    attended_ref,
    grad_middle_ref,
    grad_branch_ref,
    grad_logits_ref,
    grad_project_ref,
    gain_ref,
    project_ref,
    down_ref,
    grad_tokens_ref,
    mine_ref,
    down_back,
    grad_hidden,
    gain_one,
    partial_ref,
    pair_send,
    pair_land,
    land_core,
    land_x,
    land_z,
    scatter_send,
    recv_core,
    recv_x,
    recv_z,
    pair_sem,
    weight_send,
    weight_recv,
    weight_local,
):
    tok_count, model_width = tokens_ref.shape
    width = grad_project_ref.shape[1]
    dp_count = lax.axis_size("dp")
    device_count = dp_count * lax.axis_size("expert")
    shard = mine_ref.shape[0]
    place = Place()
    chunk = 32
    enter(device_count, dp_count)
    weights = WeightReturn(
        place, ((down_ref, down_back),), weight_send, weight_recv, weight_local, dp_count
    )
    weights.start(1, dp_count)
    weights.start_own()
    scatter = Scatter(
        place,
        lambda index: partial_ref.at[index],
        (land_core, land_x, land_z),
        scatter_send,
        (recv_core, recv_x, recv_z),
    )

    @pl.loop(0, model_width // TILE)
    def _(tile):
        grad_hidden[:, columns(tile)] = dot_f32(
            grad_project_ref[...], project_ref[rows_of(tile, TILE), :width], ((1,), (1,))
        )

    gain = gain_rows(project_ref[:, width:])[0:1]
    gain_one[...] = jnp.zeros(gain_one.shape, jnp.float32)

    @pl.loop(0, tok_count // chunk)
    def _(index):
        cut = rows_of(index, chunk)
        value = tokens_ref[cut].astype(jnp.float32)
        row_scale = lax.rsqrt(jnp.mean(value * value, axis=-1, keepdims=True) + epsilon)
        normed = value * row_scale
        grad = grad_hidden[cut]
        gain_one[0:1] += jnp.sum(grad * normed, axis=0, keepdims=True)
        grad = grad * gain
        grad_tokens_ref[cut] = grad_middle_ref[cut] + row_scale * (
            grad - normed * jnp.mean(grad * normed, axis=-1, keepdims=True)
        )

    one_lane = one_hot((8, LANES), lambda r, col: (r == 0) & (col == EXPERTS))
    two_lane = one_hot((8, LANES), lambda r, col: (r == 0) & (col == EXPERTS + 1))
    group = 4 * shard

    @pl.loop(0, model_width // group)
    def _(index):
        cut = columns(index, group)

        def put(at, value):
            for i in range(4):
                partial_ref[index * 4 + i, :, at] = value[i * shard : (i + 1) * shard].astype(
                    jnp.bfloat16
                )

        step = 512
        left = hidden_one[:, cut]
        for n in range(width // step):
            at = slice(n * step, (n + 1) * step)
            put(at, dot_f32(left, grad_project_ref[:, at], ((0,), (0,))))
        small = dot_f32(hidden_two[:, cut], grad_logits_ref[...], ((0,), (0,)))
        for part in split3(gain_one[:, cut]):
            small += dot_f32(part, one_lane, ((0,), (0,)))
        for part in split3(gain_ref[:, cut]):
            small += dot_f32(part, two_lane, ((0,), (0,)))
        put(slice(width, width + LANES), small)
        left = attended_ref[:, cut]
        for n in range(model_width // step):
            at = slice(n * step, (n + 1) * step)
            put(
                slice(width + LANES + n * step, width + LANES + (n + 1) * step),
                dot_f32(left, grad_branch_ref[:, at], ((0,), (0,))),
            )

    scatter.start()
    scatter.pass_core()
    scatter.pass_x()

    def keep(cut, value):
        pair_send[cut] = value.astype(jnp.bfloat16)

    scatter.pass_z(keep)
    pair = remote(
        pair_send, pair_land, pair_sem.at[0], pair_sem.at[1], place.dp, 1 - place.side
    )
    pair.start()
    scatter.finish()
    pair.wait()
    weights.finish()

    @pl.loop(0, shard // chunk)
    def _(index):
        cut = rows_of(index, chunk)
        mine_ref[cut] = pair_send[cut].astype(jnp.float32) + pair_land[cut].astype(jnp.float32)


def finish(
    tokens, hidden_one, hidden_two, attended, grad_middle, grad_branch, grad_logits, grad_project,
    gain, project, down_grad, shard, half,
):
    tok_count, model_width = tokens.shape
    dp_count = lax.axis_size("dp")
    width = project.shape[1] + model_width
    vmem = pl.BlockSpec(memory_space=pltpu.VMEM)
    anywhere = pl.BlockSpec(memory_space=pl.ANY)
    low, full = jnp.bfloat16, jnp.float32
    shape = jax.ShapeDtypeStruct
    dma = pltpu.SemaphoreType.DMA
    return pl.pallas_call(
        finish_kernel,
        out_shape=(
            shape((tok_count, model_width), full),
            shape((shard, width), full),
            shape((dp_count, half, model_width), low),
        ),
        in_specs=[vmem] * 10 + [anywhere],
        out_specs=(vmem, vmem, anywhere),
        scratch_shapes=[
            pltpu.VMEM((tok_count, model_width), full),
            pltpu.VMEM((8, model_width), full),
            pltpu.VMEM((dp_count, shard, width), low),
            pltpu.VMEM((shard, width), low),
            pltpu.VMEM((shard, width), low),
            pltpu.VMEM((8, shard, width), low),
            pltpu.VMEM((4, shard, width), low),
            pltpu.VMEM((3, shard, width), low),
            dma((15,)),
            dma((8,)),
            dma((4,)),
            dma((3,)),
            dma((2,)),
            dma((dp_count, 1)),
            dma((dp_count, 1)),
            dma((1,)),
        ],
        compiler_params=pltpu.CompilerParams(
            collective_id=3, has_side_effects=True, vmem_limit_bytes=58 * 1024 * 1024
        ),
    )(
        tokens, hidden_one, hidden_two, attended, grad_middle, grad_branch, grad_logits,
        grad_project, gain, project, down_grad,
    )


def local_owned(
    tokens,
    attn_gain,
    query_weight,
    key_weight,
    value_weight,
    out_weight,
    moe_gain,
    router_weight,
    gate_weight,
    up_weight,
    down_weight,
    parents,
    routes,
    claim_order,
    cotangent,
):
    tok_count = tokens.shape[1]
    segment = lax.axis_index("dp")
    query_width = HEADS * HEAD
    key_width = KV_HEADS * HEAD

    route_rows = routes[0]
    expert_ids = route_rows.reshape(-1)
    order_row = claim_order[0, 0]
    member = (expert_ids[:, None] == jnp.arange(EXPERTS, dtype=jnp.int32)[None, :]).astype(
        jnp.bfloat16
    )
    earlier = (order_row[None, :] < order_row[:, None]).astype(jnp.bfloat16)
    before = jnp.dot(earlier, member, preferred_element_type=jnp.float32)
    slot_index = jnp.sum(before * member.astype(jnp.float32), axis=1).astype(jnp.int32)
    target = jnp.where(slot_index < CAP, expert_ids * SLOTS + slot_index, -1).reshape(
        tok_count, TOP
    )
    row_labels = jnp.arange(EXPERTS * SLOTS, dtype=jnp.int32)
    placed_rows = sum(
        (target[:, c : c + 1] == row_labels[None, :]).astype(jnp.bfloat16) for c in range(TOP)
    )
    target_rows = jnp.full((8, TILE), -1.0, jnp.float32)
    target_rows = target_rows.at[:TOP, :tok_count].set(target.T.astype(jnp.float32))
    route_lanes = jnp.pad(route_rows, ((0, 0), (0, LANES - TOP)), constant_values=-1)

    small = jnp.concatenate(
        [
            router_weight,
            attn_gain[:, None],
            moe_gain[:, None],
            jnp.zeros((router_weight.shape[0], LANES - EXPERTS - 2), jnp.bfloat16),
        ],
        axis=1,
    )
    project_shard = jnp.concatenate([query_weight, key_weight, value_weight, small], axis=1)
    reach_row = ancestry(parents[0])[segment]
    path_depth = jnp.sum(reach_row) - 1.0
    positions = path_depth * tok_count + jnp.arange(tok_count, dtype=jnp.float32)
    cosine, sine_part = rope_tables(positions, HEAD)
    cosine_wide = jnp.concatenate([cosine[:, 0], cosine[:, 0]], axis=1)
    sine_wide = jnp.concatenate([-sine_part[:, 0], sine_part[:, 0]], axis=1)
    on_path = reach_row > 0.5
    bias = jnp.where(on_path, 0.0, -1e30).astype(jnp.float32)
    (
        project_full,
        out_full,
        keys,
        query_rot,
        attended,
        exact_out,
        stats,
        middle,
        hidden_two,
        probs,
        rows_in,
        grad_rows_in,
        gate_own,
        up_own,
        down_own,
        hidden_one,
    ) = front(
        bias,
        tokens[0],
        cotangent[0],
        project_shard,
        out_weight,
        target_rows,
        route_lanes,
        cosine_wide,
        sine_wide,
        gate_weight,
        up_weight,
        down_weight,
    )
    small_at = query_width + 2 * key_width
    rows_back, outs_back, gate_grad, up_grad, down_grad = experts(
        rows_in, grad_rows_in, gate_own, up_own, down_own
    )
    (
        block_out,
        grad_middle,
        grad_branch,
        grad_logits,
        grad_project,
        gain_row,
        gate_back,
        up_back,
    ) = back(
        bias,
        cotangent[0],
        middle,
        probs,
        exact_out,
        stats,
        query_rot,
        keys,
        project_full[:, small_at:],
        out_full,
        placed_rows,
        rows_back,
        outs_back,
        cosine_wide,
        sine_wide,
        gate_grad,
        up_grad,
        gate_weight.shape[1],
    )
    grad_tokens, mine, down_back = finish(
        tokens[0],
        hidden_one,
        hidden_two,
        attended,
        grad_middle,
        grad_branch,
        grad_logits,
        grad_project,
        gain_row,
        project_full,
        down_grad,
        query_weight.shape[0],
        down_weight.shape[1],
    )
    return (
        block_out[None],
        grad_tokens[None],
        mine[:, small_at + EXPERTS],
        mine[:, :query_width],
        mine[:, query_width : query_width + key_width],
        mine[:, query_width + key_width : small_at],
        mine[:, small_at + LANES :],
        mine[:, small_at + EXPERTS + 1],
        mine[:, small_at : small_at + EXPERTS],
        gate_back.astype(jnp.float32),
        up_back.astype(jnp.float32),
        down_back.astype(jnp.float32),
    )


def solution(mesh):
    placed = (
        P("expert", "dp", None),
        P("dp"),
        P("dp", None),
        P("dp", None),
        P("dp", None),
        P("dp", None),
        P("dp"),
        P("dp", None),
        P("expert", "dp", None),
        P("expert", "dp", None),
        P("expert", "dp", None),
        P("expert", None),
        P("expert", "dp", None),
        P("expert", "dp", None),
        P("expert", "dp", None),
    )
    owned = mesh.shape["dp"] == 16 and mesh.shape["expert"] == 2
    return jax.shard_map(
        local_owned if owned else local_gathered,
        mesh=mesh,
        in_specs=placed,
        out_specs=(
            P("expert", "dp", None),
            P("expert", "dp", None),
            P("dp"),
            P("dp", None),
            P("dp", None),
            P("dp", None),
            P("dp", None),
            P("dp"),
            P("dp", None),
            P("expert", "dp", None),
            P("expert", "dp", None),
            P("expert", "dp", None),
        ),
        check_vma=False,
    )
```

```python
import functools

import jax
import jax.numpy as jnp
from jax import lax
from jax.experimental import pallas as pl
from jax.experimental.pallas import tpu as pltpu
from jax.sharding import PartitionSpec as P

HEADS = 12
KV_HEADS = 2
HEAD = 128
EXPERTS = 32
TOP = 4
CAP = 28


epsilon = 1e-06
theta = 10000.0
highest = lax.Precision.HIGHEST


def ancestry(parents):
    row_count = parents.shape[0]
    labels = jnp.arange(row_count, dtype=jnp.int32)
    linked = (parents[:, None] == labels[None, :]).astype(jnp.float32)
    reach_all = jnp.minimum(jnp.eye(row_count, dtype=jnp.float32) + linked, 1.0)
    for doubling in range(max(1, (row_count - 1).bit_length())):
        reach_all = jnp.minimum(jnp.dot(reach_all, reach_all, precision=highest), 1.0)
    return reach_all


def rope_tables(positions, head_size):
    halfway = head_size // 2
    frequency = theta ** (-jnp.arange(halfway, dtype=jnp.float32) * 2.0 / head_size)
    angles = positions[:, None] * frequency[None, :]
    return (jnp.cos(angles)[:, None, :], jnp.sin(angles)[:, None, :])


def rotate(values, cosine, sine_part):
    halfway = values.shape[-1] // 2
    first_half = values[..., :halfway]
    second = values[..., halfway:]
    return jnp.concatenate(
        [first_half * cosine - second * sine_part, second * cosine + first_half * sine_part],
        axis=-1,
    )


def norm_backward(grad_hidden, normed, row_scale, gain):
    grad_normed = grad_hidden * gain
    grad_gain = jnp.sum(grad_hidden * normed, axis=0)
    grad_rows = row_scale * (
        grad_normed - normed * jnp.mean(grad_normed * normed, axis=-1, keepdims=True)
    )
    return (grad_rows, grad_gain)


def local_gathered(
    tokens,
    attn_gain,
    query_weight,
    key_weight,
    value_weight,
    out_weight,
    moe_gain,
    router_weight,
    gate_weight,
    up_weight,
    down_weight,
    parents,
    routes,
    claim_order,
    cotangent,
):
    (
        gain_one,
        query_full,
        key_full,
        value_full,
        out_full,
        gain_two,
        router_full,
        gate_full,
        up_full,
        down_full,
    ) = (
        lax.all_gather(attn_gain, "dp", axis=0, tiled=True),
        lax.all_gather(query_weight, "dp", axis=0, tiled=True),
        lax.all_gather(key_weight, "dp", axis=0, tiled=True),
        lax.all_gather(value_weight, "dp", axis=0, tiled=True),
        lax.all_gather(out_weight, "dp", axis=0, tiled=True),
        lax.all_gather(moe_gain, "dp", axis=0, tiled=True),
        lax.all_gather(router_weight, "dp", axis=0, tiled=True),
        lax.all_gather(gate_weight, "dp", axis=1, tiled=True),
        lax.all_gather(up_weight, "dp", axis=1, tiled=True),
        lax.all_gather(down_weight, "dp", axis=1, tiled=True),
    )
    tok_count = tokens.shape[1]
    model_width = tokens.shape[2]
    segment = lax.axis_index("dp")
    segment_count = lax.axis_size("dp")
    expert_peers = lax.axis_size("expert")
    local_experts = gate_weight.shape[0]
    repeat_heads = HEADS // KV_HEADS
    score_scale = HEAD ** (-0.5)
    query_rows = repeat_heads * tok_count
    reach_all = ancestry(parents[0])
    reach_row = reach_all[segment]
    path_depth = jnp.sum(reach_row) - 1.0
    positions = path_depth * tok_count + jnp.arange(tok_count, dtype=jnp.float32)
    cosine, sine_part = rope_tables(positions, HEAD)
    inputs = tokens[0].astype(jnp.float32)
    scale_one = lax.rsqrt(jnp.mean(inputs * inputs, axis=-1, keepdims=True) + epsilon)
    normed_one = inputs * scale_one
    gain_first = gain_one.astype(jnp.float32)
    hidden_one = (normed_one * gain_first).astype(jnp.bfloat16)
    query_raw = jnp.dot(hidden_one, query_full, preferred_element_type=jnp.float32).reshape(
        tok_count, HEADS, HEAD
    )
    key_raw = jnp.dot(hidden_one, key_full, preferred_element_type=jnp.float32).reshape(
        tok_count, KV_HEADS, HEAD
    )
    value_low = jnp.dot(hidden_one, value_full, preferred_element_type=jnp.float32).astype(
        jnp.bfloat16
    )
    query_rot = rotate(query_raw, cosine, sine_part).astype(jnp.bfloat16)
    key_rot = (
        rotate(key_raw, cosine, sine_part).astype(jnp.bfloat16).reshape(tok_count, KV_HEADS * HEAD)
    )
    key_all, value_all = (
        lax.all_gather(key_rot, "dp", axis=0, tiled=True),
        lax.all_gather(value_low, "dp", axis=0, tiled=True),
    )
    total_keys = key_all.shape[0]
    key_blocks = key_all.reshape(segment_count, tok_count, KV_HEADS, HEAD)
    value_blocks = value_all.reshape(segment_count, tok_count, KV_HEADS, HEAD)
    segment_labels = jnp.arange(segment_count, dtype=jnp.int32)
    query_groups = (
        query_rot.reshape(tok_count, KV_HEADS, repeat_heads, HEAD)
        .transpose(1, 2, 0, 3)
        .reshape(KV_HEADS, query_rows, HEAD)
    )
    query_offsets = jnp.arange(tok_count, dtype=jnp.int32)
    causal_tile = jnp.tile(query_offsets[None, :] <= query_offsets[:, None], (repeat_heads, 1))

    def scores_of(key_block, label):
        raw_scores = (
            jnp.einsum("grh,kgh->grk", query_groups, key_block, preferred_element_type=jnp.float32)
            * score_scale
        )
        allowed = causal_tile | (label != segment)
        return jnp.where(allowed[None], raw_scores, -1000000000.0)

    def on_path(label):
        return reach_row[label] > 0.5

    def pass_stats(state_pair, inputs_block):
        key_block, value_block, label = inputs_block

        def visit(state):
            row_max, row_sum = state
            scores = scores_of(key_block, label)
            new_max = jnp.maximum(row_max, jnp.max(scores, axis=-1))
            new_sum = row_sum * jnp.exp(row_max - new_max) + jnp.sum(
                jnp.exp(scores - new_max[..., None]), axis=-1
            )
            return (new_max, new_sum)

        return (lax.cond(on_path(label), visit, lambda state: state, state_pair), None)

    start_max = jnp.full((KV_HEADS, query_rows), -1e30, jnp.float32)
    start_sum = jnp.zeros((KV_HEADS, query_rows), jnp.float32)
    (row_max, row_sum), unused = lax.scan(
        pass_stats, (start_max, start_sum), (key_blocks, value_blocks, segment_labels)
    )

    def probs_of(key_block, label):
        return jnp.exp(scores_of(key_block, label) - row_max[..., None]) / row_sum[..., None]

    def pass_values(state_pair, inputs_block):
        key_block, value_block, label = inputs_block

        def visit(state):
            accumulated, exact_out = state
            prob_block = probs_of(key_block, label)
            accumulated = accumulated + jnp.einsum(
                "grk,kgh->grh",
                prob_block.astype(jnp.bfloat16),
                value_block,
                preferred_element_type=jnp.float32,
            )
            exact_out = exact_out + jnp.einsum(
                "grk,kgh->grh",
                prob_block,
                value_block.astype(jnp.float32),
                preferred_element_type=jnp.float32,
                precision=highest,
            )
            return (accumulated, exact_out)

        return (lax.cond(on_path(label), visit, lambda state: state, state_pair), None)

    zero_out = jnp.zeros((KV_HEADS, query_rows, HEAD), jnp.float32)
    (accumulated, exact_out), unused = lax.scan(
        pass_values, (zero_out, zero_out), (key_blocks, value_blocks, segment_labels)
    )
    attended = (
        accumulated.reshape(KV_HEADS, repeat_heads, tok_count, HEAD)
        .transpose(2, 0, 1, 3)
        .reshape(tok_count, HEADS * HEAD)
        .astype(jnp.bfloat16)
    )
    branch = jnp.dot(attended, out_full, preferred_element_type=jnp.float32)
    middle = inputs + branch
    scale_two = lax.rsqrt(jnp.mean(middle * middle, axis=-1, keepdims=True) + epsilon)
    normed_two = middle * scale_two
    gain_second = gain_two.astype(jnp.float32)
    hidden_two = (normed_two * gain_second).astype(jnp.bfloat16)
    logits = jnp.dot(hidden_two, router_full, preferred_element_type=jnp.float32)
    picked_one = (
        routes[0][:, :, None] == jnp.arange(EXPERTS, dtype=jnp.int32)[None, None, :]
    ).astype(jnp.float32)
    chosen = jnp.sum(picked_one * logits[:, None, :], axis=-1)
    gate_probs = jax.nn.softmax(chosen, axis=-1)
    expert_ids = routes[0].reshape(-1)
    order_row = claim_order[0, 0]
    pair_count = expert_ids.shape[0]
    member = (expert_ids[:, None] == jnp.arange(EXPERTS, dtype=jnp.int32)[None, :]).astype(
        jnp.bfloat16
    )
    earlier = (order_row[None, :] < order_row[:, None]).astype(jnp.bfloat16)
    before = jnp.dot(earlier, member, preferred_element_type=jnp.float32)
    slot_index = jnp.sum(before * member.astype(jnp.float32), axis=1).astype(jnp.int32)
    owner_rank = expert_ids // local_experts
    local_rank = expert_ids % local_experts
    target = jnp.where(
        slot_index < CAP, (local_rank * expert_peers + owner_rank) * CAP + slot_index, EXPERTS * CAP
    )
    slot_pairs = (
        jnp.full((EXPERTS * CAP + 1,), pair_count, jnp.int32)
        .at[target]
        .set(jnp.arange(pair_count, dtype=jnp.int32))[: EXPERTS * CAP]
    )
    padded_two = jnp.concatenate([hidden_two, jnp.zeros((1, model_width), jnp.bfloat16)], axis=0)
    send_rows = padded_two[slot_pairs // TOP].reshape(local_experts, expert_peers, CAP, model_width)
    arrived = lax.all_to_all(send_rows, "expert", split_axis=1, concat_axis=1, tiled=True)
    expert_rows = arrived.reshape(local_experts, expert_peers * CAP, model_width)
    gate_act = jnp.einsum(
        "erd,edf->erf", expert_rows, gate_full, preferred_element_type=jnp.float32
    )
    up_act = jnp.einsum("erd,edf->erf", expert_rows, up_full, preferred_element_type=jnp.float32)
    inner = (jax.nn.silu(gate_act) * up_act).astype(jnp.bfloat16)
    expert_out = jnp.einsum(
        "erf,efd->erd", inner, down_full, preferred_element_type=jnp.float32
    ).astype(jnp.bfloat16)
    returned = lax.all_to_all(
        expert_out.reshape(local_experts, expert_peers, CAP, model_width),
        "expert",
        split_axis=1,
        concat_axis=1,
        tiled=True,
    )
    returned = jnp.concatenate(
        [returned.reshape(EXPERTS * CAP, model_width), jnp.zeros((1, model_width), jnp.bfloat16)],
        axis=0,
    )
    pair_out = returned[target].reshape(tok_count, TOP, model_width).astype(jnp.float32)
    mixture = jnp.sum(gate_probs[:, :, None] * pair_out, axis=1)
    block_out = (middle + mixture).astype(jnp.bfloat16)
    grad_result = cotangent[0].astype(jnp.float32)
    grad_gates = jnp.sum(pair_out * grad_result[:, None, :], axis=-1)
    grad_pairs = (
        (gate_probs[:, :, None] * grad_result[:, None, :])
        .astype(jnp.bfloat16)
        .reshape(pair_count, model_width)
    )
    grad_padded = jnp.concatenate([grad_pairs, jnp.zeros((1, model_width), jnp.bfloat16)], axis=0)
    grad_send = grad_padded[slot_pairs].reshape(local_experts, expert_peers, CAP, model_width)
    grad_arrived, rows_back = (
        lax.all_to_all(grad_send, "expert", split_axis=1, concat_axis=1, tiled=True),
        lax.all_to_all(send_rows, "expert", split_axis=1, concat_axis=1, tiled=True),
    )
    rows_again = rows_back.reshape(local_experts, expert_peers * CAP, model_width)
    gate_again = jnp.einsum(
        "erd,edf->erf", rows_again, gate_full, preferred_element_type=jnp.float32
    )
    up_again = jnp.einsum("erd,edf->erf", rows_again, up_full, preferred_element_type=jnp.float32)
    inner_again = (jax.nn.silu(gate_again) * up_again).astype(jnp.bfloat16)
    grad_expert_out = grad_arrived.reshape(local_experts, expert_peers * CAP, model_width)
    grad_inner = jnp.einsum(
        "erd,efd->erf", grad_expert_out, down_full, preferred_element_type=jnp.float32
    )
    grad_down_local = jnp.einsum(
        "erf,erd->efd", inner_again, grad_expert_out, preferred_element_type=jnp.float32
    )
    sigmoid_gate = jax.nn.sigmoid(gate_again)
    swish = gate_again * sigmoid_gate
    grad_gate_act = (
        grad_inner * up_again * (sigmoid_gate * (1.0 + gate_again * (1.0 - sigmoid_gate)))
    ).astype(jnp.bfloat16)
    grad_up_act = (grad_inner * swish).astype(jnp.bfloat16)
    grad_gate_local = jnp.einsum(
        "erd,erf->edf", rows_again, grad_gate_act, preferred_element_type=jnp.float32
    )
    grad_up_local = jnp.einsum(
        "erd,erf->edf", rows_again, grad_up_act, preferred_element_type=jnp.float32
    )
    grad_rows = (
        jnp.einsum("erf,edf->erd", grad_gate_act, gate_full, preferred_element_type=jnp.float32)
        + jnp.einsum("erf,edf->erd", grad_up_act, up_full, preferred_element_type=jnp.float32)
    ).astype(jnp.bfloat16)
    grad_back = lax.all_to_all(
        grad_rows.reshape(local_experts, expert_peers, CAP, model_width),
        "expert",
        split_axis=1,
        concat_axis=1,
        tiled=True,
    )
    grad_back = jnp.concatenate(
        [grad_back.reshape(EXPERTS * CAP, model_width), jnp.zeros((1, model_width), jnp.bfloat16)],
        axis=0,
    )
    grad_hidden_two = jnp.sum(
        grad_back[target].reshape(tok_count, TOP, model_width).astype(jnp.float32), axis=1
    )
    grad_chosen = gate_probs * (
        grad_gates - jnp.sum(gate_probs * grad_gates, axis=-1, keepdims=True)
    )
    grad_logits = jnp.sum(picked_one * grad_chosen[:, :, None], axis=1).astype(jnp.bfloat16)
    grad_hidden_two = grad_hidden_two + jnp.dot(
        grad_logits, router_full.T, preferred_element_type=jnp.float32
    )
    grad_router_local = jnp.dot(hidden_two.T, grad_logits, preferred_element_type=jnp.float32)
    grad_middle_norm, grad_gain_two = norm_backward(
        grad_hidden_two, normed_two, scale_two, gain_second
    )
    grad_middle = grad_result + grad_middle_norm
    grad_branch = grad_middle.astype(jnp.bfloat16)
    grad_out_local = jnp.dot(attended.T, grad_branch, preferred_element_type=jnp.float32)
    grad_attended = jnp.dot(grad_branch, out_full.T, preferred_element_type=jnp.float32).astype(
        jnp.bfloat16
    )
    grad_groups = (
        grad_attended.reshape(tok_count, KV_HEADS, repeat_heads, HEAD)
        .transpose(1, 2, 0, 3)
        .reshape(KV_HEADS, query_rows, HEAD)
    )
    row_delta = jnp.sum(grad_groups.astype(jnp.float32) * exact_out, axis=-1)
    zero_key = jnp.zeros((tok_count, KV_HEADS, HEAD), jnp.float32)

    def pass_grads(grad_query, inputs_block):
        key_block, value_block, label = inputs_block

        def visit(carried):
            prob_block = probs_of(key_block, label)
            grad_probs = jnp.einsum(
                "grh,kgh->grk", grad_groups, value_block, preferred_element_type=jnp.float32
            )
            grad_scores = (prob_block * (grad_probs - row_delta[..., None])).astype(jnp.bfloat16)
            carried = carried + jnp.einsum(
                "grk,kgh->grh", grad_scores, key_block, preferred_element_type=jnp.float32
            )
            grad_key_block = (
                jnp.einsum(
                    "grk,grh->kgh", grad_scores, query_groups, preferred_element_type=jnp.float32
                )
                * score_scale
            )
            grad_value_block = jnp.einsum(
                "grk,grh->kgh",
                prob_block.astype(jnp.bfloat16),
                grad_groups,
                preferred_element_type=jnp.float32,
            )
            return (carried, (grad_key_block, grad_value_block))

        def skip(carried):
            return (carried, (zero_key, zero_key))

        return lax.cond(on_path(label), visit, skip, grad_query)

    grad_query_groups, (grad_key_blocks, grad_value_blocks) = lax.scan(
        pass_grads,
        jnp.zeros((KV_HEADS, query_rows, HEAD), jnp.float32),
        (key_blocks, value_blocks, segment_labels),
    )
    grad_key_all = grad_key_blocks.reshape(total_keys, KV_HEADS * HEAD)
    grad_value_all = grad_value_blocks.reshape(total_keys, KV_HEADS * HEAD)
    grad_key_mine, grad_value_mine = (
        lax.psum_scatter(
            grad_key_all.astype(jnp.bfloat16), "dp", scatter_dimension=0, tiled=True
        ).astype(jnp.float32),
        lax.psum_scatter(
            grad_value_all.astype(jnp.bfloat16), "dp", scatter_dimension=0, tiled=True
        ).astype(jnp.float32),
    )
    grad_query_rot = (
        (grad_query_groups * score_scale)
        .reshape(KV_HEADS, repeat_heads, tok_count, HEAD)
        .transpose(2, 0, 1, 3)
        .reshape(tok_count, HEADS, HEAD)
    )
    grad_query_raw = (
        rotate(grad_query_rot, cosine, -sine_part)
        .reshape(tok_count, HEADS * HEAD)
        .astype(jnp.bfloat16)
    )
    grad_key_raw = (
        rotate(grad_key_mine.reshape(tok_count, KV_HEADS, HEAD), cosine, -sine_part)
        .reshape(tok_count, KV_HEADS * HEAD)
        .astype(jnp.bfloat16)
    )
    grad_value_raw = grad_value_mine.astype(jnp.bfloat16)
    grad_query_local = jnp.dot(hidden_one.T, grad_query_raw, preferred_element_type=jnp.float32)
    grad_key_local = jnp.dot(hidden_one.T, grad_key_raw, preferred_element_type=jnp.float32)
    grad_value_local = jnp.dot(hidden_one.T, grad_value_raw, preferred_element_type=jnp.float32)
    grad_hidden_one = (
        jnp.dot(grad_query_raw, query_full.T, preferred_element_type=jnp.float32)
        + jnp.dot(grad_key_raw, key_full.T, preferred_element_type=jnp.float32)
        + jnp.dot(grad_value_raw, value_full.T, preferred_element_type=jnp.float32)
    )
    grad_inputs_norm, grad_gain_one = norm_backward(
        grad_hidden_one, normed_one, scale_one, gain_first
    )
    grad_inputs = grad_middle + grad_inputs_norm
    grad_gate_mine, grad_up_mine, grad_down_mine = (
        lax.psum_scatter(
            grad_gate_local.astype(jnp.bfloat16), "dp", scatter_dimension=1, tiled=True
        ).astype(jnp.float32),
        lax.psum_scatter(
            grad_up_local.astype(jnp.bfloat16), "dp", scatter_dimension=1, tiled=True
        ).astype(jnp.float32),
        lax.psum_scatter(
            grad_down_local.astype(jnp.bfloat16), "dp", scatter_dimension=1, tiled=True
        ).astype(jnp.float32),
    )
    shard_rows = (
        lax.psum_scatter(
            grad_gain_one.astype(jnp.bfloat16), "dp", scatter_dimension=0, tiled=True
        ).astype(jnp.float32),
        lax.psum_scatter(
            grad_query_local.astype(jnp.bfloat16), "dp", scatter_dimension=0, tiled=True
        ).astype(jnp.float32),
        lax.psum_scatter(
            grad_key_local.astype(jnp.bfloat16), "dp", scatter_dimension=0, tiled=True
        ).astype(jnp.float32),
        lax.psum_scatter(
            grad_value_local.astype(jnp.bfloat16), "dp", scatter_dimension=0, tiled=True
        ).astype(jnp.float32),
        lax.psum_scatter(
            grad_out_local.astype(jnp.bfloat16), "dp", scatter_dimension=0, tiled=True
        ).astype(jnp.float32),
        lax.psum_scatter(
            grad_gain_two.astype(jnp.bfloat16), "dp", scatter_dimension=0, tiled=True
        ).astype(jnp.float32),
        lax.psum_scatter(
            grad_router_local.astype(jnp.bfloat16), "dp", scatter_dimension=0, tiled=True
        ).astype(jnp.float32),
    )
    shared = (
        lax.psum(shard_rows[0].astype(jnp.bfloat16), "expert").astype(jnp.float32),
        lax.psum(shard_rows[1].astype(jnp.bfloat16), "expert").astype(jnp.float32),
        lax.psum(shard_rows[2].astype(jnp.bfloat16), "expert").astype(jnp.float32),
        lax.psum(shard_rows[3].astype(jnp.bfloat16), "expert").astype(jnp.float32),
        lax.psum(shard_rows[4].astype(jnp.bfloat16), "expert").astype(jnp.float32),
        lax.psum(shard_rows[5].astype(jnp.bfloat16), "expert").astype(jnp.float32),
        lax.psum(shard_rows[6].astype(jnp.bfloat16), "expert").astype(jnp.float32),
    )
    return (
        block_out[None],
        grad_inputs[None],
        shared[0],
        shared[1],
        shared[2],
        shared[3],
        shared[4],
        shared[5],
        shared[6],
        grad_gate_mine,
        grad_up_mine,
        grad_down_mine,
    )


SLOTS = 32
PAD_TOKENS = 32
LANES = 128
TILE = 256
MESH = pl.DeviceIdType.MESH
log2e = 1.4426950408889634


def dot_f32(a, b, dims=((1,), (0,))):
    return lax.dot_general(a, b, (dims, ((), ())), preferred_element_type=jnp.float32)


def split3(value):
    high = value.astype(jnp.bfloat16)
    rest = value - high.astype(jnp.float32)
    middle = rest.astype(jnp.bfloat16)
    low = (rest - middle.astype(jnp.float32)).astype(jnp.bfloat16)
    return high, middle, low


def one_hot(shape, test):
    row = lax.broadcasted_iota(jnp.int32, shape, 0)
    column = lax.broadcasted_iota(jnp.int32, shape, 1)
    return jnp.where(test(row, column), 1.0, 0.0).astype(jnp.bfloat16)


class Place:
    def __init__(self):
        self.dp = lax.axis_index("dp")
        self.side = lax.axis_index("expert")
        self.z = self.dp // 4
        self.x = (self.dp // 2) % 2
        self.c = self.dp % 2

    def index(self, z, x, c):
        return z * 4 + x * 2 + c

    def others(self):
        return [self.z + 1 - 2 * (self.z % 2), (self.z + 2) % 4, 3 - self.z]


def remote(src, dst, send, recv, dp, side):
    return pltpu.make_async_remote_copy(
        src_ref=src,
        dst_ref=dst,
        send_sem=send,
        recv_sem=recv,
        device_id={"dp": dp, "expert": side},
        device_id_type=MESH,
    )


def enter(device_count, dp_count):
    rank = lax.axis_index("expert") * dp_count + lax.axis_index("dp")
    barrier = pltpu.get_barrier_semaphore()

    @pl.loop(1, device_count)
    def _(step):
        other = (rank + step) % device_count
        pl.semaphore_signal(
            barrier,
            inc=1,
            device_id={"dp": other % dp_count, "expert": other // dp_count},
            device_id_type=MESH,
        )

    pl.semaphore_wait(barrier, device_count - 1)


class Column:
    def __init__(self, place, own, slot, send, recv, local):
        self.place, self.own, self.slot = place, own, slot
        self.send, self.recv, self.local = send, recv, local

    def hop(self, z, step, own=False):
        p = self.place
        source = self.own if own else self.slot(z)
        number = z if step > 0 else 4 + z
        target = p.index(p.z + step, p.x, p.c)
        return remote(source, self.slot(z), self.send.at[number], self.recv(z), target, p.side)

    def own_copy(self):
        return pltpu.make_async_copy(self.own, self.slot(self.place.z), self.local)

    def upward(self, act):
        pl.when(self.place.z < 3)(act)

    def downward(self, act):
        pl.when(self.place.z > 0)(act)

    def start(self):
        z = self.place.z
        self.upward(lambda: self.hop(z, 1, True).start())
        self.downward(lambda: self.hop(z, -1, True).start())
        self.own_copy().start()

    def forward(self, low=1, high=4, then=None):
        z = self.place.z

        @pl.loop(low, high)
        def _(away):
            @pl.when(z - away >= 0)
            def _():
                self.hop(z - away, 1).wait_recv()
                self.upward(lambda: self.hop(z - away, 1).start())
                if then is not None:
                    then(z - away)

            @pl.when(z + away <= 3)
            def _():
                self.hop(z + away, -1).wait_recv()
                self.downward(lambda: self.hop(z + away, -1).start())
                if then is not None:
                    then(z + away)

    def finish(self):
        z = self.place.z

        @pl.loop(0, 4)
        def _(origin):
            @pl.when((origin <= z) & (z < 3))
            def _():
                self.hop(origin, 1).wait_send()

            @pl.when((origin >= z) & (z > 0))
            def _():
                self.hop(origin, -1).wait_send()


class Gather:
    def __init__(self, place, own, slot, send, recv, local):
        self.place, self.own, self.slot = place, own, slot
        self.send, self.recv = send, recv
        self.column = Column(
            place,
            own,
            lambda z: slot(place.index(z, place.x, place.c)),
            send,
            lambda z: recv.at[place.index(z, place.x, place.c)],
            local,
        )

    def copy(self, z, x, c, to_x, to_c, number, own=False):
        p = self.place
        shard = p.index(z, x, c)
        source = self.own if own else self.slot(shard)
        target = p.index(p.z, to_x, to_c)
        return remote(
            source, self.slot(shard), self.send.at[number], self.recv.at[shard], target, p.side
        )

    def to_x(self, z, own=False):
        p = self.place
        return self.copy(z, p.x, p.c, 1 - p.x, p.c, 8 + z, own)

    def to_core(self, z, x, own=False):
        p = self.place
        return self.copy(z, x, p.c, p.x, 1 - p.c, 12 + z * 2 + x, own)

    def start(self):
        p = self.place
        self.column.start()
        self.to_x(p.z, True).start()
        self.to_core(p.z, p.x, True).start()

    def forward_z(self):
        def then(z):
            self.to_x(z).start()
            self.to_core(z, self.place.x).start()

        self.column.forward(then=then)

    def forward_x(self):
        p = self.place

        def pass_on(z):
            self.to_core(z, 1 - p.x).wait_recv()
            self.to_core(z, 1 - p.x).start()

        pass_on(p.z)

        @pl.loop(1, 4)
        def _(away):
            pl.when(p.z - away >= 0)(lambda: pass_on(p.z - away))
            pl.when(p.z + away <= 3)(lambda: pass_on(p.z + away))

    def finish(self):
        p = self.place

        @pl.loop(0, 4)
        def _(z):
            for x in range(2):
                self.copy(z, x, 1 - p.c, p.x, 1 - p.c, 12).wait_recv()
                self.to_core(z, x).wait_send()
            self.to_x(z).wait_send()

        self.column.finish()
        self.column.own_copy().wait()


class PlaneSwap:
    def __init__(self, place, source, target, send, recv, local, dp_count):
        self.place, self.source, self.target = place, source, target
        self.send, self.recv, self.local = send, recv, local
        self.dp_count = dp_count

    def of(self, member):
        return member // 4, (member // 2) % 2, member % 2

    def rank(self, z, side, x, c):
        return side * self.dp_count + self.place.index(z, x, c)

    def me(self):
        p = self.place
        return p.side * 4 + p.x * 2 + p.c

    def block(self, rank):
        return self.target.at[rows_of(rank, SLOTS)]

    def copy(self, z, step, to, origin):
        p = self.place
        side, x, c = self.of(to)
        return remote(
            self.source.at[z, rows_of(to, SLOTS)],
            self.block(self.rank(z, *self.of(origin))),
            self.send.at[z, step],
            self.recv.at[z, step],
            p.index(p.z, x, c),
            side,
        )

    def own_copy(self, z):
        return pltpu.make_async_copy(
            self.source.at[z, rows_of(self.me(), SLOTS)],
            self.block(self.rank(z, *self.of(self.me()))),
            self.local.at[z],
        )

    def start(self, z):
        for step in range(1, 8):
            self.copy(z, step, (self.me() + step) % 8, self.me()).start()
        self.own_copy(z).start()

    def finish(self):
        @pl.loop(0, 4)
        def _(z):
            for step in range(1, 8):
                other = (self.me() + 8 - step) % 8
                self.copy(z, step, other, other).wait()
            self.own_copy(z).wait()


class RowSwap:
    def __init__(self, source, target, send, recv, local, dp_count, device_count):
        self.source, self.target = source, target
        self.send, self.recv, self.local = send, recv, local
        self.dp_count, self.device_count = dp_count, device_count
        self.rank = lax.axis_index("expert") * dp_count + lax.axis_index("dp")

    def block(self, ref, index):
        return ref.at[pl.ds(pl.multiple_of(index * SLOTS, SLOTS), SLOTS)]

    def copy(self, step, to, landing):
        return remote(
            self.block(self.source, to),
            self.block(self.target, landing),
            self.send.at[step],
            self.recv.at[step],
            to % self.dp_count,
            to // self.dp_count,
        )

    def own_copy(self):
        return pltpu.make_async_copy(
            self.block(self.source, self.rank), self.block(self.target, self.rank), self.local
        )

    def start(self):
        @pl.loop(1, self.device_count)
        def _(step):
            self.copy(step, (self.rank + step) % self.device_count, self.rank).start()

        self.own_copy().start()

    def start_one(self, to):
        @pl.when(to != self.rank)
        def _():
            step = (to + self.device_count - self.rank) % self.device_count
            self.copy(step, to, self.rank).start()

    def finish(self):
        @pl.loop(1, self.device_count)
        def _(step):
            other = (self.rank + self.device_count - step) % self.device_count
            self.copy(step, other, other).wait()

        self.own_copy().wait()


class WeightSwap:
    def __init__(self, place, pairs, send, recv, local, dp_count):
        self.place, self.pairs = place, pairs
        self.send, self.recv, self.local = send, recv, local
        self.dp_count = dp_count

    def copies(self, step, to, landing):
        out = []
        for i, (source, target) in enumerate(self.pairs):
            rows = source.shape[1]
            out.append(
                remote(
                    source.at[to],
                    target.at[pl.ds(pl.multiple_of(landing * rows, rows), rows)],
                    self.send.at[step, i],
                    self.recv.at[step, i],
                    to,
                    self.place.side,
                )
            )
        return out

    def own_copies(self):
        dp = self.place.dp
        return [
            pltpu.make_async_copy(
                source.at[dp],
                target.at[pl.ds(pl.multiple_of(dp * source.shape[1], source.shape[1]), source.shape[1])],
                self.local.at[i],
            )
            for i, (source, target) in enumerate(self.pairs)
        ]

    def start(self, low, high):
        @pl.loop(low, high)
        def _(step):
            for copy in self.copies(step, (self.place.dp + step) % self.dp_count, self.place.dp):
                copy.start()

    def start_own(self):
        for copy in self.own_copies():
            copy.start()

    def finish(self):
        @pl.loop(1, self.dp_count)
        def _(step):
            other = (self.place.dp + self.dp_count - step) % self.dp_count
            for copy in self.copies(step, other, other):
                copy.wait()

        for copy in self.own_copies():
            copy.wait()


def columns(tile, width=TILE):
    return pl.ds(pl.multiple_of(tile * width, width), width)


def rows_of(index, count):
    return pl.ds(pl.multiple_of(index * count, count), count)


def front_kernel(
    bias_ref,
    tokens_ref,
    cotangent_ref,
    project_ref,
    out_ref,
    target_ref,
    route_ref,
    cosine_ref,
    sine_ref,
    gate_ref,
    up_ref,
    down_ref,
    project_full,
    out_full,
    keys_ref,
    query_ref,
    attended_ref,
    exact_ref,
    stat_ref,
    middle_ref,
    hidden_ref,
    probs_ref,
    rows_in,
    grads_in,
    gate_own,
    up_own,
    down_own,
    hidden_one,
    keys_own,
    row_send,
    grad_send,
    target_all,
    gate_own_row,
    gate_all,
    hidden_all,
    grad_all,
    placed,
    acc,
    top,
    project_send,
    project_recv,
    out_send,
    out_recv,
    keys_send,
    keys_recv,
    row_send_sem,
    row_recv_sem,
    row_local,
    grad_send_sem,
    grad_recv_sem,
    grad_local,
    column_send,
    column_recv,
    weight_send,
    weight_recv,
    weight_local,
    local,
):
    dp_count = keys_ref.shape[0]
    device_count = rows_in.shape[0] // SLOTS
    tok_count, model_width = tokens_ref.shape
    query_width = HEADS * HEAD
    key_width = KV_HEADS * HEAD
    repeat_heads = HEADS // KV_HEADS
    factor = log2e * HEAD ** (-0.5)
    place = Place()
    shard_rows = project_ref.shape[0]

    def shard_of(full):
        return lambda index: full.at[rows_of(index, shard_rows)]

    project = Gather(
        place, project_ref, shard_of(project_full), project_send, project_recv, local.at[0]
    )
    out = Gather(place, out_ref, shard_of(out_full), out_send, out_recv, local.at[1])
    keys = Gather(
        place, keys_own, lambda index: keys_ref.at[index], keys_send, keys_recv, local.at[2]
    )
    rows = PlaneSwap(place, row_send, rows_in, row_send_sem, row_recv_sem, row_local, dp_count)
    grads = PlaneSwap(place, grad_send, grads_in, grad_send_sem, grad_recv_sem, grad_local, dp_count)

    def column(number, own, land):
        return Column(
            place,
            own,
            land,
            column_send.at[number],
            lambda z: column_recv.at[number, z],
            local.at[3 + number],
        )

    targets = column(0, target_ref, lambda z: target_all.at[z])
    gates = column(1, gate_own_row, lambda z: gate_all.at[z])
    hidden = column(2, hidden_ref, lambda z: hidden_all.at[z, pl.ds(0, tok_count)])
    cotangents = column(3, cotangent_ref, lambda z: grad_all.at[z])
    weights = WeightSwap(
        place,
        ((gate_ref, gate_own), (up_ref, up_own), (down_ref, down_own)),
        weight_send,
        weight_recv,
        weight_local,
        dp_count,
    )

    enter(device_count, dp_count)
    targets.start()
    project.start()
    cotangents.start()
    plane_slots = 8 * SLOTS
    targets.forward()
    targets.own_copy().wait()
    slot_row = lax.broadcasted_iota(jnp.int32, (plane_slots, TILE), 0)
    slot_lane = lax.broadcasted_iota(jnp.int32, (plane_slots, TILE), 1)
    member = slot_row // SLOTS
    label = ((member // 4) * dp_count + place.z * 4 + member % 4) * SLOTS + slot_row % SLOTS
    label = label.astype(jnp.float32)
    spare = (slot_lane - tok_count == member) & (slot_row % SLOTS == CAP)

    def match(z, choice):
        return label == target_all[z, choice : choice + 1]

    for z in range(4):
        hit = spare
        for choice in range(TOP):
            hit = hit | match(z, choice)
        placed[z] = jnp.where(hit, 1.0, 0.0).astype(jnp.bfloat16)
    hidden_all[:, tok_count:] = jnp.zeros((4, PAD_TOKENS, model_width), jnp.bfloat16)

    project.forward_z()
    project.forward_x()
    project.finish()
    cotangents.forward(1, 2)

    lanes_of = one_hot((8, LANES), lambda row, column: column == row + EXPERTS)
    gains = dot_f32(lanes_of, project_full[:, query_width + 2 * key_width :], ((1,), (1,)))
    gain_first, gain_second = gains[0:1], gains[1:2]
    chunk = 32

    @pl.loop(0, tok_count // chunk)
    def _(index):
        value = tokens_ref[rows_of(index, chunk)].astype(jnp.float32)
        scale = lax.rsqrt(jnp.mean(value * value, axis=-1, keepdims=True) + epsilon)
        hidden_one[rows_of(index, chunk)] = (value * scale * gain_first).astype(jnp.bfloat16)

    def turned(tile):
        value = dot_f32(hidden_one[...], project_full[:, columns(tile)])
        halves = []
        for half in range(TILE // HEAD):
            part = value[:, half * HEAD : (half + 1) * HEAD]
            halves.append(
                part * cosine_ref[...] + pltpu.roll(part, HEAD // 2, 1) * sine_ref[...]
            )
        return jnp.concatenate(halves, axis=1).astype(jnp.bfloat16)

    keys_own[:, :key_width] = turned(query_width // TILE)
    keys_own[:, key_width:] = dot_f32(
        hidden_one[...], project_full[:, query_width + key_width : query_width + 2 * key_width]
    ).astype(jnp.bfloat16)
    keys.start()

    @pl.loop(0, query_width // TILE)
    def _(tile):
        query_ref[:, columns(tile)] = turned(tile)

    keys.forward_z()
    keys.forward_x()
    keys.finish()
    out.start()
    cotangents.forward(2, 4)
    weights.start(1, dp_count)
    weights.start_own()

    row = lax.broadcasted_iota(jnp.int32, (tok_count, tok_count), 0)
    column_index = lax.broadcasted_iota(jnp.int32, (tok_count, tok_count), 1)
    causal = column_index <= row
    ones = jnp.ones((tok_count, LANES), jnp.bfloat16)

    def visit(label, own):
        for group in range(KV_HEADS):
            key = keys_ref[label, :, group * HEAD : (group + 1) * HEAD]
            value = keys_ref[label, :, (KV_HEADS + group) * HEAD : (KV_HEADS + group + 1) * HEAD]
            value = jnp.concatenate([value, ones], axis=1)
            for head in range(group * repeat_heads, (group + 1) * repeat_heads):
                query = query_ref[:, head * HEAD : (head + 1) * HEAD]
                scores = dot_f32(query, key, ((1,), (1,))) * factor
                if own:
                    scores = jnp.where(causal, scores, -1e30)
                    peak = jnp.ceil(jnp.max(scores, axis=-1, keepdims=True))
                    shift = peak
                else:
                    bias = bias_ref[label]
                    peak = jnp.ceil(
                        jnp.maximum(top[head], jnp.max(scores, axis=-1, keepdims=True) + bias)
                    )
                    shift = peak - bias
                prob = jnp.exp2(scores - shift).astype(jnp.bfloat16)
                part = dot_f32(prob, value)
                if own:
                    acc[head] = part
                else:
                    acc[head] = acc[head] * jnp.exp2(top[head] - peak) + part
                top[head] = peak

    visit(place.dp, True)

    @pl.loop(0, place.dp)
    def _(label):
        visit(label, False)

    out.forward_z()
    out.forward_x()
    cotangents.own_copy().wait()

    @pl.loop(0, 4)
    def _(z):
        @pl.loop(0, model_width // TILE)
        def _(tile):
            grad_send[z, :, columns(tile)] = dot_f32(
                placed[z, :, :tok_count], grad_all[z, :, columns(tile)]
            ).astype(jnp.bfloat16)

        grads.start(z)

    lane = lax.broadcasted_iota(jnp.int32, (tok_count, LANES), 1)
    stats = jnp.zeros((tok_count, LANES), jnp.float32)
    for head in range(HEADS):
        exact = acc[head, :, :HEAD] / acc[head, :, HEAD:]
        exact_ref[:, head * HEAD : (head + 1) * HEAD] = exact
        attended_ref[:, head * HEAD : (head + 1) * HEAD] = exact.astype(jnp.bfloat16)
        stats = jnp.where(lane == head, top[head], stats)
        stats = jnp.where(lane == HEADS + head, 1.0 / acc[head, :, HEAD:], stats)
    stat_ref[...] = stats
    out.finish()

    @pl.loop(0, model_width // TILE)
    def _(tile):
        middle_ref[:, columns(tile)] = tokens_ref[:, columns(tile)].astype(jnp.float32) + dot_f32(
            attended_ref[...], out_full[:, columns(tile)]
        )

    @pl.loop(0, tok_count // chunk)
    def _(index):
        value = middle_ref[rows_of(index, chunk)]
        scale = lax.rsqrt(jnp.mean(value * value, axis=-1, keepdims=True) + epsilon)
        hidden_ref[rows_of(index, chunk)] = (value * scale * gain_second).astype(jnp.bfloat16)

    hidden.start()
    router = project_full[:, query_width + 2 * key_width :]
    chosen = [route_ref[:, choice : choice + 1] == lane for choice in range(TOP)]
    mask = chosen[0]
    for choice in range(1, TOP):
        mask = mask | chosen[choice]
    logits = jnp.where(mask, dot_f32(hidden_ref[...], router), -1e30)
    weight = jnp.exp(logits - jnp.max(logits, axis=-1, keepdims=True))
    probs = weight / jnp.sum(weight, axis=-1, keepdims=True)
    probs_ref[...] = probs
    by_choice = jnp.zeros((tok_count, LANES), jnp.float32)
    for choice in range(TOP):
        gate = jnp.sum(jnp.where(chosen[choice], probs, 0.0), axis=-1, keepdims=True)
        by_choice = jnp.where(lane == choice, gate, by_choice)
    first_lanes = one_hot((8, LANES), lambda r, col: r == col)
    gate_own_row[...] = jnp.zeros(gate_own_row.shape, jnp.float32)
    gate_own_row[:, :tok_count] = sum(
        dot_f32(first_lanes, part, ((1,), (1,))) for part in split3(by_choice)
    )
    gates.start()
    fold = one_hot((8, plane_slots), lambda r, col: col // SLOTS == r)
    def dispatch(z):
        gate = jnp.zeros((plane_slots, 1), jnp.float32)
        for choice in range(TOP):
            gate += jnp.sum(
                jnp.where(match(z, choice), gate_all[z, choice : choice + 1], 0.0),
                axis=-1,
                keepdims=True,
            )
        numbers = dot_f32(fold, put_parts(gate)).astype(jnp.bfloat16)
        numbers = jnp.concatenate([numbers, jnp.zeros((8, LANES), jnp.bfloat16)], axis=0)
        hidden_all[z, tok_count : tok_count + 16, :LANES] = numbers

        @pl.loop(0, model_width // TILE)
        def _(tile):
            row_send[z, :, columns(tile)] = dot_f32(
                placed[z], hidden_all[z, :, columns(tile)]
            ).astype(jnp.bfloat16)

        rows.start(z)
    hidden.own_copy().wait()
    gates.own_copy().wait()
    dispatch(place.z)
    gates.forward()
    hidden.forward(then=dispatch)
    for gather in (targets, cotangents, hidden, gates):
        gather.finish()
    weights.finish()
    grads.finish()
    rows.finish()


def front(bias, tokens, cotangent, project, out, target, route, cosine, sine, gate, up, down):
    dp_count = lax.axis_size("dp")
    device_count = dp_count * lax.axis_size("expert")
    tok_count, model_width = tokens.shape
    query_width = HEADS * HEAD
    key_width = KV_HEADS * HEAD
    vmem = pl.BlockSpec(memory_space=pltpu.VMEM)
    anywhere = pl.BlockSpec(memory_space=pl.ANY)
    slots = device_count * SLOTS
    low, full = jnp.bfloat16, jnp.float32
    shape = jax.ShapeDtypeStruct
    ff_width = gate.shape[2]
    outs = (
        (shape((model_width, project.shape[1]), low), vmem),
        (shape((model_width, model_width), low), vmem),
        (shape((dp_count, tok_count, 2 * key_width), low), vmem),
        (shape((tok_count, query_width), low), vmem),
        (shape((tok_count, query_width), low), vmem),
        (shape((tok_count, query_width), full), vmem),
        (shape((tok_count, LANES), full), vmem),
        (shape((tok_count, model_width), full), vmem),
        (shape((tok_count, model_width), low), vmem),
        (shape((tok_count, LANES), full), vmem),
        (shape((slots, model_width), low), anywhere),
        (shape((slots, model_width), low), anywhere),
        (shape((model_width, ff_width), low), anywhere),
        (shape((model_width, ff_width), low), anywhere),
        (shape((ff_width, model_width), low), anywhere),
        (shape((tok_count, model_width), low), vmem),
    )
    dma = pltpu.SemaphoreType.DMA
    return pl.pallas_call(
        front_kernel,
        out_shape=tuple(o[0] for o in outs),
        in_specs=[pl.BlockSpec(memory_space=pltpu.SMEM)] + [vmem] * 8 + [anywhere] * 3,
        out_specs=tuple(o[1] for o in outs),
        scratch_shapes=[
            pltpu.VMEM((tok_count, 2 * key_width), low),
            pltpu.VMEM((4, 8 * SLOTS, model_width), low),
            pltpu.VMEM((4, 8 * SLOTS, model_width), low),
            pltpu.VMEM((4, 8, TILE), full),
            pltpu.VMEM((8, TILE), full),
            pltpu.VMEM((4, 8, TILE), full),
            pltpu.VMEM((4, tok_count + PAD_TOKENS, model_width), low),
            pltpu.VMEM((4, tok_count, model_width), low),
            pltpu.VMEM((4, 8 * SLOTS, TILE), low),
            pltpu.VMEM((HEADS, tok_count, 2 * HEAD), full),
            pltpu.VMEM((HEADS, tok_count, 1), full),
        ]
        + [dma((20,)), dma((dp_count,))] * 3
        + [dma((4, 8)), dma((4, 8)), dma((4,))] * 2
        + [dma((4, 8)), dma((4, 4))]
        + [dma((dp_count, 3))] * 2
        + [dma((3,)), dma((7,))],
        compiler_params=pltpu.CompilerParams(
            collective_id=0, has_side_effects=True, vmem_limit_bytes=58 * 1024 * 1024
        ),
    )(bias, tokens, cotangent, project, out, target, route, cosine, sine, gate, up, down)


def pick_gates(block):
    rows = block.shape[0]
    blocks = rows // SLOTS
    spare = one_hot((blocks, rows), lambda r, col: col == r * SLOTS + CAP)
    member = one_hot((rows, blocks), lambda r, col: r // SLOTS == col)
    parts = dot_f32(member, dot_f32(spare, block).astype(jnp.bfloat16))
    row = lax.broadcasted_iota(jnp.int32, parts.shape, 0)
    lane = lax.broadcasted_iota(jnp.int32, parts.shape, 1)
    mine = (lane % SLOTS == row % SLOTS) & (lane < 3 * SLOTS)
    return jnp.sum(jnp.where(mine, parts, 0.0), axis=-1, keepdims=True)


def put_parts(column):
    shape = (column.shape[0], LANES)
    row = lax.broadcasted_iota(jnp.int32, shape, 0)
    lane = lax.broadcasted_iota(jnp.int32, shape, 1)
    high, mid, low = (part.astype(jnp.float32) for part in split3(column))
    part = jnp.where(lane < SLOTS, high, jnp.where(lane < 2 * SLOTS, mid, low))
    mine = (lane % SLOTS == row % SLOTS) & (lane < 3 * SLOTS)
    return jnp.where(mine, part, 0.0).astype(jnp.bfloat16)


def expert_kernel(
    rows_ref,
    grads_ref,
    gate_ref,
    up_ref,
    down_ref,
    rows_back,
    outs_back,
    gate_grad_ref,
    up_grad_ref,
    down_grad_ref,
    out_send,
    row_send,
    grad_out,
    inner_ref,
    gate_act_grad,
    up_act_grad,
    row_send_sem,
    row_recv_sem,
    out_send_sem,
    out_recv_sem,
    local,
):
    dp_count = lax.axis_size("dp")
    slots, model_width = rows_ref.shape
    ff_width = gate_ref.shape[1]
    device_count = slots // SLOTS
    enter(device_count, dp_count)
    rows = RowSwap(row_send, rows_back, row_send_sem, row_recv_sem, local.at[0], dp_count, device_count)
    outs = RowSwap(out_send, outs_back, out_send_sem, out_recv_sem, local.at[1], dp_count, device_count)
    tiles = slots // TILE
    per_tile = TILE // SLOTS

    @pl.loop(0, tiles)
    def _(step):
        tile = (step + rows.rank // per_tile) % tiles
        cut = rows_of(tile, TILE)
        row = rows_ref[cut]
        gate = pick_gates(row[:, :LANES])
        saved = []
        for n in range(ff_width // TILE):
            part = slice(n * TILE, (n + 1) * TILE)
            gate_act = dot_f32(row, gate_ref[:, part])
            up_act = dot_f32(row, up_ref[:, part])
            sigmoid = 1.0 / (1.0 + jnp.exp(-gate_act))
            swish = gate_act * sigmoid
            inner_ref[cut, part] = (swish * up_act).astype(jnp.bfloat16)
            saved.append((swish, up_act * (sigmoid * (1.0 + gate_act * (1.0 - sigmoid)))))
        inner = inner_ref[cut]
        gate_grad = jnp.zeros((TILE, 1), jnp.float32)
        for n in range(model_width // TILE):
            part = slice(n * TILE, (n + 1) * TILE)
            expert_out = dot_f32(inner, down_ref[:, part]).astype(jnp.bfloat16)
            out_send[cut, part] = expert_out
            grad = grads_ref[cut, part].astype(jnp.float32)
            gate_grad += jnp.sum(expert_out.astype(jnp.float32) * grad, axis=-1, keepdims=True)
            grad_out[cut, part] = (gate * grad).astype(jnp.bfloat16)
        grad = grad_out[cut]
        for n in range(ff_width // TILE):
            part = slice(n * TILE, (n + 1) * TILE)
            swish, slope = saved[n]
            grad_inner = dot_f32(grad, down_ref[part, :], ((1,), (1,)))
            gate_act_grad[cut, part] = (grad_inner * slope).astype(jnp.bfloat16)
            up_act_grad[cut, part] = (grad_inner * swish).astype(jnp.bfloat16)
        fold = one_hot((per_tile, TILE), lambda r, col: col // SLOTS == r)
        spread = one_hot((TILE, per_tile), lambda r, col: r == col * SLOTS + CAP)
        extra = dot_f32(spread, dot_f32(fold, put_parts(gate_grad)).astype(jnp.bfloat16))
        for n in range(model_width // TILE):
            part = slice(n * TILE, (n + 1) * TILE)
            back = dot_f32(gate_act_grad[cut], gate_ref[part, :], ((1,), (1,))) + dot_f32(
                up_act_grad[cut], up_ref[part, :], ((1,), (1,))
            )
            row_send[cut, part] = back.astype(jnp.bfloat16)
            if n == 0:
                row_send[cut, :LANES] = (back[:, :LANES] + extra).astype(jnp.bfloat16)

        @pl.loop(0, per_tile)
        def _(index):
            rows.start_one(tile * per_tile + index)

    rows.own_copy().start()
    outs.start()

    @pl.loop(0, model_width // TILE)
    def _(tile):
        row = rows_ref[:, columns(tile)]
        gate_grad_ref[rows_of(tile, TILE)] = dot_f32(row, gate_act_grad[...], ((0,), (0,))).astype(
            jnp.bfloat16
        )
        up_grad_ref[rows_of(tile, TILE)] = dot_f32(row, up_act_grad[...], ((0,), (0,))).astype(
            jnp.bfloat16
        )

    @pl.loop(0, ff_width // TILE)
    def _(tile):
        inner = inner_ref[:, columns(tile)]
        for n in range(model_width // ff_width):
            part = slice(n * ff_width, (n + 1) * ff_width)
            down_grad_ref[rows_of(tile, TILE), part] = dot_f32(
                inner, grad_out[:, part], ((0,), (0,))
            ).astype(jnp.bfloat16)

    rows.finish()
    outs.finish()


def experts(rows, grads, gate, up, down):
    slots, model_width = rows.shape
    ff_width = gate.shape[1]
    device_count = slots // SLOTS
    vmem = pl.BlockSpec(memory_space=pltpu.VMEM)
    anywhere = pl.BlockSpec(memory_space=pl.ANY)
    low = jnp.bfloat16
    shape = jax.ShapeDtypeStruct
    dma = pltpu.SemaphoreType.DMA
    return pl.pallas_call(
        expert_kernel,
        out_shape=(
            shape((slots, model_width), low),
            shape((slots, model_width), low),
            shape((model_width, ff_width), low),
            shape((model_width, ff_width), low),
            shape((ff_width, model_width), low),
        ),
        in_specs=[vmem] * 5,
        out_specs=(anywhere, anywhere, vmem, vmem, vmem),
        scratch_shapes=[
            pltpu.VMEM((slots, model_width), low),
            pltpu.VMEM((slots, model_width), low),
            pltpu.VMEM((slots, model_width), low),
            pltpu.VMEM((slots, ff_width), low),
            pltpu.VMEM((slots, ff_width), low),
            pltpu.VMEM((slots, ff_width), low),
        ]
        + [dma((device_count,))] * 4
        + [dma((2,))],
        compiler_params=pltpu.CompilerParams(
            collective_id=1, has_side_effects=True, vmem_limit_bytes=58 * 1024 * 1024
        ),
    )(rows, grads, gate, up, down)


def halves_turned(value, cosine, sine):
    parts = []
    for half in range(value.shape[1] // HEAD):
        part = value[:, half * HEAD : (half + 1) * HEAD]
        parts.append(part * cosine + pltpu.roll(part, HEAD // 2, 1) * sine)
    return jnp.concatenate(parts, axis=1)


def gain_rows(small):
    lanes_of = one_hot((8, LANES), lambda row, column: column == row + EXPERTS)
    return dot_f32(lanes_of, small, ((1,), (1,)))


class Scatter:
    def __init__(self, place, block, lands, send, recvs):
        self.place, self.block = place, block
        self.lands, self.send, self.recvs = lands, send, recvs

    def hop_core(self, z, x):
        p = self.place
        number = z * 2 + x
        return remote(
            self.block(p.index(z, x, 1 - p.c)),
            self.lands[0].at[number],
            self.send.at[number],
            self.recvs[0].at[number],
            p.index(p.z, p.x, 1 - p.c),
            p.side,
        )

    def hop_x(self, z):
        p = self.place
        return remote(
            self.block(p.index(z, 1 - p.x, p.c)),
            self.lands[1].at[z],
            self.send.at[8 + z],
            self.recvs[1].at[z],
            p.index(p.z, 1 - p.x, p.c),
            p.side,
        )

    def hop_z(self, i):
        p = self.place
        z = p.others()[i]
        return remote(
            self.block(p.index(z, p.x, p.c)),
            self.lands[2].at[i],
            self.send.at[12 + i],
            self.recvs[2].at[i],
            p.index(z, p.x, p.c),
            p.side,
        )

    def add(self, shard, land):
        block = self.block(shard)
        chunk = 32

        @pl.loop(0, block.shape[0] // chunk)
        def _(index):
            cut = rows_of(index, chunk)
            block[cut] = (block[cut].astype(jnp.float32) + land[cut].astype(jnp.float32)).astype(
                jnp.bfloat16
            )

    def start(self):
        for z in range(4):
            for x in range(2):
                self.hop_core(z, x).start()

    def order(self):
        return self.place.others() + [self.place.z]

    def pass_core(self):
        p = self.place
        for z in self.order():
            for x in (1 - p.x, p.x):
                self.hop_core(z, x).wait_recv()
                self.add(p.index(z, x, p.c), self.lands[0].at[z * 2 + x])
            self.hop_x(z).start()

    def pass_x(self):
        p = self.place
        for i, z in enumerate(self.order()):
            self.hop_x(z).wait_recv()
            self.add(p.index(z, p.x, p.c), self.lands[1].at[z])
            if i < 3:
                self.hop_z(i).start()

    def pass_z(self, put):
        p = self.place
        for i in range(3):
            self.hop_z(i).wait_recv()
        block = self.block(p.dp)
        chunk = 32

        @pl.loop(0, block.shape[0] // chunk)
        def _(index):
            cut = rows_of(index, chunk)
            value = block[cut].astype(jnp.float32)
            for i in range(3):
                value += self.lands[2][i, cut].astype(jnp.float32)
            put(cut, value)

    def finish(self):
        for z in range(4):
            for x in range(2):
                self.hop_core(z, x).wait_send()
            self.hop_x(z).wait_send()
        for i in range(3):
            self.hop_z(i).wait_send()


def add_rows(block, land, low, count):
    chunk = 16

    @pl.loop(0, count // chunk)
    def _(index):
        cut = pl.ds(pl.multiple_of(low + index * chunk, chunk), chunk)
        value = block[cut].astype(jnp.float32) + land[rows_of(index, chunk)].astype(jnp.float32)
        block[cut] = value.astype(jnp.bfloat16)


class TotalSum:
    def __init__(self, place, part, lands, send, recv, x_first):
        self.place, self.part, self.lands = place, part, lands
        self.send, self.recv, self.x_first = send, recv, x_first
        self.rows = part.shape[1]
        self.half = self.rows // 2

    def kept(self, side):
        return pl.ds(pl.multiple_of(side * self.half, self.half), self.half)

    def hop(self, source, land, number, dp, side):
        return remote(source, land, self.send.at[number], self.recv.at[number], dp, side)

    def core(self, z, x):
        p = self.place
        return self.hop(
            self.part.at[p.index(z, x, 1 - p.c)],
            self.lands[0].at[z * 2 + x],
            z * 2 + x,
            p.index(p.z, p.x, 1 - p.c),
            p.side,
        )

    def over_x(self, z):
        p = self.place
        source = self.part.at[p.index(z, 1 - p.x, p.c)]
        if not self.x_first:
            source = source.at[self.kept(p.side)]
        return self.hop(source, self.lands[1].at[z], 8 + z, p.index(p.z, 1 - p.x, p.c), p.side)

    def over_side(self, z, x):
        p = self.place
        number = z if self.x_first else z * 2 + x
        return self.hop(
            self.part.at[p.index(z, x, p.c), self.kept(1 - p.side)],
            self.lands[2].at[number],
            12 + number,
            p.dp,
            1 - p.side,
        )

    def over_z(self, i):
        p = self.place
        z = p.others()[i]
        return self.hop(
            self.part.at[p.index(z, p.x, p.c), self.kept(p.side)],
            self.lands[3].at[i],
            20 + i,
            p.index(z, p.x, p.c),
            p.side,
        )

    def home(self):
        p = self.place
        block = self.part.at[p.dp, self.kept(p.side)]
        return self.hop(block, self.lands[4], 23, p.dp, 1 - p.side)

    def start(self, z):
        for x in range(2):
            self.core(z, x).start()

    def sides(self):
        return (self.place.x,) if self.x_first else (1 - self.place.x, self.place.x)

    def first(self, z):
        p = self.place
        for x in (1 - p.x, p.x):
            self.core(z, x).wait_recv()
            add_rows(self.part.at[p.index(z, x, p.c)], self.lands[0].at[z * 2 + x], 0, self.rows)
            if not self.x_first:
                self.over_side(z, x).start()
        if self.x_first:
            self.over_x(z).start()

    def take_side(self, z):
        p = self.place
        for x in self.sides():
            self.over_side(z, x).wait_recv()
            number = z if self.x_first else z * 2 + x
            add_rows(
                self.part.at[p.index(z, x, p.c)],
                self.lands[2].at[number],
                p.side * self.half,
                self.half,
            )

    def take_x(self, z):
        p = self.place
        self.over_x(z).wait_recv()
        low, count = (0, self.rows) if self.x_first else (p.side * self.half, self.half)
        add_rows(self.part.at[p.index(z, p.x, p.c)], self.lands[1].at[z], low, count)

    def second(self, z):
        if self.x_first:
            self.take_x(z)
            self.over_side(z, self.place.x).start()
        else:
            self.take_side(z)
            self.over_x(z).start()

    def third(self, z, i):
        if self.x_first:
            self.take_side(z)
        else:
            self.take_x(z)
        if i < 3:
            self.over_z(i).start()

    def fourth(self):
        p = self.place
        for i in range(3):
            self.over_z(i).wait_recv()
        chunk = 16

        @pl.loop(0, self.half // chunk)
        def _(index):
            cut = pl.ds(pl.multiple_of(p.side * self.half + index * chunk, chunk), chunk)
            value = self.part[p.dp, cut].astype(jnp.float32)
            for i in range(3):
                value += self.lands[3][i, rows_of(index, chunk)].astype(jnp.float32)
            self.part[p.dp, cut] = value.astype(jnp.bfloat16)

        self.home().start()

    def finish(self, mine, at):
        p = self.place
        mine[self.kept(p.side), at] = self.part[p.dp, self.kept(p.side)].astype(jnp.float32)
        self.home().wait()
        mine[self.kept(1 - p.side), at] = self.lands[4][...].astype(jnp.float32)
        for z in range(4):
            for x in range(2):
                self.core(z, x).wait_send()
            self.over_x(z).wait_send()
            for x in self.sides():
                self.over_side(z, x).wait_send()
        for i in range(3):
            self.over_z(i).wait_send()


class WeightReturn(WeightSwap):
    def copies(self, step, to, landing):
        out = []
        for i, (source, target) in enumerate(self.pairs):
            rows = target.shape[1]
            out.append(
                remote(
                    source.at[rows_of(to, rows)],
                    target.at[landing],
                    self.send.at[step, i],
                    self.recv.at[step, i],
                    to,
                    self.place.side,
                )
            )
        return out

    def own_copies(self):
        dp = self.place.dp
        return [
            pltpu.make_async_copy(
                source.at[rows_of(dp, target.shape[1])], target.at[dp], self.local.at[i]
            )
            for i, (source, target) in enumerate(self.pairs)
        ]


def back_kernel(
    bias_ref,
    cotangent_ref,
    middle_ref,
    probs_ref,
    exact_ref,
    stat_ref,
    query_ref,
    keys_ref,
    small_ref,
    out_ref,
    placed_ref,
    rows_ref,
    outs_ref,
    cosine_ref,
    sine_ref,
    gate_ref,
    up_ref,
    result_ref,
    grad_middle_ref,
    grad_branch_ref,
    grad_logits_ref,
    grad_project_ref,
    gain_ref,
    gate_back,
    up_back,
    grad_hidden,
    grad_ref,
    acc,
    delta,
    grad_keys_ref,
    land_core,
    land_x,
    land_z,
    scatter_send,
    recv_core,
    recv_x,
    recv_z,
    weight_send,
    weight_recv,
    weight_local,
):
    dp_count = keys_ref.shape[0]
    slots = rows_ref.shape[0]
    device_count = slots // SLOTS
    tok_count, model_width = middle_ref.shape
    query_width = HEADS * HEAD
    key_width = KV_HEADS * HEAD
    repeat_heads = HEADS // KV_HEADS
    scale = HEAD ** (-0.5)
    factor = log2e * scale
    chunk = 32
    place = Place()
    enter(device_count, dp_count)
    weights = WeightReturn(
        place,
        ((gate_ref, gate_back), (up_ref, up_back)),
        weight_send,
        weight_recv,
        weight_local,
        dp_count,
    )
    weights.start(1, dp_count)
    weights.start_own()
    scatter = Scatter(
        place,
        lambda index: grad_keys_ref.at[index],
        (land_core, land_x, land_z),
        scatter_send,
        (recv_core, recv_x, recv_z),
    )

    probs = probs_ref[...]
    gate_grads = pick_gates(rows_ref[:, :LANES])
    slot_row = lax.broadcasted_iota(jnp.int32, (slots, LANES), 0)
    slot_lane = lax.broadcasted_iota(jnp.int32, (slots, LANES), 1)
    by_expert = jnp.where(slot_lane == slot_row // SLOTS, gate_grads, 0.0)
    grad_probs = sum(dot_f32(placed_ref[...], part) for part in split3(by_expert))
    grad_logits = (
        probs * (grad_probs - jnp.sum(probs * grad_probs, axis=-1, keepdims=True))
    ).astype(jnp.bfloat16)
    grad_logits_ref[...] = grad_logits

    @pl.loop(0, model_width // TILE)
    def _(tile):
        grad_hidden[:, columns(tile)] = dot_f32(
            placed_ref[...], rows_ref[:, columns(tile)]
        ) + dot_f32(grad_logits_ref[...], small_ref[rows_of(tile, TILE)], ((1,), (1,)))

    gain = gain_rows(small_ref[...])[1:2]
    gain_ref[...] = jnp.zeros(gain_ref.shape, jnp.float32)

    @pl.loop(0, tok_count // chunk)
    def _(index):
        cut = rows_of(index, chunk)
        value = middle_ref[cut]
        row_scale = lax.rsqrt(jnp.mean(value * value, axis=-1, keepdims=True) + epsilon)
        normed = value * row_scale
        grad = grad_hidden[cut]
        gain_ref[0:1] += jnp.sum(grad * normed, axis=0, keepdims=True)
        grad = grad * gain
        total = cotangent_ref[cut].astype(jnp.float32) + row_scale * (
            grad - normed * jnp.mean(grad * normed, axis=-1, keepdims=True)
        )
        grad_middle_ref[cut] = total
        grad_branch_ref[cut] = total.astype(jnp.bfloat16)

    @pl.loop(0, model_width // TILE)
    def _(tile):
        grad_ref[:, columns(tile)] = dot_f32(
            grad_branch_ref[...], out_ref[rows_of(tile, TILE)], ((1,), (1,))
        ).astype(jnp.bfloat16)

    for head in range(HEADS):
        cut = slice(head * HEAD, (head + 1) * HEAD)
        scaled = (
            grad_ref[:, cut].astype(jnp.float32) * stat_ref[:, HEADS + head : HEADS + head + 1]
        ).astype(jnp.bfloat16)
        grad_ref[:, cut] = scaled
        delta[head] = jnp.sum(
            scaled.astype(jnp.float32) * exact_ref[:, cut], axis=-1, keepdims=True
        )
    row = lax.broadcasted_iota(jnp.int32, (tok_count, tok_count), 0)
    column = lax.broadcasted_iota(jnp.int32, (tok_count, tok_count), 1)
    causal = column <= row

    @pl.loop(place.dp + 1, dp_count)
    def _(label):
        grad_keys_ref[label] = jnp.zeros(grad_keys_ref.shape[1:], jnp.bfloat16)

    def visit(label, own):
        for group in range(KV_HEADS):
            key_cut = slice(group * HEAD, (group + 1) * HEAD)
            value_cut = slice((KV_HEADS + group) * HEAD, (KV_HEADS + group + 1) * HEAD)
            key = keys_ref[label, :, key_cut]
            value = keys_ref[label, :, value_cut]
            grad_key = jnp.zeros((tok_count, HEAD), jnp.float32)
            grad_value = jnp.zeros((tok_count, HEAD), jnp.float32)
            for head in range(group * repeat_heads, (group + 1) * repeat_heads):
                cut = slice(head * HEAD, (head + 1) * HEAD)
                query = query_ref[:, cut]
                grad = grad_ref[:, cut]
                shift = stat_ref[:, head : head + 1]
                if not own:
                    shift = shift - bias_ref[label]
                scores = dot_f32(query, key, ((1,), (1,)))
                prob = jnp.exp2(scores * factor - shift)
                if own:
                    prob = jnp.where(causal, prob, 0.0)
                prob = prob.astype(jnp.bfloat16)
                grad_prob = dot_f32(grad, value, ((1,), (1,)))
                grad_score = (prob.astype(jnp.float32) * (grad_prob - delta[head])).astype(
                    jnp.bfloat16
                )
                grad_value += dot_f32(prob, grad, ((0,), (0,)))
                grad_key += dot_f32(grad_score, query, ((0,), (0,)))
                grad_query = dot_f32(grad_score, key)
                if own:
                    acc[head] = grad_query
                else:
                    acc[head] += grad_query
            grad_keys_ref[label, :, key_cut] = (grad_key * scale).astype(jnp.bfloat16)
            grad_keys_ref[label, :, value_cut] = grad_value.astype(jnp.bfloat16)

    visit(place.dp, True)

    @pl.loop(0, place.dp)
    def _(label):
        visit(label, False)

    scatter.start()
    cosine, sine = cosine_ref[...], -sine_ref[...]
    for head in range(HEADS):
        grad_project_ref[:, head * HEAD : (head + 1) * HEAD] = halves_turned(
            acc[head] * scale, cosine, sine
        ).astype(jnp.bfloat16)
    scatter.pass_core()
    scatter.pass_x()

    expand = one_hot((LANES, slots), lambda r, col: col // SLOTS == r)
    high, mid, low = split3(probs_ref[...])
    gates = (dot_f32(high, expand) + dot_f32(mid, expand)) * placed_ref[...].astype(jnp.float32)
    gate_high = gates.astype(jnp.bfloat16)
    gate_low = (gates - gate_high.astype(jnp.float32)).astype(jnp.bfloat16)

    @pl.loop(0, model_width // TILE)
    def _(tile):
        outs = outs_ref[:, columns(tile)]
        result_ref[:, columns(tile)] = (
            middle_ref[:, columns(tile)] + dot_f32(gate_high, outs) + dot_f32(gate_low, outs)
        ).astype(jnp.bfloat16)

    def put(cut, value):
        grad_project_ref[cut, query_width : query_width + key_width] = halves_turned(
            value[:, :key_width], cosine_ref[cut], -sine_ref[cut]
        ).astype(jnp.bfloat16)
        grad_project_ref[cut, query_width + key_width :] = value[:, key_width:].astype(jnp.bfloat16)

    scatter.pass_z(put)
    scatter.finish()
    weights.finish()


def back(
    bias, cotangent, middle, probs, exact, stats, query, keys, small, out, placed, rows, outs,
    cosine, sine, gate_grad, up_grad, shard,
):
    dp_count, tok_count, both = keys.shape
    model_width = middle.shape[1]
    slots = rows.shape[0]
    ff_width = gate_grad.shape[1]
    vmem = pl.BlockSpec(memory_space=pltpu.VMEM)
    anywhere = pl.BlockSpec(memory_space=pl.ANY)
    low, full = jnp.bfloat16, jnp.float32
    shape = jax.ShapeDtypeStruct
    dma = pltpu.SemaphoreType.DMA
    return pl.pallas_call(
        back_kernel,
        out_shape=(
            shape((tok_count, model_width), low),
            shape((tok_count, model_width), full),
            shape((tok_count, model_width), low),
            shape((tok_count, LANES), low),
            shape((tok_count, query.shape[1] + both), low),
            shape((8, model_width), full),
            shape((dp_count, shard, ff_width), low),
            shape((dp_count, shard, ff_width), low),
        ),
        in_specs=[pl.BlockSpec(memory_space=pltpu.SMEM)] + [vmem] * 14 + [anywhere] * 2,
        out_specs=(vmem,) * 6 + (anywhere,) * 2,
        scratch_shapes=[
            pltpu.VMEM((tok_count, model_width), full),
            pltpu.VMEM((tok_count, model_width), low),
            pltpu.VMEM((HEADS, tok_count, HEAD), full),
            pltpu.VMEM((HEADS, tok_count, 1), full),
            pltpu.VMEM((dp_count, tok_count, both), low),
            pltpu.VMEM((8, tok_count, both), low),
            pltpu.VMEM((4, tok_count, both), low),
            pltpu.VMEM((3, tok_count, both), low),
            dma((15,)),
            dma((8,)),
            dma((4,)),
            dma((3,)),
            dma((dp_count, 2)),
            dma((dp_count, 2)),
            dma((2,)),
        ],
        compiler_params=pltpu.CompilerParams(
            collective_id=2, has_side_effects=True, vmem_limit_bytes=60 * 1024 * 1024
        ),
    )(
        bias, cotangent, middle, probs, exact, stats, query, keys, small, out, placed, rows, outs,
        cosine, sine, gate_grad, up_grad,
    )


def finish_kernel(
    tokens_ref,
    hidden_one,
    hidden_two,
    attended_ref,
    grad_middle_ref,
    grad_branch_ref,
    grad_logits_ref,
    grad_project_ref,
    gain_ref,
    project_ref,
    down_ref,
    grad_tokens_ref,
    mine_ref,
    down_back,
    grad_hidden,
    gain_one,
    part_one,
    core_one,
    x_one,
    side_one,
    z_one,
    home_one,
    part_two,
    core_two,
    x_two,
    side_two,
    z_two,
    home_two,
    send_one,
    recv_one,
    send_two,
    recv_two,
    weight_send,
    weight_recv,
    weight_local,
):
    tok_count, model_width = tokens_ref.shape
    width = grad_project_ref.shape[1]
    dp_count = lax.axis_size("dp")
    device_count = dp_count * lax.axis_size("expert")
    shard = mine_ref.shape[0]
    place = Place()
    chunk = 32
    enter(device_count, dp_count)
    weights = WeightReturn(
        place, ((down_ref, down_back),), weight_send, weight_recv, weight_local, dp_count
    )
    weights.start(1, dp_count)
    weights.start_own()
    one = TotalSum(place, part_one, (core_one, x_one, side_one, z_one, home_one), send_one, recv_one, True)
    two = TotalSum(place, part_two, (core_two, x_two, side_two, z_two, home_two), send_two, recv_two, False)
    cut_at = part_one.shape[2]

    @pl.loop(0, model_width // TILE)
    def _(tile):
        grad_hidden[:, columns(tile)] = dot_f32(
            grad_project_ref[...], project_ref[rows_of(tile, TILE), :width], ((1,), (1,))
        )

    gain = gain_rows(project_ref[:, width:])[0:1]
    gain_one[...] = jnp.zeros(gain_one.shape, jnp.float32)

    @pl.loop(0, tok_count // chunk)
    def _(index):
        cut = rows_of(index, chunk)
        value = tokens_ref[cut].astype(jnp.float32)
        row_scale = lax.rsqrt(jnp.mean(value * value, axis=-1, keepdims=True) + epsilon)
        normed = value * row_scale
        grad = grad_hidden[cut]
        gain_one[0:1] += jnp.sum(grad * normed, axis=0, keepdims=True)
        grad = grad * gain
        grad_tokens_ref[cut] = grad_middle_ref[cut] + row_scale * (
            grad - normed * jnp.mean(grad * normed, axis=-1, keepdims=True)
        )

    one_lane = one_hot((8, LANES), lambda r, col: (r == 0) & (col == EXPERTS))
    two_lane = one_hot((8, LANES), lambda r, col: (r == 0) & (col == EXPERTS + 1))
    group = 4 * shard

    @pl.loop(0, model_width // group)
    def _(index):
        cut = columns(index, group)

        def put(part, low, value):
            for i in range(4):
                part[index * 4 + i, :, low : low + value.shape[1]] = value[
                    i * shard : (i + 1) * shard
                ].astype(jnp.bfloat16)

        left = hidden_one[:, cut]
        step = 3 * LANES
        for low in range(0, cut_at, step):
            put(part_one, low, dot_f32(left, grad_project_ref[:, low : low + step], ((0,), (0,))))
        rest = width - cut_at
        put(part_two, 0, dot_f32(left, grad_project_ref[:, cut_at:], ((0,), (0,))))
        small = dot_f32(hidden_two[:, cut], grad_logits_ref[...], ((0,), (0,)))
        for part in split3(gain_one[:, cut]):
            small += dot_f32(part, one_lane, ((0,), (0,)))
        for part in split3(gain_ref[:, cut]):
            small += dot_f32(part, two_lane, ((0,), (0,)))
        put(part_two, rest, small)
        left = attended_ref[:, cut]
        for low in range(0, model_width, step):
            put(
                part_two,
                rest + LANES + low,
                dot_f32(left, grad_branch_ref[:, low : low + step], ((0,), (0,))),
            )
        for total in (one, two):
            total.start(index)

    order = place.others() + [place.z]
    both = (one, two)
    for z in order:
        for total in both:
            total.first(z)
    for z in order:
        for total in both:
            total.second(z)
    for i, z in enumerate(order):
        for total in both:
            total.third(z, i)
    for total in both:
        total.fourth()
    one.finish(mine_ref, slice(0, cut_at))
    two.finish(mine_ref, slice(cut_at, mine_ref.shape[1]))
    weights.finish()


def finish(
    tokens, hidden_one, hidden_two, attended, grad_middle, grad_branch, grad_logits, grad_project,
    gain, project, down_grad, shard, half,
):
    tok_count, model_width = tokens.shape
    dp_count = lax.axis_size("dp")
    width = project.shape[1] + model_width
    first = 15 * LANES
    vmem = pl.BlockSpec(memory_space=pltpu.VMEM)
    anywhere = pl.BlockSpec(memory_space=pl.ANY)
    low, full = jnp.bfloat16, jnp.float32
    shape = jax.ShapeDtypeStruct
    dma = pltpu.SemaphoreType.DMA
    return pl.pallas_call(
        finish_kernel,
        out_shape=(
            shape((tok_count, model_width), full),
            shape((shard, width), full),
            shape((dp_count, half, model_width), low),
        ),
        in_specs=[vmem] * 10 + [anywhere],
        out_specs=(vmem, vmem, anywhere),
        scratch_shapes=[
            pltpu.VMEM((tok_count, model_width), full),
            pltpu.VMEM((8, model_width), full),
            *(
                pltpu.VMEM(lead + (columns_of,), low)
                for columns_of, lead in (
                    (first, (dp_count, shard)),
                    (first, (8, shard)),
                    (first, (4, shard)),
                    (first, (4, shard // 2)),
                    (first, (3, shard // 2)),
                    (first, (shard // 2,)),
                    (width - first, (dp_count, shard)),
                    (width - first, (8, shard)),
                    (width - first, (4, shard // 2)),
                    (width - first, (8, shard // 2)),
                    (width - first, (3, shard // 2)),
                    (width - first, (shard // 2,)),
                )
            ),
            dma((24,)),
            dma((24,)),
            dma((24,)),
            dma((24,)),
            dma((dp_count, 1)),
            dma((dp_count, 1)),
            dma((1,)),
        ],
        compiler_params=pltpu.CompilerParams(
            collective_id=3, has_side_effects=True, vmem_limit_bytes=58 * 1024 * 1024
        ),
    )(
        tokens, hidden_one, hidden_two, attended, grad_middle, grad_branch, grad_logits,
        grad_project, gain, project, down_grad,
    )


def local_owned(
    tokens,
    attn_gain,
    query_weight,
    key_weight,
    value_weight,
    out_weight,
    moe_gain,
    router_weight,
    gate_weight,
    up_weight,
    down_weight,
    parents,
    routes,
    claim_order,
    cotangent,
):
    tok_count = tokens.shape[1]
    segment = lax.axis_index("dp")
    query_width = HEADS * HEAD
    key_width = KV_HEADS * HEAD

    route_rows = routes[0]
    expert_ids = route_rows.reshape(-1)
    order_row = claim_order[0, 0]
    member = (expert_ids[:, None] == jnp.arange(EXPERTS, dtype=jnp.int32)[None, :]).astype(
        jnp.bfloat16
    )
    earlier = (order_row[None, :] < order_row[:, None]).astype(jnp.bfloat16)
    before = jnp.dot(earlier, member, preferred_element_type=jnp.float32)
    slot_index = jnp.sum(before * member.astype(jnp.float32), axis=1).astype(jnp.int32)
    target = jnp.where(slot_index < CAP, expert_ids * SLOTS + slot_index, -1).reshape(
        tok_count, TOP
    )
    row_labels = jnp.arange(EXPERTS * SLOTS, dtype=jnp.int32)
    placed_rows = sum(
        (target[:, c : c + 1] == row_labels[None, :]).astype(jnp.bfloat16) for c in range(TOP)
    )
    target_rows = jnp.full((8, TILE), -1.0, jnp.float32)
    target_rows = target_rows.at[:TOP, :tok_count].set(target.T.astype(jnp.float32))
    route_lanes = jnp.pad(route_rows, ((0, 0), (0, LANES - TOP)), constant_values=-1)

    small = jnp.concatenate(
        [
            router_weight,
            attn_gain[:, None],
            moe_gain[:, None],
            jnp.zeros((router_weight.shape[0], LANES - EXPERTS - 2), jnp.bfloat16),
        ],
        axis=1,
    )
    project_shard = jnp.concatenate([query_weight, key_weight, value_weight, small], axis=1)
    reach_row = ancestry(parents[0])[segment]
    path_depth = jnp.sum(reach_row) - 1.0
    positions = path_depth * tok_count + jnp.arange(tok_count, dtype=jnp.float32)
    cosine, sine_part = rope_tables(positions, HEAD)
    cosine_wide = jnp.concatenate([cosine[:, 0], cosine[:, 0]], axis=1)
    sine_wide = jnp.concatenate([-sine_part[:, 0], sine_part[:, 0]], axis=1)
    on_path = reach_row > 0.5
    bias = jnp.where(on_path, 0.0, -1e30).astype(jnp.float32)
    (
        project_full,
        out_full,
        keys,
        query_rot,
        attended,
        exact_out,
        stats,
        middle,
        hidden_two,
        probs,
        rows_in,
        grad_rows_in,
        gate_own,
        up_own,
        down_own,
        hidden_one,
    ) = front(
        bias,
        tokens[0],
        cotangent[0],
        project_shard,
        out_weight,
        target_rows,
        route_lanes,
        cosine_wide,
        sine_wide,
        gate_weight,
        up_weight,
        down_weight,
    )
    small_at = query_width + 2 * key_width
    rows_back, outs_back, gate_grad, up_grad, down_grad = experts(
        rows_in, grad_rows_in, gate_own, up_own, down_own
    )
    (
        block_out,
        grad_middle,
        grad_branch,
        grad_logits,
        grad_project,
        gain_row,
        gate_back,
        up_back,
    ) = back(
        bias,
        cotangent[0],
        middle,
        probs,
        exact_out,
        stats,
        query_rot,
        keys,
        project_full[:, small_at:],
        out_full,
        placed_rows,
        rows_back,
        outs_back,
        cosine_wide,
        sine_wide,
        gate_grad,
        up_grad,
        gate_weight.shape[1],
    )
    grad_tokens, mine, down_back = finish(
        tokens[0],
        hidden_one,
        hidden_two,
        attended,
        grad_middle,
        grad_branch,
        grad_logits,
        grad_project,
        gain_row,
        project_full,
        down_grad,
        query_weight.shape[0],
        down_weight.shape[1],
    )
    return (
        block_out[None],
        grad_tokens[None],
        mine[:, small_at + EXPERTS],
        mine[:, :query_width],
        mine[:, query_width : query_width + key_width],
        mine[:, query_width + key_width : small_at],
        mine[:, small_at + LANES :],
        mine[:, small_at + EXPERTS + 1],
        mine[:, small_at : small_at + EXPERTS],
        gate_back.astype(jnp.float32),
        up_back.astype(jnp.float32),
        down_back.astype(jnp.float32),
    )


def solution(mesh):
    placed = (
        P("expert", "dp", None),
        P("dp"),
        P("dp", None),
        P("dp", None),
        P("dp", None),
        P("dp", None),
        P("dp"),
        P("dp", None),
        P("expert", "dp", None),
        P("expert", "dp", None),
        P("expert", "dp", None),
        P("expert", None),
        P("expert", "dp", None),
        P("expert", "dp", None),
        P("expert", "dp", None),
    )
    owned = mesh.shape["dp"] == 16 and mesh.shape["expert"] == 2
    return jax.shard_map(
        local_owned if owned else local_gathered,
        mesh=mesh,
        in_specs=placed,
        out_specs=(
            P("expert", "dp", None),
            P("expert", "dp", None),
            P("dp"),
            P("dp", None),
            P("dp", None),
            P("dp", None),
            P("dp", None),
            P("dp"),
            P("dp", None),
            P("expert", "dp", None),
            P("expert", "dp", None),
            P("expert", "dp", None),
        ),
        check_vma=False,
    )
```

```python
import functools

import jax
import jax.numpy as jnp
from jax import lax
from jax.experimental import pallas as pl
from jax.experimental.pallas import tpu as pltpu
from jax.sharding import PartitionSpec as P

HEADS = 12
KV_HEADS = 2
HEAD = 128
EXPERTS = 32
TOP = 4
CAP = 28


epsilon = 1e-06
theta = 10000.0
highest = lax.Precision.HIGHEST


def ancestry(parents):
    row_count = parents.shape[0]
    labels = jnp.arange(row_count, dtype=jnp.int32)
    linked = (parents[:, None] == labels[None, :]).astype(jnp.float32)
    reach_all = jnp.minimum(jnp.eye(row_count, dtype=jnp.float32) + linked, 1.0)
    for doubling in range(max(1, (row_count - 1).bit_length())):
        reach_all = jnp.minimum(jnp.dot(reach_all, reach_all, precision=highest), 1.0)
    return reach_all


def rope_tables(positions, head_size):
    halfway = head_size // 2
    frequency = theta ** (-jnp.arange(halfway, dtype=jnp.float32) * 2.0 / head_size)
    angles = positions[:, None] * frequency[None, :]
    return (jnp.cos(angles)[:, None, :], jnp.sin(angles)[:, None, :])


def rotate(values, cosine, sine_part):
    halfway = values.shape[-1] // 2
    first_half = values[..., :halfway]
    second = values[..., halfway:]
    return jnp.concatenate(
        [first_half * cosine - second * sine_part, second * cosine + first_half * sine_part],
        axis=-1,
    )


def norm_backward(grad_hidden, normed, row_scale, gain):
    grad_normed = grad_hidden * gain
    grad_gain = jnp.sum(grad_hidden * normed, axis=0)
    grad_rows = row_scale * (
        grad_normed - normed * jnp.mean(grad_normed * normed, axis=-1, keepdims=True)
    )
    return (grad_rows, grad_gain)


def local_gathered(
    tokens,
    attn_gain,
    query_weight,
    key_weight,
    value_weight,
    out_weight,
    moe_gain,
    router_weight,
    gate_weight,
    up_weight,
    down_weight,
    parents,
    routes,
    claim_order,
    cotangent,
):
    (
        gain_one,
        query_full,
        key_full,
        value_full,
        out_full,
        gain_two,
        router_full,
        gate_full,
        up_full,
        down_full,
    ) = (
        lax.all_gather(attn_gain, "dp", axis=0, tiled=True),
        lax.all_gather(query_weight, "dp", axis=0, tiled=True),
        lax.all_gather(key_weight, "dp", axis=0, tiled=True),
        lax.all_gather(value_weight, "dp", axis=0, tiled=True),
        lax.all_gather(out_weight, "dp", axis=0, tiled=True),
        lax.all_gather(moe_gain, "dp", axis=0, tiled=True),
        lax.all_gather(router_weight, "dp", axis=0, tiled=True),
        lax.all_gather(gate_weight, "dp", axis=1, tiled=True),
        lax.all_gather(up_weight, "dp", axis=1, tiled=True),
        lax.all_gather(down_weight, "dp", axis=1, tiled=True),
    )
    tok_count = tokens.shape[1]
    model_width = tokens.shape[2]
    segment = lax.axis_index("dp")
    segment_count = lax.axis_size("dp")
    expert_peers = lax.axis_size("expert")
    local_experts = gate_weight.shape[0]
    repeat_heads = HEADS // KV_HEADS
    score_scale = HEAD ** (-0.5)
    query_rows = repeat_heads * tok_count
    reach_all = ancestry(parents[0])
    reach_row = reach_all[segment]
    path_depth = jnp.sum(reach_row) - 1.0
    positions = path_depth * tok_count + jnp.arange(tok_count, dtype=jnp.float32)
    cosine, sine_part = rope_tables(positions, HEAD)
    inputs = tokens[0].astype(jnp.float32)
    scale_one = lax.rsqrt(jnp.mean(inputs * inputs, axis=-1, keepdims=True) + epsilon)
    normed_one = inputs * scale_one
    gain_first = gain_one.astype(jnp.float32)
    hidden_one = (normed_one * gain_first).astype(jnp.bfloat16)
    query_raw = jnp.dot(hidden_one, query_full, preferred_element_type=jnp.float32).reshape(
        tok_count, HEADS, HEAD
    )
    key_raw = jnp.dot(hidden_one, key_full, preferred_element_type=jnp.float32).reshape(
        tok_count, KV_HEADS, HEAD
    )
    value_low = jnp.dot(hidden_one, value_full, preferred_element_type=jnp.float32).astype(
        jnp.bfloat16
    )
    query_rot = rotate(query_raw, cosine, sine_part).astype(jnp.bfloat16)
    key_rot = (
        rotate(key_raw, cosine, sine_part).astype(jnp.bfloat16).reshape(tok_count, KV_HEADS * HEAD)
    )
    key_all, value_all = (
        lax.all_gather(key_rot, "dp", axis=0, tiled=True),
        lax.all_gather(value_low, "dp", axis=0, tiled=True),
    )
    total_keys = key_all.shape[0]
    key_blocks = key_all.reshape(segment_count, tok_count, KV_HEADS, HEAD)
    value_blocks = value_all.reshape(segment_count, tok_count, KV_HEADS, HEAD)
    segment_labels = jnp.arange(segment_count, dtype=jnp.int32)
    query_groups = (
        query_rot.reshape(tok_count, KV_HEADS, repeat_heads, HEAD)
        .transpose(1, 2, 0, 3)
        .reshape(KV_HEADS, query_rows, HEAD)
    )
    query_offsets = jnp.arange(tok_count, dtype=jnp.int32)
    causal_tile = jnp.tile(query_offsets[None, :] <= query_offsets[:, None], (repeat_heads, 1))

    def scores_of(key_block, label):
        raw_scores = (
            jnp.einsum("grh,kgh->grk", query_groups, key_block, preferred_element_type=jnp.float32)
            * score_scale
        )
        allowed = causal_tile | (label != segment)
        return jnp.where(allowed[None], raw_scores, -1000000000.0)

    def on_path(label):
        return reach_row[label] > 0.5

    def pass_stats(state_pair, inputs_block):
        key_block, value_block, label = inputs_block

        def visit(state):
            row_max, row_sum = state
            scores = scores_of(key_block, label)
            new_max = jnp.maximum(row_max, jnp.max(scores, axis=-1))
            new_sum = row_sum * jnp.exp(row_max - new_max) + jnp.sum(
                jnp.exp(scores - new_max[..., None]), axis=-1
            )
            return (new_max, new_sum)

        return (lax.cond(on_path(label), visit, lambda state: state, state_pair), None)

    start_max = jnp.full((KV_HEADS, query_rows), -1e30, jnp.float32)
    start_sum = jnp.zeros((KV_HEADS, query_rows), jnp.float32)
    (row_max, row_sum), unused = lax.scan(
        pass_stats, (start_max, start_sum), (key_blocks, value_blocks, segment_labels)
    )

    def probs_of(key_block, label):
        return jnp.exp(scores_of(key_block, label) - row_max[..., None]) / row_sum[..., None]

    def pass_values(state_pair, inputs_block):
        key_block, value_block, label = inputs_block

        def visit(state):
            accumulated, exact_out = state
            prob_block = probs_of(key_block, label)
            accumulated = accumulated + jnp.einsum(
                "grk,kgh->grh",
                prob_block.astype(jnp.bfloat16),
                value_block,
                preferred_element_type=jnp.float32,
            )
            exact_out = exact_out + jnp.einsum(
                "grk,kgh->grh",
                prob_block,
                value_block.astype(jnp.float32),
                preferred_element_type=jnp.float32,
                precision=highest,
            )
            return (accumulated, exact_out)

        return (lax.cond(on_path(label), visit, lambda state: state, state_pair), None)

    zero_out = jnp.zeros((KV_HEADS, query_rows, HEAD), jnp.float32)
    (accumulated, exact_out), unused = lax.scan(
        pass_values, (zero_out, zero_out), (key_blocks, value_blocks, segment_labels)
    )
    attended = (
        accumulated.reshape(KV_HEADS, repeat_heads, tok_count, HEAD)
        .transpose(2, 0, 1, 3)
        .reshape(tok_count, HEADS * HEAD)
        .astype(jnp.bfloat16)
    )
    branch = jnp.dot(attended, out_full, preferred_element_type=jnp.float32)
    middle = inputs + branch
    scale_two = lax.rsqrt(jnp.mean(middle * middle, axis=-1, keepdims=True) + epsilon)
    normed_two = middle * scale_two
    gain_second = gain_two.astype(jnp.float32)
    hidden_two = (normed_two * gain_second).astype(jnp.bfloat16)
    logits = jnp.dot(hidden_two, router_full, preferred_element_type=jnp.float32)
    picked_one = (
        routes[0][:, :, None] == jnp.arange(EXPERTS, dtype=jnp.int32)[None, None, :]
    ).astype(jnp.float32)
    chosen = jnp.sum(picked_one * logits[:, None, :], axis=-1)
    gate_probs = jax.nn.softmax(chosen, axis=-1)
    expert_ids = routes[0].reshape(-1)
    order_row = claim_order[0, 0]
    pair_count = expert_ids.shape[0]
    member = (expert_ids[:, None] == jnp.arange(EXPERTS, dtype=jnp.int32)[None, :]).astype(
        jnp.bfloat16
    )
    earlier = (order_row[None, :] < order_row[:, None]).astype(jnp.bfloat16)
    before = jnp.dot(earlier, member, preferred_element_type=jnp.float32)
    slot_index = jnp.sum(before * member.astype(jnp.float32), axis=1).astype(jnp.int32)
    owner_rank = expert_ids // local_experts
    local_rank = expert_ids % local_experts
    target = jnp.where(
        slot_index < CAP, (local_rank * expert_peers + owner_rank) * CAP + slot_index, EXPERTS * CAP
    )
    slot_pairs = (
        jnp.full((EXPERTS * CAP + 1,), pair_count, jnp.int32)
        .at[target]
        .set(jnp.arange(pair_count, dtype=jnp.int32))[: EXPERTS * CAP]
    )
    padded_two = jnp.concatenate([hidden_two, jnp.zeros((1, model_width), jnp.bfloat16)], axis=0)
    send_rows = padded_two[slot_pairs // TOP].reshape(local_experts, expert_peers, CAP, model_width)
    arrived = lax.all_to_all(send_rows, "expert", split_axis=1, concat_axis=1, tiled=True)
    expert_rows = arrived.reshape(local_experts, expert_peers * CAP, model_width)
    gate_act = jnp.einsum(
        "erd,edf->erf", expert_rows, gate_full, preferred_element_type=jnp.float32
    )
    up_act = jnp.einsum("erd,edf->erf", expert_rows, up_full, preferred_element_type=jnp.float32)
    inner = (jax.nn.silu(gate_act) * up_act).astype(jnp.bfloat16)
    expert_out = jnp.einsum(
        "erf,efd->erd", inner, down_full, preferred_element_type=jnp.float32
    ).astype(jnp.bfloat16)
    returned = lax.all_to_all(
        expert_out.reshape(local_experts, expert_peers, CAP, model_width),
        "expert",
        split_axis=1,
        concat_axis=1,
        tiled=True,
    )
    returned = jnp.concatenate(
        [returned.reshape(EXPERTS * CAP, model_width), jnp.zeros((1, model_width), jnp.bfloat16)],
        axis=0,
    )
    pair_out = returned[target].reshape(tok_count, TOP, model_width).astype(jnp.float32)
    mixture = jnp.sum(gate_probs[:, :, None] * pair_out, axis=1)
    block_out = (middle + mixture).astype(jnp.bfloat16)
    grad_result = cotangent[0].astype(jnp.float32)
    grad_gates = jnp.sum(pair_out * grad_result[:, None, :], axis=-1)
    grad_pairs = (
        (gate_probs[:, :, None] * grad_result[:, None, :])
        .astype(jnp.bfloat16)
        .reshape(pair_count, model_width)
    )
    grad_padded = jnp.concatenate([grad_pairs, jnp.zeros((1, model_width), jnp.bfloat16)], axis=0)
    grad_send = grad_padded[slot_pairs].reshape(local_experts, expert_peers, CAP, model_width)
    grad_arrived, rows_back = (
        lax.all_to_all(grad_send, "expert", split_axis=1, concat_axis=1, tiled=True),
        lax.all_to_all(send_rows, "expert", split_axis=1, concat_axis=1, tiled=True),
    )
    rows_again = rows_back.reshape(local_experts, expert_peers * CAP, model_width)
    gate_again = jnp.einsum(
        "erd,edf->erf", rows_again, gate_full, preferred_element_type=jnp.float32
    )
    up_again = jnp.einsum("erd,edf->erf", rows_again, up_full, preferred_element_type=jnp.float32)
    inner_again = (jax.nn.silu(gate_again) * up_again).astype(jnp.bfloat16)
    grad_expert_out = grad_arrived.reshape(local_experts, expert_peers * CAP, model_width)
    grad_inner = jnp.einsum(
        "erd,efd->erf", grad_expert_out, down_full, preferred_element_type=jnp.float32
    )
    grad_down_local = jnp.einsum(
        "erf,erd->efd", inner_again, grad_expert_out, preferred_element_type=jnp.float32
    )
    sigmoid_gate = jax.nn.sigmoid(gate_again)
    swish = gate_again * sigmoid_gate
    grad_gate_act = (
        grad_inner * up_again * (sigmoid_gate * (1.0 + gate_again * (1.0 - sigmoid_gate)))
    ).astype(jnp.bfloat16)
    grad_up_act = (grad_inner * swish).astype(jnp.bfloat16)
    grad_gate_local = jnp.einsum(
        "erd,erf->edf", rows_again, grad_gate_act, preferred_element_type=jnp.float32
    )
    grad_up_local = jnp.einsum(
        "erd,erf->edf", rows_again, grad_up_act, preferred_element_type=jnp.float32
    )
    grad_rows = (
        jnp.einsum("erf,edf->erd", grad_gate_act, gate_full, preferred_element_type=jnp.float32)
        + jnp.einsum("erf,edf->erd", grad_up_act, up_full, preferred_element_type=jnp.float32)
    ).astype(jnp.bfloat16)
    grad_back = lax.all_to_all(
        grad_rows.reshape(local_experts, expert_peers, CAP, model_width),
        "expert",
        split_axis=1,
        concat_axis=1,
        tiled=True,
    )
    grad_back = jnp.concatenate(
        [grad_back.reshape(EXPERTS * CAP, model_width), jnp.zeros((1, model_width), jnp.bfloat16)],
        axis=0,
    )
    grad_hidden_two = jnp.sum(
        grad_back[target].reshape(tok_count, TOP, model_width).astype(jnp.float32), axis=1
    )
    grad_chosen = gate_probs * (
        grad_gates - jnp.sum(gate_probs * grad_gates, axis=-1, keepdims=True)
    )
    grad_logits = jnp.sum(picked_one * grad_chosen[:, :, None], axis=1).astype(jnp.bfloat16)
    grad_hidden_two = grad_hidden_two + jnp.dot(
        grad_logits, router_full.T, preferred_element_type=jnp.float32
    )
    grad_router_local = jnp.dot(hidden_two.T, grad_logits, preferred_element_type=jnp.float32)
    grad_middle_norm, grad_gain_two = norm_backward(
        grad_hidden_two, normed_two, scale_two, gain_second
    )
    grad_middle = grad_result + grad_middle_norm
    grad_branch = grad_middle.astype(jnp.bfloat16)
    grad_out_local = jnp.dot(attended.T, grad_branch, preferred_element_type=jnp.float32)
    grad_attended = jnp.dot(grad_branch, out_full.T, preferred_element_type=jnp.float32).astype(
        jnp.bfloat16
    )
    grad_groups = (
        grad_attended.reshape(tok_count, KV_HEADS, repeat_heads, HEAD)
        .transpose(1, 2, 0, 3)
        .reshape(KV_HEADS, query_rows, HEAD)
    )
    row_delta = jnp.sum(grad_groups.astype(jnp.float32) * exact_out, axis=-1)
    zero_key = jnp.zeros((tok_count, KV_HEADS, HEAD), jnp.float32)

    def pass_grads(grad_query, inputs_block):
        key_block, value_block, label = inputs_block

        def visit(carried):
            prob_block = probs_of(key_block, label)
            grad_probs = jnp.einsum(
                "grh,kgh->grk", grad_groups, value_block, preferred_element_type=jnp.float32
            )
            grad_scores = (prob_block * (grad_probs - row_delta[..., None])).astype(jnp.bfloat16)
            carried = carried + jnp.einsum(
                "grk,kgh->grh", grad_scores, key_block, preferred_element_type=jnp.float32
            )
            grad_key_block = (
                jnp.einsum(
                    "grk,grh->kgh", grad_scores, query_groups, preferred_element_type=jnp.float32
                )
                * score_scale
            )
            grad_value_block = jnp.einsum(
                "grk,grh->kgh",
                prob_block.astype(jnp.bfloat16),
                grad_groups,
                preferred_element_type=jnp.float32,
            )
            return (carried, (grad_key_block, grad_value_block))

        def skip(carried):
            return (carried, (zero_key, zero_key))

        return lax.cond(on_path(label), visit, skip, grad_query)

    grad_query_groups, (grad_key_blocks, grad_value_blocks) = lax.scan(
        pass_grads,
        jnp.zeros((KV_HEADS, query_rows, HEAD), jnp.float32),
        (key_blocks, value_blocks, segment_labels),
    )
    grad_key_all = grad_key_blocks.reshape(total_keys, KV_HEADS * HEAD)
    grad_value_all = grad_value_blocks.reshape(total_keys, KV_HEADS * HEAD)
    grad_key_mine, grad_value_mine = (
        lax.psum_scatter(
            grad_key_all.astype(jnp.bfloat16), "dp", scatter_dimension=0, tiled=True
        ).astype(jnp.float32),
        lax.psum_scatter(
            grad_value_all.astype(jnp.bfloat16), "dp", scatter_dimension=0, tiled=True
        ).astype(jnp.float32),
    )
    grad_query_rot = (
        (grad_query_groups * score_scale)
        .reshape(KV_HEADS, repeat_heads, tok_count, HEAD)
        .transpose(2, 0, 1, 3)
        .reshape(tok_count, HEADS, HEAD)
    )
    grad_query_raw = (
        rotate(grad_query_rot, cosine, -sine_part)
        .reshape(tok_count, HEADS * HEAD)
        .astype(jnp.bfloat16)
    )
    grad_key_raw = (
        rotate(grad_key_mine.reshape(tok_count, KV_HEADS, HEAD), cosine, -sine_part)
        .reshape(tok_count, KV_HEADS * HEAD)
        .astype(jnp.bfloat16)
    )
    grad_value_raw = grad_value_mine.astype(jnp.bfloat16)
    grad_query_local = jnp.dot(hidden_one.T, grad_query_raw, preferred_element_type=jnp.float32)
    grad_key_local = jnp.dot(hidden_one.T, grad_key_raw, preferred_element_type=jnp.float32)
    grad_value_local = jnp.dot(hidden_one.T, grad_value_raw, preferred_element_type=jnp.float32)
    grad_hidden_one = (
        jnp.dot(grad_query_raw, query_full.T, preferred_element_type=jnp.float32)
        + jnp.dot(grad_key_raw, key_full.T, preferred_element_type=jnp.float32)
        + jnp.dot(grad_value_raw, value_full.T, preferred_element_type=jnp.float32)
    )
    grad_inputs_norm, grad_gain_one = norm_backward(
        grad_hidden_one, normed_one, scale_one, gain_first
    )
    grad_inputs = grad_middle + grad_inputs_norm
    grad_gate_mine, grad_up_mine, grad_down_mine = (
        lax.psum_scatter(
            grad_gate_local.astype(jnp.bfloat16), "dp", scatter_dimension=1, tiled=True
        ).astype(jnp.float32),
        lax.psum_scatter(
            grad_up_local.astype(jnp.bfloat16), "dp", scatter_dimension=1, tiled=True
        ).astype(jnp.float32),
        lax.psum_scatter(
            grad_down_local.astype(jnp.bfloat16), "dp", scatter_dimension=1, tiled=True
        ).astype(jnp.float32),
    )
    shard_rows = (
        lax.psum_scatter(
            grad_gain_one.astype(jnp.bfloat16), "dp", scatter_dimension=0, tiled=True
        ).astype(jnp.float32),
        lax.psum_scatter(
            grad_query_local.astype(jnp.bfloat16), "dp", scatter_dimension=0, tiled=True
        ).astype(jnp.float32),
        lax.psum_scatter(
            grad_key_local.astype(jnp.bfloat16), "dp", scatter_dimension=0, tiled=True
        ).astype(jnp.float32),
        lax.psum_scatter(
            grad_value_local.astype(jnp.bfloat16), "dp", scatter_dimension=0, tiled=True
        ).astype(jnp.float32),
        lax.psum_scatter(
            grad_out_local.astype(jnp.bfloat16), "dp", scatter_dimension=0, tiled=True
        ).astype(jnp.float32),
        lax.psum_scatter(
            grad_gain_two.astype(jnp.bfloat16), "dp", scatter_dimension=0, tiled=True
        ).astype(jnp.float32),
        lax.psum_scatter(
            grad_router_local.astype(jnp.bfloat16), "dp", scatter_dimension=0, tiled=True
        ).astype(jnp.float32),
    )
    shared = (
        lax.psum(shard_rows[0].astype(jnp.bfloat16), "expert").astype(jnp.float32),
        lax.psum(shard_rows[1].astype(jnp.bfloat16), "expert").astype(jnp.float32),
        lax.psum(shard_rows[2].astype(jnp.bfloat16), "expert").astype(jnp.float32),
        lax.psum(shard_rows[3].astype(jnp.bfloat16), "expert").astype(jnp.float32),
        lax.psum(shard_rows[4].astype(jnp.bfloat16), "expert").astype(jnp.float32),
        lax.psum(shard_rows[5].astype(jnp.bfloat16), "expert").astype(jnp.float32),
        lax.psum(shard_rows[6].astype(jnp.bfloat16), "expert").astype(jnp.float32),
    )
    return (
        block_out[None],
        grad_inputs[None],
        shared[0],
        shared[1],
        shared[2],
        shared[3],
        shared[4],
        shared[5],
        shared[6],
        grad_gate_mine,
        grad_up_mine,
        grad_down_mine,
    )


SLOTS = 32
PAD_TOKENS = 32
LANES = 128
TILE = 256
MESH = pl.DeviceIdType.MESH
log2e = 1.4426950408889634


def dot_f32(a, b, dims=((1,), (0,))):
    return lax.dot_general(a, b, (dims, ((), ())), preferred_element_type=jnp.float32)


def split3(value):
    high = value.astype(jnp.bfloat16)
    rest = value - high.astype(jnp.float32)
    middle = rest.astype(jnp.bfloat16)
    low = (rest - middle.astype(jnp.float32)).astype(jnp.bfloat16)
    return high, middle, low


def one_hot(shape, test):
    row = lax.broadcasted_iota(jnp.int32, shape, 0)
    column = lax.broadcasted_iota(jnp.int32, shape, 1)
    return jnp.where(test(row, column), 1.0, 0.0).astype(jnp.bfloat16)


class Place:
    def __init__(self):
        self.dp = lax.axis_index("dp")
        self.side = lax.axis_index("expert")
        self.z = self.dp // 4
        self.x = (self.dp // 2) % 2
        self.c = self.dp % 2

    def index(self, z, x, c):
        return z * 4 + x * 2 + c

    def others(self):
        return [self.z + 1 - 2 * (self.z % 2), (self.z + 2) % 4, 3 - self.z]


def remote(src, dst, send, recv, dp, side):
    return pltpu.make_async_remote_copy(
        src_ref=src,
        dst_ref=dst,
        send_sem=send,
        recv_sem=recv,
        device_id={"dp": dp, "expert": side},
        device_id_type=MESH,
    )


def enter(device_count, dp_count):
    rank = lax.axis_index("expert") * dp_count + lax.axis_index("dp")
    barrier = pltpu.get_barrier_semaphore()

    @pl.loop(1, device_count)
    def _(step):
        other = (rank + step) % device_count
        pl.semaphore_signal(
            barrier,
            inc=1,
            device_id={"dp": other % dp_count, "expert": other // dp_count},
            device_id_type=MESH,
        )

    pl.semaphore_wait(barrier, device_count - 1)


class Column:
    def __init__(self, place, own, slot, send, recv, local):
        self.place, self.own, self.slot = place, own, slot
        self.send, self.recv, self.local = send, recv, local

    def hop(self, z, step, own=False):
        p = self.place
        source = self.own if own else self.slot(z)
        number = z if step > 0 else 4 + z
        target = p.index(p.z + step, p.x, p.c)
        return remote(source, self.slot(z), self.send.at[number], self.recv(z), target, p.side)

    def own_copy(self):
        return pltpu.make_async_copy(self.own, self.slot(self.place.z), self.local)

    def upward(self, act):
        pl.when(self.place.z < 3)(act)

    def downward(self, act):
        pl.when(self.place.z > 0)(act)

    def start(self):
        z = self.place.z
        self.upward(lambda: self.hop(z, 1, True).start())
        self.downward(lambda: self.hop(z, -1, True).start())
        self.own_copy().start()

    def forward(self, low=1, high=4, then=None):
        z = self.place.z

        @pl.loop(low, high)
        def _(away):
            @pl.when(z - away >= 0)
            def _():
                self.hop(z - away, 1).wait_recv()
                self.upward(lambda: self.hop(z - away, 1).start())
                if then is not None:
                    then(z - away)

            @pl.when(z + away <= 3)
            def _():
                self.hop(z + away, -1).wait_recv()
                self.downward(lambda: self.hop(z + away, -1).start())
                if then is not None:
                    then(z + away)

    def finish(self):
        z = self.place.z

        @pl.loop(0, 4)
        def _(origin):
            @pl.when((origin <= z) & (z < 3))
            def _():
                self.hop(origin, 1).wait_send()

            @pl.when((origin >= z) & (z > 0))
            def _():
                self.hop(origin, -1).wait_send()


class Gather:
    def __init__(self, place, own, slot, send, recv, local):
        self.place, self.own, self.slot = place, own, slot
        self.send, self.recv = send, recv
        self.column = Column(
            place,
            own,
            lambda z: slot(place.index(z, place.x, place.c)),
            send,
            lambda z: recv.at[place.index(z, place.x, place.c)],
            local,
        )

    def copy(self, z, x, c, to_x, to_c, number, own=False):
        p = self.place
        shard = p.index(z, x, c)
        source = self.own if own else self.slot(shard)
        target = p.index(p.z, to_x, to_c)
        return remote(
            source, self.slot(shard), self.send.at[number], self.recv.at[shard], target, p.side
        )

    def to_x(self, z, own=False):
        p = self.place
        return self.copy(z, p.x, p.c, 1 - p.x, p.c, 8 + z, own)

    def to_core(self, z, x, own=False):
        p = self.place
        return self.copy(z, x, p.c, p.x, 1 - p.c, 12 + z * 2 + x, own)

    def start(self):
        p = self.place
        self.column.start()
        self.to_x(p.z, True).start()
        self.to_core(p.z, p.x, True).start()

    def forward_z(self):
        def then(z):
            self.to_x(z).start()
            self.to_core(z, self.place.x).start()

        self.column.forward(then=then)

    def forward_x(self):
        p = self.place

        def pass_on(z):
            self.to_core(z, 1 - p.x).wait_recv()
            self.to_core(z, 1 - p.x).start()

        pass_on(p.z)

        @pl.loop(1, 4)
        def _(away):
            pl.when(p.z - away >= 0)(lambda: pass_on(p.z - away))
            pl.when(p.z + away <= 3)(lambda: pass_on(p.z + away))

    def finish(self):
        p = self.place

        @pl.loop(0, 4)
        def _(z):
            for x in range(2):
                self.copy(z, x, 1 - p.c, p.x, 1 - p.c, 12).wait_recv()
                self.to_core(z, x).wait_send()
            self.to_x(z).wait_send()

        self.column.finish()
        self.column.own_copy().wait()


class PlaneSwap:
    def __init__(self, place, source, target, send, recv, local, dp_count):
        self.place, self.source, self.target = place, source, target
        self.send, self.recv, self.local = send, recv, local
        self.dp_count = dp_count

    def of(self, member):
        return member // 4, (member // 2) % 2, member % 2

    def me(self):
        p = self.place
        return p.side * 4 + p.x * 2 + p.c

    def block(self, z, origin):
        return self.target.at[rows_of(z * 8 + origin, SLOTS)]

    def copy(self, z, step, to, origin):
        p = self.place
        side, x, c = self.of(to)
        return remote(
            self.source.at[z, rows_of(to, SLOTS)],
            self.block(z, origin),
            self.send.at[z, step],
            self.recv.at[z, step],
            p.index(p.z, x, c),
            side,
        )

    def own_copy(self, z):
        return pltpu.make_async_copy(
            self.source.at[z, rows_of(self.me(), SLOTS)],
            self.block(z, self.me()),
            self.local.at[z],
        )

    def start(self, z):
        for step in range(1, 8):
            self.copy(z, step, (self.me() + step) % 8, self.me()).start()
        self.own_copy(z).start()

    def arrived(self, z):
        for step in range(1, 8):
            other = (self.me() + 8 - step) % 8
            self.copy(z, step, other, other).wait_recv()
        self.own_copy(z).wait()

    def sent(self):
        @pl.loop(0, 4)
        def _(z):
            for step in range(1, 8):
                self.copy(z, step, (self.me() + step) % 8, self.me()).wait_send()

    def finish(self):
        pl.loop(0, 4)(self.arrived)
        self.sent()


class Chain:
    def __init__(self, place, part, land, send, recv):
        self.place, self.part, self.land = place, part, land
        self.send, self.recv = send, recv

    def hop(self, z, step):
        p = self.place
        if step > 0:
            slot = z
        else:
            slot = z + (4 - z) * ((3 - (p.z - 1 - z)) // 3)
        target = p.index(p.z + step, p.x, p.c)
        return remote(
            self.part.at[z], self.land.at[slot], self.send.at[z], self.recv.at[slot], target, p.side
        )

    def arrived(self, slot, step):
        p = self.place
        target = p.index(p.z + step, p.x, p.c)
        remote(
            self.part.at[0], self.land.at[slot], self.send.at[0], self.recv.at[slot], target, p.side
        ).wait_recv()

    def take(self, z, step):
        self.arrived(z, step)
        add_rows(self.part.at[z], self.land.at[z], 0, self.part.shape[1])

    def run(self, number):
        here = self.place.z
        up, down = 3 - number, number

        @pl.when(up > here)
        def _():
            pl.when(here > 0)(lambda: self.take(up, -1))
            self.hop(up, 1).start()

        @pl.when(down < here)
        def _():
            pl.when(here < 3)(lambda: self.take(down, 1))
            self.hop(down, -1).start()

    def finish(self, out):
        here = self.place.z
        chunk = 16

        def take(slot, step):
            self.arrived(slot, step)

            @pl.loop(0, out.shape[0] // chunk)
            def _(index):
                cut = rows_of(index, chunk)
                out[cut] += self.land[slot, cut].astype(jnp.float32)

        @pl.loop(0, out.shape[0] // chunk)
        def _(index):
            cut = rows_of(index, chunk)
            out[cut] = self.part[here, cut].astype(jnp.float32)

        pl.when(here > 0)(lambda: take(here, -1))
        pl.when(here < 3)(lambda: take(4, 1))

        @pl.loop(0, 4)
        def _(z):
            pl.when(z > here)(lambda: self.hop(z, 1).wait_send())
            pl.when(z < here)(lambda: self.hop(z, -1).wait_send())


class WeightSwap:
    def __init__(self, place, pairs, send, recv, local, dp_count):
        self.place, self.pairs = place, pairs
        self.send, self.recv, self.local = send, recv, local
        self.dp_count = dp_count

    def copies(self, step, to, landing):
        out = []
        for i, (source, target) in enumerate(self.pairs):
            rows = source.shape[1]
            out.append(
                remote(
                    source.at[to],
                    target.at[pl.ds(pl.multiple_of(landing * rows, rows), rows)],
                    self.send.at[step, i],
                    self.recv.at[step, i],
                    to,
                    self.place.side,
                )
            )
        return out

    def own_copies(self):
        dp = self.place.dp
        return [
            pltpu.make_async_copy(
                source.at[dp],
                target.at[pl.ds(pl.multiple_of(dp * source.shape[1], source.shape[1]), source.shape[1])],
                self.local.at[i],
            )
            for i, (source, target) in enumerate(self.pairs)
        ]

    def start(self, low, high):
        @pl.loop(low, high)
        def _(step):
            for copy in self.copies(step, (self.place.dp + step) % self.dp_count, self.place.dp):
                copy.start()

    def start_own(self):
        for copy in self.own_copies():
            copy.start()

    def finish(self):
        @pl.loop(1, self.dp_count)
        def _(step):
            other = (self.place.dp + self.dp_count - step) % self.dp_count
            for copy in self.copies(step, other, other):
                copy.wait()

        for copy in self.own_copies():
            copy.wait()


def columns(tile, width=TILE):
    return pl.ds(pl.multiple_of(tile * width, width), width)


def rows_of(index, count):
    return pl.ds(pl.multiple_of(index * count, count), count)


def slot_labels(place, dp_count):
    row = lax.broadcasted_iota(jnp.int32, (8 * SLOTS, TILE), 0)
    member = row // SLOTS
    label = ((member // 4) * dp_count + place.z * 4 + member % 4) * SLOTS + row % SLOTS
    return label.astype(jnp.float32)


def front_kernel(
    bias_ref,
    tokens_ref,
    cotangent_ref,
    project_ref,
    out_ref,
    target_ref,
    route_ref,
    cosine_ref,
    sine_ref,
    gate_ref,
    up_ref,
    down_ref,
    project_full,
    out_full,
    keys_ref,
    query_ref,
    attended_ref,
    exact_ref,
    stat_ref,
    middle_ref,
    hidden_ref,
    probs_ref,
    rows_in,
    grads_in,
    gate_own,
    up_own,
    down_own,
    hidden_one,
    target_all,
    gate_all,
    keys_own,
    row_send,
    grad_send,
    gate_own_row,
    hidden_all,
    grad_all,
    placed,
    acc,
    top,
    project_send,
    project_recv,
    out_send,
    out_recv,
    keys_send,
    keys_recv,
    row_send_sem,
    row_recv_sem,
    row_local,
    grad_send_sem,
    grad_recv_sem,
    grad_local,
    column_send,
    column_recv,
    weight_send,
    weight_recv,
    weight_local,
    local,
):
    dp_count = keys_ref.shape[0]
    device_count = rows_in.shape[0] // SLOTS
    tok_count, model_width = tokens_ref.shape
    query_width = HEADS * HEAD
    key_width = KV_HEADS * HEAD
    repeat_heads = HEADS // KV_HEADS
    factor = log2e * HEAD ** (-0.5)
    place = Place()
    shard_rows = project_ref.shape[0]

    def shard_of(full):
        return lambda index: full.at[rows_of(index, shard_rows)]

    project = Gather(
        place, project_ref, shard_of(project_full), project_send, project_recv, local.at[0]
    )
    out = Gather(place, out_ref, shard_of(out_full), out_send, out_recv, local.at[1])
    keys = Gather(
        place, keys_own, lambda index: keys_ref.at[index], keys_send, keys_recv, local.at[2]
    )
    rows = PlaneSwap(place, row_send, rows_in, row_send_sem, row_recv_sem, row_local, dp_count)
    grads = PlaneSwap(place, grad_send, grads_in, grad_send_sem, grad_recv_sem, grad_local, dp_count)

    def column(number, own, land):
        return Column(
            place,
            own,
            land,
            column_send.at[number],
            lambda z: column_recv.at[number, z],
            local.at[3 + number],
        )

    targets = column(0, target_ref, lambda z: target_all.at[z])
    gates = column(1, gate_own_row, lambda z: gate_all.at[z])
    hidden = column(2, hidden_ref, lambda z: hidden_all.at[z, pl.ds(0, tok_count)])
    cotangents = column(3, cotangent_ref, lambda z: grad_all.at[z])
    weights = WeightSwap(
        place,
        ((gate_ref, gate_own), (up_ref, up_own), (down_ref, down_own)),
        weight_send,
        weight_recv,
        weight_local,
        dp_count,
    )

    enter(device_count, dp_count)
    targets.start()
    project.start()
    cotangents.start()
    plane_slots = 8 * SLOTS
    targets.forward()
    targets.own_copy().wait()
    slot_row = lax.broadcasted_iota(jnp.int32, (plane_slots, TILE), 0)
    slot_lane = lax.broadcasted_iota(jnp.int32, (plane_slots, TILE), 1)
    member = slot_row // SLOTS
    label = slot_labels(place, dp_count)
    spare = (slot_lane - tok_count == member) & (slot_row % SLOTS == CAP)

    def match(z, choice):
        return label == target_all[z, choice : choice + 1]

    for z in range(4):
        hit = spare
        for choice in range(TOP):
            hit = hit | match(z, choice)
        placed[z] = jnp.where(hit, 1.0, 0.0).astype(jnp.bfloat16)
    hidden_all[:, tok_count:] = jnp.zeros((4, PAD_TOKENS, model_width), jnp.bfloat16)

    project.forward_z()
    project.forward_x()
    project.finish()
    cotangents.forward(1, 2)

    lanes_of = one_hot((8, LANES), lambda row, column: column == row + EXPERTS)
    gains = dot_f32(lanes_of, project_full[:, query_width + 2 * key_width :], ((1,), (1,)))
    gain_first, gain_second = gains[0:1], gains[1:2]
    chunk = 32

    @pl.loop(0, tok_count // chunk)
    def _(index):
        value = tokens_ref[rows_of(index, chunk)].astype(jnp.float32)
        scale = lax.rsqrt(jnp.mean(value * value, axis=-1, keepdims=True) + epsilon)
        hidden_one[rows_of(index, chunk)] = (value * scale * gain_first).astype(jnp.bfloat16)

    def turned(tile):
        value = dot_f32(hidden_one[...], project_full[:, columns(tile)])
        halves = []
        for half in range(TILE // HEAD):
            part = value[:, half * HEAD : (half + 1) * HEAD]
            halves.append(
                part * cosine_ref[...] + pltpu.roll(part, HEAD // 2, 1) * sine_ref[...]
            )
        return jnp.concatenate(halves, axis=1).astype(jnp.bfloat16)

    keys_own[:, :key_width] = turned(query_width // TILE)
    keys_own[:, key_width:] = dot_f32(
        hidden_one[...], project_full[:, query_width + key_width : query_width + 2 * key_width]
    ).astype(jnp.bfloat16)
    keys.start()

    @pl.loop(0, query_width // TILE)
    def _(tile):
        query_ref[:, columns(tile)] = turned(tile)

    keys.forward_z()
    keys.forward_x()
    keys.finish()
    out.start()
    cotangents.forward(2, 4)
    weights.start(1, dp_count)
    weights.start_own()

    row = lax.broadcasted_iota(jnp.int32, (tok_count, tok_count), 0)
    column_index = lax.broadcasted_iota(jnp.int32, (tok_count, tok_count), 1)
    causal = column_index <= row
    ones = jnp.ones((tok_count, LANES), jnp.bfloat16)

    def visit(label, own):
        for group in range(KV_HEADS):
            key = keys_ref[label, :, group * HEAD : (group + 1) * HEAD]
            value = keys_ref[label, :, (KV_HEADS + group) * HEAD : (KV_HEADS + group + 1) * HEAD]
            value = jnp.concatenate([value, ones], axis=1)
            for head in range(group * repeat_heads, (group + 1) * repeat_heads):
                query = query_ref[:, head * HEAD : (head + 1) * HEAD]
                scores = dot_f32(query, key, ((1,), (1,))) * factor
                if own:
                    scores = jnp.where(causal, scores, -1e30)
                    peak = jnp.ceil(jnp.max(scores, axis=-1, keepdims=True))
                    shift = peak
                else:
                    bias = bias_ref[label]
                    peak = jnp.ceil(
                        jnp.maximum(top[head], jnp.max(scores, axis=-1, keepdims=True) + bias)
                    )
                    shift = peak - bias
                prob = jnp.exp2(scores - shift).astype(jnp.bfloat16)
                part = dot_f32(prob, value)
                if own:
                    acc[head] = part
                else:
                    acc[head] = acc[head] * jnp.exp2(top[head] - peak) + part
                top[head] = peak

    visit(place.dp, True)

    @pl.loop(0, place.dp)
    def _(label):
        visit(label, False)

    out.forward_z()
    out.forward_x()
    cotangents.own_copy().wait()

    @pl.loop(0, 4)
    def _(z):
        @pl.loop(0, model_width // TILE)
        def _(tile):
            grad_send[z, :, columns(tile)] = dot_f32(
                placed[z, :, :tok_count], grad_all[z, :, columns(tile)]
            ).astype(jnp.bfloat16)

        grads.start(z)

    lane = lax.broadcasted_iota(jnp.int32, (tok_count, LANES), 1)
    stats = jnp.zeros((tok_count, LANES), jnp.float32)
    for head in range(HEADS):
        exact = acc[head, :, :HEAD] / acc[head, :, HEAD:]
        exact_ref[:, head * HEAD : (head + 1) * HEAD] = exact
        attended_ref[:, head * HEAD : (head + 1) * HEAD] = exact.astype(jnp.bfloat16)
        stats = jnp.where(lane == head, top[head], stats)
        stats = jnp.where(lane == HEADS + head, 1.0 / acc[head, :, HEAD:], stats)
    stat_ref[...] = stats
    out.finish()

    @pl.loop(0, model_width // TILE)
    def _(tile):
        middle_ref[:, columns(tile)] = tokens_ref[:, columns(tile)].astype(jnp.float32) + dot_f32(
            attended_ref[...], out_full[:, columns(tile)]
        )

    @pl.loop(0, tok_count // chunk)
    def _(index):
        value = middle_ref[rows_of(index, chunk)]
        scale = lax.rsqrt(jnp.mean(value * value, axis=-1, keepdims=True) + epsilon)
        hidden_ref[rows_of(index, chunk)] = (value * scale * gain_second).astype(jnp.bfloat16)

    hidden.start()
    router = project_full[:, query_width + 2 * key_width :]
    chosen = [route_ref[:, choice : choice + 1] == lane for choice in range(TOP)]
    mask = chosen[0]
    for choice in range(1, TOP):
        mask = mask | chosen[choice]
    logits = jnp.where(mask, dot_f32(hidden_ref[...], router), -1e30)
    weight = jnp.exp(logits - jnp.max(logits, axis=-1, keepdims=True))
    probs = weight / jnp.sum(weight, axis=-1, keepdims=True)
    probs_ref[...] = probs
    by_choice = jnp.zeros((tok_count, LANES), jnp.float32)
    for choice in range(TOP):
        gate = jnp.sum(jnp.where(chosen[choice], probs, 0.0), axis=-1, keepdims=True)
        by_choice = jnp.where(lane == choice, gate, by_choice)
    first_lanes = one_hot((8, LANES), lambda r, col: r == col)
    gate_own_row[...] = jnp.zeros(gate_own_row.shape, jnp.float32)
    gate_own_row[:, :tok_count] = sum(
        dot_f32(first_lanes, part, ((1,), (1,))) for part in split3(by_choice)
    )
    gates.start()
    fold = one_hot((8, plane_slots), lambda r, col: col // SLOTS == r)
    def dispatch(z):
        gate = jnp.zeros((plane_slots, 1), jnp.float32)
        for choice in range(TOP):
            gate += jnp.sum(
                jnp.where(match(z, choice), gate_all[z, choice : choice + 1], 0.0),
                axis=-1,
                keepdims=True,
            )
        numbers = dot_f32(fold, put_parts(gate)).astype(jnp.bfloat16)
        numbers = jnp.concatenate([numbers, jnp.zeros((8, LANES), jnp.bfloat16)], axis=0)
        hidden_all[z, tok_count : tok_count + 16, :LANES] = numbers

        @pl.loop(0, model_width // TILE)
        def _(tile):
            row_send[z, :, columns(tile)] = dot_f32(
                placed[z], hidden_all[z, :, columns(tile)]
            ).astype(jnp.bfloat16)

        rows.start(z)
    hidden.own_copy().wait()
    gates.own_copy().wait()
    dispatch(place.z)
    gates.forward()
    hidden.forward(then=dispatch)
    for gather in (targets, cotangents, hidden, gates):
        gather.finish()
    weights.finish()
    grads.finish()
    rows.finish()


def front(bias, tokens, cotangent, project, out, target, route, cosine, sine, gate, up, down):
    dp_count = lax.axis_size("dp")
    device_count = dp_count * lax.axis_size("expert")
    tok_count, model_width = tokens.shape
    query_width = HEADS * HEAD
    key_width = KV_HEADS * HEAD
    vmem = pl.BlockSpec(memory_space=pltpu.VMEM)
    anywhere = pl.BlockSpec(memory_space=pl.ANY)
    slots = device_count * SLOTS
    low, full = jnp.bfloat16, jnp.float32
    shape = jax.ShapeDtypeStruct
    ff_width = gate.shape[2]
    outs = (
        (shape((model_width, project.shape[1]), low), vmem),
        (shape((model_width, model_width), low), vmem),
        (shape((dp_count, tok_count, 2 * key_width), low), vmem),
        (shape((tok_count, query_width), low), vmem),
        (shape((tok_count, query_width), low), vmem),
        (shape((tok_count, query_width), full), vmem),
        (shape((tok_count, LANES), full), vmem),
        (shape((tok_count, model_width), full), vmem),
        (shape((tok_count, model_width), low), vmem),
        (shape((tok_count, LANES), full), vmem),
        (shape((slots, model_width), low), anywhere),
        (shape((slots, model_width), low), anywhere),
        (shape((model_width, ff_width), low), anywhere),
        (shape((model_width, ff_width), low), anywhere),
        (shape((ff_width, model_width), low), anywhere),
        (shape((tok_count, model_width), low), vmem),
        (shape((4, 8, TILE), full), vmem),
        (shape((4, 8, TILE), full), vmem),
    )
    dma = pltpu.SemaphoreType.DMA
    return pl.pallas_call(
        front_kernel,
        out_shape=tuple(o[0] for o in outs),
        in_specs=[pl.BlockSpec(memory_space=pltpu.SMEM)] + [vmem] * 8 + [anywhere] * 3,
        out_specs=tuple(o[1] for o in outs),
        scratch_shapes=[
            pltpu.VMEM((tok_count, 2 * key_width), low),
            pltpu.VMEM((4, 8 * SLOTS, model_width), low),
            pltpu.VMEM((4, 8 * SLOTS, model_width), low),
            pltpu.VMEM((8, TILE), full),
            pltpu.VMEM((4, tok_count + PAD_TOKENS, model_width), low),
            pltpu.VMEM((4, tok_count, model_width), low),
            pltpu.VMEM((4, 8 * SLOTS, TILE), low),
            pltpu.VMEM((HEADS, tok_count, 2 * HEAD), full),
            pltpu.VMEM((HEADS, tok_count, 1), full),
        ]
        + [dma((20,)), dma((dp_count,))] * 3
        + [dma((4, 8)), dma((4, 8)), dma((4,))] * 2
        + [dma((4, 8)), dma((4, 4))]
        + [dma((dp_count, 3))] * 2
        + [dma((3,)), dma((7,))],
        compiler_params=pltpu.CompilerParams(
            collective_id=0, has_side_effects=True, vmem_limit_bytes=58 * 1024 * 1024
        ),
    )(bias, tokens, cotangent, project, out, target, route, cosine, sine, gate, up, down)


def pick_gates(block):
    rows = block.shape[0]
    blocks = rows // SLOTS
    spare = one_hot((blocks, rows), lambda r, col: col == r * SLOTS + CAP)
    member = one_hot((rows, blocks), lambda r, col: r // SLOTS == col)
    parts = dot_f32(member, dot_f32(spare, block).astype(jnp.bfloat16))
    row = lax.broadcasted_iota(jnp.int32, parts.shape, 0)
    lane = lax.broadcasted_iota(jnp.int32, parts.shape, 1)
    mine = (lane % SLOTS == row % SLOTS) & (lane < 3 * SLOTS)
    return jnp.sum(jnp.where(mine, parts, 0.0), axis=-1, keepdims=True)


def put_parts(column):
    shape = (column.shape[0], LANES)
    row = lax.broadcasted_iota(jnp.int32, shape, 0)
    lane = lax.broadcasted_iota(jnp.int32, shape, 1)
    high, mid, low = (part.astype(jnp.float32) for part in split3(column))
    part = jnp.where(lane < SLOTS, high, jnp.where(lane < 2 * SLOTS, mid, low))
    mine = (lane % SLOTS == row % SLOTS) & (lane < 3 * SLOTS)
    return jnp.where(mine, part, 0.0).astype(jnp.bfloat16)


def expert_kernel(
    rows_ref,
    grads_ref,
    gate_ref,
    up_ref,
    down_ref,
    target_all,
    gate_all,
    row_sum,
    out_sum,
    gate_sum,
    gate_grad_ref,
    up_grad_ref,
    down_grad_ref,
    row_send,
    row_plane,
    row_part,
    row_land,
    out_send,
    out_plane,
    out_part,
    out_land,
    gate_part,
    gate_land,
    grad_out,
    inner_ref,
    gate_act_grad,
    up_act_grad,
    row_send_sem,
    row_recv_sem,
    row_local,
    out_send_sem,
    out_recv_sem,
    out_local,
    row_chain_send,
    row_chain_recv,
    out_chain_send,
    out_chain_recv,
    gate_send_sem,
    gate_recv_sem,
):
    dp_count = lax.axis_size("dp")
    slots, model_width = rows_ref.shape
    ff_width = gate_ref.shape[1]
    tok_count = row_sum.shape[0]
    device_count = slots // SLOTS
    place = Place()
    enter(device_count, dp_count)
    rows = PlaneSwap(place, row_send, row_plane, row_send_sem, row_recv_sem, row_local, dp_count)
    outs = PlaneSwap(place, out_send, out_plane, out_send_sem, out_recv_sem, out_local, dp_count)
    row_chain = Chain(place, row_part, row_land, row_chain_send, row_chain_recv)
    out_chain = Chain(place, out_part, out_land, out_chain_send, out_chain_recv)

    digits = 27 + 72 * place.z - 15 * (place.z // 2)

    def level(step):
        power = 1 + 3 * step + 9 * (step * (step - 1) // 2)
        power += 27 * (step * (step - 1) * (step - 2) // 6)
        return (digits // power) % 4

    @pl.loop(0, 4)
    def _(step):
        tile = level(step)
        cut = rows_of(tile, TILE)
        row = rows_ref[cut]
        gate = pick_gates(row[:, :LANES])
        saved = []
        for n in range(ff_width // TILE):
            part = slice(n * TILE, (n + 1) * TILE)
            gate_act = dot_f32(row, gate_ref[:, part])
            up_act = dot_f32(row, up_ref[:, part])
            sigmoid = 1.0 / (1.0 + jnp.exp(-gate_act))
            swish = gate_act * sigmoid
            inner_ref[cut, part] = (swish * up_act).astype(jnp.bfloat16)
            saved.append((swish, up_act * (sigmoid * (1.0 + gate_act * (1.0 - sigmoid)))))
        inner = inner_ref[cut]
        gate_grad = jnp.zeros((TILE, 1), jnp.float32)
        for n in range(model_width // TILE):
            part = slice(n * TILE, (n + 1) * TILE)
            expert_out = dot_f32(inner, down_ref[:, part]).astype(jnp.bfloat16)
            out_send[tile, :, part] = expert_out
            grad = grads_ref[cut, part].astype(jnp.float32)
            gate_grad += jnp.sum(expert_out.astype(jnp.float32) * grad, axis=-1, keepdims=True)
            grad_out[cut, part] = (gate * grad).astype(jnp.bfloat16)
        grad = grad_out[cut]
        for n in range(ff_width // TILE):
            part = slice(n * TILE, (n + 1) * TILE)
            swish, slope = saved[n]
            grad_inner = dot_f32(grad, down_ref[part, :], ((1,), (1,)))
            gate_act_grad[cut, part] = (grad_inner * slope).astype(jnp.bfloat16)
            up_act_grad[cut, part] = (grad_inner * swish).astype(jnp.bfloat16)
        blocks = TILE // SLOTS
        fold = one_hot((blocks, TILE), lambda r, col: col // SLOTS == r)
        spread = one_hot((TILE, blocks), lambda r, col: r == col * SLOTS + CAP)
        extra = dot_f32(spread, dot_f32(fold, put_parts(gate_grad)).astype(jnp.bfloat16))
        for n in range(model_width // TILE):
            part = slice(n * TILE, (n + 1) * TILE)
            back = dot_f32(gate_act_grad[cut], gate_ref[part, :], ((1,), (1,))) + dot_f32(
                up_act_grad[cut], up_ref[part, :], ((1,), (1,))
            )
            row_send[tile, :, part] = back.astype(jnp.bfloat16)
            if n == 0:
                row_send[tile, :, :LANES] = (back[:, :LANES] + extra).astype(jnp.bfloat16)
        rows.start(tile)

    @pl.loop(0, 4)
    def _(step):
        outs.start(level(step))

    label = slot_labels(place, dp_count)
    shape = (8 * SLOTS, LANES)
    member = lax.broadcasted_iota(jnp.int32, shape, 0) // SLOTS
    lane = lax.broadcasted_iota(jnp.int32, shape, 1)
    expert = (member // 4) * dp_count + place.z * 4 + member % 4

    def match(z, choice):
        return label == target_all[z, choice : choice + 1]

    def row_partial(step):
        z = level(step)
        rows.arrived(z)
        hit = match(z, 0)
        for choice in range(1, TOP):
            hit = hit | match(z, choice)
        placed = jnp.where(hit, 1.0, 0.0).astype(jnp.bfloat16)
        cut = rows_of(z, TILE)
        numbers = jnp.where(lane == expert, pick_gates(row_plane[cut, :LANES]), 0.0)
        gate_part[z] = sum(dot_f32(placed, part, ((0,), (0,))) for part in split3(numbers))[
            :tok_count
        ]
        for n in range(model_width // TILE):
            part = slice(n * TILE, (n + 1) * TILE)
            row_part[z, :, part] = dot_f32(placed, row_plane[cut, part], ((0,), (0,)))[
                :tok_count
            ].astype(jnp.bfloat16)

    row_partial(0)
    row_partial(1)
    row_chain.run(0)
    row_partial(2)
    row_chain.run(1)
    row_partial(3)
    row_chain.run(2)

    def gate_hop(i):
        z = place.others()[i]
        target = place.index(z, place.x, place.c)
        return remote(
            gate_part.at[z],
            gate_land.at[i],
            gate_send_sem.at[i],
            gate_recv_sem.at[i],
            target,
            place.side,
        )

    for i in range(3):
        gate_hop(i).start()

    def out_partial(step):
        z = level(step)
        outs.arrived(z)
        gates = jnp.zeros((8 * SLOTS, TILE), jnp.float32)
        for choice in range(TOP):
            gates += jnp.where(match(z, choice), gate_all[z, choice : choice + 1], 0.0)
        high = gates.astype(jnp.bfloat16)
        low = (gates - high.astype(jnp.float32)).astype(jnp.bfloat16)
        cut = rows_of(z, TILE)
        for n in range(model_width // TILE):
            part = slice(n * TILE, (n + 1) * TILE)
            out = out_plane[cut, part]
            value = dot_f32(high, out, ((0,), (0,))) + dot_f32(low, out, ((0,), (0,)))
            out_part[z, :, part] = value[:tok_count].astype(jnp.bfloat16)

    def weight_grad(target, act):
        @pl.loop(0, model_width // TILE)
        def _(tile):
            target[rows_of(tile, TILE)] = dot_f32(
                rows_ref[:, columns(tile)], act[...], ((0,), (0,))
            ).astype(jnp.bfloat16)

    out_partial(0)
    out_partial(1)
    out_chain.run(0)
    weight_grad(gate_grad_ref, gate_act_grad)
    out_partial(2)
    out_chain.run(1)
    weight_grad(up_grad_ref, up_act_grad)
    out_partial(3)
    out_chain.run(2)

    @pl.loop(0, ff_width // TILE)
    def _(tile):
        inner = inner_ref[:, columns(tile)]
        for n in range(model_width // ff_width):
            part = slice(n * ff_width, (n + 1) * ff_width)
            down_grad_ref[rows_of(tile, TILE), part] = dot_f32(
                inner, grad_out[:, part], ((0,), (0,))
            ).astype(jnp.bfloat16)

    row_chain.finish(row_sum)
    gate_sum[...] = gate_part[place.z]
    for i in range(3):
        gate_hop(i).wait()
        gate_sum[...] += gate_land[i]
    out_chain.finish(out_sum)
    rows.sent()
    outs.sent()


def experts(rows, grads, gate, up, down, target, gates, tok_count):
    slots, model_width = rows.shape
    ff_width = gate.shape[1]
    vmem = pl.BlockSpec(memory_space=pltpu.VMEM)
    low, full = jnp.bfloat16, jnp.float32
    shape = jax.ShapeDtypeStruct
    dma = pltpu.SemaphoreType.DMA
    return pl.pallas_call(
        expert_kernel,
        out_shape=(
            shape((tok_count, model_width), full),
            shape((tok_count, model_width), full),
            shape((tok_count, LANES), full),
            shape((model_width, ff_width), low),
            shape((model_width, ff_width), low),
            shape((ff_width, model_width), low),
        ),
        in_specs=[vmem] * 7,
        out_specs=(vmem,) * 6,
        scratch_shapes=[
            pltpu.VMEM((4, 8 * SLOTS, model_width), low),
            pltpu.VMEM((slots, model_width), low),
            pltpu.VMEM((4, tok_count, model_width), low),
            pltpu.VMEM((5, tok_count, model_width), low),
        ]
        * 2
        + [
            pltpu.VMEM((4, tok_count, LANES), full),
            pltpu.VMEM((3, tok_count, LANES), full),
            pltpu.VMEM((slots, model_width), low),
            pltpu.VMEM((slots, ff_width), low),
            pltpu.VMEM((slots, ff_width), low),
            pltpu.VMEM((slots, ff_width), low),
        ]
        + [dma((4, 8)), dma((4, 8)), dma((4,))] * 2
        + [dma((4,)), dma((5,))] * 2
        + [dma((3,))] * 2,
        compiler_params=pltpu.CompilerParams(
            collective_id=1, has_side_effects=True, vmem_limit_bytes=60 * 1024 * 1024
        ),
    )(rows, grads, gate, up, down, target, gates)


def halves_turned(value, cosine, sine):
    parts = []
    for half in range(value.shape[1] // HEAD):
        part = value[:, half * HEAD : (half + 1) * HEAD]
        parts.append(part * cosine + pltpu.roll(part, HEAD // 2, 1) * sine)
    return jnp.concatenate(parts, axis=1)


def gain_rows(small):
    lanes_of = one_hot((8, LANES), lambda row, column: column == row + EXPERTS)
    return dot_f32(lanes_of, small, ((1,), (1,)))


class Scatter:
    def __init__(self, place, block, lands, send, recvs):
        self.place, self.block = place, block
        self.lands, self.send, self.recvs = lands, send, recvs

    def hop_core(self, z, x):
        p = self.place
        number = z * 2 + x
        return remote(
            self.block(p.index(z, x, 1 - p.c)),
            self.lands[0].at[number],
            self.send.at[number],
            self.recvs[0].at[number],
            p.index(p.z, p.x, 1 - p.c),
            p.side,
        )

    def hop_x(self, z):
        p = self.place
        return remote(
            self.block(p.index(z, 1 - p.x, p.c)),
            self.lands[1].at[z],
            self.send.at[8 + z],
            self.recvs[1].at[z],
            p.index(p.z, 1 - p.x, p.c),
            p.side,
        )

    def hop_z(self, i):
        p = self.place
        z = p.others()[i]
        return remote(
            self.block(p.index(z, p.x, p.c)),
            self.lands[2].at[i],
            self.send.at[12 + i],
            self.recvs[2].at[i],
            p.index(z, p.x, p.c),
            p.side,
        )

    def add(self, shard, land):
        block = self.block(shard)
        chunk = 32

        @pl.loop(0, block.shape[0] // chunk)
        def _(index):
            cut = rows_of(index, chunk)
            block[cut] = (block[cut].astype(jnp.float32) + land[cut].astype(jnp.float32)).astype(
                jnp.bfloat16
            )

    def start(self):
        for z in range(4):
            for x in range(2):
                self.hop_core(z, x).start()

    def order(self):
        return self.place.others() + [self.place.z]

    def pass_core(self):
        p = self.place
        for z in self.order():
            for x in (1 - p.x, p.x):
                self.hop_core(z, x).wait_recv()
                self.add(p.index(z, x, p.c), self.lands[0].at[z * 2 + x])
            self.hop_x(z).start()

    def pass_x(self):
        p = self.place
        for i, z in enumerate(self.order()):
            self.hop_x(z).wait_recv()
            self.add(p.index(z, p.x, p.c), self.lands[1].at[z])
            if i < 3:
                self.hop_z(i).start()

    def pass_z(self, put):
        p = self.place
        for i in range(3):
            self.hop_z(i).wait_recv()
        block = self.block(p.dp)
        chunk = 32

        @pl.loop(0, block.shape[0] // chunk)
        def _(index):
            cut = rows_of(index, chunk)
            value = block[cut].astype(jnp.float32)
            for i in range(3):
                value += self.lands[2][i, cut].astype(jnp.float32)
            put(cut, value)

    def finish(self):
        for z in range(4):
            for x in range(2):
                self.hop_core(z, x).wait_send()
            self.hop_x(z).wait_send()
        for i in range(3):
            self.hop_z(i).wait_send()


def add_rows(block, land, low, count):
    chunk = 16

    @pl.loop(0, count // chunk)
    def _(index):
        cut = pl.ds(pl.multiple_of(low + index * chunk, chunk), chunk)
        value = block[cut].astype(jnp.float32) + land[rows_of(index, chunk)].astype(jnp.float32)
        block[cut] = value.astype(jnp.bfloat16)


class TotalSum:
    def __init__(self, place, part, lands, send, recv, x_first):
        self.place, self.part, self.lands = place, part, lands
        self.send, self.recv, self.x_first = send, recv, x_first
        self.rows = part.shape[1]
        self.half = self.rows // 2

    def kept(self, side):
        return pl.ds(pl.multiple_of(side * self.half, self.half), self.half)

    def hop(self, source, land, number, dp, side):
        return remote(source, land, self.send.at[number], self.recv.at[number], dp, side)

    def core(self, z, x):
        p = self.place
        return self.hop(
            self.part.at[p.index(z, x, 1 - p.c)],
            self.lands[0].at[z * 2 + x],
            z * 2 + x,
            p.index(p.z, p.x, 1 - p.c),
            p.side,
        )

    def over_x(self, z):
        p = self.place
        source = self.part.at[p.index(z, 1 - p.x, p.c)]
        if not self.x_first:
            source = source.at[self.kept(p.side)]
        return self.hop(source, self.lands[1].at[z], 8 + z, p.index(p.z, 1 - p.x, p.c), p.side)

    def over_side(self, z, x):
        p = self.place
        number = z if self.x_first else z * 2 + x
        return self.hop(
            self.part.at[p.index(z, x, p.c), self.kept(1 - p.side)],
            self.lands[2].at[number],
            12 + number,
            p.dp,
            1 - p.side,
        )

    def over_z(self, i):
        p = self.place
        z = p.others()[i]
        return self.hop(
            self.part.at[p.index(z, p.x, p.c), self.kept(p.side)],
            self.lands[3].at[i],
            20 + i,
            p.index(z, p.x, p.c),
            p.side,
        )

    def home(self):
        p = self.place
        block = self.part.at[p.dp, self.kept(p.side)]
        return self.hop(block, self.lands[4], 23, p.dp, 1 - p.side)

    def start(self, z):
        for x in range(2):
            self.core(z, x).start()

    def sides(self):
        return (self.place.x,) if self.x_first else (1 - self.place.x, self.place.x)

    def first(self, z):
        p = self.place
        for x in (1 - p.x, p.x):
            self.core(z, x).wait_recv()
            add_rows(self.part.at[p.index(z, x, p.c)], self.lands[0].at[z * 2 + x], 0, self.rows)
            if not self.x_first:
                self.over_side(z, x).start()
        if self.x_first:
            self.over_x(z).start()

    def take_side(self, z):
        p = self.place
        for x in self.sides():
            self.over_side(z, x).wait_recv()
            number = z if self.x_first else z * 2 + x
            add_rows(
                self.part.at[p.index(z, x, p.c)],
                self.lands[2].at[number],
                p.side * self.half,
                self.half,
            )

    def take_x(self, z):
        p = self.place
        self.over_x(z).wait_recv()
        low, count = (0, self.rows) if self.x_first else (p.side * self.half, self.half)
        add_rows(self.part.at[p.index(z, p.x, p.c)], self.lands[1].at[z], low, count)

    def second(self, z):
        if self.x_first:
            self.take_x(z)
            self.over_side(z, self.place.x).start()
        else:
            self.take_side(z)
            self.over_x(z).start()

    def third(self, z, i):
        if self.x_first:
            self.take_side(z)
        else:
            self.take_x(z)
        if i < 3:
            self.over_z(i).start()

    def fourth(self):
        p = self.place
        for i in range(3):
            self.over_z(i).wait_recv()
        chunk = 16

        @pl.loop(0, self.half // chunk)
        def _(index):
            cut = pl.ds(pl.multiple_of(p.side * self.half + index * chunk, chunk), chunk)
            value = self.part[p.dp, cut].astype(jnp.float32)
            for i in range(3):
                value += self.lands[3][i, rows_of(index, chunk)].astype(jnp.float32)
            self.part[p.dp, cut] = value.astype(jnp.bfloat16)

        self.home().start()

    def finish(self, mine, at):
        p = self.place
        mine[self.kept(p.side), at] = self.part[p.dp, self.kept(p.side)].astype(jnp.float32)
        self.home().wait()
        mine[self.kept(1 - p.side), at] = self.lands[4][...].astype(jnp.float32)
        for z in range(4):
            for x in range(2):
                self.core(z, x).wait_send()
            self.over_x(z).wait_send()
            for x in self.sides():
                self.over_side(z, x).wait_send()
        for i in range(3):
            self.over_z(i).wait_send()


class WeightReturn(WeightSwap):
    def copies(self, step, to, landing):
        out = []
        for i, (source, target) in enumerate(self.pairs):
            rows = target.shape[1]
            out.append(
                remote(
                    source.at[rows_of(to, rows)],
                    target.at[landing],
                    self.send.at[step, i],
                    self.recv.at[step, i],
                    to,
                    self.place.side,
                )
            )
        return out

    def own_copies(self):
        dp = self.place.dp
        return [
            pltpu.make_async_copy(
                source.at[rows_of(dp, target.shape[1])], target.at[dp], self.local.at[i]
            )
            for i, (source, target) in enumerate(self.pairs)
        ]


def back_kernel(
    bias_ref,
    cotangent_ref,
    middle_ref,
    probs_ref,
    exact_ref,
    stat_ref,
    query_ref,
    keys_ref,
    small_ref,
    out_ref,
    row_sum,
    out_sum,
    gate_sum,
    cosine_ref,
    sine_ref,
    gate_ref,
    up_ref,
    result_ref,
    grad_middle_ref,
    grad_branch_ref,
    grad_logits_ref,
    grad_project_ref,
    gain_ref,
    gate_back,
    up_back,
    grad_hidden,
    grad_ref,
    acc,
    delta,
    grad_keys_ref,
    land_core,
    land_x,
    land_z,
    scatter_send,
    recv_core,
    recv_x,
    recv_z,
    weight_send,
    weight_recv,
    weight_local,
):
    dp_count = keys_ref.shape[0]
    device_count = dp_count * lax.axis_size("expert")
    tok_count, model_width = middle_ref.shape
    query_width = HEADS * HEAD
    key_width = KV_HEADS * HEAD
    repeat_heads = HEADS // KV_HEADS
    scale = HEAD ** (-0.5)
    factor = log2e * scale
    chunk = 32
    place = Place()
    enter(device_count, dp_count)
    weights = WeightReturn(
        place,
        ((gate_ref, gate_back), (up_ref, up_back)),
        weight_send,
        weight_recv,
        weight_local,
        dp_count,
    )
    weights.start(1, dp_count)
    weights.start_own()
    scatter = Scatter(
        place,
        lambda index: grad_keys_ref.at[index],
        (land_core, land_x, land_z),
        scatter_send,
        (recv_core, recv_x, recv_z),
    )

    probs = probs_ref[...]
    grad_probs = gate_sum[...]
    grad_logits = (
        probs * (grad_probs - jnp.sum(probs * grad_probs, axis=-1, keepdims=True))
    ).astype(jnp.bfloat16)
    grad_logits_ref[...] = grad_logits

    @pl.loop(0, model_width // TILE)
    def _(tile):
        grad_hidden[:, columns(tile)] = row_sum[:, columns(tile)] + dot_f32(
            grad_logits_ref[...], small_ref[rows_of(tile, TILE)], ((1,), (1,))
        )

    gain = gain_rows(small_ref[...])[1:2]
    gain_ref[...] = jnp.zeros(gain_ref.shape, jnp.float32)

    @pl.loop(0, tok_count // chunk)
    def _(index):
        cut = rows_of(index, chunk)
        value = middle_ref[cut]
        row_scale = lax.rsqrt(jnp.mean(value * value, axis=-1, keepdims=True) + epsilon)
        normed = value * row_scale
        grad = grad_hidden[cut]
        gain_ref[0:1] += jnp.sum(grad * normed, axis=0, keepdims=True)
        grad = grad * gain
        total = cotangent_ref[cut].astype(jnp.float32) + row_scale * (
            grad - normed * jnp.mean(grad * normed, axis=-1, keepdims=True)
        )
        grad_middle_ref[cut] = total
        grad_branch_ref[cut] = total.astype(jnp.bfloat16)

    @pl.loop(0, model_width // TILE)
    def _(tile):
        grad_ref[:, columns(tile)] = dot_f32(
            grad_branch_ref[...], out_ref[rows_of(tile, TILE)], ((1,), (1,))
        ).astype(jnp.bfloat16)

    for head in range(HEADS):
        cut = slice(head * HEAD, (head + 1) * HEAD)
        scaled = (
            grad_ref[:, cut].astype(jnp.float32) * stat_ref[:, HEADS + head : HEADS + head + 1]
        ).astype(jnp.bfloat16)
        grad_ref[:, cut] = scaled
        delta[head] = jnp.sum(
            scaled.astype(jnp.float32) * exact_ref[:, cut], axis=-1, keepdims=True
        )
    row = lax.broadcasted_iota(jnp.int32, (tok_count, tok_count), 0)
    column = lax.broadcasted_iota(jnp.int32, (tok_count, tok_count), 1)
    causal = column <= row

    @pl.loop(place.dp + 1, dp_count)
    def _(label):
        grad_keys_ref[label] = jnp.zeros(grad_keys_ref.shape[1:], jnp.bfloat16)

    def visit(label, own):
        for group in range(KV_HEADS):
            key_cut = slice(group * HEAD, (group + 1) * HEAD)
            value_cut = slice((KV_HEADS + group) * HEAD, (KV_HEADS + group + 1) * HEAD)
            key = keys_ref[label, :, key_cut]
            value = keys_ref[label, :, value_cut]
            grad_key = jnp.zeros((tok_count, HEAD), jnp.float32)
            grad_value = jnp.zeros((tok_count, HEAD), jnp.float32)
            for head in range(group * repeat_heads, (group + 1) * repeat_heads):
                cut = slice(head * HEAD, (head + 1) * HEAD)
                query = query_ref[:, cut]
                grad = grad_ref[:, cut]
                shift = stat_ref[:, head : head + 1]
                if not own:
                    shift = shift - bias_ref[label]
                scores = dot_f32(query, key, ((1,), (1,)))
                prob = jnp.exp2(scores * factor - shift)
                if own:
                    prob = jnp.where(causal, prob, 0.0)
                prob = prob.astype(jnp.bfloat16)
                grad_prob = dot_f32(grad, value, ((1,), (1,)))
                grad_score = (prob.astype(jnp.float32) * (grad_prob - delta[head])).astype(
                    jnp.bfloat16
                )
                grad_value += dot_f32(prob, grad, ((0,), (0,)))
                grad_key += dot_f32(grad_score, query, ((0,), (0,)))
                grad_query = dot_f32(grad_score, key)
                if own:
                    acc[head] = grad_query
                else:
                    acc[head] += grad_query
            grad_keys_ref[label, :, key_cut] = (grad_key * scale).astype(jnp.bfloat16)
            grad_keys_ref[label, :, value_cut] = grad_value.astype(jnp.bfloat16)

    visit(place.dp, True)

    @pl.loop(0, place.dp)
    def _(label):
        visit(label, False)

    scatter.start()
    cosine, sine = cosine_ref[...], -sine_ref[...]
    for head in range(HEADS):
        grad_project_ref[:, head * HEAD : (head + 1) * HEAD] = halves_turned(
            acc[head] * scale, cosine, sine
        ).astype(jnp.bfloat16)
    scatter.pass_core()
    scatter.pass_x()

    result_ref[...] = (middle_ref[...] + out_sum[...]).astype(jnp.bfloat16)

    def put(cut, value):
        grad_project_ref[cut, query_width : query_width + key_width] = halves_turned(
            value[:, :key_width], cosine_ref[cut], -sine_ref[cut]
        ).astype(jnp.bfloat16)
        grad_project_ref[cut, query_width + key_width :] = value[:, key_width:].astype(jnp.bfloat16)

    scatter.pass_z(put)
    scatter.finish()
    weights.finish()


def back(
    bias, cotangent, middle, probs, exact, stats, query, keys, small, out, row_sum, out_sum, gate_sum,
    cosine, sine, gate_grad, up_grad, shard,
):
    dp_count, tok_count, both = keys.shape
    model_width = middle.shape[1]
    ff_width = gate_grad.shape[1]
    vmem = pl.BlockSpec(memory_space=pltpu.VMEM)
    anywhere = pl.BlockSpec(memory_space=pl.ANY)
    low, full = jnp.bfloat16, jnp.float32
    shape = jax.ShapeDtypeStruct
    dma = pltpu.SemaphoreType.DMA
    return pl.pallas_call(
        back_kernel,
        out_shape=(
            shape((tok_count, model_width), low),
            shape((tok_count, model_width), full),
            shape((tok_count, model_width), low),
            shape((tok_count, LANES), low),
            shape((tok_count, query.shape[1] + both), low),
            shape((8, model_width), full),
            shape((dp_count, shard, ff_width), low),
            shape((dp_count, shard, ff_width), low),
        ),
        in_specs=[pl.BlockSpec(memory_space=pltpu.SMEM)] + [vmem] * 14 + [anywhere] * 2,
        out_specs=(vmem,) * 6 + (anywhere,) * 2,
        scratch_shapes=[
            pltpu.VMEM((tok_count, model_width), full),
            pltpu.VMEM((tok_count, model_width), low),
            pltpu.VMEM((HEADS, tok_count, HEAD), full),
            pltpu.VMEM((HEADS, tok_count, 1), full),
            pltpu.VMEM((dp_count, tok_count, both), low),
            pltpu.VMEM((8, tok_count, both), low),
            pltpu.VMEM((4, tok_count, both), low),
            pltpu.VMEM((3, tok_count, both), low),
            dma((15,)),
            dma((8,)),
            dma((4,)),
            dma((3,)),
            dma((dp_count, 2)),
            dma((dp_count, 2)),
            dma((2,)),
        ],
        compiler_params=pltpu.CompilerParams(
            collective_id=2, has_side_effects=True, vmem_limit_bytes=60 * 1024 * 1024
        ),
    )(
        bias, cotangent, middle, probs, exact, stats, query, keys, small, out, row_sum, out_sum, gate_sum,
        cosine, sine, gate_grad, up_grad,
    )


def finish_kernel(
    tokens_ref,
    hidden_one,
    hidden_two,
    attended_ref,
    grad_middle_ref,
    grad_branch_ref,
    grad_logits_ref,
    grad_project_ref,
    gain_ref,
    project_ref,
    down_ref,
    grad_tokens_ref,
    mine_ref,
    down_back,
    grad_hidden,
    gain_one,
    part_one,
    core_one,
    x_one,
    side_one,
    z_one,
    home_one,
    part_two,
    core_two,
    x_two,
    side_two,
    z_two,
    home_two,
    send_one,
    recv_one,
    send_two,
    recv_two,
    weight_send,
    weight_recv,
    weight_local,
):
    tok_count, model_width = tokens_ref.shape
    width = grad_project_ref.shape[1]
    dp_count = lax.axis_size("dp")
    device_count = dp_count * lax.axis_size("expert")
    shard = mine_ref.shape[0]
    place = Place()
    chunk = 32
    enter(device_count, dp_count)
    weights = WeightReturn(
        place, ((down_ref, down_back),), weight_send, weight_recv, weight_local, dp_count
    )
    weights.start(1, dp_count)
    weights.start_own()
    one = TotalSum(place, part_one, (core_one, x_one, side_one, z_one, home_one), send_one, recv_one, True)
    two = TotalSum(place, part_two, (core_two, x_two, side_two, z_two, home_two), send_two, recv_two, False)
    cut_at = part_one.shape[2]

    @pl.loop(0, model_width // TILE)
    def _(tile):
        grad_hidden[:, columns(tile)] = dot_f32(
            grad_project_ref[...], project_ref[rows_of(tile, TILE), :width], ((1,), (1,))
        )

    gain = gain_rows(project_ref[:, width:])[0:1]
    gain_one[...] = jnp.zeros(gain_one.shape, jnp.float32)

    @pl.loop(0, tok_count // chunk)
    def _(index):
        cut = rows_of(index, chunk)
        value = tokens_ref[cut].astype(jnp.float32)
        row_scale = lax.rsqrt(jnp.mean(value * value, axis=-1, keepdims=True) + epsilon)
        normed = value * row_scale
        grad = grad_hidden[cut]
        gain_one[0:1] += jnp.sum(grad * normed, axis=0, keepdims=True)
        grad = grad * gain
        grad_tokens_ref[cut] = grad_middle_ref[cut] + row_scale * (
            grad - normed * jnp.mean(grad * normed, axis=-1, keepdims=True)
        )

    one_lane = one_hot((8, LANES), lambda r, col: (r == 0) & (col == EXPERTS))
    two_lane = one_hot((8, LANES), lambda r, col: (r == 0) & (col == EXPERTS + 1))
    group = 4 * shard

    @pl.loop(0, model_width // group)
    def _(index):
        cut = columns(index, group)

        def put(part, low, value):
            for i in range(4):
                part[index * 4 + i, :, low : low + value.shape[1]] = value[
                    i * shard : (i + 1) * shard
                ].astype(jnp.bfloat16)

        left = hidden_one[:, cut]
        step = 3 * LANES
        for low in range(0, cut_at, step):
            put(part_one, low, dot_f32(left, grad_project_ref[:, low : low + step], ((0,), (0,))))
        rest = width - cut_at
        put(part_two, 0, dot_f32(left, grad_project_ref[:, cut_at:], ((0,), (0,))))
        small = dot_f32(hidden_two[:, cut], grad_logits_ref[...], ((0,), (0,)))
        for part in split3(gain_one[:, cut]):
            small += dot_f32(part, one_lane, ((0,), (0,)))
        for part in split3(gain_ref[:, cut]):
            small += dot_f32(part, two_lane, ((0,), (0,)))
        put(part_two, rest, small)
        left = attended_ref[:, cut]
        for low in range(0, model_width, step):
            put(
                part_two,
                rest + LANES + low,
                dot_f32(left, grad_branch_ref[:, low : low + step], ((0,), (0,))),
            )
        for total in (one, two):
            total.start(index)

    order = place.others() + [place.z]
    both = (one, two)
    for z in order:
        for total in both:
            total.first(z)
    for z in order:
        for total in both:
            total.second(z)
    for i, z in enumerate(order):
        for total in both:
            total.third(z, i)
    for total in both:
        total.fourth()
    one.finish(mine_ref, slice(0, cut_at))
    two.finish(mine_ref, slice(cut_at, mine_ref.shape[1]))
    weights.finish()


def finish(
    tokens, hidden_one, hidden_two, attended, grad_middle, grad_branch, grad_logits, grad_project,
    gain, project, down_grad, shard, half,
):
    tok_count, model_width = tokens.shape
    dp_count = lax.axis_size("dp")
    width = project.shape[1] + model_width
    first = 15 * LANES
    vmem = pl.BlockSpec(memory_space=pltpu.VMEM)
    anywhere = pl.BlockSpec(memory_space=pl.ANY)
    low, full = jnp.bfloat16, jnp.float32
    shape = jax.ShapeDtypeStruct
    dma = pltpu.SemaphoreType.DMA
    return pl.pallas_call(
        finish_kernel,
        out_shape=(
            shape((tok_count, model_width), full),
            shape((shard, width), full),
            shape((dp_count, half, model_width), low),
        ),
        in_specs=[vmem] * 10 + [anywhere],
        out_specs=(vmem, vmem, anywhere),
        scratch_shapes=[
            pltpu.VMEM((tok_count, model_width), full),
            pltpu.VMEM((8, model_width), full),
            *(
                pltpu.VMEM(lead + (columns_of,), low)
                for columns_of, lead in (
                    (first, (dp_count, shard)),
                    (first, (8, shard)),
                    (first, (4, shard)),
                    (first, (4, shard // 2)),
                    (first, (3, shard // 2)),
                    (first, (shard // 2,)),
                    (width - first, (dp_count, shard)),
                    (width - first, (8, shard)),
                    (width - first, (4, shard // 2)),
                    (width - first, (8, shard // 2)),
                    (width - first, (3, shard // 2)),
                    (width - first, (shard // 2,)),
                )
            ),
            dma((24,)),
            dma((24,)),
            dma((24,)),
            dma((24,)),
            dma((dp_count, 1)),
            dma((dp_count, 1)),
            dma((1,)),
        ],
        compiler_params=pltpu.CompilerParams(
            collective_id=3, has_side_effects=True, vmem_limit_bytes=58 * 1024 * 1024
        ),
    )(
        tokens, hidden_one, hidden_two, attended, grad_middle, grad_branch, grad_logits,
        grad_project, gain, project, down_grad,
    )


def local_owned(
    tokens,
    attn_gain,
    query_weight,
    key_weight,
    value_weight,
    out_weight,
    moe_gain,
    router_weight,
    gate_weight,
    up_weight,
    down_weight,
    parents,
    routes,
    claim_order,
    cotangent,
):
    tok_count = tokens.shape[1]
    segment = lax.axis_index("dp")
    query_width = HEADS * HEAD
    key_width = KV_HEADS * HEAD

    route_rows = routes[0]
    expert_ids = route_rows.reshape(-1)
    order_row = claim_order[0, 0]
    member = (expert_ids[:, None] == jnp.arange(EXPERTS, dtype=jnp.int32)[None, :]).astype(
        jnp.bfloat16
    )
    earlier = (order_row[None, :] < order_row[:, None]).astype(jnp.bfloat16)
    before = jnp.dot(earlier, member, preferred_element_type=jnp.float32)
    slot_index = jnp.sum(before * member.astype(jnp.float32), axis=1).astype(jnp.int32)
    target = jnp.where(slot_index < CAP, expert_ids * SLOTS + slot_index, -1).reshape(
        tok_count, TOP
    )
    target_rows = jnp.full((8, TILE), -1.0, jnp.float32)
    target_rows = target_rows.at[:TOP, :tok_count].set(target.T.astype(jnp.float32))
    route_lanes = jnp.pad(route_rows, ((0, 0), (0, LANES - TOP)), constant_values=-1)

    small = jnp.concatenate(
        [
            router_weight,
            attn_gain[:, None],
            moe_gain[:, None],
            jnp.zeros((router_weight.shape[0], LANES - EXPERTS - 2), jnp.bfloat16),
        ],
        axis=1,
    )
    project_shard = jnp.concatenate([query_weight, key_weight, value_weight, small], axis=1)
    reach_row = ancestry(parents[0])[segment]
    path_depth = jnp.sum(reach_row) - 1.0
    positions = path_depth * tok_count + jnp.arange(tok_count, dtype=jnp.float32)
    cosine, sine_part = rope_tables(positions, HEAD)
    cosine_wide = jnp.concatenate([cosine[:, 0], cosine[:, 0]], axis=1)
    sine_wide = jnp.concatenate([-sine_part[:, 0], sine_part[:, 0]], axis=1)
    on_path = reach_row > 0.5
    bias = jnp.where(on_path, 0.0, -1e30).astype(jnp.float32)
    (
        project_full,
        out_full,
        keys,
        query_rot,
        attended,
        exact_out,
        stats,
        middle,
        hidden_two,
        probs,
        rows_in,
        grad_rows_in,
        gate_own,
        up_own,
        down_own,
        hidden_one,
        target_all,
        gate_all,
    ) = front(
        bias,
        tokens[0],
        cotangent[0],
        project_shard,
        out_weight,
        target_rows,
        route_lanes,
        cosine_wide,
        sine_wide,
        gate_weight,
        up_weight,
        down_weight,
    )
    small_at = query_width + 2 * key_width
    row_sum, out_sum, gate_sum, gate_grad, up_grad, down_grad = experts(
        rows_in, grad_rows_in, gate_own, up_own, down_own, target_all, gate_all, tok_count
    )
    (
        block_out,
        grad_middle,
        grad_branch,
        grad_logits,
        grad_project,
        gain_row,
        gate_back,
        up_back,
    ) = back(
        bias,
        cotangent[0],
        middle,
        probs,
        exact_out,
        stats,
        query_rot,
        keys,
        project_full[:, small_at:],
        out_full,
        row_sum,
        out_sum,
        gate_sum,
        cosine_wide,
        sine_wide,
        gate_grad,
        up_grad,
        gate_weight.shape[1],
    )
    grad_tokens, mine, down_back = finish(
        tokens[0],
        hidden_one,
        hidden_two,
        attended,
        grad_middle,
        grad_branch,
        grad_logits,
        grad_project,
        gain_row,
        project_full,
        down_grad,
        query_weight.shape[0],
        down_weight.shape[1],
    )
    return (
        block_out[None],
        grad_tokens[None],
        mine[:, small_at + EXPERTS],
        mine[:, :query_width],
        mine[:, query_width : query_width + key_width],
        mine[:, query_width + key_width : small_at],
        mine[:, small_at + LANES :],
        mine[:, small_at + EXPERTS + 1],
        mine[:, small_at : small_at + EXPERTS],
        gate_back.astype(jnp.float32),
        up_back.astype(jnp.float32),
        down_back.astype(jnp.float32),
    )


def solution(mesh):
    placed = (
        P("expert", "dp", None),
        P("dp"),
        P("dp", None),
        P("dp", None),
        P("dp", None),
        P("dp", None),
        P("dp"),
        P("dp", None),
        P("expert", "dp", None),
        P("expert", "dp", None),
        P("expert", "dp", None),
        P("expert", None),
        P("expert", "dp", None),
        P("expert", "dp", None),
        P("expert", "dp", None),
    )
    owned = mesh.shape["dp"] == 16 and mesh.shape["expert"] == 2
    return jax.shard_map(
        local_owned if owned else local_gathered,
        mesh=mesh,
        in_specs=placed,
        out_specs=(
            P("expert", "dp", None),
            P("expert", "dp", None),
            P("dp"),
            P("dp", None),
            P("dp", None),
            P("dp", None),
            P("dp", None),
            P("dp"),
            P("dp", None),
            P("expert", "dp", None),
            P("expert", "dp", None),
            P("expert", "dp", None),
        ),
        check_vma=False,
    )
```

```python
import functools

import jax
import jax.numpy as jnp
from jax import lax
from jax.experimental import pallas as pl
from jax.experimental.pallas import tpu as pltpu
from jax.sharding import PartitionSpec as P

HEADS = 12
KV_HEADS = 2
HEAD = 128
EXPERTS = 32
TOP = 4
CAP = 28


epsilon = 1e-06
theta = 10000.0
highest = lax.Precision.HIGHEST


def ancestry(parents):
    row_count = parents.shape[0]
    labels = jnp.arange(row_count, dtype=jnp.int32)
    linked = (parents[:, None] == labels[None, :]).astype(jnp.float32)
    reach_all = jnp.minimum(jnp.eye(row_count, dtype=jnp.float32) + linked, 1.0)
    for doubling in range(max(1, (row_count - 1).bit_length())):
        reach_all = jnp.minimum(jnp.dot(reach_all, reach_all, precision=highest), 1.0)
    return reach_all


def rope_tables(positions, head_size):
    halfway = head_size // 2
    frequency = theta ** (-jnp.arange(halfway, dtype=jnp.float32) * 2.0 / head_size)
    angles = positions[:, None] * frequency[None, :]
    return (jnp.cos(angles)[:, None, :], jnp.sin(angles)[:, None, :])


def rotate(values, cosine, sine_part):
    halfway = values.shape[-1] // 2
    first_half = values[..., :halfway]
    second = values[..., halfway:]
    return jnp.concatenate(
        [first_half * cosine - second * sine_part, second * cosine + first_half * sine_part],
        axis=-1,
    )


def norm_backward(grad_hidden, normed, row_scale, gain):
    grad_normed = grad_hidden * gain
    grad_gain = jnp.sum(grad_hidden * normed, axis=0)
    grad_rows = row_scale * (
        grad_normed - normed * jnp.mean(grad_normed * normed, axis=-1, keepdims=True)
    )
    return (grad_rows, grad_gain)


def local_gathered(
    tokens,
    attn_gain,
    query_weight,
    key_weight,
    value_weight,
    out_weight,
    moe_gain,
    router_weight,
    gate_weight,
    up_weight,
    down_weight,
    parents,
    routes,
    claim_order,
    cotangent,
):
    (
        gain_one,
        query_full,
        key_full,
        value_full,
        out_full,
        gain_two,
        router_full,
        gate_full,
        up_full,
        down_full,
    ) = (
        lax.all_gather(attn_gain, "dp", axis=0, tiled=True),
        lax.all_gather(query_weight, "dp", axis=0, tiled=True),
        lax.all_gather(key_weight, "dp", axis=0, tiled=True),
        lax.all_gather(value_weight, "dp", axis=0, tiled=True),
        lax.all_gather(out_weight, "dp", axis=0, tiled=True),
        lax.all_gather(moe_gain, "dp", axis=0, tiled=True),
        lax.all_gather(router_weight, "dp", axis=0, tiled=True),
        lax.all_gather(gate_weight, "dp", axis=1, tiled=True),
        lax.all_gather(up_weight, "dp", axis=1, tiled=True),
        lax.all_gather(down_weight, "dp", axis=1, tiled=True),
    )
    tok_count = tokens.shape[1]
    model_width = tokens.shape[2]
    segment = lax.axis_index("dp")
    segment_count = lax.axis_size("dp")
    expert_peers = lax.axis_size("expert")
    local_experts = gate_weight.shape[0]
    repeat_heads = HEADS // KV_HEADS
    score_scale = HEAD ** (-0.5)
    query_rows = repeat_heads * tok_count
    reach_all = ancestry(parents[0])
    reach_row = reach_all[segment]
    path_depth = jnp.sum(reach_row) - 1.0
    positions = path_depth * tok_count + jnp.arange(tok_count, dtype=jnp.float32)
    cosine, sine_part = rope_tables(positions, HEAD)
    inputs = tokens[0].astype(jnp.float32)
    scale_one = lax.rsqrt(jnp.mean(inputs * inputs, axis=-1, keepdims=True) + epsilon)
    normed_one = inputs * scale_one
    gain_first = gain_one.astype(jnp.float32)
    hidden_one = (normed_one * gain_first).astype(jnp.bfloat16)
    query_raw = jnp.dot(hidden_one, query_full, preferred_element_type=jnp.float32).reshape(
        tok_count, HEADS, HEAD
    )
    key_raw = jnp.dot(hidden_one, key_full, preferred_element_type=jnp.float32).reshape(
        tok_count, KV_HEADS, HEAD
    )
    value_low = jnp.dot(hidden_one, value_full, preferred_element_type=jnp.float32).astype(
        jnp.bfloat16
    )
    query_rot = rotate(query_raw, cosine, sine_part).astype(jnp.bfloat16)
    key_rot = (
        rotate(key_raw, cosine, sine_part).astype(jnp.bfloat16).reshape(tok_count, KV_HEADS * HEAD)
    )
    key_all, value_all = (
        lax.all_gather(key_rot, "dp", axis=0, tiled=True),
        lax.all_gather(value_low, "dp", axis=0, tiled=True),
    )
    total_keys = key_all.shape[0]
    key_blocks = key_all.reshape(segment_count, tok_count, KV_HEADS, HEAD)
    value_blocks = value_all.reshape(segment_count, tok_count, KV_HEADS, HEAD)
    segment_labels = jnp.arange(segment_count, dtype=jnp.int32)
    query_groups = (
        query_rot.reshape(tok_count, KV_HEADS, repeat_heads, HEAD)
        .transpose(1, 2, 0, 3)
        .reshape(KV_HEADS, query_rows, HEAD)
    )
    query_offsets = jnp.arange(tok_count, dtype=jnp.int32)
    causal_tile = jnp.tile(query_offsets[None, :] <= query_offsets[:, None], (repeat_heads, 1))

    def scores_of(key_block, label):
        raw_scores = (
            jnp.einsum("grh,kgh->grk", query_groups, key_block, preferred_element_type=jnp.float32)
            * score_scale
        )
        allowed = causal_tile | (label != segment)
        return jnp.where(allowed[None], raw_scores, -1000000000.0)

    def on_path(label):
        return reach_row[label] > 0.5

    def pass_stats(state_pair, inputs_block):
        key_block, value_block, label = inputs_block

        def visit(state):
            row_max, row_sum = state
            scores = scores_of(key_block, label)
            new_max = jnp.maximum(row_max, jnp.max(scores, axis=-1))
            new_sum = row_sum * jnp.exp(row_max - new_max) + jnp.sum(
                jnp.exp(scores - new_max[..., None]), axis=-1
            )
            return (new_max, new_sum)

        return (lax.cond(on_path(label), visit, lambda state: state, state_pair), None)

    start_max = jnp.full((KV_HEADS, query_rows), -1e30, jnp.float32)
    start_sum = jnp.zeros((KV_HEADS, query_rows), jnp.float32)
    (row_max, row_sum), unused = lax.scan(
        pass_stats, (start_max, start_sum), (key_blocks, value_blocks, segment_labels)
    )

    def probs_of(key_block, label):
        return jnp.exp(scores_of(key_block, label) - row_max[..., None]) / row_sum[..., None]

    def pass_values(state_pair, inputs_block):
        key_block, value_block, label = inputs_block

        def visit(state):
            accumulated, exact_out = state
            prob_block = probs_of(key_block, label)
            accumulated = accumulated + jnp.einsum(
                "grk,kgh->grh",
                prob_block.astype(jnp.bfloat16),
                value_block,
                preferred_element_type=jnp.float32,
            )
            exact_out = exact_out + jnp.einsum(
                "grk,kgh->grh",
                prob_block,
                value_block.astype(jnp.float32),
                preferred_element_type=jnp.float32,
                precision=highest,
            )
            return (accumulated, exact_out)

        return (lax.cond(on_path(label), visit, lambda state: state, state_pair), None)

    zero_out = jnp.zeros((KV_HEADS, query_rows, HEAD), jnp.float32)
    (accumulated, exact_out), unused = lax.scan(
        pass_values, (zero_out, zero_out), (key_blocks, value_blocks, segment_labels)
    )
    attended = (
        accumulated.reshape(KV_HEADS, repeat_heads, tok_count, HEAD)
        .transpose(2, 0, 1, 3)
        .reshape(tok_count, HEADS * HEAD)
        .astype(jnp.bfloat16)
    )
    branch = jnp.dot(attended, out_full, preferred_element_type=jnp.float32)
    middle = inputs + branch
    scale_two = lax.rsqrt(jnp.mean(middle * middle, axis=-1, keepdims=True) + epsilon)
    normed_two = middle * scale_two
    gain_second = gain_two.astype(jnp.float32)
    hidden_two = (normed_two * gain_second).astype(jnp.bfloat16)
    logits = jnp.dot(hidden_two, router_full, preferred_element_type=jnp.float32)
    picked_one = (
        routes[0][:, :, None] == jnp.arange(EXPERTS, dtype=jnp.int32)[None, None, :]
    ).astype(jnp.float32)
    chosen = jnp.sum(picked_one * logits[:, None, :], axis=-1)
    gate_probs = jax.nn.softmax(chosen, axis=-1)
    expert_ids = routes[0].reshape(-1)
    order_row = claim_order[0, 0]
    pair_count = expert_ids.shape[0]
    member = (expert_ids[:, None] == jnp.arange(EXPERTS, dtype=jnp.int32)[None, :]).astype(
        jnp.bfloat16
    )
    earlier = (order_row[None, :] < order_row[:, None]).astype(jnp.bfloat16)
    before = jnp.dot(earlier, member, preferred_element_type=jnp.float32)
    slot_index = jnp.sum(before * member.astype(jnp.float32), axis=1).astype(jnp.int32)
    owner_rank = expert_ids // local_experts
    local_rank = expert_ids % local_experts
    target = jnp.where(
        slot_index < CAP, (local_rank * expert_peers + owner_rank) * CAP + slot_index, EXPERTS * CAP
    )
    slot_pairs = (
        jnp.full((EXPERTS * CAP + 1,), pair_count, jnp.int32)
        .at[target]
        .set(jnp.arange(pair_count, dtype=jnp.int32))[: EXPERTS * CAP]
    )
    padded_two = jnp.concatenate([hidden_two, jnp.zeros((1, model_width), jnp.bfloat16)], axis=0)
    send_rows = padded_two[slot_pairs // TOP].reshape(local_experts, expert_peers, CAP, model_width)
    arrived = lax.all_to_all(send_rows, "expert", split_axis=1, concat_axis=1, tiled=True)
    expert_rows = arrived.reshape(local_experts, expert_peers * CAP, model_width)
    gate_act = jnp.einsum(
        "erd,edf->erf", expert_rows, gate_full, preferred_element_type=jnp.float32
    )
    up_act = jnp.einsum("erd,edf->erf", expert_rows, up_full, preferred_element_type=jnp.float32)
    inner = (jax.nn.silu(gate_act) * up_act).astype(jnp.bfloat16)
    expert_out = jnp.einsum(
        "erf,efd->erd", inner, down_full, preferred_element_type=jnp.float32
    ).astype(jnp.bfloat16)
    returned = lax.all_to_all(
        expert_out.reshape(local_experts, expert_peers, CAP, model_width),
        "expert",
        split_axis=1,
        concat_axis=1,
        tiled=True,
    )
    returned = jnp.concatenate(
        [returned.reshape(EXPERTS * CAP, model_width), jnp.zeros((1, model_width), jnp.bfloat16)],
        axis=0,
    )
    pair_out = returned[target].reshape(tok_count, TOP, model_width).astype(jnp.float32)
    mixture = jnp.sum(gate_probs[:, :, None] * pair_out, axis=1)
    block_out = (middle + mixture).astype(jnp.bfloat16)
    grad_result = cotangent[0].astype(jnp.float32)
    grad_gates = jnp.sum(pair_out * grad_result[:, None, :], axis=-1)
    grad_pairs = (
        (gate_probs[:, :, None] * grad_result[:, None, :])
        .astype(jnp.bfloat16)
        .reshape(pair_count, model_width)
    )
    grad_padded = jnp.concatenate([grad_pairs, jnp.zeros((1, model_width), jnp.bfloat16)], axis=0)
    grad_send = grad_padded[slot_pairs].reshape(local_experts, expert_peers, CAP, model_width)
    grad_arrived, rows_back = (
        lax.all_to_all(grad_send, "expert", split_axis=1, concat_axis=1, tiled=True),
        lax.all_to_all(send_rows, "expert", split_axis=1, concat_axis=1, tiled=True),
    )
    rows_again = rows_back.reshape(local_experts, expert_peers * CAP, model_width)
    gate_again = jnp.einsum(
        "erd,edf->erf", rows_again, gate_full, preferred_element_type=jnp.float32
    )
    up_again = jnp.einsum("erd,edf->erf", rows_again, up_full, preferred_element_type=jnp.float32)
    inner_again = (jax.nn.silu(gate_again) * up_again).astype(jnp.bfloat16)
    grad_expert_out = grad_arrived.reshape(local_experts, expert_peers * CAP, model_width)
    grad_inner = jnp.einsum(
        "erd,efd->erf", grad_expert_out, down_full, preferred_element_type=jnp.float32
    )
    grad_down_local = jnp.einsum(
        "erf,erd->efd", inner_again, grad_expert_out, preferred_element_type=jnp.float32
    )
    sigmoid_gate = jax.nn.sigmoid(gate_again)
    swish = gate_again * sigmoid_gate
    grad_gate_act = (
        grad_inner * up_again * (sigmoid_gate * (1.0 + gate_again * (1.0 - sigmoid_gate)))
    ).astype(jnp.bfloat16)
    grad_up_act = (grad_inner * swish).astype(jnp.bfloat16)
    grad_gate_local = jnp.einsum(
        "erd,erf->edf", rows_again, grad_gate_act, preferred_element_type=jnp.float32
    )
    grad_up_local = jnp.einsum(
        "erd,erf->edf", rows_again, grad_up_act, preferred_element_type=jnp.float32
    )
    grad_rows = (
        jnp.einsum("erf,edf->erd", grad_gate_act, gate_full, preferred_element_type=jnp.float32)
        + jnp.einsum("erf,edf->erd", grad_up_act, up_full, preferred_element_type=jnp.float32)
    ).astype(jnp.bfloat16)
    grad_back = lax.all_to_all(
        grad_rows.reshape(local_experts, expert_peers, CAP, model_width),
        "expert",
        split_axis=1,
        concat_axis=1,
        tiled=True,
    )
    grad_back = jnp.concatenate(
        [grad_back.reshape(EXPERTS * CAP, model_width), jnp.zeros((1, model_width), jnp.bfloat16)],
        axis=0,
    )
    grad_hidden_two = jnp.sum(
        grad_back[target].reshape(tok_count, TOP, model_width).astype(jnp.float32), axis=1
    )
    grad_chosen = gate_probs * (
        grad_gates - jnp.sum(gate_probs * grad_gates, axis=-1, keepdims=True)
    )
    grad_logits = jnp.sum(picked_one * grad_chosen[:, :, None], axis=1).astype(jnp.bfloat16)
    grad_hidden_two = grad_hidden_two + jnp.dot(
        grad_logits, router_full.T, preferred_element_type=jnp.float32
    )
    grad_router_local = jnp.dot(hidden_two.T, grad_logits, preferred_element_type=jnp.float32)
    grad_middle_norm, grad_gain_two = norm_backward(
        grad_hidden_two, normed_two, scale_two, gain_second
    )
    grad_middle = grad_result + grad_middle_norm
    grad_branch = grad_middle.astype(jnp.bfloat16)
    grad_out_local = jnp.dot(attended.T, grad_branch, preferred_element_type=jnp.float32)
    grad_attended = jnp.dot(grad_branch, out_full.T, preferred_element_type=jnp.float32).astype(
        jnp.bfloat16
    )
    grad_groups = (
        grad_attended.reshape(tok_count, KV_HEADS, repeat_heads, HEAD)
        .transpose(1, 2, 0, 3)
        .reshape(KV_HEADS, query_rows, HEAD)
    )
    row_delta = jnp.sum(grad_groups.astype(jnp.float32) * exact_out, axis=-1)
    zero_key = jnp.zeros((tok_count, KV_HEADS, HEAD), jnp.float32)

    def pass_grads(grad_query, inputs_block):
        key_block, value_block, label = inputs_block

        def visit(carried):
            prob_block = probs_of(key_block, label)
            grad_probs = jnp.einsum(
                "grh,kgh->grk", grad_groups, value_block, preferred_element_type=jnp.float32
            )
            grad_scores = (prob_block * (grad_probs - row_delta[..., None])).astype(jnp.bfloat16)
            carried = carried + jnp.einsum(
                "grk,kgh->grh", grad_scores, key_block, preferred_element_type=jnp.float32
            )
            grad_key_block = (
                jnp.einsum(
                    "grk,grh->kgh", grad_scores, query_groups, preferred_element_type=jnp.float32
                )
                * score_scale
            )
            grad_value_block = jnp.einsum(
                "grk,grh->kgh",
                prob_block.astype(jnp.bfloat16),
                grad_groups,
                preferred_element_type=jnp.float32,
            )
            return (carried, (grad_key_block, grad_value_block))

        def skip(carried):
            return (carried, (zero_key, zero_key))

        return lax.cond(on_path(label), visit, skip, grad_query)

    grad_query_groups, (grad_key_blocks, grad_value_blocks) = lax.scan(
        pass_grads,
        jnp.zeros((KV_HEADS, query_rows, HEAD), jnp.float32),
        (key_blocks, value_blocks, segment_labels),
    )
    grad_key_all = grad_key_blocks.reshape(total_keys, KV_HEADS * HEAD)
    grad_value_all = grad_value_blocks.reshape(total_keys, KV_HEADS * HEAD)
    grad_key_mine, grad_value_mine = (
        lax.psum_scatter(
            grad_key_all.astype(jnp.bfloat16), "dp", scatter_dimension=0, tiled=True
        ).astype(jnp.float32),
        lax.psum_scatter(
            grad_value_all.astype(jnp.bfloat16), "dp", scatter_dimension=0, tiled=True
        ).astype(jnp.float32),
    )
    grad_query_rot = (
        (grad_query_groups * score_scale)
        .reshape(KV_HEADS, repeat_heads, tok_count, HEAD)
        .transpose(2, 0, 1, 3)
        .reshape(tok_count, HEADS, HEAD)
    )
    grad_query_raw = (
        rotate(grad_query_rot, cosine, -sine_part)
        .reshape(tok_count, HEADS * HEAD)
        .astype(jnp.bfloat16)
    )
    grad_key_raw = (
        rotate(grad_key_mine.reshape(tok_count, KV_HEADS, HEAD), cosine, -sine_part)
        .reshape(tok_count, KV_HEADS * HEAD)
        .astype(jnp.bfloat16)
    )
    grad_value_raw = grad_value_mine.astype(jnp.bfloat16)
    grad_query_local = jnp.dot(hidden_one.T, grad_query_raw, preferred_element_type=jnp.float32)
    grad_key_local = jnp.dot(hidden_one.T, grad_key_raw, preferred_element_type=jnp.float32)
    grad_value_local = jnp.dot(hidden_one.T, grad_value_raw, preferred_element_type=jnp.float32)
    grad_hidden_one = (
        jnp.dot(grad_query_raw, query_full.T, preferred_element_type=jnp.float32)
        + jnp.dot(grad_key_raw, key_full.T, preferred_element_type=jnp.float32)
        + jnp.dot(grad_value_raw, value_full.T, preferred_element_type=jnp.float32)
    )
    grad_inputs_norm, grad_gain_one = norm_backward(
        grad_hidden_one, normed_one, scale_one, gain_first
    )
    grad_inputs = grad_middle + grad_inputs_norm
    grad_gate_mine, grad_up_mine, grad_down_mine = (
        lax.psum_scatter(
            grad_gate_local.astype(jnp.bfloat16), "dp", scatter_dimension=1, tiled=True
        ).astype(jnp.float32),
        lax.psum_scatter(
            grad_up_local.astype(jnp.bfloat16), "dp", scatter_dimension=1, tiled=True
        ).astype(jnp.float32),
        lax.psum_scatter(
            grad_down_local.astype(jnp.bfloat16), "dp", scatter_dimension=1, tiled=True
        ).astype(jnp.float32),
    )
    shard_rows = (
        lax.psum_scatter(
            grad_gain_one.astype(jnp.bfloat16), "dp", scatter_dimension=0, tiled=True
        ).astype(jnp.float32),
        lax.psum_scatter(
            grad_query_local.astype(jnp.bfloat16), "dp", scatter_dimension=0, tiled=True
        ).astype(jnp.float32),
        lax.psum_scatter(
            grad_key_local.astype(jnp.bfloat16), "dp", scatter_dimension=0, tiled=True
        ).astype(jnp.float32),
        lax.psum_scatter(
            grad_value_local.astype(jnp.bfloat16), "dp", scatter_dimension=0, tiled=True
        ).astype(jnp.float32),
        lax.psum_scatter(
            grad_out_local.astype(jnp.bfloat16), "dp", scatter_dimension=0, tiled=True
        ).astype(jnp.float32),
        lax.psum_scatter(
            grad_gain_two.astype(jnp.bfloat16), "dp", scatter_dimension=0, tiled=True
        ).astype(jnp.float32),
        lax.psum_scatter(
            grad_router_local.astype(jnp.bfloat16), "dp", scatter_dimension=0, tiled=True
        ).astype(jnp.float32),
    )
    shared = (
        lax.psum(shard_rows[0].astype(jnp.bfloat16), "expert").astype(jnp.float32),
        lax.psum(shard_rows[1].astype(jnp.bfloat16), "expert").astype(jnp.float32),
        lax.psum(shard_rows[2].astype(jnp.bfloat16), "expert").astype(jnp.float32),
        lax.psum(shard_rows[3].astype(jnp.bfloat16), "expert").astype(jnp.float32),
        lax.psum(shard_rows[4].astype(jnp.bfloat16), "expert").astype(jnp.float32),
        lax.psum(shard_rows[5].astype(jnp.bfloat16), "expert").astype(jnp.float32),
        lax.psum(shard_rows[6].astype(jnp.bfloat16), "expert").astype(jnp.float32),
    )
    return (
        block_out[None],
        grad_inputs[None],
        shared[0],
        shared[1],
        shared[2],
        shared[3],
        shared[4],
        shared[5],
        shared[6],
        grad_gate_mine,
        grad_up_mine,
        grad_down_mine,
    )


SLOTS = 32
PAD_TOKENS = 32
LANES = 128
TILE = 256
MESH = pl.DeviceIdType.MESH
log2e = 1.4426950408889634


def dot_f32(a, b, dims=((1,), (0,))):
    return lax.dot_general(a, b, (dims, ((), ())), preferred_element_type=jnp.float32)


def split3(value):
    high = value.astype(jnp.bfloat16)
    rest = value - high.astype(jnp.float32)
    middle = rest.astype(jnp.bfloat16)
    low = (rest - middle.astype(jnp.float32)).astype(jnp.bfloat16)
    return high, middle, low


def one_hot(shape, test):
    row = lax.broadcasted_iota(jnp.int32, shape, 0)
    column = lax.broadcasted_iota(jnp.int32, shape, 1)
    return jnp.where(test(row, column), 1.0, 0.0).astype(jnp.bfloat16)


class Place:
    def __init__(self):
        self.dp = lax.axis_index("dp")
        self.side = lax.axis_index("expert")
        self.z = self.dp // 4
        self.x = (self.dp // 2) % 2
        self.c = self.dp % 2

    def index(self, z, x, c):
        return z * 4 + x * 2 + c

    def others(self):
        return [self.z + 1 - 2 * (self.z % 2), (self.z + 2) % 4, 3 - self.z]


def remote(src, dst, send, recv, dp, side):
    return pltpu.make_async_remote_copy(
        src_ref=src,
        dst_ref=dst,
        send_sem=send,
        recv_sem=recv,
        device_id={"dp": dp, "expert": side},
        device_id_type=MESH,
    )


def enter(device_count, dp_count):
    rank = lax.axis_index("expert") * dp_count + lax.axis_index("dp")
    barrier = pltpu.get_barrier_semaphore()

    @pl.loop(1, device_count)
    def _(step):
        other = (rank + step) % device_count
        pl.semaphore_signal(
            barrier,
            inc=1,
            device_id={"dp": other % dp_count, "expert": other // dp_count},
            device_id_type=MESH,
        )

    pl.semaphore_wait(barrier, device_count - 1)


class Column:
    def __init__(self, place, own, slot, send, recv, local):
        self.place, self.own, self.slot = place, own, slot
        self.send, self.recv, self.local = send, recv, local

    def hop(self, z, step, own=False):
        p = self.place
        source = self.own if own else self.slot(z)
        number = z if step > 0 else 4 + z
        target = p.index(p.z + step, p.x, p.c)
        return remote(source, self.slot(z), self.send.at[number], self.recv(z), target, p.side)

    def own_copy(self):
        return pltpu.make_async_copy(self.own, self.slot(self.place.z), self.local)

    def upward(self, act):
        pl.when(self.place.z < 3)(act)

    def downward(self, act):
        pl.when(self.place.z > 0)(act)

    def start(self):
        z = self.place.z
        self.upward(lambda: self.hop(z, 1, True).start())
        self.downward(lambda: self.hop(z, -1, True).start())
        self.own_copy().start()

    def forward(self, low=1, high=4, then=None):
        z = self.place.z

        @pl.loop(low, high)
        def _(away):
            @pl.when(z - away >= 0)
            def _():
                self.hop(z - away, 1).wait_recv()
                self.upward(lambda: self.hop(z - away, 1).start())
                if then is not None:
                    then(z - away)

            @pl.when(z + away <= 3)
            def _():
                self.hop(z + away, -1).wait_recv()
                self.downward(lambda: self.hop(z + away, -1).start())
                if then is not None:
                    then(z + away)

    def finish(self):
        z = self.place.z

        @pl.loop(0, 4)
        def _(origin):
            @pl.when((origin <= z) & (z < 3))
            def _():
                self.hop(origin, 1).wait_send()

            @pl.when((origin >= z) & (z > 0))
            def _():
                self.hop(origin, -1).wait_send()


class Gather:
    def __init__(self, place, own, slot, send, recv, local):
        self.place, self.own, self.slot = place, own, slot
        self.send, self.recv = send, recv
        self.column = Column(
            place,
            own,
            lambda z: slot(place.index(z, place.x, place.c)),
            send,
            lambda z: recv.at[place.index(z, place.x, place.c)],
            local,
        )

    def copy(self, z, x, c, to_x, to_c, number, own=False):
        p = self.place
        shard = p.index(z, x, c)
        source = self.own if own else self.slot(shard)
        target = p.index(p.z, to_x, to_c)
        return remote(
            source, self.slot(shard), self.send.at[number], self.recv.at[shard], target, p.side
        )

    def to_x(self, z, own=False):
        p = self.place
        return self.copy(z, p.x, p.c, 1 - p.x, p.c, 8 + z, own)

    def to_core(self, z, x, own=False):
        p = self.place
        return self.copy(z, x, p.c, p.x, 1 - p.c, 12 + z * 2 + x, own)

    def start(self):
        p = self.place
        self.column.start()
        self.to_x(p.z, True).start()
        self.to_core(p.z, p.x, True).start()

    def forward_z(self):
        def then(z):
            self.to_x(z).start()
            self.to_core(z, self.place.x).start()

        self.column.forward(then=then)

    def forward_x(self):
        p = self.place

        def pass_on(z):
            self.to_core(z, 1 - p.x).wait_recv()
            self.to_core(z, 1 - p.x).start()

        pass_on(p.z)

        @pl.loop(1, 4)
        def _(away):
            pl.when(p.z - away >= 0)(lambda: pass_on(p.z - away))
            pl.when(p.z + away <= 3)(lambda: pass_on(p.z + away))

    def finish(self):
        p = self.place

        @pl.loop(0, 4)
        def _(z):
            for x in range(2):
                self.copy(z, x, 1 - p.c, p.x, 1 - p.c, 12).wait_recv()
                self.to_core(z, x).wait_send()
            self.to_x(z).wait_send()

        self.column.finish()
        self.column.own_copy().wait()


class PlaneSwap:
    def __init__(self, place, source, target, send, recv, local, dp_count):
        self.place, self.source, self.target = place, source, target
        self.send, self.recv, self.local = send, recv, local
        self.dp_count = dp_count

    def of(self, member):
        return member // 4, (member // 2) % 2, member % 2

    def me(self):
        p = self.place
        return p.side * 4 + p.x * 2 + p.c

    def block(self, z, origin):
        return self.target.at[rows_of(z * 8 + origin, SLOTS)]

    def copy(self, z, step, to, origin):
        p = self.place
        side, x, c = self.of(to)
        return remote(
            self.source.at[z, rows_of(to, SLOTS)],
            self.block(z, origin),
            self.send.at[z, step],
            self.recv.at[z, step],
            p.index(p.z, x, c),
            side,
        )

    def own_copy(self, z):
        return pltpu.make_async_copy(
            self.source.at[z, rows_of(self.me(), SLOTS)],
            self.block(z, self.me()),
            self.local.at[z],
        )

    def start(self, z):
        for step in range(1, 8):
            self.copy(z, step, (self.me() + step) % 8, self.me()).start()
        self.own_copy(z).start()

    def arrived(self, z):
        for step in range(1, 8):
            other = (self.me() + 8 - step) % 8
            self.copy(z, step, other, other).wait_recv()
        self.own_copy(z).wait()

    def sent(self):
        @pl.loop(0, 4)
        def _(z):
            for step in range(1, 8):
                self.copy(z, step, (self.me() + step) % 8, self.me()).wait_send()

    def finish(self):
        pl.loop(0, 4)(self.arrived)
        self.sent()


class Chain:
    def __init__(self, place, part, land, send, recv):
        self.place, self.part, self.land = place, part, land
        self.send, self.recv = send, recv

    def hop(self, z, step):
        p = self.place
        if step > 0:
            slot = z
        else:
            slot = z + (4 - z) * ((3 - (p.z - 1 - z)) // 3)
        target = p.index(p.z + step, p.x, p.c)
        return remote(
            self.part.at[z], self.land.at[slot], self.send.at[z], self.recv.at[slot], target, p.side
        )

    def arrived(self, slot, step):
        p = self.place
        target = p.index(p.z + step, p.x, p.c)
        remote(
            self.part.at[0], self.land.at[slot], self.send.at[0], self.recv.at[slot], target, p.side
        ).wait_recv()

    def take(self, z, step):
        self.arrived(z, step)
        add_rows(self.part.at[z], self.land.at[z], 0, self.part.shape[1])

    def run(self, number):
        here = self.place.z
        up, down = 3 - number, number

        @pl.when(up > here)
        def _():
            pl.when(here > 0)(lambda: self.take(up, -1))
            self.hop(up, 1).start()

        @pl.when(down < here)
        def _():
            pl.when(here < 3)(lambda: self.take(down, 1))
            self.hop(down, -1).start()

    def finish(self, out):
        here = self.place.z
        chunk = 16

        def take(slot, step):
            self.arrived(slot, step)

            @pl.loop(0, out.shape[0] // chunk)
            def _(index):
                cut = rows_of(index, chunk)
                out[cut] += self.land[slot, cut].astype(jnp.float32)

        @pl.loop(0, out.shape[0] // chunk)
        def _(index):
            cut = rows_of(index, chunk)
            out[cut] = self.part[here, cut].astype(jnp.float32)

        pl.when(here > 0)(lambda: take(here, -1))
        pl.when(here < 3)(lambda: take(4, 1))

        @pl.loop(0, 4)
        def _(z):
            pl.when(z > here)(lambda: self.hop(z, 1).wait_send())
            pl.when(z < here)(lambda: self.hop(z, -1).wait_send())


class WeightSwap:
    def __init__(self, place, pairs, send, recv, local, dp_count):
        self.place, self.pairs = place, pairs
        self.send, self.recv, self.local = send, recv, local
        self.dp_count = dp_count

    def copies(self, step, to, landing):
        out = []
        for i, (source, target) in enumerate(self.pairs):
            rows = source.shape[1]
            out.append(
                remote(
                    source.at[to],
                    target.at[pl.ds(pl.multiple_of(landing * rows, rows), rows)],
                    self.send.at[step, i],
                    self.recv.at[step, i],
                    to,
                    self.place.side,
                )
            )
        return out

    def own_copies(self):
        dp = self.place.dp
        return [
            pltpu.make_async_copy(
                source.at[dp],
                target.at[pl.ds(pl.multiple_of(dp * source.shape[1], source.shape[1]), source.shape[1])],
                self.local.at[i],
            )
            for i, (source, target) in enumerate(self.pairs)
        ]

    def start(self, low, high):
        @pl.loop(low, high)
        def _(step):
            for copy in self.copies(step, (self.place.dp + step) % self.dp_count, self.place.dp):
                copy.start()

    def start_own(self):
        for copy in self.own_copies():
            copy.start()

    def finish(self):
        @pl.loop(1, self.dp_count)
        def _(step):
            other = (self.place.dp + self.dp_count - step) % self.dp_count
            for copy in self.copies(step, other, other):
                copy.wait()

        for copy in self.own_copies():
            copy.wait()


def columns(tile, width=TILE):
    return pl.ds(pl.multiple_of(tile * width, width), width)


def rows_of(index, count):
    return pl.ds(pl.multiple_of(index * count, count), count)


def slot_labels(place, dp_count):
    row = lax.broadcasted_iota(jnp.int32, (8 * SLOTS, TILE), 0)
    member = row // SLOTS
    label = ((member // 4) * dp_count + place.z * 4 + member % 4) * SLOTS + row % SLOTS
    return label.astype(jnp.float32)


def front_kernel(
    bias_ref,
    tokens_ref,
    cotangent_ref,
    project_ref,
    out_ref,
    target_ref,
    route_ref,
    cosine_ref,
    sine_ref,
    gate_ref,
    up_ref,
    down_ref,
    project_full,
    out_full,
    keys_ref,
    query_ref,
    attended_ref,
    exact_ref,
    stat_ref,
    middle_ref,
    hidden_ref,
    probs_ref,
    rows_in,
    grads_in,
    gate_own,
    up_own,
    down_own,
    hidden_one,
    target_all,
    gate_all,
    keys_own,
    row_send,
    grad_send,
    gate_own_row,
    hidden_all,
    grad_all,
    placed,
    acc,
    top,
    project_send,
    project_recv,
    out_send,
    out_recv,
    keys_send,
    keys_recv,
    row_send_sem,
    row_recv_sem,
    row_local,
    grad_send_sem,
    grad_recv_sem,
    grad_local,
    column_send,
    column_recv,
    weight_send,
    weight_recv,
    weight_local,
    local,
):
    dp_count = keys_ref.shape[0]
    device_count = rows_in.shape[0] // SLOTS
    tok_count, model_width = tokens_ref.shape
    query_width = HEADS * HEAD
    key_width = KV_HEADS * HEAD
    repeat_heads = HEADS // KV_HEADS
    factor = log2e * HEAD ** (-0.5)
    place = Place()
    shard_rows = project_ref.shape[0]

    def shard_of(full):
        return lambda index: full.at[rows_of(index, shard_rows)]

    project = Gather(
        place, project_ref, shard_of(project_full), project_send, project_recv, local.at[0]
    )
    out = Gather(place, out_ref, shard_of(out_full), out_send, out_recv, local.at[1])
    keys = Gather(
        place, keys_own, lambda index: keys_ref.at[index], keys_send, keys_recv, local.at[2]
    )
    rows = PlaneSwap(place, row_send, rows_in, row_send_sem, row_recv_sem, row_local, dp_count)
    grads = PlaneSwap(place, grad_send, grads_in, grad_send_sem, grad_recv_sem, grad_local, dp_count)

    def column(number, own, land):
        return Column(
            place,
            own,
            land,
            column_send.at[number],
            lambda z: column_recv.at[number, z],
            local.at[3 + number],
        )

    targets = column(0, target_ref, lambda z: target_all.at[z])
    gates = column(1, gate_own_row, lambda z: gate_all.at[z])
    hidden = column(2, hidden_ref, lambda z: hidden_all.at[z, pl.ds(0, tok_count)])
    cotangents = column(3, cotangent_ref, lambda z: grad_all.at[z])
    weights = WeightSwap(
        place,
        ((gate_ref, gate_own), (up_ref, up_own), (down_ref, down_own)),
        weight_send,
        weight_recv,
        weight_local,
        dp_count,
    )

    enter(device_count, dp_count)
    targets.start()
    project.start()
    cotangents.start()
    plane_slots = 8 * SLOTS
    targets.forward()
    targets.own_copy().wait()
    slot_row = lax.broadcasted_iota(jnp.int32, (plane_slots, TILE), 0)
    slot_lane = lax.broadcasted_iota(jnp.int32, (plane_slots, TILE), 1)
    member = slot_row // SLOTS
    label = slot_labels(place, dp_count)
    spare = (slot_lane - tok_count == member) & (slot_row % SLOTS == CAP)

    def match(z, choice):
        return label == target_all[z, choice : choice + 1]

    for z in range(4):
        hit = spare
        for choice in range(TOP):
            hit = hit | match(z, choice)
        placed[z] = jnp.where(hit, 1.0, 0.0).astype(jnp.bfloat16)
    hidden_all[:, tok_count:] = jnp.zeros((4, PAD_TOKENS, model_width), jnp.bfloat16)

    project.forward_z()
    project.forward_x()
    project.finish()
    cotangents.forward(1, 2)

    lanes_of = one_hot((8, LANES), lambda row, column: column == row + EXPERTS)
    gains = dot_f32(lanes_of, project_full[:, query_width + 2 * key_width :], ((1,), (1,)))
    gain_first, gain_second = gains[0:1], gains[1:2]
    chunk = 32

    @pl.loop(0, tok_count // chunk)
    def _(index):
        value = tokens_ref[rows_of(index, chunk)].astype(jnp.float32)
        scale = lax.rsqrt(jnp.mean(value * value, axis=-1, keepdims=True) + epsilon)
        hidden_one[rows_of(index, chunk)] = (value * scale * gain_first).astype(jnp.bfloat16)

    def turned(tile):
        value = dot_f32(hidden_one[...], project_full[:, columns(tile)])
        halves = []
        for half in range(TILE // HEAD):
            part = value[:, half * HEAD : (half + 1) * HEAD]
            halves.append(
                part * cosine_ref[...] + pltpu.roll(part, HEAD // 2, 1) * sine_ref[...]
            )
        return jnp.concatenate(halves, axis=1).astype(jnp.bfloat16)

    keys_own[:, :key_width] = turned(query_width // TILE)
    keys_own[:, key_width:] = dot_f32(
        hidden_one[...], project_full[:, query_width + key_width : query_width + 2 * key_width]
    ).astype(jnp.bfloat16)
    keys.start()

    @pl.loop(0, query_width // TILE)
    def _(tile):
        query_ref[:, columns(tile)] = turned(tile)

    cotangents.forward(2, 3)

    keys.forward_z()
    keys.forward_x()
    keys.finish()
    out.start()
    weights.start(1, dp_count)
    weights.start_own()

    row = lax.broadcasted_iota(jnp.int32, (tok_count, tok_count), 0)
    column_index = lax.broadcasted_iota(jnp.int32, (tok_count, tok_count), 1)
    causal = column_index <= row
    ones = jnp.ones((tok_count, LANES), jnp.bfloat16)

    def visit(label, own):
        for group in range(KV_HEADS):
            key = keys_ref[label, :, group * HEAD : (group + 1) * HEAD]
            value = keys_ref[label, :, (KV_HEADS + group) * HEAD : (KV_HEADS + group + 1) * HEAD]
            value = jnp.concatenate([value, ones], axis=1)
            for head in range(group * repeat_heads, (group + 1) * repeat_heads):
                query = query_ref[:, head * HEAD : (head + 1) * HEAD]
                scores = dot_f32(query, key, ((1,), (1,))) * factor
                if own:
                    scores = jnp.where(causal, scores, -1e30)
                    peak = jnp.ceil(jnp.max(scores, axis=-1, keepdims=True))
                    shift = peak
                else:
                    bias = bias_ref[label]
                    peak = jnp.ceil(
                        jnp.maximum(top[head], jnp.max(scores, axis=-1, keepdims=True) + bias)
                    )
                    shift = peak - bias
                prob = jnp.exp2(scores - shift).astype(jnp.bfloat16)
                part = dot_f32(prob, value)
                if own:
                    acc[head] = part
                else:
                    acc[head] = acc[head] * jnp.exp2(top[head] - peak) + part
                top[head] = peak

    visit(place.dp, True)

    @pl.loop(0, place.dp)
    def _(label):
        visit(label, False)

    out.forward_z()
    out.forward_x()
    cotangents.forward(3, 4)
    cotangents.own_copy().wait()

    @pl.loop(0, 4)
    def _(z):
        @pl.loop(0, model_width // TILE)
        def _(tile):
            grad_send[z, :, columns(tile)] = dot_f32(
                placed[z, :, :tok_count], grad_all[z, :, columns(tile)]
            ).astype(jnp.bfloat16)

        grads.start(z)

    lane = lax.broadcasted_iota(jnp.int32, (tok_count, LANES), 1)
    stats = jnp.zeros((tok_count, LANES), jnp.float32)
    for head in range(HEADS):
        exact = acc[head, :, :HEAD] / acc[head, :, HEAD:]
        exact_ref[:, head * HEAD : (head + 1) * HEAD] = exact
        attended_ref[:, head * HEAD : (head + 1) * HEAD] = exact.astype(jnp.bfloat16)
        stats = jnp.where(lane == head, top[head], stats)
        stats = jnp.where(lane == HEADS + head, 1.0 / acc[head, :, HEAD:], stats)
    stat_ref[...] = stats
    out.finish()

    @pl.loop(0, model_width // TILE)
    def _(tile):
        middle_ref[:, columns(tile)] = tokens_ref[:, columns(tile)].astype(jnp.float32) + dot_f32(
            attended_ref[...], out_full[:, columns(tile)]
        )

    @pl.loop(0, tok_count // chunk)
    def _(index):
        value = middle_ref[rows_of(index, chunk)]
        scale = lax.rsqrt(jnp.mean(value * value, axis=-1, keepdims=True) + epsilon)
        hidden_ref[rows_of(index, chunk)] = (value * scale * gain_second).astype(jnp.bfloat16)

    hidden.start()
    router = project_full[:, query_width + 2 * key_width :]
    chosen = [route_ref[:, choice : choice + 1] == lane for choice in range(TOP)]
    mask = chosen[0]
    for choice in range(1, TOP):
        mask = mask | chosen[choice]
    logits = jnp.where(mask, dot_f32(hidden_ref[...], router), -1e30)
    weight = jnp.exp(logits - jnp.max(logits, axis=-1, keepdims=True))
    probs = weight / jnp.sum(weight, axis=-1, keepdims=True)
    probs_ref[...] = probs
    by_choice = jnp.zeros((tok_count, LANES), jnp.float32)
    for choice in range(TOP):
        gate = jnp.sum(jnp.where(chosen[choice], probs, 0.0), axis=-1, keepdims=True)
        by_choice = jnp.where(lane == choice, gate, by_choice)
    first_lanes = one_hot((8, LANES), lambda r, col: r == col)
    gate_own_row[...] = jnp.zeros(gate_own_row.shape, jnp.float32)
    gate_own_row[:, :tok_count] = sum(
        dot_f32(first_lanes, part, ((1,), (1,))) for part in split3(by_choice)
    )
    gates.start()
    fold = one_hot((8, plane_slots), lambda r, col: col // SLOTS == r)
    def dispatch(z):
        gate = jnp.zeros((plane_slots, 1), jnp.float32)
        for choice in range(TOP):
            gate += jnp.sum(
                jnp.where(match(z, choice), gate_all[z, choice : choice + 1], 0.0),
                axis=-1,
                keepdims=True,
            )
        numbers = dot_f32(fold, put_parts(gate)).astype(jnp.bfloat16)
        numbers = jnp.concatenate([numbers, jnp.zeros((8, LANES), jnp.bfloat16)], axis=0)
        hidden_all[z, tok_count : tok_count + 16, :LANES] = numbers

        @pl.loop(0, model_width // TILE)
        def _(tile):
            row_send[z, :, columns(tile)] = dot_f32(
                placed[z], hidden_all[z, :, columns(tile)]
            ).astype(jnp.bfloat16)

        rows.start(z)
    hidden.own_copy().wait()
    gates.own_copy().wait()
    dispatch(place.z)
    gates.forward()
    hidden.forward(then=dispatch)
    for gather in (targets, cotangents, hidden, gates):
        gather.finish()
    weights.finish()
    grads.finish()
    rows.finish()


def front(bias, tokens, cotangent, project, out, target, route, cosine, sine, gate, up, down):
    dp_count = lax.axis_size("dp")
    device_count = dp_count * lax.axis_size("expert")
    tok_count, model_width = tokens.shape
    query_width = HEADS * HEAD
    key_width = KV_HEADS * HEAD
    vmem = pl.BlockSpec(memory_space=pltpu.VMEM)
    anywhere = pl.BlockSpec(memory_space=pl.ANY)
    slots = device_count * SLOTS
    low, full = jnp.bfloat16, jnp.float32
    shape = jax.ShapeDtypeStruct
    ff_width = gate.shape[2]
    outs = (
        (shape((model_width, project.shape[1]), low), vmem),
        (shape((model_width, model_width), low), vmem),
        (shape((dp_count, tok_count, 2 * key_width), low), vmem),
        (shape((tok_count, query_width), low), vmem),
        (shape((tok_count, query_width), low), vmem),
        (shape((tok_count, query_width), full), vmem),
        (shape((tok_count, LANES), full), vmem),
        (shape((tok_count, model_width), full), vmem),
        (shape((tok_count, model_width), low), vmem),
        (shape((tok_count, LANES), full), vmem),
        (shape((slots, model_width), low), anywhere),
        (shape((slots, model_width), low), anywhere),
        (shape((model_width, ff_width), low), anywhere),
        (shape((model_width, ff_width), low), anywhere),
        (shape((ff_width, model_width), low), anywhere),
        (shape((tok_count, model_width), low), vmem),
        (shape((4, 8, TILE), full), vmem),
        (shape((4, 8, TILE), full), vmem),
    )
    dma = pltpu.SemaphoreType.DMA
    return pl.pallas_call(
        front_kernel,
        out_shape=tuple(o[0] for o in outs),
        in_specs=[pl.BlockSpec(memory_space=pltpu.SMEM)] + [vmem] * 8 + [anywhere] * 3,
        out_specs=tuple(o[1] for o in outs),
        scratch_shapes=[
            pltpu.VMEM((tok_count, 2 * key_width), low),
            pltpu.VMEM((4, 8 * SLOTS, model_width), low),
            pltpu.VMEM((4, 8 * SLOTS, model_width), low),
            pltpu.VMEM((8, TILE), full),
            pltpu.VMEM((4, tok_count + PAD_TOKENS, model_width), low),
            pltpu.VMEM((4, tok_count, model_width), low),
            pltpu.VMEM((4, 8 * SLOTS, TILE), low),
            pltpu.VMEM((HEADS, tok_count, 2 * HEAD), full),
            pltpu.VMEM((HEADS, tok_count, 1), full),
        ]
        + [dma((20,)), dma((dp_count,))] * 3
        + [dma((4, 8)), dma((4, 8)), dma((4,))] * 2
        + [dma((4, 8)), dma((4, 4))]
        + [dma((dp_count, 3))] * 2
        + [dma((3,)), dma((7,))],
        compiler_params=pltpu.CompilerParams(
            collective_id=0, has_side_effects=True, vmem_limit_bytes=58 * 1024 * 1024
        ),
    )(bias, tokens, cotangent, project, out, target, route, cosine, sine, gate, up, down)


def pick_gates(block):
    rows = block.shape[0]
    blocks = rows // SLOTS
    spare = one_hot((blocks, rows), lambda r, col: col == r * SLOTS + CAP)
    member = one_hot((rows, blocks), lambda r, col: r // SLOTS == col)
    parts = dot_f32(member, dot_f32(spare, block).astype(jnp.bfloat16))
    row = lax.broadcasted_iota(jnp.int32, parts.shape, 0)
    lane = lax.broadcasted_iota(jnp.int32, parts.shape, 1)
    mine = (lane % SLOTS == row % SLOTS) & (lane < 3 * SLOTS)
    return jnp.sum(jnp.where(mine, parts, 0.0), axis=-1, keepdims=True)


def put_parts(column):
    shape = (column.shape[0], LANES)
    row = lax.broadcasted_iota(jnp.int32, shape, 0)
    lane = lax.broadcasted_iota(jnp.int32, shape, 1)
    high, mid, low = (part.astype(jnp.float32) for part in split3(column))
    part = jnp.where(lane < SLOTS, high, jnp.where(lane < 2 * SLOTS, mid, low))
    mine = (lane % SLOTS == row % SLOTS) & (lane < 3 * SLOTS)
    return jnp.where(mine, part, 0.0).astype(jnp.bfloat16)


def expert_kernel(
    rows_ref,
    grads_ref,
    gate_ref,
    up_ref,
    down_ref,
    target_all,
    gate_all,
    row_sum,
    out_sum,
    gate_sum,
    gate_grad_ref,
    up_grad_ref,
    down_grad_ref,
    row_send,
    row_plane,
    row_part,
    row_land,
    out_send,
    out_plane,
    out_part,
    out_land,
    gate_part,
    gate_land,
    grad_out,
    inner_ref,
    gate_act_grad,
    up_act_grad,
    row_send_sem,
    row_recv_sem,
    row_local,
    out_send_sem,
    out_recv_sem,
    out_local,
    row_chain_send,
    row_chain_recv,
    out_chain_send,
    out_chain_recv,
    gate_send_sem,
    gate_recv_sem,
):
    dp_count = lax.axis_size("dp")
    slots, model_width = rows_ref.shape
    ff_width = gate_ref.shape[1]
    tok_count = row_sum.shape[0]
    device_count = slots // SLOTS
    place = Place()
    enter(device_count, dp_count)
    rows = PlaneSwap(place, row_send, row_plane, row_send_sem, row_recv_sem, row_local, dp_count)
    outs = PlaneSwap(place, out_send, out_plane, out_send_sem, out_recv_sem, out_local, dp_count)
    row_chain = Chain(place, row_part, row_land, row_chain_send, row_chain_recv)
    out_chain = Chain(place, out_part, out_land, out_chain_send, out_chain_recv)

    digits = 27 + 72 * place.z - 15 * (place.z // 2)

    def level(step):
        power = 1 + 3 * step + 9 * (step * (step - 1) // 2)
        power += 27 * (step * (step - 1) * (step - 2) // 6)
        return (digits // power) % 4

    @pl.loop(0, 4)
    def _(step):
        tile = level(step)
        cut = rows_of(tile, TILE)
        row = rows_ref[cut]
        gate = pick_gates(row[:, :LANES])
        saved = []
        for n in range(ff_width // TILE):
            part = slice(n * TILE, (n + 1) * TILE)
            gate_act = dot_f32(row, gate_ref[:, part])
            up_act = dot_f32(row, up_ref[:, part])
            sigmoid = 1.0 / (1.0 + jnp.exp(-gate_act))
            swish = gate_act * sigmoid
            inner_ref[cut, part] = (swish * up_act).astype(jnp.bfloat16)
            saved.append((swish, up_act * (sigmoid * (1.0 + gate_act * (1.0 - sigmoid)))))
        inner = inner_ref[cut]
        gate_grad = jnp.zeros((TILE, 1), jnp.float32)
        for n in range(model_width // TILE):
            part = slice(n * TILE, (n + 1) * TILE)
            expert_out = dot_f32(inner, down_ref[:, part]).astype(jnp.bfloat16)
            out_send[tile, :, part] = expert_out
            grad = grads_ref[cut, part].astype(jnp.float32)
            gate_grad += jnp.sum(expert_out.astype(jnp.float32) * grad, axis=-1, keepdims=True)
            grad_out[cut, part] = (gate * grad).astype(jnp.bfloat16)
        grad = grad_out[cut]
        for n in range(ff_width // TILE):
            part = slice(n * TILE, (n + 1) * TILE)
            swish, slope = saved[n]
            grad_inner = dot_f32(grad, down_ref[part, :], ((1,), (1,)))
            gate_act_grad[cut, part] = (grad_inner * slope).astype(jnp.bfloat16)
            up_act_grad[cut, part] = (grad_inner * swish).astype(jnp.bfloat16)
        blocks = TILE // SLOTS
        fold = one_hot((blocks, TILE), lambda r, col: col // SLOTS == r)
        spread = one_hot((TILE, blocks), lambda r, col: r == col * SLOTS + CAP)
        extra = dot_f32(spread, dot_f32(fold, put_parts(gate_grad)).astype(jnp.bfloat16))
        for n in range(model_width // TILE):
            part = slice(n * TILE, (n + 1) * TILE)
            back = dot_f32(gate_act_grad[cut], gate_ref[part, :], ((1,), (1,))) + dot_f32(
                up_act_grad[cut], up_ref[part, :], ((1,), (1,))
            )
            row_send[tile, :, part] = back.astype(jnp.bfloat16)
            if n == 0:
                row_send[tile, :, :LANES] = (back[:, :LANES] + extra).astype(jnp.bfloat16)
        rows.start(tile)

    @pl.loop(0, 4)
    def _(step):
        outs.start(level(step))

    label = slot_labels(place, dp_count)
    shape = (8 * SLOTS, LANES)
    member = lax.broadcasted_iota(jnp.int32, shape, 0) // SLOTS
    lane = lax.broadcasted_iota(jnp.int32, shape, 1)
    expert = (member // 4) * dp_count + place.z * 4 + member % 4

    def match(z, choice):
        return label == target_all[z, choice : choice + 1]

    def row_partial(step):
        z = level(step)
        rows.arrived(z)
        hit = match(z, 0)
        for choice in range(1, TOP):
            hit = hit | match(z, choice)
        placed = jnp.where(hit, 1.0, 0.0).astype(jnp.bfloat16)
        cut = rows_of(z, TILE)
        numbers = jnp.where(lane == expert, pick_gates(row_plane[cut, :LANES]), 0.0)
        gate_part[z] = sum(dot_f32(placed, part, ((0,), (0,))) for part in split3(numbers))[
            :tok_count
        ]
        for n in range(model_width // TILE):
            part = slice(n * TILE, (n + 1) * TILE)
            row_part[z, :, part] = dot_f32(placed, row_plane[cut, part], ((0,), (0,)))[
                :tok_count
            ].astype(jnp.bfloat16)

    row_partial(0)
    row_partial(1)
    row_chain.run(0)
    row_partial(2)
    row_chain.run(1)
    row_partial(3)
    row_chain.run(2)

    def gate_hop(i):
        z = place.others()[i]
        target = place.index(z, place.x, place.c)
        return remote(
            gate_part.at[z],
            gate_land.at[i],
            gate_send_sem.at[i],
            gate_recv_sem.at[i],
            target,
            place.side,
        )

    for i in range(3):
        gate_hop(i).start()

    def out_partial(step):
        z = level(step)
        outs.arrived(z)
        gates = jnp.zeros((8 * SLOTS, TILE), jnp.float32)
        for choice in range(TOP):
            gates += jnp.where(match(z, choice), gate_all[z, choice : choice + 1], 0.0)
        high = gates.astype(jnp.bfloat16)
        low = (gates - high.astype(jnp.float32)).astype(jnp.bfloat16)
        cut = rows_of(z, TILE)
        for n in range(model_width // TILE):
            part = slice(n * TILE, (n + 1) * TILE)
            out = out_plane[cut, part]
            value = dot_f32(high, out, ((0,), (0,))) + dot_f32(low, out, ((0,), (0,)))
            out_part[z, :, part] = value[:tok_count].astype(jnp.bfloat16)

    def weight_grad(target, act):
        @pl.loop(0, model_width // TILE)
        def _(tile):
            target[rows_of(tile, TILE)] = dot_f32(
                rows_ref[:, columns(tile)], act[...], ((0,), (0,))
            ).astype(jnp.bfloat16)

    out_partial(0)
    out_partial(1)
    out_chain.run(0)
    weight_grad(gate_grad_ref, gate_act_grad)
    out_partial(2)
    out_chain.run(1)
    weight_grad(up_grad_ref, up_act_grad)
    out_partial(3)
    out_chain.run(2)

    @pl.loop(0, ff_width // TILE)
    def _(tile):
        inner = inner_ref[:, columns(tile)]
        for n in range(model_width // ff_width):
            part = slice(n * ff_width, (n + 1) * ff_width)
            down_grad_ref[rows_of(tile, TILE), part] = dot_f32(
                inner, grad_out[:, part], ((0,), (0,))
            ).astype(jnp.bfloat16)

    row_chain.finish(row_sum)
    gate_sum[...] = gate_part[place.z]
    for i in range(3):
        gate_hop(i).wait()
        gate_sum[...] += gate_land[i]
    out_chain.finish(out_sum)
    rows.sent()
    outs.sent()


def experts(rows, grads, gate, up, down, target, gates, tok_count):
    slots, model_width = rows.shape
    ff_width = gate.shape[1]
    vmem = pl.BlockSpec(memory_space=pltpu.VMEM)
    low, full = jnp.bfloat16, jnp.float32
    shape = jax.ShapeDtypeStruct
    dma = pltpu.SemaphoreType.DMA
    return pl.pallas_call(
        expert_kernel,
        out_shape=(
            shape((tok_count, model_width), full),
            shape((tok_count, model_width), full),
            shape((tok_count, LANES), full),
            shape((model_width, ff_width), low),
            shape((model_width, ff_width), low),
            shape((ff_width, model_width), low),
        ),
        in_specs=[vmem] * 7,
        out_specs=(vmem,) * 6,
        scratch_shapes=[
            pltpu.VMEM((4, 8 * SLOTS, model_width), low),
            pltpu.VMEM((slots, model_width), low),
            pltpu.VMEM((4, tok_count, model_width), low),
            pltpu.VMEM((5, tok_count, model_width), low),
        ]
        * 2
        + [
            pltpu.VMEM((4, tok_count, LANES), full),
            pltpu.VMEM((3, tok_count, LANES), full),
            pltpu.VMEM((slots, model_width), low),
            pltpu.VMEM((slots, ff_width), low),
            pltpu.VMEM((slots, ff_width), low),
            pltpu.VMEM((slots, ff_width), low),
        ]
        + [dma((4, 8)), dma((4, 8)), dma((4,))] * 2
        + [dma((4,)), dma((5,))] * 2
        + [dma((3,))] * 2,
        compiler_params=pltpu.CompilerParams(
            collective_id=1, has_side_effects=True, vmem_limit_bytes=60 * 1024 * 1024
        ),
    )(rows, grads, gate, up, down, target, gates)


def halves_turned(value, cosine, sine):
    parts = []
    for half in range(value.shape[1] // HEAD):
        part = value[:, half * HEAD : (half + 1) * HEAD]
        parts.append(part * cosine + pltpu.roll(part, HEAD // 2, 1) * sine)
    return jnp.concatenate(parts, axis=1)


def gain_rows(small):
    lanes_of = one_hot((8, LANES), lambda row, column: column == row + EXPERTS)
    return dot_f32(lanes_of, small, ((1,), (1,)))


class Scatter:
    def __init__(self, place, block, lands, send, recvs):
        self.place, self.block = place, block
        self.lands, self.send, self.recvs = lands, send, recvs

    def hop_core(self, z, x):
        p = self.place
        number = z * 2 + x
        return remote(
            self.block(p.index(z, x, 1 - p.c)),
            self.lands[0].at[number],
            self.send.at[number],
            self.recvs[0].at[number],
            p.index(p.z, p.x, 1 - p.c),
            p.side,
        )

    def hop_x(self, z):
        p = self.place
        return remote(
            self.block(p.index(z, 1 - p.x, p.c)),
            self.lands[1].at[z],
            self.send.at[8 + z],
            self.recvs[1].at[z],
            p.index(p.z, 1 - p.x, p.c),
            p.side,
        )

    def hop_z(self, i):
        p = self.place
        z = p.others()[i]
        return remote(
            self.block(p.index(z, p.x, p.c)),
            self.lands[2].at[i],
            self.send.at[12 + i],
            self.recvs[2].at[i],
            p.index(z, p.x, p.c),
            p.side,
        )

    def add(self, shard, land):
        block = self.block(shard)
        chunk = 32

        @pl.loop(0, block.shape[0] // chunk)
        def _(index):
            cut = rows_of(index, chunk)
            block[cut] = (block[cut].astype(jnp.float32) + land[cut].astype(jnp.float32)).astype(
                jnp.bfloat16
            )

    def start(self):
        for z in range(4):
            for x in range(2):
                self.hop_core(z, x).start()

    def order(self):
        return self.place.others() + [self.place.z]

    def pass_core(self):
        p = self.place
        for z in self.order():
            for x in (1 - p.x, p.x):
                self.hop_core(z, x).wait_recv()
                self.add(p.index(z, x, p.c), self.lands[0].at[z * 2 + x])
            self.hop_x(z).start()

    def pass_x(self):
        p = self.place
        for i, z in enumerate(self.order()):
            self.hop_x(z).wait_recv()
            self.add(p.index(z, p.x, p.c), self.lands[1].at[z])
            if i < 3:
                self.hop_z(i).start()

    def pass_z(self, put):
        p = self.place
        for i in range(3):
            self.hop_z(i).wait_recv()
        block = self.block(p.dp)
        chunk = 32

        @pl.loop(0, block.shape[0] // chunk)
        def _(index):
            cut = rows_of(index, chunk)
            value = block[cut].astype(jnp.float32)
            for i in range(3):
                value += self.lands[2][i, cut].astype(jnp.float32)
            put(cut, value)

    def finish(self):
        for z in range(4):
            for x in range(2):
                self.hop_core(z, x).wait_send()
            self.hop_x(z).wait_send()
        for i in range(3):
            self.hop_z(i).wait_send()


def add_rows(block, land, low, count):
    chunk = 16

    @pl.loop(0, count // chunk)
    def _(index):
        cut = pl.ds(pl.multiple_of(low + index * chunk, chunk), chunk)
        value = block[cut].astype(jnp.float32) + land[rows_of(index, chunk)].astype(jnp.float32)
        block[cut] = value.astype(jnp.bfloat16)


class TotalSum:
    def __init__(self, place, part, lands, send, recv, x_first):
        self.place, self.part, self.lands = place, part, lands
        self.send, self.recv, self.x_first = send, recv, x_first
        self.rows = part.shape[1]
        self.half = self.rows // 2

    def kept(self, side):
        return pl.ds(pl.multiple_of(side * self.half, self.half), self.half)

    def hop(self, source, land, number, dp, side):
        return remote(source, land, self.send.at[number], self.recv.at[number], dp, side)

    def core(self, z, x):
        p = self.place
        return self.hop(
            self.part.at[p.index(z, x, 1 - p.c)],
            self.lands[0].at[z * 2 + x],
            z * 2 + x,
            p.index(p.z, p.x, 1 - p.c),
            p.side,
        )

    def over_x(self, z):
        p = self.place
        source = self.part.at[p.index(z, 1 - p.x, p.c)]
        if not self.x_first:
            source = source.at[self.kept(p.side)]
        return self.hop(source, self.lands[1].at[z], 8 + z, p.index(p.z, 1 - p.x, p.c), p.side)

    def over_side(self, z, x):
        p = self.place
        number = z if self.x_first else z * 2 + x
        return self.hop(
            self.part.at[p.index(z, x, p.c), self.kept(1 - p.side)],
            self.lands[2].at[number],
            12 + number,
            p.dp,
            1 - p.side,
        )

    def over_z(self, i):
        p = self.place
        z = p.others()[i]
        return self.hop(
            self.part.at[p.index(z, p.x, p.c), self.kept(p.side)],
            self.lands[3].at[i],
            20 + i,
            p.index(z, p.x, p.c),
            p.side,
        )

    def home(self):
        p = self.place
        block = self.part.at[p.dp, self.kept(p.side)]
        return self.hop(block, self.lands[4], 23, p.dp, 1 - p.side)

    def start(self, z):
        for x in range(2):
            self.core(z, x).start()

    def sides(self):
        return (self.place.x,) if self.x_first else (1 - self.place.x, self.place.x)

    def first(self, z):
        p = self.place
        for x in (1 - p.x, p.x):
            self.core(z, x).wait_recv()
            add_rows(self.part.at[p.index(z, x, p.c)], self.lands[0].at[z * 2 + x], 0, self.rows)
            if not self.x_first:
                self.over_side(z, x).start()
        if self.x_first:
            self.over_x(z).start()

    def take_side(self, z):
        p = self.place
        for x in self.sides():
            self.over_side(z, x).wait_recv()
            number = z if self.x_first else z * 2 + x
            add_rows(
                self.part.at[p.index(z, x, p.c)],
                self.lands[2].at[number],
                p.side * self.half,
                self.half,
            )

    def take_x(self, z):
        p = self.place
        self.over_x(z).wait_recv()
        low, count = (0, self.rows) if self.x_first else (p.side * self.half, self.half)
        add_rows(self.part.at[p.index(z, p.x, p.c)], self.lands[1].at[z], low, count)

    def second(self, z):
        if self.x_first:
            self.take_x(z)
            self.over_side(z, self.place.x).start()
        else:
            self.take_side(z)
            self.over_x(z).start()

    def third(self, z, i):
        if self.x_first:
            self.take_side(z)
        else:
            self.take_x(z)
        if i < 3:
            self.over_z(i).start()

    def fourth(self):
        p = self.place
        for i in range(3):
            self.over_z(i).wait_recv()
        chunk = 16

        @pl.loop(0, self.half // chunk)
        def _(index):
            cut = pl.ds(pl.multiple_of(p.side * self.half + index * chunk, chunk), chunk)
            value = self.part[p.dp, cut].astype(jnp.float32)
            for i in range(3):
                value += self.lands[3][i, rows_of(index, chunk)].astype(jnp.float32)
            self.part[p.dp, cut] = value.astype(jnp.bfloat16)

        self.home().start()

    def finish(self, mine, at):
        p = self.place
        mine[self.kept(p.side), at] = self.part[p.dp, self.kept(p.side)].astype(jnp.float32)
        self.home().wait()
        mine[self.kept(1 - p.side), at] = self.lands[4][...].astype(jnp.float32)
        for z in range(4):
            for x in range(2):
                self.core(z, x).wait_send()
            self.over_x(z).wait_send()
            for x in self.sides():
                self.over_side(z, x).wait_send()
        for i in range(3):
            self.over_z(i).wait_send()


class WeightReturn(WeightSwap):
    def copies(self, step, to, landing):
        out = []
        for i, (source, target) in enumerate(self.pairs):
            rows = target.shape[1]
            out.append(
                remote(
                    source.at[rows_of(to, rows)],
                    target.at[landing],
                    self.send.at[step, i],
                    self.recv.at[step, i],
                    to,
                    self.place.side,
                )
            )
        return out

    def own_copies(self):
        dp = self.place.dp
        return [
            pltpu.make_async_copy(
                source.at[rows_of(dp, target.shape[1])], target.at[dp], self.local.at[i]
            )
            for i, (source, target) in enumerate(self.pairs)
        ]


def back_kernel(
    bias_ref,
    cotangent_ref,
    middle_ref,
    probs_ref,
    exact_ref,
    stat_ref,
    query_ref,
    keys_ref,
    small_ref,
    out_ref,
    row_sum,
    out_sum,
    gate_sum,
    cosine_ref,
    sine_ref,
    gate_ref,
    up_ref,
    result_ref,
    grad_middle_ref,
    grad_branch_ref,
    grad_logits_ref,
    grad_project_ref,
    gain_ref,
    gate_back,
    up_back,
    grad_hidden,
    grad_ref,
    acc,
    delta,
    grad_keys_ref,
    land_core,
    land_x,
    land_z,
    scatter_send,
    recv_core,
    recv_x,
    recv_z,
    weight_send,
    weight_recv,
    weight_local,
):
    dp_count = keys_ref.shape[0]
    device_count = dp_count * lax.axis_size("expert")
    tok_count, model_width = middle_ref.shape
    query_width = HEADS * HEAD
    key_width = KV_HEADS * HEAD
    repeat_heads = HEADS // KV_HEADS
    scale = HEAD ** (-0.5)
    factor = log2e * scale
    chunk = 32
    place = Place()
    enter(device_count, dp_count)
    weights = WeightReturn(
        place,
        ((gate_ref, gate_back), (up_ref, up_back)),
        weight_send,
        weight_recv,
        weight_local,
        dp_count,
    )
    weights.start(1, dp_count)
    weights.start_own()
    scatter = Scatter(
        place,
        lambda index: grad_keys_ref.at[index],
        (land_core, land_x, land_z),
        scatter_send,
        (recv_core, recv_x, recv_z),
    )

    probs = probs_ref[...]
    grad_probs = gate_sum[...]
    grad_logits = (
        probs * (grad_probs - jnp.sum(probs * grad_probs, axis=-1, keepdims=True))
    ).astype(jnp.bfloat16)
    grad_logits_ref[...] = grad_logits

    @pl.loop(0, model_width // TILE)
    def _(tile):
        grad_hidden[:, columns(tile)] = row_sum[:, columns(tile)] + dot_f32(
            grad_logits_ref[...], small_ref[rows_of(tile, TILE)], ((1,), (1,))
        )

    gain = gain_rows(small_ref[...])[1:2]
    gain_ref[...] = jnp.zeros(gain_ref.shape, jnp.float32)

    @pl.loop(0, tok_count // chunk)
    def _(index):
        cut = rows_of(index, chunk)
        value = middle_ref[cut]
        row_scale = lax.rsqrt(jnp.mean(value * value, axis=-1, keepdims=True) + epsilon)
        normed = value * row_scale
        grad = grad_hidden[cut]
        gain_ref[0:1] += jnp.sum(grad * normed, axis=0, keepdims=True)
        grad = grad * gain
        total = cotangent_ref[cut].astype(jnp.float32) + row_scale * (
            grad - normed * jnp.mean(grad * normed, axis=-1, keepdims=True)
        )
        grad_middle_ref[cut] = total
        grad_branch_ref[cut] = total.astype(jnp.bfloat16)

    @pl.loop(0, model_width // TILE)
    def _(tile):
        grad_ref[:, columns(tile)] = dot_f32(
            grad_branch_ref[...], out_ref[rows_of(tile, TILE)], ((1,), (1,))
        ).astype(jnp.bfloat16)

    for head in range(HEADS):
        cut = slice(head * HEAD, (head + 1) * HEAD)
        scaled = (
            grad_ref[:, cut].astype(jnp.float32) * stat_ref[:, HEADS + head : HEADS + head + 1]
        ).astype(jnp.bfloat16)
        grad_ref[:, cut] = scaled
        delta[head] = jnp.sum(
            scaled.astype(jnp.float32) * exact_ref[:, cut], axis=-1, keepdims=True
        )
    row = lax.broadcasted_iota(jnp.int32, (tok_count, tok_count), 0)
    column = lax.broadcasted_iota(jnp.int32, (tok_count, tok_count), 1)
    causal = column <= row

    @pl.loop(place.dp + 1, dp_count)
    def _(label):
        grad_keys_ref[label] = jnp.zeros(grad_keys_ref.shape[1:], jnp.bfloat16)

    def visit(label, own):
        for group in range(KV_HEADS):
            key_cut = slice(group * HEAD, (group + 1) * HEAD)
            value_cut = slice((KV_HEADS + group) * HEAD, (KV_HEADS + group + 1) * HEAD)
            key = keys_ref[label, :, key_cut]
            value = keys_ref[label, :, value_cut]
            grad_key = jnp.zeros((tok_count, HEAD), jnp.float32)
            grad_value = jnp.zeros((tok_count, HEAD), jnp.float32)
            for head in range(group * repeat_heads, (group + 1) * repeat_heads):
                cut = slice(head * HEAD, (head + 1) * HEAD)
                query = query_ref[:, cut]
                grad = grad_ref[:, cut]
                shift = stat_ref[:, head : head + 1]
                if not own:
                    shift = shift - bias_ref[label]
                scores = dot_f32(query, key, ((1,), (1,)))
                prob = jnp.exp2(scores * factor - shift)
                if own:
                    prob = jnp.where(causal, prob, 0.0)
                prob = prob.astype(jnp.bfloat16)
                grad_prob = dot_f32(grad, value, ((1,), (1,)))
                grad_score = (prob.astype(jnp.float32) * (grad_prob - delta[head])).astype(
                    jnp.bfloat16
                )
                grad_value += dot_f32(prob, grad, ((0,), (0,)))
                grad_key += dot_f32(grad_score, query, ((0,), (0,)))
                grad_query = dot_f32(grad_score, key)
                if own:
                    acc[head] = grad_query
                else:
                    acc[head] += grad_query
            grad_keys_ref[label, :, key_cut] = (grad_key * scale).astype(jnp.bfloat16)
            grad_keys_ref[label, :, value_cut] = grad_value.astype(jnp.bfloat16)

    visit(place.dp, True)

    @pl.loop(0, place.dp)
    def _(label):
        visit(label, False)

    scatter.start()
    cosine, sine = cosine_ref[...], -sine_ref[...]
    for head in range(HEADS):
        grad_project_ref[:, head * HEAD : (head + 1) * HEAD] = halves_turned(
            acc[head] * scale, cosine, sine
        ).astype(jnp.bfloat16)
    scatter.pass_core()
    scatter.pass_x()

    result_ref[...] = (middle_ref[...] + out_sum[...]).astype(jnp.bfloat16)

    def put(cut, value):
        grad_project_ref[cut, query_width : query_width + key_width] = halves_turned(
            value[:, :key_width], cosine_ref[cut], -sine_ref[cut]
        ).astype(jnp.bfloat16)
        grad_project_ref[cut, query_width + key_width :] = value[:, key_width:].astype(jnp.bfloat16)

    scatter.pass_z(put)
    scatter.finish()
    weights.finish()


def back(
    bias, cotangent, middle, probs, exact, stats, query, keys, small, out, row_sum, out_sum, gate_sum,
    cosine, sine, gate_grad, up_grad, shard,
):
    dp_count, tok_count, both = keys.shape
    model_width = middle.shape[1]
    ff_width = gate_grad.shape[1]
    vmem = pl.BlockSpec(memory_space=pltpu.VMEM)
    anywhere = pl.BlockSpec(memory_space=pl.ANY)
    low, full = jnp.bfloat16, jnp.float32
    shape = jax.ShapeDtypeStruct
    dma = pltpu.SemaphoreType.DMA
    return pl.pallas_call(
        back_kernel,
        out_shape=(
            shape((tok_count, model_width), low),
            shape((tok_count, model_width), full),
            shape((tok_count, model_width), low),
            shape((tok_count, LANES), low),
            shape((tok_count, query.shape[1] + both), low),
            shape((8, model_width), full),
            shape((dp_count, shard, ff_width), low),
            shape((dp_count, shard, ff_width), low),
        ),
        in_specs=[pl.BlockSpec(memory_space=pltpu.SMEM)] + [vmem] * 14 + [anywhere] * 2,
        out_specs=(vmem,) * 6 + (anywhere,) * 2,
        scratch_shapes=[
            pltpu.VMEM((tok_count, model_width), full),
            pltpu.VMEM((tok_count, model_width), low),
            pltpu.VMEM((HEADS, tok_count, HEAD), full),
            pltpu.VMEM((HEADS, tok_count, 1), full),
            pltpu.VMEM((dp_count, tok_count, both), low),
            pltpu.VMEM((8, tok_count, both), low),
            pltpu.VMEM((4, tok_count, both), low),
            pltpu.VMEM((3, tok_count, both), low),
            dma((15,)),
            dma((8,)),
            dma((4,)),
            dma((3,)),
            dma((dp_count, 2)),
            dma((dp_count, 2)),
            dma((2,)),
        ],
        compiler_params=pltpu.CompilerParams(
            collective_id=2, has_side_effects=True, vmem_limit_bytes=60 * 1024 * 1024
        ),
    )(
        bias, cotangent, middle, probs, exact, stats, query, keys, small, out, row_sum, out_sum, gate_sum,
        cosine, sine, gate_grad, up_grad,
    )


def finish_kernel(
    tokens_ref,
    hidden_one,
    hidden_two,
    attended_ref,
    grad_middle_ref,
    grad_branch_ref,
    grad_logits_ref,
    grad_project_ref,
    gain_ref,
    project_ref,
    down_ref,
    grad_tokens_ref,
    mine_ref,
    down_back,
    grad_hidden,
    gain_one,
    part_one,
    core_one,
    x_one,
    side_one,
    z_one,
    home_one,
    part_two,
    core_two,
    x_two,
    side_two,
    z_two,
    home_two,
    send_one,
    recv_one,
    send_two,
    recv_two,
    weight_send,
    weight_recv,
    weight_local,
):
    tok_count, model_width = tokens_ref.shape
    width = grad_project_ref.shape[1]
    dp_count = lax.axis_size("dp")
    device_count = dp_count * lax.axis_size("expert")
    shard = mine_ref.shape[0]
    place = Place()
    chunk = 32
    enter(device_count, dp_count)
    weights = WeightReturn(
        place, ((down_ref, down_back),), weight_send, weight_recv, weight_local, dp_count
    )
    weights.start(1, dp_count)
    weights.start_own()
    one = TotalSum(place, part_one, (core_one, x_one, side_one, z_one, home_one), send_one, recv_one, True)
    two = TotalSum(place, part_two, (core_two, x_two, side_two, z_two, home_two), send_two, recv_two, False)
    cut_at = part_one.shape[2]

    @pl.loop(0, model_width // TILE)
    def _(tile):
        grad_hidden[:, columns(tile)] = dot_f32(
            grad_project_ref[...], project_ref[rows_of(tile, TILE), :width], ((1,), (1,))
        )

    gain = gain_rows(project_ref[:, width:])[0:1]
    gain_one[...] = jnp.zeros(gain_one.shape, jnp.float32)

    @pl.loop(0, tok_count // chunk)
    def _(index):
        cut = rows_of(index, chunk)
        value = tokens_ref[cut].astype(jnp.float32)
        row_scale = lax.rsqrt(jnp.mean(value * value, axis=-1, keepdims=True) + epsilon)
        normed = value * row_scale
        grad = grad_hidden[cut]
        gain_one[0:1] += jnp.sum(grad * normed, axis=0, keepdims=True)
        grad = grad * gain
        grad_tokens_ref[cut] = grad_middle_ref[cut] + row_scale * (
            grad - normed * jnp.mean(grad * normed, axis=-1, keepdims=True)
        )

    one_lane = one_hot((8, LANES), lambda r, col: (r == 0) & (col == EXPERTS))
    two_lane = one_hot((8, LANES), lambda r, col: (r == 0) & (col == EXPERTS + 1))
    group = 4 * shard

    @pl.loop(0, model_width // group)
    def _(index):
        cut = columns(index, group)

        def put(part, low, value):
            for i in range(4):
                part[index * 4 + i, :, low : low + value.shape[1]] = value[
                    i * shard : (i + 1) * shard
                ].astype(jnp.bfloat16)

        left = hidden_one[:, cut]
        step = 3 * LANES
        for low in range(0, cut_at, step):
            put(part_one, low, dot_f32(left, grad_project_ref[:, low : low + step], ((0,), (0,))))
        rest = width - cut_at
        put(part_two, 0, dot_f32(left, grad_project_ref[:, cut_at:], ((0,), (0,))))
        small = dot_f32(hidden_two[:, cut], grad_logits_ref[...], ((0,), (0,)))
        for part in split3(gain_one[:, cut]):
            small += dot_f32(part, one_lane, ((0,), (0,)))
        for part in split3(gain_ref[:, cut]):
            small += dot_f32(part, two_lane, ((0,), (0,)))
        put(part_two, rest, small)
        left = attended_ref[:, cut]
        for low in range(0, model_width, step):
            put(
                part_two,
                rest + LANES + low,
                dot_f32(left, grad_branch_ref[:, low : low + step], ((0,), (0,))),
            )
        for total in (one, two):
            total.start(index)

    order = place.others() + [place.z]
    both = (one, two)
    for z in order:
        for total in both:
            total.first(z)
    for z in order:
        for total in both:
            total.second(z)
    for i, z in enumerate(order):
        for total in both:
            total.third(z, i)
    for total in both:
        total.fourth()
    one.finish(mine_ref, slice(0, cut_at))
    two.finish(mine_ref, slice(cut_at, mine_ref.shape[1]))
    weights.finish()


def finish(
    tokens, hidden_one, hidden_two, attended, grad_middle, grad_branch, grad_logits, grad_project,
    gain, project, down_grad, shard, half,
):
    tok_count, model_width = tokens.shape
    dp_count = lax.axis_size("dp")
    width = project.shape[1] + model_width
    first = 15 * LANES
    vmem = pl.BlockSpec(memory_space=pltpu.VMEM)
    anywhere = pl.BlockSpec(memory_space=pl.ANY)
    low, full = jnp.bfloat16, jnp.float32
    shape = jax.ShapeDtypeStruct
    dma = pltpu.SemaphoreType.DMA
    return pl.pallas_call(
        finish_kernel,
        out_shape=(
            shape((tok_count, model_width), full),
            shape((shard, width), full),
            shape((dp_count, half, model_width), low),
        ),
        in_specs=[vmem] * 10 + [anywhere],
        out_specs=(vmem, vmem, anywhere),
        scratch_shapes=[
            pltpu.VMEM((tok_count, model_width), full),
            pltpu.VMEM((8, model_width), full),
            *(
                pltpu.VMEM(lead + (columns_of,), low)
                for columns_of, lead in (
                    (first, (dp_count, shard)),
                    (first, (8, shard)),
                    (first, (4, shard)),
                    (first, (4, shard // 2)),
                    (first, (3, shard // 2)),
                    (first, (shard // 2,)),
                    (width - first, (dp_count, shard)),
                    (width - first, (8, shard)),
                    (width - first, (4, shard // 2)),
                    (width - first, (8, shard // 2)),
                    (width - first, (3, shard // 2)),
                    (width - first, (shard // 2,)),
                )
            ),
            dma((24,)),
            dma((24,)),
            dma((24,)),
            dma((24,)),
            dma((dp_count, 1)),
            dma((dp_count, 1)),
            dma((1,)),
        ],
        compiler_params=pltpu.CompilerParams(
            collective_id=3, has_side_effects=True, vmem_limit_bytes=58 * 1024 * 1024
        ),
    )(
        tokens, hidden_one, hidden_two, attended, grad_middle, grad_branch, grad_logits,
        grad_project, gain, project, down_grad,
    )


def local_owned(
    tokens,
    attn_gain,
    query_weight,
    key_weight,
    value_weight,
    out_weight,
    moe_gain,
    router_weight,
    gate_weight,
    up_weight,
    down_weight,
    parents,
    routes,
    claim_order,
    cotangent,
):
    tok_count = tokens.shape[1]
    segment = lax.axis_index("dp")
    query_width = HEADS * HEAD
    key_width = KV_HEADS * HEAD

    route_rows = routes[0]
    expert_ids = route_rows.reshape(-1)
    order_row = claim_order[0, 0]
    member = (expert_ids[:, None] == jnp.arange(EXPERTS, dtype=jnp.int32)[None, :]).astype(
        jnp.bfloat16
    )
    earlier = (order_row[None, :] < order_row[:, None]).astype(jnp.bfloat16)
    before = jnp.dot(earlier, member, preferred_element_type=jnp.float32)
    slot_index = jnp.sum(before * member.astype(jnp.float32), axis=1).astype(jnp.int32)
    target = jnp.where(slot_index < CAP, expert_ids * SLOTS + slot_index, -1).reshape(
        tok_count, TOP
    )
    target_rows = jnp.full((8, TILE), -1.0, jnp.float32)
    target_rows = target_rows.at[:TOP, :tok_count].set(target.T.astype(jnp.float32))
    route_lanes = jnp.pad(route_rows, ((0, 0), (0, LANES - TOP)), constant_values=-1)

    small = jnp.concatenate(
        [
            router_weight,
            attn_gain[:, None],
            moe_gain[:, None],
            jnp.zeros((router_weight.shape[0], LANES - EXPERTS - 2), jnp.bfloat16),
        ],
        axis=1,
    )
    project_shard = jnp.concatenate([query_weight, key_weight, value_weight, small], axis=1)
    reach_row = ancestry(parents[0])[segment]
    path_depth = jnp.sum(reach_row) - 1.0
    positions = path_depth * tok_count + jnp.arange(tok_count, dtype=jnp.float32)
    cosine, sine_part = rope_tables(positions, HEAD)
    cosine_wide = jnp.concatenate([cosine[:, 0], cosine[:, 0]], axis=1)
    sine_wide = jnp.concatenate([-sine_part[:, 0], sine_part[:, 0]], axis=1)
    on_path = reach_row > 0.5
    bias = jnp.where(on_path, 0.0, -1e30).astype(jnp.float32)
    (
        project_full,
        out_full,
        keys,
        query_rot,
        attended,
        exact_out,
        stats,
        middle,
        hidden_two,
        probs,
        rows_in,
        grad_rows_in,
        gate_own,
        up_own,
        down_own,
        hidden_one,
        target_all,
        gate_all,
    ) = front(
        bias,
        tokens[0],
        cotangent[0],
        project_shard,
        out_weight,
        target_rows,
        route_lanes,
        cosine_wide,
        sine_wide,
        gate_weight,
        up_weight,
        down_weight,
    )
    small_at = query_width + 2 * key_width
    row_sum, out_sum, gate_sum, gate_grad, up_grad, down_grad = experts(
        rows_in, grad_rows_in, gate_own, up_own, down_own, target_all, gate_all, tok_count
    )
    (
        block_out,
        grad_middle,
        grad_branch,
        grad_logits,
        grad_project,
        gain_row,
        gate_back,
        up_back,
    ) = back(
        bias,
        cotangent[0],
        middle,
        probs,
        exact_out,
        stats,
        query_rot,
        keys,
        project_full[:, small_at:],
        out_full,
        row_sum,
        out_sum,
        gate_sum,
        cosine_wide,
        sine_wide,
        gate_grad,
        up_grad,
        gate_weight.shape[1],
    )
    grad_tokens, mine, down_back = finish(
        tokens[0],
        hidden_one,
        hidden_two,
        attended,
        grad_middle,
        grad_branch,
        grad_logits,
        grad_project,
        gain_row,
        project_full,
        down_grad,
        query_weight.shape[0],
        down_weight.shape[1],
    )
    return (
        block_out[None],
        grad_tokens[None],
        mine[:, small_at + EXPERTS],
        mine[:, :query_width],
        mine[:, query_width : query_width + key_width],
        mine[:, query_width + key_width : small_at],
        mine[:, small_at + LANES :],
        mine[:, small_at + EXPERTS + 1],
        mine[:, small_at : small_at + EXPERTS],
        gate_back.astype(jnp.float32),
        up_back.astype(jnp.float32),
        down_back.astype(jnp.float32),
    )


def solution(mesh):
    placed = (
        P("expert", "dp", None),
        P("dp"),
        P("dp", None),
        P("dp", None),
        P("dp", None),
        P("dp", None),
        P("dp"),
        P("dp", None),
        P("expert", "dp", None),
        P("expert", "dp", None),
        P("expert", "dp", None),
        P("expert", None),
        P("expert", "dp", None),
        P("expert", "dp", None),
        P("expert", "dp", None),
    )
    owned = mesh.shape["dp"] == 16 and mesh.shape["expert"] == 2
    return jax.shard_map(
        local_owned if owned else local_gathered,
        mesh=mesh,
        in_specs=placed,
        out_specs=(
            P("expert", "dp", None),
            P("expert", "dp", None),
            P("dp"),
            P("dp", None),
            P("dp", None),
            P("dp", None),
            P("dp", None),
            P("dp"),
            P("dp", None),
            P("expert", "dp", None),
            P("expert", "dp", None),
            P("expert", "dp", None),
        ),
        check_vma=False,
    )
```

```python
import functools

import jax
import jax.numpy as jnp
from jax import lax
from jax.experimental import pallas as pl
from jax.experimental.pallas import tpu as pltpu
from jax.sharding import PartitionSpec as P

HEADS = 12
KV_HEADS = 2
HEAD = 128
EXPERTS = 32
TOP = 4
CAP = 28


epsilon = 1e-06
theta = 10000.0
highest = lax.Precision.HIGHEST


def ancestry(parents):
    row_count = parents.shape[0]
    labels = jnp.arange(row_count, dtype=jnp.int32)
    linked = (parents[:, None] == labels[None, :]).astype(jnp.float32)
    reach_all = jnp.minimum(jnp.eye(row_count, dtype=jnp.float32) + linked, 1.0)
    for doubling in range(max(1, (row_count - 1).bit_length())):
        reach_all = jnp.minimum(jnp.dot(reach_all, reach_all, precision=highest), 1.0)
    return reach_all


def rope_tables(positions, head_size):
    halfway = head_size // 2
    frequency = theta ** (-jnp.arange(halfway, dtype=jnp.float32) * 2.0 / head_size)
    angles = positions[:, None] * frequency[None, :]
    return (jnp.cos(angles)[:, None, :], jnp.sin(angles)[:, None, :])


def rotate(values, cosine, sine_part):
    halfway = values.shape[-1] // 2
    first_half = values[..., :halfway]
    second = values[..., halfway:]
    return jnp.concatenate(
        [first_half * cosine - second * sine_part, second * cosine + first_half * sine_part],
        axis=-1,
    )


def norm_backward(grad_hidden, normed, row_scale, gain):
    grad_normed = grad_hidden * gain
    grad_gain = jnp.sum(grad_hidden * normed, axis=0)
    grad_rows = row_scale * (
        grad_normed - normed * jnp.mean(grad_normed * normed, axis=-1, keepdims=True)
    )
    return (grad_rows, grad_gain)


def local_gathered(
    tokens,
    attn_gain,
    query_weight,
    key_weight,
    value_weight,
    out_weight,
    moe_gain,
    router_weight,
    gate_weight,
    up_weight,
    down_weight,
    parents,
    routes,
    claim_order,
    cotangent,
):
    (
        gain_one,
        query_full,
        key_full,
        value_full,
        out_full,
        gain_two,
        router_full,
        gate_full,
        up_full,
        down_full,
    ) = (
        lax.all_gather(attn_gain, "dp", axis=0, tiled=True),
        lax.all_gather(query_weight, "dp", axis=0, tiled=True),
        lax.all_gather(key_weight, "dp", axis=0, tiled=True),
        lax.all_gather(value_weight, "dp", axis=0, tiled=True),
        lax.all_gather(out_weight, "dp", axis=0, tiled=True),
        lax.all_gather(moe_gain, "dp", axis=0, tiled=True),
        lax.all_gather(router_weight, "dp", axis=0, tiled=True),
        lax.all_gather(gate_weight, "dp", axis=1, tiled=True),
        lax.all_gather(up_weight, "dp", axis=1, tiled=True),
        lax.all_gather(down_weight, "dp", axis=1, tiled=True),
    )
    tok_count = tokens.shape[1]
    model_width = tokens.shape[2]
    segment = lax.axis_index("dp")
    segment_count = lax.axis_size("dp")
    expert_peers = lax.axis_size("expert")
    local_experts = gate_weight.shape[0]
    repeat_heads = HEADS // KV_HEADS
    score_scale = HEAD ** (-0.5)
    query_rows = repeat_heads * tok_count
    reach_all = ancestry(parents[0])
    reach_row = reach_all[segment]
    path_depth = jnp.sum(reach_row) - 1.0
    positions = path_depth * tok_count + jnp.arange(tok_count, dtype=jnp.float32)
    cosine, sine_part = rope_tables(positions, HEAD)
    inputs = tokens[0].astype(jnp.float32)
    scale_one = lax.rsqrt(jnp.mean(inputs * inputs, axis=-1, keepdims=True) + epsilon)
    normed_one = inputs * scale_one
    gain_first = gain_one.astype(jnp.float32)
    hidden_one = (normed_one * gain_first).astype(jnp.bfloat16)
    query_raw = jnp.dot(hidden_one, query_full, preferred_element_type=jnp.float32).reshape(
        tok_count, HEADS, HEAD
    )
    key_raw = jnp.dot(hidden_one, key_full, preferred_element_type=jnp.float32).reshape(
        tok_count, KV_HEADS, HEAD
    )
    value_low = jnp.dot(hidden_one, value_full, preferred_element_type=jnp.float32).astype(
        jnp.bfloat16
    )
    query_rot = rotate(query_raw, cosine, sine_part).astype(jnp.bfloat16)
    key_rot = (
        rotate(key_raw, cosine, sine_part).astype(jnp.bfloat16).reshape(tok_count, KV_HEADS * HEAD)
    )
    key_all, value_all = (
        lax.all_gather(key_rot, "dp", axis=0, tiled=True),
        lax.all_gather(value_low, "dp", axis=0, tiled=True),
    )
    total_keys = key_all.shape[0]
    key_blocks = key_all.reshape(segment_count, tok_count, KV_HEADS, HEAD)
    value_blocks = value_all.reshape(segment_count, tok_count, KV_HEADS, HEAD)
    segment_labels = jnp.arange(segment_count, dtype=jnp.int32)
    query_groups = (
        query_rot.reshape(tok_count, KV_HEADS, repeat_heads, HEAD)
        .transpose(1, 2, 0, 3)
        .reshape(KV_HEADS, query_rows, HEAD)
    )
    query_offsets = jnp.arange(tok_count, dtype=jnp.int32)
    causal_tile = jnp.tile(query_offsets[None, :] <= query_offsets[:, None], (repeat_heads, 1))

    def scores_of(key_block, label):
        raw_scores = (
            jnp.einsum("grh,kgh->grk", query_groups, key_block, preferred_element_type=jnp.float32)
            * score_scale
        )
        allowed = causal_tile | (label != segment)
        return jnp.where(allowed[None], raw_scores, -1000000000.0)

    def on_path(label):
        return reach_row[label] > 0.5

    def pass_stats(state_pair, inputs_block):
        key_block, value_block, label = inputs_block

        def visit(state):
            row_max, row_sum = state
            scores = scores_of(key_block, label)
            new_max = jnp.maximum(row_max, jnp.max(scores, axis=-1))
            new_sum = row_sum * jnp.exp(row_max - new_max) + jnp.sum(
                jnp.exp(scores - new_max[..., None]), axis=-1
            )
            return (new_max, new_sum)

        return (lax.cond(on_path(label), visit, lambda state: state, state_pair), None)

    start_max = jnp.full((KV_HEADS, query_rows), -1e30, jnp.float32)
    start_sum = jnp.zeros((KV_HEADS, query_rows), jnp.float32)
    (row_max, row_sum), unused = lax.scan(
        pass_stats, (start_max, start_sum), (key_blocks, value_blocks, segment_labels)
    )

    def probs_of(key_block, label):
        return jnp.exp(scores_of(key_block, label) - row_max[..., None]) / row_sum[..., None]

    def pass_values(state_pair, inputs_block):
        key_block, value_block, label = inputs_block

        def visit(state):
            accumulated, exact_out = state
            prob_block = probs_of(key_block, label)
            accumulated = accumulated + jnp.einsum(
                "grk,kgh->grh",
                prob_block.astype(jnp.bfloat16),
                value_block,
                preferred_element_type=jnp.float32,
            )
            exact_out = exact_out + jnp.einsum(
                "grk,kgh->grh",
                prob_block,
                value_block.astype(jnp.float32),
                preferred_element_type=jnp.float32,
                precision=highest,
            )
            return (accumulated, exact_out)

        return (lax.cond(on_path(label), visit, lambda state: state, state_pair), None)

    zero_out = jnp.zeros((KV_HEADS, query_rows, HEAD), jnp.float32)
    (accumulated, exact_out), unused = lax.scan(
        pass_values, (zero_out, zero_out), (key_blocks, value_blocks, segment_labels)
    )
    attended = (
        accumulated.reshape(KV_HEADS, repeat_heads, tok_count, HEAD)
        .transpose(2, 0, 1, 3)
        .reshape(tok_count, HEADS * HEAD)
        .astype(jnp.bfloat16)
    )
    branch = jnp.dot(attended, out_full, preferred_element_type=jnp.float32)
    middle = inputs + branch
    scale_two = lax.rsqrt(jnp.mean(middle * middle, axis=-1, keepdims=True) + epsilon)
    normed_two = middle * scale_two
    gain_second = gain_two.astype(jnp.float32)
    hidden_two = (normed_two * gain_second).astype(jnp.bfloat16)
    logits = jnp.dot(hidden_two, router_full, preferred_element_type=jnp.float32)
    picked_one = (
        routes[0][:, :, None] == jnp.arange(EXPERTS, dtype=jnp.int32)[None, None, :]
    ).astype(jnp.float32)
    chosen = jnp.sum(picked_one * logits[:, None, :], axis=-1)
    gate_probs = jax.nn.softmax(chosen, axis=-1)
    expert_ids = routes[0].reshape(-1)
    order_row = claim_order[0, 0]
    pair_count = expert_ids.shape[0]
    member = (expert_ids[:, None] == jnp.arange(EXPERTS, dtype=jnp.int32)[None, :]).astype(
        jnp.bfloat16
    )
    earlier = (order_row[None, :] < order_row[:, None]).astype(jnp.bfloat16)
    before = jnp.dot(earlier, member, preferred_element_type=jnp.float32)
    slot_index = jnp.sum(before * member.astype(jnp.float32), axis=1).astype(jnp.int32)
    owner_rank = expert_ids // local_experts
    local_rank = expert_ids % local_experts
    target = jnp.where(
        slot_index < CAP, (local_rank * expert_peers + owner_rank) * CAP + slot_index, EXPERTS * CAP
    )
    slot_pairs = (
        jnp.full((EXPERTS * CAP + 1,), pair_count, jnp.int32)
        .at[target]
        .set(jnp.arange(pair_count, dtype=jnp.int32))[: EXPERTS * CAP]
    )
    padded_two = jnp.concatenate([hidden_two, jnp.zeros((1, model_width), jnp.bfloat16)], axis=0)
    send_rows = padded_two[slot_pairs // TOP].reshape(local_experts, expert_peers, CAP, model_width)
    arrived = lax.all_to_all(send_rows, "expert", split_axis=1, concat_axis=1, tiled=True)
    expert_rows = arrived.reshape(local_experts, expert_peers * CAP, model_width)
    gate_act = jnp.einsum(
        "erd,edf->erf", expert_rows, gate_full, preferred_element_type=jnp.float32
    )
    up_act = jnp.einsum("erd,edf->erf", expert_rows, up_full, preferred_element_type=jnp.float32)
    inner = (jax.nn.silu(gate_act) * up_act).astype(jnp.bfloat16)
    expert_out = jnp.einsum(
        "erf,efd->erd", inner, down_full, preferred_element_type=jnp.float32
    ).astype(jnp.bfloat16)
    returned = lax.all_to_all(
        expert_out.reshape(local_experts, expert_peers, CAP, model_width),
        "expert",
        split_axis=1,
        concat_axis=1,
        tiled=True,
    )
    returned = jnp.concatenate(
        [returned.reshape(EXPERTS * CAP, model_width), jnp.zeros((1, model_width), jnp.bfloat16)],
        axis=0,
    )
    pair_out = returned[target].reshape(tok_count, TOP, model_width).astype(jnp.float32)
    mixture = jnp.sum(gate_probs[:, :, None] * pair_out, axis=1)
    block_out = (middle + mixture).astype(jnp.bfloat16)
    grad_result = cotangent[0].astype(jnp.float32)
    grad_gates = jnp.sum(pair_out * grad_result[:, None, :], axis=-1)
    grad_pairs = (
        (gate_probs[:, :, None] * grad_result[:, None, :])
        .astype(jnp.bfloat16)
        .reshape(pair_count, model_width)
    )
    grad_padded = jnp.concatenate([grad_pairs, jnp.zeros((1, model_width), jnp.bfloat16)], axis=0)
    grad_send = grad_padded[slot_pairs].reshape(local_experts, expert_peers, CAP, model_width)
    grad_arrived, rows_back = (
        lax.all_to_all(grad_send, "expert", split_axis=1, concat_axis=1, tiled=True),
        lax.all_to_all(send_rows, "expert", split_axis=1, concat_axis=1, tiled=True),
    )
    rows_again = rows_back.reshape(local_experts, expert_peers * CAP, model_width)
    gate_again = jnp.einsum(
        "erd,edf->erf", rows_again, gate_full, preferred_element_type=jnp.float32
    )
    up_again = jnp.einsum("erd,edf->erf", rows_again, up_full, preferred_element_type=jnp.float32)
    inner_again = (jax.nn.silu(gate_again) * up_again).astype(jnp.bfloat16)
    grad_expert_out = grad_arrived.reshape(local_experts, expert_peers * CAP, model_width)
    grad_inner = jnp.einsum(
        "erd,efd->erf", grad_expert_out, down_full, preferred_element_type=jnp.float32
    )
    grad_down_local = jnp.einsum(
        "erf,erd->efd", inner_again, grad_expert_out, preferred_element_type=jnp.float32
    )
    sigmoid_gate = jax.nn.sigmoid(gate_again)
    swish = gate_again * sigmoid_gate
    grad_gate_act = (
        grad_inner * up_again * (sigmoid_gate * (1.0 + gate_again * (1.0 - sigmoid_gate)))
    ).astype(jnp.bfloat16)
    grad_up_act = (grad_inner * swish).astype(jnp.bfloat16)
    grad_gate_local = jnp.einsum(
        "erd,erf->edf", rows_again, grad_gate_act, preferred_element_type=jnp.float32
    )
    grad_up_local = jnp.einsum(
        "erd,erf->edf", rows_again, grad_up_act, preferred_element_type=jnp.float32
    )
    grad_rows = (
        jnp.einsum("erf,edf->erd", grad_gate_act, gate_full, preferred_element_type=jnp.float32)
        + jnp.einsum("erf,edf->erd", grad_up_act, up_full, preferred_element_type=jnp.float32)
    ).astype(jnp.bfloat16)
    grad_back = lax.all_to_all(
        grad_rows.reshape(local_experts, expert_peers, CAP, model_width),
        "expert",
        split_axis=1,
        concat_axis=1,
        tiled=True,
    )
    grad_back = jnp.concatenate(
        [grad_back.reshape(EXPERTS * CAP, model_width), jnp.zeros((1, model_width), jnp.bfloat16)],
        axis=0,
    )
    grad_hidden_two = jnp.sum(
        grad_back[target].reshape(tok_count, TOP, model_width).astype(jnp.float32), axis=1
    )
    grad_chosen = gate_probs * (
        grad_gates - jnp.sum(gate_probs * grad_gates, axis=-1, keepdims=True)
    )
    grad_logits = jnp.sum(picked_one * grad_chosen[:, :, None], axis=1).astype(jnp.bfloat16)
    grad_hidden_two = grad_hidden_two + jnp.dot(
        grad_logits, router_full.T, preferred_element_type=jnp.float32
    )
    grad_router_local = jnp.dot(hidden_two.T, grad_logits, preferred_element_type=jnp.float32)
    grad_middle_norm, grad_gain_two = norm_backward(
        grad_hidden_two, normed_two, scale_two, gain_second
    )
    grad_middle = grad_result + grad_middle_norm
    grad_branch = grad_middle.astype(jnp.bfloat16)
    grad_out_local = jnp.dot(attended.T, grad_branch, preferred_element_type=jnp.float32)
    grad_attended = jnp.dot(grad_branch, out_full.T, preferred_element_type=jnp.float32).astype(
        jnp.bfloat16
    )
    grad_groups = (
        grad_attended.reshape(tok_count, KV_HEADS, repeat_heads, HEAD)
        .transpose(1, 2, 0, 3)
        .reshape(KV_HEADS, query_rows, HEAD)
    )
    row_delta = jnp.sum(grad_groups.astype(jnp.float32) * exact_out, axis=-1)
    zero_key = jnp.zeros((tok_count, KV_HEADS, HEAD), jnp.float32)

    def pass_grads(grad_query, inputs_block):
        key_block, value_block, label = inputs_block

        def visit(carried):
            prob_block = probs_of(key_block, label)
            grad_probs = jnp.einsum(
                "grh,kgh->grk", grad_groups, value_block, preferred_element_type=jnp.float32
            )
            grad_scores = (prob_block * (grad_probs - row_delta[..., None])).astype(jnp.bfloat16)
            carried = carried + jnp.einsum(
                "grk,kgh->grh", grad_scores, key_block, preferred_element_type=jnp.float32
            )
            grad_key_block = (
                jnp.einsum(
                    "grk,grh->kgh", grad_scores, query_groups, preferred_element_type=jnp.float32
                )
                * score_scale
            )
            grad_value_block = jnp.einsum(
                "grk,grh->kgh",
                prob_block.astype(jnp.bfloat16),
                grad_groups,
                preferred_element_type=jnp.float32,
            )
            return (carried, (grad_key_block, grad_value_block))

        def skip(carried):
            return (carried, (zero_key, zero_key))

        return lax.cond(on_path(label), visit, skip, grad_query)

    grad_query_groups, (grad_key_blocks, grad_value_blocks) = lax.scan(
        pass_grads,
        jnp.zeros((KV_HEADS, query_rows, HEAD), jnp.float32),
        (key_blocks, value_blocks, segment_labels),
    )
    grad_key_all = grad_key_blocks.reshape(total_keys, KV_HEADS * HEAD)
    grad_value_all = grad_value_blocks.reshape(total_keys, KV_HEADS * HEAD)
    grad_key_mine, grad_value_mine = (
        lax.psum_scatter(
            grad_key_all.astype(jnp.bfloat16), "dp", scatter_dimension=0, tiled=True
        ).astype(jnp.float32),
        lax.psum_scatter(
            grad_value_all.astype(jnp.bfloat16), "dp", scatter_dimension=0, tiled=True
        ).astype(jnp.float32),
    )
    grad_query_rot = (
        (grad_query_groups * score_scale)
        .reshape(KV_HEADS, repeat_heads, tok_count, HEAD)
        .transpose(2, 0, 1, 3)
        .reshape(tok_count, HEADS, HEAD)
    )
    grad_query_raw = (
        rotate(grad_query_rot, cosine, -sine_part)
        .reshape(tok_count, HEADS * HEAD)
        .astype(jnp.bfloat16)
    )
    grad_key_raw = (
        rotate(grad_key_mine.reshape(tok_count, KV_HEADS, HEAD), cosine, -sine_part)
        .reshape(tok_count, KV_HEADS * HEAD)
        .astype(jnp.bfloat16)
    )
    grad_value_raw = grad_value_mine.astype(jnp.bfloat16)
    grad_query_local = jnp.dot(hidden_one.T, grad_query_raw, preferred_element_type=jnp.float32)
    grad_key_local = jnp.dot(hidden_one.T, grad_key_raw, preferred_element_type=jnp.float32)
    grad_value_local = jnp.dot(hidden_one.T, grad_value_raw, preferred_element_type=jnp.float32)
    grad_hidden_one = (
        jnp.dot(grad_query_raw, query_full.T, preferred_element_type=jnp.float32)
        + jnp.dot(grad_key_raw, key_full.T, preferred_element_type=jnp.float32)
        + jnp.dot(grad_value_raw, value_full.T, preferred_element_type=jnp.float32)
    )
    grad_inputs_norm, grad_gain_one = norm_backward(
        grad_hidden_one, normed_one, scale_one, gain_first
    )
    grad_inputs = grad_middle + grad_inputs_norm
    grad_gate_mine, grad_up_mine, grad_down_mine = (
        lax.psum_scatter(
            grad_gate_local.astype(jnp.bfloat16), "dp", scatter_dimension=1, tiled=True
        ).astype(jnp.float32),
        lax.psum_scatter(
            grad_up_local.astype(jnp.bfloat16), "dp", scatter_dimension=1, tiled=True
        ).astype(jnp.float32),
        lax.psum_scatter(
            grad_down_local.astype(jnp.bfloat16), "dp", scatter_dimension=1, tiled=True
        ).astype(jnp.float32),
    )
    shard_rows = (
        lax.psum_scatter(
            grad_gain_one.astype(jnp.bfloat16), "dp", scatter_dimension=0, tiled=True
        ).astype(jnp.float32),
        lax.psum_scatter(
            grad_query_local.astype(jnp.bfloat16), "dp", scatter_dimension=0, tiled=True
        ).astype(jnp.float32),
        lax.psum_scatter(
            grad_key_local.astype(jnp.bfloat16), "dp", scatter_dimension=0, tiled=True
        ).astype(jnp.float32),
        lax.psum_scatter(
            grad_value_local.astype(jnp.bfloat16), "dp", scatter_dimension=0, tiled=True
        ).astype(jnp.float32),
        lax.psum_scatter(
            grad_out_local.astype(jnp.bfloat16), "dp", scatter_dimension=0, tiled=True
        ).astype(jnp.float32),
        lax.psum_scatter(
            grad_gain_two.astype(jnp.bfloat16), "dp", scatter_dimension=0, tiled=True
        ).astype(jnp.float32),
        lax.psum_scatter(
            grad_router_local.astype(jnp.bfloat16), "dp", scatter_dimension=0, tiled=True
        ).astype(jnp.float32),
    )
    shared = (
        lax.psum(shard_rows[0].astype(jnp.bfloat16), "expert").astype(jnp.float32),
        lax.psum(shard_rows[1].astype(jnp.bfloat16), "expert").astype(jnp.float32),
        lax.psum(shard_rows[2].astype(jnp.bfloat16), "expert").astype(jnp.float32),
        lax.psum(shard_rows[3].astype(jnp.bfloat16), "expert").astype(jnp.float32),
        lax.psum(shard_rows[4].astype(jnp.bfloat16), "expert").astype(jnp.float32),
        lax.psum(shard_rows[5].astype(jnp.bfloat16), "expert").astype(jnp.float32),
        lax.psum(shard_rows[6].astype(jnp.bfloat16), "expert").astype(jnp.float32),
    )
    return (
        block_out[None],
        grad_inputs[None],
        shared[0],
        shared[1],
        shared[2],
        shared[3],
        shared[4],
        shared[5],
        shared[6],
        grad_gate_mine,
        grad_up_mine,
        grad_down_mine,
    )


SLOTS = 32
PAD_TOKENS = 32
LANES = 128
TILE = 256
MESH = pl.DeviceIdType.MESH
log2e = 1.4426950408889634


def dot_f32(a, b, dims=((1,), (0,))):
    return lax.dot_general(a, b, (dims, ((), ())), preferred_element_type=jnp.float32)


def split3(value):
    high = value.astype(jnp.bfloat16)
    rest = value - high.astype(jnp.float32)
    middle = rest.astype(jnp.bfloat16)
    low = (rest - middle.astype(jnp.float32)).astype(jnp.bfloat16)
    return high, middle, low


def one_hot(shape, test):
    row = lax.broadcasted_iota(jnp.int32, shape, 0)
    column = lax.broadcasted_iota(jnp.int32, shape, 1)
    return jnp.where(test(row, column), 1.0, 0.0).astype(jnp.bfloat16)


class Place:
    def __init__(self):
        self.dp = lax.axis_index("dp")
        self.side = lax.axis_index("expert")
        self.z = self.dp // 4
        self.x = (self.dp // 2) % 2
        self.c = self.dp % 2

    def index(self, z, x, c):
        return z * 4 + x * 2 + c

    def others(self):
        return [self.z + 1 - 2 * (self.z % 2), (self.z + 2) % 4, 3 - self.z]


def remote(src, dst, send, recv, dp, side):
    return pltpu.make_async_remote_copy(
        src_ref=src,
        dst_ref=dst,
        send_sem=send,
        recv_sem=recv,
        device_id={"dp": dp, "expert": side},
        device_id_type=MESH,
    )


def enter(device_count, dp_count):
    rank = lax.axis_index("expert") * dp_count + lax.axis_index("dp")
    barrier = pltpu.get_barrier_semaphore()

    @pl.loop(1, device_count)
    def _(step):
        other = (rank + step) % device_count
        pl.semaphore_signal(
            barrier,
            inc=1,
            device_id={"dp": other % dp_count, "expert": other // dp_count},
            device_id_type=MESH,
        )

    pl.semaphore_wait(barrier, device_count - 1)


class Column:
    def __init__(self, place, own, slot, send, recv, local):
        self.place, self.own, self.slot = place, own, slot
        self.send, self.recv, self.local = send, recv, local

    def hop(self, z, step, own=False):
        p = self.place
        source = self.own if own else self.slot(z)
        number = z if step > 0 else 4 + z
        target = p.index(p.z + step, p.x, p.c)
        return remote(source, self.slot(z), self.send.at[number], self.recv(z), target, p.side)

    def own_copy(self):
        return pltpu.make_async_copy(self.own, self.slot(self.place.z), self.local)

    def upward(self, act):
        pl.when(self.place.z < 3)(act)

    def downward(self, act):
        pl.when(self.place.z > 0)(act)

    def start(self):
        z = self.place.z
        self.upward(lambda: self.hop(z, 1, True).start())
        self.downward(lambda: self.hop(z, -1, True).start())
        self.own_copy().start()

    def forward(self, low=1, high=4, then=None):
        z = self.place.z

        @pl.loop(low, high)
        def _(away):
            @pl.when(z - away >= 0)
            def _():
                self.hop(z - away, 1).wait_recv()
                self.upward(lambda: self.hop(z - away, 1).start())
                if then is not None:
                    then(z - away)

            @pl.when(z + away <= 3)
            def _():
                self.hop(z + away, -1).wait_recv()
                self.downward(lambda: self.hop(z + away, -1).start())
                if then is not None:
                    then(z + away)

    def finish(self):
        z = self.place.z

        @pl.loop(0, 4)
        def _(origin):
            @pl.when((origin <= z) & (z < 3))
            def _():
                self.hop(origin, 1).wait_send()

            @pl.when((origin >= z) & (z > 0))
            def _():
                self.hop(origin, -1).wait_send()


class Gather:
    def __init__(self, place, own, slot, send, recv, local):
        self.place, self.own, self.slot = place, own, slot
        self.send, self.recv = send, recv
        self.column = Column(
            place,
            own,
            lambda z: slot(place.index(z, place.x, place.c)),
            send,
            lambda z: recv.at[place.index(z, place.x, place.c)],
            local,
        )

    def copy(self, z, x, c, to_x, to_c, number, own=False):
        p = self.place
        shard = p.index(z, x, c)
        source = self.own if own else self.slot(shard)
        target = p.index(p.z, to_x, to_c)
        return remote(
            source, self.slot(shard), self.send.at[number], self.recv.at[shard], target, p.side
        )

    def to_x(self, z, own=False):
        p = self.place
        return self.copy(z, p.x, p.c, 1 - p.x, p.c, 8 + z, own)

    def to_core(self, z, x, own=False):
        p = self.place
        return self.copy(z, x, p.c, p.x, 1 - p.c, 12 + z * 2 + x, own)

    def start(self):
        p = self.place
        self.column.start()
        self.to_x(p.z, True).start()
        self.to_core(p.z, p.x, True).start()

    def forward_z(self):
        def then(z):
            self.to_x(z).start()
            self.to_core(z, self.place.x).start()

        self.column.forward(then=then)

    def forward_x(self):
        p = self.place

        def pass_on(z):
            self.to_core(z, 1 - p.x).wait_recv()
            self.to_core(z, 1 - p.x).start()

        pass_on(p.z)

        @pl.loop(1, 4)
        def _(away):
            pl.when(p.z - away >= 0)(lambda: pass_on(p.z - away))
            pl.when(p.z + away <= 3)(lambda: pass_on(p.z + away))

    def finish(self):
        p = self.place

        @pl.loop(0, 4)
        def _(z):
            for x in range(2):
                self.copy(z, x, 1 - p.c, p.x, 1 - p.c, 12).wait_recv()
                self.to_core(z, x).wait_send()
            self.to_x(z).wait_send()

        self.column.finish()
        self.column.own_copy().wait()


class PlaneSwap:
    def __init__(self, place, source, target, send, recv, local, dp_count):
        self.place, self.source, self.target = place, source, target
        self.send, self.recv, self.local = send, recv, local
        self.dp_count = dp_count

    def of(self, member):
        return member // 4, (member // 2) % 2, member % 2

    def me(self):
        p = self.place
        return p.side * 4 + p.x * 2 + p.c

    def block(self, z, origin):
        return self.target.at[rows_of(z * 8 + origin, SLOTS)]

    def copy(self, z, step, to, origin):
        p = self.place
        side, x, c = self.of(to)
        return remote(
            self.source.at[z, rows_of(to, SLOTS)],
            self.block(z, origin),
            self.send.at[z, step],
            self.recv.at[z, step],
            p.index(p.z, x, c),
            side,
        )

    def own_copy(self, z):
        return pltpu.make_async_copy(
            self.source.at[z, rows_of(self.me(), SLOTS)],
            self.block(z, self.me()),
            self.local.at[z],
        )

    def start(self, z):
        for step in range(1, 8):
            self.copy(z, step, (self.me() + step) % 8, self.me()).start()
        self.own_copy(z).start()

    def arrived(self, z):
        for step in range(1, 8):
            other = (self.me() + 8 - step) % 8
            self.copy(z, step, other, other).wait_recv()
        self.own_copy(z).wait()

    def sent(self):
        @pl.loop(0, 4)
        def _(z):
            for step in range(1, 8):
                self.copy(z, step, (self.me() + step) % 8, self.me()).wait_send()

    def finish(self):
        pl.loop(0, 4)(self.arrived)
        self.sent()


class Chain:
    def __init__(self, place, part, land, send, recv):
        self.place, self.part, self.land = place, part, land
        self.send, self.recv = send, recv

    def hop(self, z, step):
        p = self.place
        if step > 0:
            slot = z
        else:
            slot = z + (4 - z) * ((3 - (p.z - 1 - z)) // 3)
        target = p.index(p.z + step, p.x, p.c)
        return remote(
            self.part.at[z], self.land.at[slot], self.send.at[z], self.recv.at[slot], target, p.side
        )

    def arrived(self, slot, step):
        p = self.place
        target = p.index(p.z + step, p.x, p.c)
        remote(
            self.part.at[0], self.land.at[slot], self.send.at[0], self.recv.at[slot], target, p.side
        ).wait_recv()

    def take(self, z, step):
        self.arrived(z, step)
        add_rows(self.part.at[z], self.land.at[z], 0, self.part.shape[1])

    def run(self, number):
        here = self.place.z
        up, down = 3 - number, number

        @pl.when(up > here)
        def _():
            pl.when(here > 0)(lambda: self.take(up, -1))
            self.hop(up, 1).start()

        @pl.when(down < here)
        def _():
            pl.when(here < 3)(lambda: self.take(down, 1))
            self.hop(down, -1).start()

    def finish(self, out):
        here = self.place.z
        chunk = 16

        def take(slot, step):
            self.arrived(slot, step)

            @pl.loop(0, out.shape[0] // chunk)
            def _(index):
                cut = rows_of(index, chunk)
                out[cut] += self.land[slot, cut].astype(jnp.float32)

        @pl.loop(0, out.shape[0] // chunk)
        def _(index):
            cut = rows_of(index, chunk)
            out[cut] = self.part[here, cut].astype(jnp.float32)

        pl.when(here > 0)(lambda: take(here, -1))
        pl.when(here < 3)(lambda: take(4, 1))

        @pl.loop(0, 4)
        def _(z):
            pl.when(z > here)(lambda: self.hop(z, 1).wait_send())
            pl.when(z < here)(lambda: self.hop(z, -1).wait_send())


class WeightSwap:
    def __init__(self, place, pairs, send, recv, local, dp_count):
        self.place, self.pairs = place, pairs
        self.send, self.recv, self.local = send, recv, local
        self.dp_count = dp_count

    def copies(self, step, to, landing):
        out = []
        for i, (source, target) in enumerate(self.pairs):
            rows = source.shape[1]
            out.append(
                remote(
                    source.at[to],
                    target.at[pl.ds(pl.multiple_of(landing * rows, rows), rows)],
                    self.send.at[step, i],
                    self.recv.at[step, i],
                    to,
                    self.place.side,
                )
            )
        return out

    def own_copies(self):
        dp = self.place.dp
        return [
            pltpu.make_async_copy(
                source.at[dp],
                target.at[pl.ds(pl.multiple_of(dp * source.shape[1], source.shape[1]), source.shape[1])],
                self.local.at[i],
            )
            for i, (source, target) in enumerate(self.pairs)
        ]

    def start(self, low, high):
        @pl.loop(low, high)
        def _(step):
            for copy in self.copies(step, (self.place.dp + step) % self.dp_count, self.place.dp):
                copy.start()

    def start_own(self):
        for copy in self.own_copies():
            copy.start()

    def finish(self):
        @pl.loop(1, self.dp_count)
        def _(step):
            other = (self.place.dp + self.dp_count - step) % self.dp_count
            for copy in self.copies(step, other, other):
                copy.wait()

        for copy in self.own_copies():
            copy.wait()


def columns(tile, width=TILE):
    return pl.ds(pl.multiple_of(tile * width, width), width)


def rows_of(index, count):
    return pl.ds(pl.multiple_of(index * count, count), count)


def slot_labels(place, dp_count):
    row = lax.broadcasted_iota(jnp.int32, (8 * SLOTS, TILE), 0)
    member = row // SLOTS
    label = ((member // 4) * dp_count + place.z * 4 + member % 4) * SLOTS + row % SLOTS
    return label.astype(jnp.float32)


def front_kernel(
    bias_ref,
    tokens_ref,
    cotangent_ref,
    project_ref,
    out_ref,
    target_ref,
    route_ref,
    cosine_ref,
    sine_ref,
    gate_ref,
    up_ref,
    down_ref,
    project_full,
    out_full,
    keys_ref,
    query_ref,
    attended_ref,
    exact_ref,
    stat_ref,
    middle_ref,
    hidden_ref,
    probs_ref,
    rows_in,
    grads_in,
    gate_own,
    up_own,
    down_own,
    hidden_one,
    target_all,
    gate_all,
    keys_own,
    row_send,
    grad_send,
    gate_own_row,
    hidden_all,
    grad_all,
    placed,
    acc,
    top,
    project_send,
    project_recv,
    out_send,
    out_recv,
    keys_send,
    keys_recv,
    row_send_sem,
    row_recv_sem,
    row_local,
    grad_send_sem,
    grad_recv_sem,
    grad_local,
    column_send,
    column_recv,
    weight_send,
    weight_recv,
    weight_local,
    local,
):
    dp_count = keys_ref.shape[0]
    device_count = rows_in.shape[0] // SLOTS
    tok_count, model_width = tokens_ref.shape
    query_width = HEADS * HEAD
    key_width = KV_HEADS * HEAD
    repeat_heads = HEADS // KV_HEADS
    factor = log2e * HEAD ** (-0.5)
    place = Place()
    shard_rows = project_ref.shape[0]

    def shard_of(full):
        return lambda index: full.at[rows_of(index, shard_rows)]

    project = Gather(
        place, project_ref, shard_of(project_full), project_send, project_recv, local.at[0]
    )
    out = Gather(place, out_ref, shard_of(out_full), out_send, out_recv, local.at[1])
    keys = Gather(
        place, keys_own, lambda index: keys_ref.at[index], keys_send, keys_recv, local.at[2]
    )
    rows = PlaneSwap(place, row_send, rows_in, row_send_sem, row_recv_sem, row_local, dp_count)
    grads = PlaneSwap(place, grad_send, grads_in, grad_send_sem, grad_recv_sem, grad_local, dp_count)

    def column(number, own, land):
        return Column(
            place,
            own,
            land,
            column_send.at[number],
            lambda z: column_recv.at[number, z],
            local.at[3 + number],
        )

    targets = column(0, target_ref, lambda z: target_all.at[z])
    gates = column(1, gate_own_row, lambda z: gate_all.at[z])
    hidden = column(2, hidden_ref, lambda z: hidden_all.at[z, pl.ds(0, tok_count)])
    cotangents = column(3, cotangent_ref, lambda z: grad_all.at[z])
    weights = WeightSwap(
        place,
        ((gate_ref, gate_own), (up_ref, up_own), (down_ref, down_own)),
        weight_send,
        weight_recv,
        weight_local,
        dp_count,
    )

    enter(device_count, dp_count)
    targets.start()
    project.start()
    cotangents.start()
    plane_slots = 8 * SLOTS
    targets.forward()
    targets.own_copy().wait()
    slot_row = lax.broadcasted_iota(jnp.int32, (plane_slots, TILE), 0)
    slot_lane = lax.broadcasted_iota(jnp.int32, (plane_slots, TILE), 1)
    member = slot_row // SLOTS
    label = slot_labels(place, dp_count)
    spare = (slot_lane - tok_count == member) & (slot_row % SLOTS == CAP)

    def match(z, choice):
        return label == target_all[z, choice : choice + 1]

    for z in range(4):
        hit = spare
        for choice in range(TOP):
            hit = hit | match(z, choice)
        placed[z] = jnp.where(hit, 1.0, 0.0).astype(jnp.bfloat16)
    hidden_all[:, tok_count:] = jnp.zeros((4, PAD_TOKENS, model_width), jnp.bfloat16)

    project.forward_z()
    project.forward_x()
    project.finish()
    cotangents.forward(1, 2)

    lanes_of = one_hot((8, LANES), lambda row, column: column == row + EXPERTS)
    gains = dot_f32(lanes_of, project_full[:, query_width + 2 * key_width :], ((1,), (1,)))
    gain_first, gain_second = gains[0:1], gains[1:2]
    chunk = 32

    @pl.loop(0, tok_count // chunk)
    def _(index):
        value = tokens_ref[rows_of(index, chunk)].astype(jnp.float32)
        scale = lax.rsqrt(jnp.mean(value * value, axis=-1, keepdims=True) + epsilon)
        hidden_one[rows_of(index, chunk)] = (value * scale * gain_first).astype(jnp.bfloat16)

    def turned(tile):
        value = dot_f32(hidden_one[...], project_full[:, columns(tile)])
        halves = []
        for half in range(TILE // HEAD):
            part = value[:, half * HEAD : (half + 1) * HEAD]
            halves.append(
                part * cosine_ref[...] + pltpu.roll(part, HEAD // 2, 1) * sine_ref[...]
            )
        return jnp.concatenate(halves, axis=1).astype(jnp.bfloat16)

    keys_own[:, :key_width] = turned(query_width // TILE)
    keys_own[:, key_width:] = dot_f32(
        hidden_one[...], project_full[:, query_width + key_width : query_width + 2 * key_width]
    ).astype(jnp.bfloat16)
    keys.start()

    @pl.loop(0, query_width // TILE)
    def _(tile):
        query_ref[:, columns(tile)] = turned(tile)

    keys.forward_z()
    keys.forward_x()
    keys.finish()
    out.start()
    weights.start(1, dp_count)
    weights.start_own()

    row = lax.broadcasted_iota(jnp.int32, (tok_count, tok_count), 0)
    column_index = lax.broadcasted_iota(jnp.int32, (tok_count, tok_count), 1)
    causal = column_index <= row
    ones = jnp.ones((tok_count, LANES), jnp.bfloat16)

    def visit(label, own):
        for group in range(KV_HEADS):
            key = keys_ref[label, :, group * HEAD : (group + 1) * HEAD]
            value = keys_ref[label, :, (KV_HEADS + group) * HEAD : (KV_HEADS + group + 1) * HEAD]
            value = jnp.concatenate([value, ones], axis=1)
            for head in range(group * repeat_heads, (group + 1) * repeat_heads):
                query = query_ref[:, head * HEAD : (head + 1) * HEAD]
                scores = dot_f32(query, key, ((1,), (1,))) * factor
                if own:
                    scores = jnp.where(causal, scores, -1e30)
                    peak = jnp.ceil(jnp.max(scores, axis=-1, keepdims=True))
                    shift = peak
                else:
                    bias = bias_ref[label]
                    peak = jnp.ceil(
                        jnp.maximum(top[head], jnp.max(scores, axis=-1, keepdims=True) + bias)
                    )
                    shift = peak - bias
                prob = jnp.exp2(scores - shift).astype(jnp.bfloat16)
                part = dot_f32(prob, value)
                if own:
                    acc[head] = part
                else:
                    acc[head] = acc[head] * jnp.exp2(top[head] - peak) + part
                top[head] = peak

    visit(place.dp, True)

    @pl.loop(0, place.dp)
    def _(label):
        visit(label, False)

    out.forward_z()
    out.forward_x()
    cotangents.forward(2, 4)
    cotangents.own_copy().wait()

    @pl.loop(0, 4)
    def _(z):
        @pl.loop(0, model_width // TILE)
        def _(tile):
            grad_send[z, :, columns(tile)] = dot_f32(
                placed[z, :, :tok_count], grad_all[z, :, columns(tile)]
            ).astype(jnp.bfloat16)

        grads.start(z)

    lane = lax.broadcasted_iota(jnp.int32, (tok_count, LANES), 1)
    stats = jnp.zeros((tok_count, LANES), jnp.float32)
    for head in range(HEADS):
        exact = acc[head, :, :HEAD] / acc[head, :, HEAD:]
        exact_ref[:, head * HEAD : (head + 1) * HEAD] = exact
        attended_ref[:, head * HEAD : (head + 1) * HEAD] = exact.astype(jnp.bfloat16)
        stats = jnp.where(lane == head, top[head], stats)
        stats = jnp.where(lane == HEADS + head, 1.0 / acc[head, :, HEAD:], stats)
    stat_ref[...] = stats
    out.finish()

    @pl.loop(0, model_width // TILE)
    def _(tile):
        middle_ref[:, columns(tile)] = tokens_ref[:, columns(tile)].astype(jnp.float32) + dot_f32(
            attended_ref[...], out_full[:, columns(tile)]
        )

    @pl.loop(0, tok_count // chunk)
    def _(index):
        value = middle_ref[rows_of(index, chunk)]
        scale = lax.rsqrt(jnp.mean(value * value, axis=-1, keepdims=True) + epsilon)
        hidden_ref[rows_of(index, chunk)] = (value * scale * gain_second).astype(jnp.bfloat16)

    hidden.start()
    router = project_full[:, query_width + 2 * key_width :]
    chosen = [route_ref[:, choice : choice + 1] == lane for choice in range(TOP)]
    mask = chosen[0]
    for choice in range(1, TOP):
        mask = mask | chosen[choice]
    logits = jnp.where(mask, dot_f32(hidden_ref[...], router), -1e30)
    weight = jnp.exp(logits - jnp.max(logits, axis=-1, keepdims=True))
    probs = weight / jnp.sum(weight, axis=-1, keepdims=True)
    probs_ref[...] = probs
    by_choice = jnp.zeros((tok_count, LANES), jnp.float32)
    for choice in range(TOP):
        gate = jnp.sum(jnp.where(chosen[choice], probs, 0.0), axis=-1, keepdims=True)
        by_choice = jnp.where(lane == choice, gate, by_choice)
    first_lanes = one_hot((8, LANES), lambda r, col: r == col)
    gate_own_row[...] = jnp.zeros(gate_own_row.shape, jnp.float32)
    gate_own_row[:, :tok_count] = sum(
        dot_f32(first_lanes, part, ((1,), (1,))) for part in split3(by_choice)
    )
    gates.start()
    fold = one_hot((8, plane_slots), lambda r, col: col // SLOTS == r)
    def dispatch(z):
        gate = jnp.zeros((plane_slots, 1), jnp.float32)
        for choice in range(TOP):
            gate += jnp.sum(
                jnp.where(match(z, choice), gate_all[z, choice : choice + 1], 0.0),
                axis=-1,
                keepdims=True,
            )
        numbers = dot_f32(fold, put_parts(gate)).astype(jnp.bfloat16)
        numbers = jnp.concatenate([numbers, jnp.zeros((8, LANES), jnp.bfloat16)], axis=0)
        hidden_all[z, tok_count : tok_count + 16, :LANES] = numbers

        @pl.loop(0, model_width // TILE)
        def _(tile):
            row_send[z, :, columns(tile)] = dot_f32(
                placed[z], hidden_all[z, :, columns(tile)]
            ).astype(jnp.bfloat16)

        rows.start(z)
    hidden.own_copy().wait()
    gates.own_copy().wait()
    dispatch(place.z)
    gates.forward()
    hidden.forward(then=dispatch)
    for gather in (targets, cotangents, hidden, gates):
        gather.finish()
    weights.finish()
    grads.finish()
    rows.finish()


def front(bias, tokens, cotangent, project, out, target, route, cosine, sine, gate, up, down):
    dp_count = lax.axis_size("dp")
    device_count = dp_count * lax.axis_size("expert")
    tok_count, model_width = tokens.shape
    query_width = HEADS * HEAD
    key_width = KV_HEADS * HEAD
    vmem = pl.BlockSpec(memory_space=pltpu.VMEM)
    anywhere = pl.BlockSpec(memory_space=pl.ANY)
    slots = device_count * SLOTS
    low, full = jnp.bfloat16, jnp.float32
    shape = jax.ShapeDtypeStruct
    ff_width = gate.shape[2]
    outs = (
        (shape((model_width, project.shape[1]), low), vmem),
        (shape((model_width, model_width), low), vmem),
        (shape((dp_count, tok_count, 2 * key_width), low), vmem),
        (shape((tok_count, query_width), low), vmem),
        (shape((tok_count, query_width), low), vmem),
        (shape((tok_count, query_width), full), vmem),
        (shape((tok_count, LANES), full), vmem),
        (shape((tok_count, model_width), full), vmem),
        (shape((tok_count, model_width), low), vmem),
        (shape((tok_count, LANES), full), vmem),
        (shape((slots, model_width), low), anywhere),
        (shape((slots, model_width), low), anywhere),
        (shape((model_width, ff_width), low), anywhere),
        (shape((model_width, ff_width), low), anywhere),
        (shape((ff_width, model_width), low), anywhere),
        (shape((tok_count, model_width), low), vmem),
        (shape((4, 8, TILE), full), vmem),
        (shape((4, 8, TILE), full), vmem),
    )
    dma = pltpu.SemaphoreType.DMA
    return pl.pallas_call(
        front_kernel,
        out_shape=tuple(o[0] for o in outs),
        in_specs=[pl.BlockSpec(memory_space=pltpu.SMEM)] + [vmem] * 8 + [anywhere] * 3,
        out_specs=tuple(o[1] for o in outs),
        scratch_shapes=[
            pltpu.VMEM((tok_count, 2 * key_width), low),
            pltpu.VMEM((4, 8 * SLOTS, model_width), low),
            pltpu.VMEM((4, 8 * SLOTS, model_width), low),
            pltpu.VMEM((8, TILE), full),
            pltpu.VMEM((4, tok_count + PAD_TOKENS, model_width), low),
            pltpu.VMEM((4, tok_count, model_width), low),
            pltpu.VMEM((4, 8 * SLOTS, TILE), low),
            pltpu.VMEM((HEADS, tok_count, 2 * HEAD), full),
            pltpu.VMEM((HEADS, tok_count, 1), full),
        ]
        + [dma((20,)), dma((dp_count,))] * 3
        + [dma((4, 8)), dma((4, 8)), dma((4,))] * 2
        + [dma((4, 8)), dma((4, 4))]
        + [dma((dp_count, 3))] * 2
        + [dma((3,)), dma((7,))],
        compiler_params=pltpu.CompilerParams(
            collective_id=0, has_side_effects=True, vmem_limit_bytes=58 * 1024 * 1024
        ),
    )(bias, tokens, cotangent, project, out, target, route, cosine, sine, gate, up, down)


def pick_gates(block):
    rows = block.shape[0]
    blocks = rows // SLOTS
    spare = one_hot((blocks, rows), lambda r, col: col == r * SLOTS + CAP)
    member = one_hot((rows, blocks), lambda r, col: r // SLOTS == col)
    parts = dot_f32(member, dot_f32(spare, block).astype(jnp.bfloat16))
    row = lax.broadcasted_iota(jnp.int32, parts.shape, 0)
    lane = lax.broadcasted_iota(jnp.int32, parts.shape, 1)
    mine = (lane % SLOTS == row % SLOTS) & (lane < 3 * SLOTS)
    return jnp.sum(jnp.where(mine, parts, 0.0), axis=-1, keepdims=True)


def put_parts(column):
    shape = (column.shape[0], LANES)
    row = lax.broadcasted_iota(jnp.int32, shape, 0)
    lane = lax.broadcasted_iota(jnp.int32, shape, 1)
    high, mid, low = (part.astype(jnp.float32) for part in split3(column))
    part = jnp.where(lane < SLOTS, high, jnp.where(lane < 2 * SLOTS, mid, low))
    mine = (lane % SLOTS == row % SLOTS) & (lane < 3 * SLOTS)
    return jnp.where(mine, part, 0.0).astype(jnp.bfloat16)


def expert_kernel(
    rows_ref,
    grads_ref,
    gate_ref,
    up_ref,
    down_ref,
    target_all,
    gate_all,
    row_sum,
    out_sum,
    gate_sum,
    gate_grad_ref,
    up_grad_ref,
    down_grad_ref,
    row_send,
    row_plane,
    row_part,
    row_land,
    out_send,
    out_plane,
    out_part,
    out_land,
    gate_part,
    gate_land,
    grad_out,
    inner_ref,
    gate_act_grad,
    up_act_grad,
    row_send_sem,
    row_recv_sem,
    row_local,
    out_send_sem,
    out_recv_sem,
    out_local,
    row_chain_send,
    row_chain_recv,
    out_chain_send,
    out_chain_recv,
    gate_send_sem,
    gate_recv_sem,
):
    dp_count = lax.axis_size("dp")
    slots, model_width = rows_ref.shape
    ff_width = gate_ref.shape[1]
    tok_count = row_sum.shape[0]
    device_count = slots // SLOTS
    place = Place()
    enter(device_count, dp_count)
    rows = PlaneSwap(place, row_send, row_plane, row_send_sem, row_recv_sem, row_local, dp_count)
    outs = PlaneSwap(place, out_send, out_plane, out_send_sem, out_recv_sem, out_local, dp_count)
    row_chain = Chain(place, row_part, row_land, row_chain_send, row_chain_recv)
    out_chain = Chain(place, out_part, out_land, out_chain_send, out_chain_recv)

    digits = 27 + 72 * place.z - 15 * (place.z // 2)

    def level(step):
        power = 1 + 3 * step + 9 * (step * (step - 1) // 2)
        power += 27 * (step * (step - 1) * (step - 2) // 6)
        return (digits // power) % 4

    @pl.loop(0, 4)
    def _(step):
        tile = level(step)
        cut = rows_of(tile, TILE)
        row = rows_ref[cut]
        gate = pick_gates(row[:, :LANES])
        saved = []
        for n in range(ff_width // TILE):
            part = slice(n * TILE, (n + 1) * TILE)
            gate_act = dot_f32(row, gate_ref[:, part])
            up_act = dot_f32(row, up_ref[:, part])
            sigmoid = 1.0 / (1.0 + jnp.exp(-gate_act))
            swish = gate_act * sigmoid
            inner_ref[cut, part] = (swish * up_act).astype(jnp.bfloat16)
            saved.append((swish, up_act * (sigmoid * (1.0 + gate_act * (1.0 - sigmoid)))))
        inner = inner_ref[cut]
        gate_grad = jnp.zeros((TILE, 1), jnp.float32)
        for n in range(model_width // TILE):
            part = slice(n * TILE, (n + 1) * TILE)
            expert_out = dot_f32(inner, down_ref[:, part]).astype(jnp.bfloat16)
            out_send[tile, :, part] = expert_out
            grad = grads_ref[cut, part].astype(jnp.float32)
            gate_grad += jnp.sum(expert_out.astype(jnp.float32) * grad, axis=-1, keepdims=True)
            grad_out[cut, part] = (gate * grad).astype(jnp.bfloat16)
        grad = grad_out[cut]
        for n in range(ff_width // TILE):
            part = slice(n * TILE, (n + 1) * TILE)
            swish, slope = saved[n]
            grad_inner = dot_f32(grad, down_ref[part, :], ((1,), (1,)))
            gate_act_grad[cut, part] = (grad_inner * slope).astype(jnp.bfloat16)
            up_act_grad[cut, part] = (grad_inner * swish).astype(jnp.bfloat16)
        blocks = TILE // SLOTS
        fold = one_hot((blocks, TILE), lambda r, col: col // SLOTS == r)
        spread = one_hot((TILE, blocks), lambda r, col: r == col * SLOTS + CAP)
        extra = dot_f32(spread, dot_f32(fold, put_parts(gate_grad)).astype(jnp.bfloat16))
        for n in range(model_width // TILE):
            part = slice(n * TILE, (n + 1) * TILE)
            back = dot_f32(gate_act_grad[cut], gate_ref[part, :], ((1,), (1,))) + dot_f32(
                up_act_grad[cut], up_ref[part, :], ((1,), (1,))
            )
            row_send[tile, :, part] = back.astype(jnp.bfloat16)
            if n == 0:
                row_send[tile, :, :LANES] = (back[:, :LANES] + extra).astype(jnp.bfloat16)
        rows.start(tile)

    @pl.loop(0, 4)
    def _(step):
        outs.start(level(step))

    label = slot_labels(place, dp_count)
    shape = (8 * SLOTS, LANES)
    member = lax.broadcasted_iota(jnp.int32, shape, 0) // SLOTS
    lane = lax.broadcasted_iota(jnp.int32, shape, 1)
    expert = (member // 4) * dp_count + place.z * 4 + member % 4

    def match(z, choice):
        return label == target_all[z, choice : choice + 1]

    def row_partial(step):
        z = level(step)
        rows.arrived(z)
        hit = match(z, 0)
        for choice in range(1, TOP):
            hit = hit | match(z, choice)
        placed = jnp.where(hit, 1.0, 0.0).astype(jnp.bfloat16)
        cut = rows_of(z, TILE)
        numbers = jnp.where(lane == expert, pick_gates(row_plane[cut, :LANES]), 0.0)
        gate_part[z] = sum(dot_f32(placed, part, ((0,), (0,))) for part in split3(numbers))[
            :tok_count
        ]
        for n in range(model_width // TILE):
            part = slice(n * TILE, (n + 1) * TILE)
            row_part[z, :, part] = dot_f32(placed, row_plane[cut, part], ((0,), (0,)))[
                :tok_count
            ].astype(jnp.bfloat16)

    row_partial(0)
    row_partial(1)
    row_chain.run(0)
    row_partial(2)
    row_chain.run(1)
    row_partial(3)
    row_chain.run(2)

    def gate_hop(i):
        z = place.others()[i]
        target = place.index(z, place.x, place.c)
        return remote(
            gate_part.at[z],
            gate_land.at[i],
            gate_send_sem.at[i],
            gate_recv_sem.at[i],
            target,
            place.side,
        )

    for i in range(3):
        gate_hop(i).start()

    def out_partial(step):
        z = level(step)
        outs.arrived(z)
        gates = jnp.zeros((8 * SLOTS, TILE), jnp.float32)
        for choice in range(TOP):
            gates += jnp.where(match(z, choice), gate_all[z, choice : choice + 1], 0.0)
        high = gates.astype(jnp.bfloat16)
        low = (gates - high.astype(jnp.float32)).astype(jnp.bfloat16)
        cut = rows_of(z, TILE)
        for n in range(model_width // TILE):
            part = slice(n * TILE, (n + 1) * TILE)
            out = out_plane[cut, part]
            value = dot_f32(high, out, ((0,), (0,))) + dot_f32(low, out, ((0,), (0,)))
            out_part[z, :, part] = value[:tok_count].astype(jnp.bfloat16)

    def weight_grad(target, act):
        @pl.loop(0, model_width // TILE)
        def _(tile):
            target[rows_of(tile, TILE)] = dot_f32(
                rows_ref[:, columns(tile)], act[...], ((0,), (0,))
            ).astype(jnp.bfloat16)

    out_partial(0)
    out_partial(1)
    out_chain.run(0)
    weight_grad(gate_grad_ref, gate_act_grad)
    out_partial(2)
    out_chain.run(1)
    weight_grad(up_grad_ref, up_act_grad)
    out_partial(3)
    out_chain.run(2)

    @pl.loop(0, ff_width // TILE)
    def _(tile):
        inner = inner_ref[:, columns(tile)]
        for n in range(model_width // ff_width):
            part = slice(n * ff_width, (n + 1) * ff_width)
            down_grad_ref[rows_of(tile, TILE), part] = dot_f32(
                inner, grad_out[:, part], ((0,), (0,))
            ).astype(jnp.bfloat16)

    row_chain.finish(row_sum)
    gate_sum[...] = gate_part[place.z]
    for i in range(3):
        gate_hop(i).wait()
        gate_sum[...] += gate_land[i]
    out_chain.finish(out_sum)
    rows.sent()
    outs.sent()


def experts(rows, grads, gate, up, down, target, gates, tok_count):
    slots, model_width = rows.shape
    ff_width = gate.shape[1]
    vmem = pl.BlockSpec(memory_space=pltpu.VMEM)
    low, full = jnp.bfloat16, jnp.float32
    shape = jax.ShapeDtypeStruct
    dma = pltpu.SemaphoreType.DMA
    return pl.pallas_call(
        expert_kernel,
        out_shape=(
            shape((tok_count, model_width), full),
            shape((tok_count, model_width), full),
            shape((tok_count, LANES), full),
            shape((model_width, ff_width), low),
            shape((model_width, ff_width), low),
            shape((ff_width, model_width), low),
        ),
        in_specs=[vmem] * 7,
        out_specs=(vmem,) * 6,
        scratch_shapes=[
            pltpu.VMEM((4, 8 * SLOTS, model_width), low),
            pltpu.VMEM((slots, model_width), low),
            pltpu.VMEM((4, tok_count, model_width), low),
            pltpu.VMEM((5, tok_count, model_width), low),
        ]
        * 2
        + [
            pltpu.VMEM((4, tok_count, LANES), full),
            pltpu.VMEM((3, tok_count, LANES), full),
            pltpu.VMEM((slots, model_width), low),
            pltpu.VMEM((slots, ff_width), low),
            pltpu.VMEM((slots, ff_width), low),
            pltpu.VMEM((slots, ff_width), low),
        ]
        + [dma((4, 8)), dma((4, 8)), dma((4,))] * 2
        + [dma((4,)), dma((5,))] * 2
        + [dma((3,))] * 2,
        compiler_params=pltpu.CompilerParams(
            collective_id=1, has_side_effects=True, vmem_limit_bytes=60 * 1024 * 1024
        ),
    )(rows, grads, gate, up, down, target, gates)


def halves_turned(value, cosine, sine):
    parts = []
    for half in range(value.shape[1] // HEAD):
        part = value[:, half * HEAD : (half + 1) * HEAD]
        parts.append(part * cosine + pltpu.roll(part, HEAD // 2, 1) * sine)
    return jnp.concatenate(parts, axis=1)


def gain_rows(small):
    lanes_of = one_hot((8, LANES), lambda row, column: column == row + EXPERTS)
    return dot_f32(lanes_of, small, ((1,), (1,)))


class Scatter:
    def __init__(self, place, block, lands, send, recvs):
        self.place, self.block = place, block
        self.lands, self.send, self.recvs = lands, send, recvs

    def hop_core(self, z, x):
        p = self.place
        number = z * 2 + x
        return remote(
            self.block(p.index(z, x, 1 - p.c)),
            self.lands[0].at[number],
            self.send.at[number],
            self.recvs[0].at[number],
            p.index(p.z, p.x, 1 - p.c),
            p.side,
        )

    def hop_x(self, z):
        p = self.place
        return remote(
            self.block(p.index(z, 1 - p.x, p.c)),
            self.lands[1].at[z],
            self.send.at[8 + z],
            self.recvs[1].at[z],
            p.index(p.z, 1 - p.x, p.c),
            p.side,
        )

    def hop_z(self, i):
        p = self.place
        z = p.others()[i]
        return remote(
            self.block(p.index(z, p.x, p.c)),
            self.lands[2].at[i],
            self.send.at[12 + i],
            self.recvs[2].at[i],
            p.index(z, p.x, p.c),
            p.side,
        )

    def add(self, shard, land):
        block = self.block(shard)
        chunk = 32

        @pl.loop(0, block.shape[0] // chunk)
        def _(index):
            cut = rows_of(index, chunk)
            block[cut] = (block[cut].astype(jnp.float32) + land[cut].astype(jnp.float32)).astype(
                jnp.bfloat16
            )

    def start(self):
        for z in range(4):
            for x in range(2):
                self.hop_core(z, x).start()

    def order(self):
        return self.place.others() + [self.place.z]

    def pass_core(self):
        p = self.place
        for z in self.order():
            for x in (1 - p.x, p.x):
                self.hop_core(z, x).wait_recv()
                self.add(p.index(z, x, p.c), self.lands[0].at[z * 2 + x])
            self.hop_x(z).start()

    def pass_x(self):
        p = self.place
        for i, z in enumerate(self.order()):
            self.hop_x(z).wait_recv()
            self.add(p.index(z, p.x, p.c), self.lands[1].at[z])
            if i < 3:
                self.hop_z(i).start()

    def pass_z(self, put):
        p = self.place
        for i in range(3):
            self.hop_z(i).wait_recv()
        block = self.block(p.dp)
        chunk = 32

        @pl.loop(0, block.shape[0] // chunk)
        def _(index):
            cut = rows_of(index, chunk)
            value = block[cut].astype(jnp.float32)
            for i in range(3):
                value += self.lands[2][i, cut].astype(jnp.float32)
            put(cut, value)

    def finish(self):
        for z in range(4):
            for x in range(2):
                self.hop_core(z, x).wait_send()
            self.hop_x(z).wait_send()
        for i in range(3):
            self.hop_z(i).wait_send()


def add_rows(block, land, low, count):
    chunk = 16

    @pl.loop(0, count // chunk)
    def _(index):
        cut = pl.ds(pl.multiple_of(low + index * chunk, chunk), chunk)
        value = block[cut].astype(jnp.float32) + land[rows_of(index, chunk)].astype(jnp.float32)
        block[cut] = value.astype(jnp.bfloat16)


class TotalSum:
    def __init__(self, place, part, lands, send, recv, x_first):
        self.place, self.part, self.lands = place, part, lands
        self.send, self.recv, self.x_first = send, recv, x_first
        self.rows = part.shape[1]
        self.half = self.rows // 2

    def kept(self, side):
        return pl.ds(pl.multiple_of(side * self.half, self.half), self.half)

    def hop(self, source, land, number, dp, side):
        return remote(source, land, self.send.at[number], self.recv.at[number], dp, side)

    def core(self, z, x):
        p = self.place
        return self.hop(
            self.part.at[p.index(z, x, 1 - p.c)],
            self.lands[0].at[z * 2 + x],
            z * 2 + x,
            p.index(p.z, p.x, 1 - p.c),
            p.side,
        )

    def over_x(self, z):
        p = self.place
        source = self.part.at[p.index(z, 1 - p.x, p.c)]
        if not self.x_first:
            source = source.at[self.kept(p.side)]
        return self.hop(source, self.lands[1].at[z], 8 + z, p.index(p.z, 1 - p.x, p.c), p.side)

    def over_side(self, z, x):
        p = self.place
        number = z if self.x_first else z * 2 + x
        return self.hop(
            self.part.at[p.index(z, x, p.c), self.kept(1 - p.side)],
            self.lands[2].at[number],
            12 + number,
            p.dp,
            1 - p.side,
        )

    def over_z(self, i):
        p = self.place
        z = p.others()[i]
        return self.hop(
            self.part.at[p.index(z, p.x, p.c), self.kept(p.side)],
            self.lands[3].at[i],
            20 + i,
            p.index(z, p.x, p.c),
            p.side,
        )

    def home(self):
        p = self.place
        block = self.part.at[p.dp, self.kept(p.side)]
        return self.hop(block, self.lands[4], 23, p.dp, 1 - p.side)

    def start(self, z):
        for x in range(2):
            self.core(z, x).start()

    def sides(self):
        return (self.place.x,) if self.x_first else (1 - self.place.x, self.place.x)

    def first(self, z):
        p = self.place
        for x in (1 - p.x, p.x):
            self.core(z, x).wait_recv()
            add_rows(self.part.at[p.index(z, x, p.c)], self.lands[0].at[z * 2 + x], 0, self.rows)
            if not self.x_first:
                self.over_side(z, x).start()
        if self.x_first:
            self.over_x(z).start()

    def take_side(self, z):
        p = self.place
        for x in self.sides():
            self.over_side(z, x).wait_recv()
            number = z if self.x_first else z * 2 + x
            add_rows(
                self.part.at[p.index(z, x, p.c)],
                self.lands[2].at[number],
                p.side * self.half,
                self.half,
            )

    def take_x(self, z):
        p = self.place
        self.over_x(z).wait_recv()
        low, count = (0, self.rows) if self.x_first else (p.side * self.half, self.half)
        add_rows(self.part.at[p.index(z, p.x, p.c)], self.lands[1].at[z], low, count)

    def second(self, z):
        if self.x_first:
            self.take_x(z)
            self.over_side(z, self.place.x).start()
        else:
            self.take_side(z)
            self.over_x(z).start()

    def third(self, z, i):
        if self.x_first:
            self.take_side(z)
        else:
            self.take_x(z)
        if i < 3:
            self.over_z(i).start()

    def fourth(self):
        p = self.place
        for i in range(3):
            self.over_z(i).wait_recv()
        chunk = 16

        @pl.loop(0, self.half // chunk)
        def _(index):
            cut = pl.ds(pl.multiple_of(p.side * self.half + index * chunk, chunk), chunk)
            value = self.part[p.dp, cut].astype(jnp.float32)
            for i in range(3):
                value += self.lands[3][i, rows_of(index, chunk)].astype(jnp.float32)
            self.part[p.dp, cut] = value.astype(jnp.bfloat16)

        self.home().start()

    def finish(self, mine, at):
        p = self.place
        mine[self.kept(p.side), at] = self.part[p.dp, self.kept(p.side)].astype(jnp.float32)
        self.home().wait()
        mine[self.kept(1 - p.side), at] = self.lands[4][...].astype(jnp.float32)
        for z in range(4):
            for x in range(2):
                self.core(z, x).wait_send()
            self.over_x(z).wait_send()
            for x in self.sides():
                self.over_side(z, x).wait_send()
        for i in range(3):
            self.over_z(i).wait_send()


class WeightReturn(WeightSwap):
    def copies(self, step, to, landing):
        out = []
        for i, (source, target) in enumerate(self.pairs):
            rows = target.shape[1]
            out.append(
                remote(
                    source.at[rows_of(to, rows)],
                    target.at[landing],
                    self.send.at[step, i],
                    self.recv.at[step, i],
                    to,
                    self.place.side,
                )
            )
        return out

    def own_copies(self):
        dp = self.place.dp
        return [
            pltpu.make_async_copy(
                source.at[rows_of(dp, target.shape[1])], target.at[dp], self.local.at[i]
            )
            for i, (source, target) in enumerate(self.pairs)
        ]


def back_kernel(
    bias_ref,
    cotangent_ref,
    middle_ref,
    probs_ref,
    exact_ref,
    stat_ref,
    query_ref,
    keys_ref,
    small_ref,
    out_ref,
    row_sum,
    out_sum,
    gate_sum,
    cosine_ref,
    sine_ref,
    gate_ref,
    up_ref,
    result_ref,
    grad_middle_ref,
    grad_branch_ref,
    grad_logits_ref,
    grad_project_ref,
    gain_ref,
    gate_back,
    up_back,
    grad_hidden,
    grad_ref,
    acc,
    delta,
    grad_keys_ref,
    land_core,
    land_x,
    land_z,
    scatter_send,
    recv_core,
    recv_x,
    recv_z,
    weight_send,
    weight_recv,
    weight_local,
):
    dp_count = keys_ref.shape[0]
    device_count = dp_count * lax.axis_size("expert")
    tok_count, model_width = middle_ref.shape
    query_width = HEADS * HEAD
    key_width = KV_HEADS * HEAD
    repeat_heads = HEADS // KV_HEADS
    scale = HEAD ** (-0.5)
    factor = log2e * scale
    chunk = 32
    place = Place()
    enter(device_count, dp_count)
    weights = WeightReturn(
        place,
        ((gate_ref, gate_back), (up_ref, up_back)),
        weight_send,
        weight_recv,
        weight_local,
        dp_count,
    )
    weights.start(1, dp_count)
    weights.start_own()
    scatter = Scatter(
        place,
        lambda index: grad_keys_ref.at[index],
        (land_core, land_x, land_z),
        scatter_send,
        (recv_core, recv_x, recv_z),
    )

    probs = probs_ref[...]
    grad_probs = gate_sum[...]
    grad_logits = (
        probs * (grad_probs - jnp.sum(probs * grad_probs, axis=-1, keepdims=True))
    ).astype(jnp.bfloat16)
    grad_logits_ref[...] = grad_logits

    @pl.loop(0, model_width // TILE)
    def _(tile):
        grad_hidden[:, columns(tile)] = row_sum[:, columns(tile)] + dot_f32(
            grad_logits_ref[...], small_ref[rows_of(tile, TILE)], ((1,), (1,))
        )

    gain = gain_rows(small_ref[...])[1:2]
    gain_ref[...] = jnp.zeros(gain_ref.shape, jnp.float32)

    @pl.loop(0, tok_count // chunk)
    def _(index):
        cut = rows_of(index, chunk)
        value = middle_ref[cut]
        row_scale = lax.rsqrt(jnp.mean(value * value, axis=-1, keepdims=True) + epsilon)
        normed = value * row_scale
        grad = grad_hidden[cut]
        gain_ref[0:1] += jnp.sum(grad * normed, axis=0, keepdims=True)
        grad = grad * gain
        total = cotangent_ref[cut].astype(jnp.float32) + row_scale * (
            grad - normed * jnp.mean(grad * normed, axis=-1, keepdims=True)
        )
        grad_middle_ref[cut] = total
        grad_branch_ref[cut] = total.astype(jnp.bfloat16)

    @pl.loop(0, model_width // TILE)
    def _(tile):
        grad_ref[:, columns(tile)] = dot_f32(
            grad_branch_ref[...], out_ref[rows_of(tile, TILE)], ((1,), (1,))
        ).astype(jnp.bfloat16)

    for head in range(HEADS):
        cut = slice(head * HEAD, (head + 1) * HEAD)
        scaled = (
            grad_ref[:, cut].astype(jnp.float32) * stat_ref[:, HEADS + head : HEADS + head + 1]
        ).astype(jnp.bfloat16)
        grad_ref[:, cut] = scaled
        delta[head] = jnp.sum(
            scaled.astype(jnp.float32) * exact_ref[:, cut], axis=-1, keepdims=True
        )
    row = lax.broadcasted_iota(jnp.int32, (tok_count, tok_count), 0)
    column = lax.broadcasted_iota(jnp.int32, (tok_count, tok_count), 1)
    causal = column <= row

    @pl.loop(place.dp + 1, dp_count)
    def _(label):
        grad_keys_ref[label] = jnp.zeros(grad_keys_ref.shape[1:], jnp.bfloat16)

    def visit(label, own):
        for group in range(KV_HEADS):
            key_cut = slice(group * HEAD, (group + 1) * HEAD)
            value_cut = slice((KV_HEADS + group) * HEAD, (KV_HEADS + group + 1) * HEAD)
            key = keys_ref[label, :, key_cut]
            value = keys_ref[label, :, value_cut]
            grad_key = jnp.zeros((tok_count, HEAD), jnp.float32)
            grad_value = jnp.zeros((tok_count, HEAD), jnp.float32)
            for head in range(group * repeat_heads, (group + 1) * repeat_heads):
                cut = slice(head * HEAD, (head + 1) * HEAD)
                query = query_ref[:, cut]
                grad = grad_ref[:, cut]
                shift = stat_ref[:, head : head + 1]
                if not own:
                    shift = shift - bias_ref[label]
                scores = dot_f32(query, key, ((1,), (1,)))
                prob = jnp.exp2(scores * factor - shift)
                if own:
                    prob = jnp.where(causal, prob, 0.0)
                prob = prob.astype(jnp.bfloat16)
                grad_prob = dot_f32(grad, value, ((1,), (1,)))
                grad_score = (prob.astype(jnp.float32) * (grad_prob - delta[head])).astype(
                    jnp.bfloat16
                )
                grad_value += dot_f32(prob, grad, ((0,), (0,)))
                grad_key += dot_f32(grad_score, query, ((0,), (0,)))
                grad_query = dot_f32(grad_score, key)
                if own:
                    acc[head] = grad_query
                else:
                    acc[head] += grad_query
            grad_keys_ref[label, :, key_cut] = (grad_key * scale).astype(jnp.bfloat16)
            grad_keys_ref[label, :, value_cut] = grad_value.astype(jnp.bfloat16)

    visit(place.dp, True)

    @pl.loop(0, place.dp)
    def _(label):
        visit(label, False)

    scatter.start()
    cosine, sine = cosine_ref[...], -sine_ref[...]
    for head in range(HEADS):
        grad_project_ref[:, head * HEAD : (head + 1) * HEAD] = halves_turned(
            acc[head] * scale, cosine, sine
        ).astype(jnp.bfloat16)
    scatter.pass_core()
    scatter.pass_x()

    result_ref[...] = (middle_ref[...] + out_sum[...]).astype(jnp.bfloat16)

    def put(cut, value):
        grad_project_ref[cut, query_width : query_width + key_width] = halves_turned(
            value[:, :key_width], cosine_ref[cut], -sine_ref[cut]
        ).astype(jnp.bfloat16)
        grad_project_ref[cut, query_width + key_width :] = value[:, key_width:].astype(jnp.bfloat16)

    scatter.pass_z(put)
    scatter.finish()
    weights.finish()


def back(
    bias, cotangent, middle, probs, exact, stats, query, keys, small, out, row_sum, out_sum, gate_sum,
    cosine, sine, gate_grad, up_grad, shard,
):
    dp_count, tok_count, both = keys.shape
    model_width = middle.shape[1]
    ff_width = gate_grad.shape[1]
    vmem = pl.BlockSpec(memory_space=pltpu.VMEM)
    anywhere = pl.BlockSpec(memory_space=pl.ANY)
    low, full = jnp.bfloat16, jnp.float32
    shape = jax.ShapeDtypeStruct
    dma = pltpu.SemaphoreType.DMA
    return pl.pallas_call(
        back_kernel,
        out_shape=(
            shape((tok_count, model_width), low),
            shape((tok_count, model_width), full),
            shape((tok_count, model_width), low),
            shape((tok_count, LANES), low),
            shape((tok_count, query.shape[1] + both), low),
            shape((8, model_width), full),
            shape((dp_count, shard, ff_width), low),
            shape((dp_count, shard, ff_width), low),
        ),
        in_specs=[pl.BlockSpec(memory_space=pltpu.SMEM)] + [vmem] * 14 + [anywhere] * 2,
        out_specs=(vmem,) * 6 + (anywhere,) * 2,
        scratch_shapes=[
            pltpu.VMEM((tok_count, model_width), full),
            pltpu.VMEM((tok_count, model_width), low),
            pltpu.VMEM((HEADS, tok_count, HEAD), full),
            pltpu.VMEM((HEADS, tok_count, 1), full),
            pltpu.VMEM((dp_count, tok_count, both), low),
            pltpu.VMEM((8, tok_count, both), low),
            pltpu.VMEM((4, tok_count, both), low),
            pltpu.VMEM((3, tok_count, both), low),
            dma((15,)),
            dma((8,)),
            dma((4,)),
            dma((3,)),
            dma((dp_count, 2)),
            dma((dp_count, 2)),
            dma((2,)),
        ],
        compiler_params=pltpu.CompilerParams(
            collective_id=2, has_side_effects=True, vmem_limit_bytes=60 * 1024 * 1024
        ),
    )(
        bias, cotangent, middle, probs, exact, stats, query, keys, small, out, row_sum, out_sum, gate_sum,
        cosine, sine, gate_grad, up_grad,
    )


def finish_kernel(
    tokens_ref,
    hidden_one,
    hidden_two,
    attended_ref,
    grad_middle_ref,
    grad_branch_ref,
    grad_logits_ref,
    grad_project_ref,
    gain_ref,
    project_ref,
    down_ref,
    grad_tokens_ref,
    mine_ref,
    down_back,
    grad_hidden,
    gain_one,
    part_one,
    core_one,
    x_one,
    side_one,
    z_one,
    home_one,
    part_two,
    core_two,
    x_two,
    side_two,
    z_two,
    home_two,
    send_one,
    recv_one,
    send_two,
    recv_two,
    weight_send,
    weight_recv,
    weight_local,
):
    tok_count, model_width = tokens_ref.shape
    width = grad_project_ref.shape[1]
    dp_count = lax.axis_size("dp")
    device_count = dp_count * lax.axis_size("expert")
    shard = mine_ref.shape[0]
    place = Place()
    chunk = 32
    enter(device_count, dp_count)
    weights = WeightReturn(
        place, ((down_ref, down_back),), weight_send, weight_recv, weight_local, dp_count
    )
    weights.start(1, dp_count)
    weights.start_own()
    one = TotalSum(place, part_one, (core_one, x_one, side_one, z_one, home_one), send_one, recv_one, True)
    two = TotalSum(place, part_two, (core_two, x_two, side_two, z_two, home_two), send_two, recv_two, False)
    cut_at = part_one.shape[2]

    @pl.loop(0, model_width // TILE)
    def _(tile):
        grad_hidden[:, columns(tile)] = dot_f32(
            grad_project_ref[...], project_ref[rows_of(tile, TILE), :width], ((1,), (1,))
        )

    gain = gain_rows(project_ref[:, width:])[0:1]
    gain_one[...] = jnp.zeros(gain_one.shape, jnp.float32)

    @pl.loop(0, tok_count // chunk)
    def _(index):
        cut = rows_of(index, chunk)
        value = tokens_ref[cut].astype(jnp.float32)
        row_scale = lax.rsqrt(jnp.mean(value * value, axis=-1, keepdims=True) + epsilon)
        normed = value * row_scale
        grad = grad_hidden[cut]
        gain_one[0:1] += jnp.sum(grad * normed, axis=0, keepdims=True)
        grad = grad * gain
        grad_tokens_ref[cut] = grad_middle_ref[cut] + row_scale * (
            grad - normed * jnp.mean(grad * normed, axis=-1, keepdims=True)
        )

    one_lane = one_hot((8, LANES), lambda r, col: (r == 0) & (col == EXPERTS))
    two_lane = one_hot((8, LANES), lambda r, col: (r == 0) & (col == EXPERTS + 1))
    group = 4 * shard

    @pl.loop(0, model_width // group)
    def _(index):
        cut = columns(index, group)

        def put(part, low, value):
            for i in range(4):
                part[index * 4 + i, :, low : low + value.shape[1]] = value[
                    i * shard : (i + 1) * shard
                ].astype(jnp.bfloat16)

        left = hidden_one[:, cut]
        step = 3 * LANES
        for low in range(0, cut_at, step):
            put(part_one, low, dot_f32(left, grad_project_ref[:, low : low + step], ((0,), (0,))))
        rest = width - cut_at
        put(part_two, 0, dot_f32(left, grad_project_ref[:, cut_at:], ((0,), (0,))))
        small = dot_f32(hidden_two[:, cut], grad_logits_ref[...], ((0,), (0,)))
        for part in split3(gain_one[:, cut]):
            small += dot_f32(part, one_lane, ((0,), (0,)))
        for part in split3(gain_ref[:, cut]):
            small += dot_f32(part, two_lane, ((0,), (0,)))
        put(part_two, rest, small)
        left = attended_ref[:, cut]
        for low in range(0, model_width, step):
            put(
                part_two,
                rest + LANES + low,
                dot_f32(left, grad_branch_ref[:, low : low + step], ((0,), (0,))),
            )
        for total in (one, two):
            total.start(index)

    order = place.others() + [place.z]
    both = (one, two)
    for z in order:
        for total in both:
            total.first(z)
    for z in order:
        for total in both:
            total.second(z)
    for i, z in enumerate(order):
        for total in both:
            total.third(z, i)
    for total in both:
        total.fourth()
    one.finish(mine_ref, slice(0, cut_at))
    two.finish(mine_ref, slice(cut_at, mine_ref.shape[1]))
    weights.finish()


def finish(
    tokens, hidden_one, hidden_two, attended, grad_middle, grad_branch, grad_logits, grad_project,
    gain, project, down_grad, shard, half,
):
    tok_count, model_width = tokens.shape
    dp_count = lax.axis_size("dp")
    width = project.shape[1] + model_width
    first = 15 * LANES
    vmem = pl.BlockSpec(memory_space=pltpu.VMEM)
    anywhere = pl.BlockSpec(memory_space=pl.ANY)
    low, full = jnp.bfloat16, jnp.float32
    shape = jax.ShapeDtypeStruct
    dma = pltpu.SemaphoreType.DMA
    return pl.pallas_call(
        finish_kernel,
        out_shape=(
            shape((tok_count, model_width), full),
            shape((shard, width), full),
            shape((dp_count, half, model_width), low),
        ),
        in_specs=[vmem] * 10 + [anywhere],
        out_specs=(vmem, vmem, anywhere),
        scratch_shapes=[
            pltpu.VMEM((tok_count, model_width), full),
            pltpu.VMEM((8, model_width), full),
            *(
                pltpu.VMEM(lead + (columns_of,), low)
                for columns_of, lead in (
                    (first, (dp_count, shard)),
                    (first, (8, shard)),
                    (first, (4, shard)),
                    (first, (4, shard // 2)),
                    (first, (3, shard // 2)),
                    (first, (shard // 2,)),
                    (width - first, (dp_count, shard)),
                    (width - first, (8, shard)),
                    (width - first, (4, shard // 2)),
                    (width - first, (8, shard // 2)),
                    (width - first, (3, shard // 2)),
                    (width - first, (shard // 2,)),
                )
            ),
            dma((24,)),
            dma((24,)),
            dma((24,)),
            dma((24,)),
            dma((dp_count, 1)),
            dma((dp_count, 1)),
            dma((1,)),
        ],
        compiler_params=pltpu.CompilerParams(
            collective_id=3, has_side_effects=True, vmem_limit_bytes=58 * 1024 * 1024
        ),
    )(
        tokens, hidden_one, hidden_two, attended, grad_middle, grad_branch, grad_logits,
        grad_project, gain, project, down_grad,
    )


def local_owned(
    tokens,
    attn_gain,
    query_weight,
    key_weight,
    value_weight,
    out_weight,
    moe_gain,
    router_weight,
    gate_weight,
    up_weight,
    down_weight,
    parents,
    routes,
    claim_order,
    cotangent,
):
    tok_count = tokens.shape[1]
    segment = lax.axis_index("dp")
    query_width = HEADS * HEAD
    key_width = KV_HEADS * HEAD

    route_rows = routes[0]
    expert_ids = route_rows.reshape(-1)
    order_row = claim_order[0, 0]
    member = (expert_ids[:, None] == jnp.arange(EXPERTS, dtype=jnp.int32)[None, :]).astype(
        jnp.bfloat16
    )
    earlier = (order_row[None, :] < order_row[:, None]).astype(jnp.bfloat16)
    before = jnp.dot(earlier, member, preferred_element_type=jnp.float32)
    slot_index = jnp.sum(before * member.astype(jnp.float32), axis=1).astype(jnp.int32)
    target = jnp.where(slot_index < CAP, expert_ids * SLOTS + slot_index, -1).reshape(
        tok_count, TOP
    )
    target_rows = jnp.full((8, TILE), -1.0, jnp.float32)
    target_rows = target_rows.at[:TOP, :tok_count].set(target.T.astype(jnp.float32))
    route_lanes = jnp.pad(route_rows, ((0, 0), (0, LANES - TOP)), constant_values=-1)

    small = jnp.concatenate(
        [
            router_weight,
            attn_gain[:, None],
            moe_gain[:, None],
            jnp.zeros((router_weight.shape[0], LANES - EXPERTS - 2), jnp.bfloat16),
        ],
        axis=1,
    )
    project_shard = jnp.concatenate([query_weight, key_weight, value_weight, small], axis=1)
    reach_row = ancestry(parents[0])[segment]
    path_depth = jnp.sum(reach_row) - 1.0
    positions = path_depth * tok_count + jnp.arange(tok_count, dtype=jnp.float32)
    cosine, sine_part = rope_tables(positions, HEAD)
    cosine_wide = jnp.concatenate([cosine[:, 0], cosine[:, 0]], axis=1)
    sine_wide = jnp.concatenate([-sine_part[:, 0], sine_part[:, 0]], axis=1)
    on_path = reach_row > 0.5
    bias = jnp.where(on_path, 0.0, -1e30).astype(jnp.float32)
    (
        project_full,
        out_full,
        keys,
        query_rot,
        attended,
        exact_out,
        stats,
        middle,
        hidden_two,
        probs,
        rows_in,
        grad_rows_in,
        gate_own,
        up_own,
        down_own,
        hidden_one,
        target_all,
        gate_all,
    ) = front(
        bias,
        tokens[0],
        cotangent[0],
        project_shard,
        out_weight,
        target_rows,
        route_lanes,
        cosine_wide,
        sine_wide,
        gate_weight,
        up_weight,
        down_weight,
    )
    small_at = query_width + 2 * key_width
    row_sum, out_sum, gate_sum, gate_grad, up_grad, down_grad = experts(
        rows_in, grad_rows_in, gate_own, up_own, down_own, target_all, gate_all, tok_count
    )
    (
        block_out,
        grad_middle,
        grad_branch,
        grad_logits,
        grad_project,
        gain_row,
        gate_back,
        up_back,
    ) = back(
        bias,
        cotangent[0],
        middle,
        probs,
        exact_out,
        stats,
        query_rot,
        keys,
        project_full[:, small_at:],
        out_full,
        row_sum,
        out_sum,
        gate_sum,
        cosine_wide,
        sine_wide,
        gate_grad,
        up_grad,
        gate_weight.shape[1],
    )
    grad_tokens, mine, down_back = finish(
        tokens[0],
        hidden_one,
        hidden_two,
        attended,
        grad_middle,
        grad_branch,
        grad_logits,
        grad_project,
        gain_row,
        project_full,
        down_grad,
        query_weight.shape[0],
        down_weight.shape[1],
    )
    return (
        block_out[None],
        grad_tokens[None],
        mine[:, small_at + EXPERTS],
        mine[:, :query_width],
        mine[:, query_width : query_width + key_width],
        mine[:, query_width + key_width : small_at],
        mine[:, small_at + LANES :],
        mine[:, small_at + EXPERTS + 1],
        mine[:, small_at : small_at + EXPERTS],
        gate_back.astype(jnp.float32),
        up_back.astype(jnp.float32),
        down_back.astype(jnp.float32),
    )


def solution(mesh):
    placed = (
        P("expert", "dp", None),
        P("dp"),
        P("dp", None),
        P("dp", None),
        P("dp", None),
        P("dp", None),
        P("dp"),
        P("dp", None),
        P("expert", "dp", None),
        P("expert", "dp", None),
        P("expert", "dp", None),
        P("expert", None),
        P("expert", "dp", None),
        P("expert", "dp", None),
        P("expert", "dp", None),
    )
    owned = mesh.shape["dp"] == 16 and mesh.shape["expert"] == 2
    return jax.shard_map(
        local_owned if owned else local_gathered,
        mesh=mesh,
        in_specs=placed,
        out_specs=(
            P("expert", "dp", None),
            P("expert", "dp", None),
            P("dp"),
            P("dp", None),
            P("dp", None),
            P("dp", None),
            P("dp", None),
            P("dp"),
            P("dp", None),
            P("expert", "dp", None),
            P("expert", "dp", None),
            P("expert", "dp", None),
        ),
        check_vma=False,
    )
```
